32 devices in a mesh: section: 2 (over core), dp: 4 (over z), ctx: 4 (over y, x).
Axes of the slice: x: 2, y: 2, z: 4, core: 2. Of those that a mesh axis runs over, the one named last changes fastest.
Arguments:
- ends: bfloat16 [2, 2, 3584, 960], P('section', None, ('dp', 'ctx')), may hold values from -6 to 6
- doc_lengths: int32 [2, 4, 2], P(None, 'dp'), may hold values from 0 to 896, as said below
- w_query: bfloat16 [960, 960], replicated, may hold values from -0.1875 to 0.1875
- key_projection_weight: bfloat16 [960, 320], replicated, may hold values from -0.1875 to 0.1875
- value_projection_weight: bfloat16 [960, 320], replicated, may hold values from -0.1875 to 0.1875
- w_out: bfloat16 [960, 960], replicated, may hold values from -0.75 to 0.75
- w_gate: bfloat16 [960, 2560], replicated, may hold values from -0.1875 to 0.1875
- w_up: bfloat16 [960, 2560], replicated, may hold values from -0.1875 to 0.1875
- w_down: bfloat16 [2560, 960], replicated, may hold values from -0.125 to 0.125
- gain_attn: bfloat16 [960], replicated, may hold values from 0.5 to 1.5
- gain_ffn: bfloat16 [960], replicated, may hold values from 0.5 to 1.5
Outputs:
- acts: bfloat16 [2, 2, 3584, 960], P('section', None, ('dp', 'ctx'))
- grads_in: bfloat16 [2, 2, 3584, 960], P('section', None, ('dp', 'ctx'))
- grad_w_query: float32 [960, 960], P('dp')
- grad_w_key: float32 [960, 320], P('dp')
- grad_w_value: float32 [960, 320], P('dp')
- grad_w_out: float32 [960, 960], P('dp')
- grad_w_gate: float32 [960, 2560], P('dp')
- grad_w_up: float32 [960, 2560], P('dp')
- grad_w_down: float32 [2560, 960], P('dp')
- grad_gain_attn: float32 [960], P('dp')
- grad_gain_ffn: float32 [960], P('dp')
The draws below stay inside these ranges and needn't reach their ends.
Inputs may be any that keep to these rules, and one draw needn't show every extreme that they name: `doc_lengths`: each row holds either one sequence of 896 tokens followed by an empty slot, or a sequence of 512 tokens followed by one of 384. Of the two micro-batches' rows at the same index of dimension 1, exactly one holds the single sequence.
All inputs are finite; a program needn't handle non-finite values.
Results may differ from the reference program's by a relative error of at most 0.028.
Values may be sent and summed in bfloat16 or wider, within the bound.
A program may use at most 192 MiB of HBM per device.

```python
import jax
import jax.numpy as jnp
from jax import lax

D = 960
QUERY_HEADS = 15
KEY_VALUE_HEADS = 5
HEAD_SIZE = 64
FF = 2560
MB = 2
NDOC = 2
QW = 960
KVW = 320
GROUP = 896
SHORTLEN = 512
TOKENS = 3584
N_DP = 4


def draw_doc_lengths(key, part):
    key = jax.random.fold_in(key, 11)
    single_micro = jax.random.randint(key, (1, N_DP), 0, MB)
    micro_index = jnp.arange(MB, dtype=jnp.int32)[:, None]
    single = micro_index == single_micro
    first_len = jnp.where(single, GROUP, SHORTLEN).astype(jnp.int32)
    second_len = (GROUP - first_len).astype(jnp.int32)
    return jnp.stack([first_len, second_len], axis=-1).astype(jnp.int32)


def steps_of(stream_key, shape, shards, smallest, high):
    def one(dim, blocks):
        draws = jax.random.uniform(jax.random.fold_in(jax.random.fold_in(stream_key, 6), dim), (blocks,), jnp.float32, smallest / len(shards), high / len(shards))
        return jnp.repeat(jnp.exp(draws), shape[dim] // blocks).reshape((-1,) + (1,) * (len(shape) - dim - 1))

    loudness = one(*shards[0])
    for cut in shards[1:]:
        loudness = loudness * one(*cut)
    return loudness


def gaussian(stream_key, shape, scale, limit, split=(), kind=jnp.bfloat16):
    loudness = steps_of(stream_key, shape, split, -0.22, 0.18) if split else 1.0
    drawn = jax.random.normal(stream_key, shape, jnp.float32) * scale * loudness
    return jnp.minimum(jnp.maximum(drawn, -limit), limit).astype(kind)


def setup_inputs(seed: int = 0) -> dict:
    key_list = jax.random.split(jax.random.key(seed), 12)
    ends = gaussian(key_list[0], (2, MB, TOKENS, D), 1.0, 6.0, ((0, 2), (2, 16)))
    doc_lengths = draw_doc_lengths(jax.random.fold_in(key_list[11], 71), 0)
    w_query = gaussian(key_list[2], (D, QW), D ** -0.5, 0.1875)
    key_projection_weight = gaussian(key_list[3], (D, KVW), D ** -0.5, 0.1875)
    value_projection_weight = gaussian(key_list[4], (D, KVW), D ** -0.5, 0.1875)
    w_out = gaussian(key_list[5], (QW, D), (D // 16) ** -0.5, 0.75)
    w_gate = gaussian(key_list[6], (D, FF), D ** -0.5, 0.1875)
    w_up = gaussian(key_list[7], (D, FF), D ** -0.5, 0.1875)
    w_down = gaussian(key_list[8], (FF, D), FF ** -0.5, 0.125)
    gain_attn = jnp.clip(1.0 + 0.1 * jax.random.normal(key_list[9], (D,), jnp.float32), 0.5, 1.5).astype(jnp.bfloat16)
    gain_ffn = jnp.clip(1.0 + 0.1 * jax.random.normal(key_list[10], (D,), jnp.float32), 0.5, 1.5).astype(jnp.bfloat16)
    return {"ends": ends, "doc_lengths": doc_lengths, "w_query": w_query, "key_projection_weight": key_projection_weight, "value_projection_weight": value_projection_weight, "w_out": w_out, "w_gate": w_gate, "w_up": w_up, "w_down": w_down, "gain_attn": gain_attn, "gain_ffn": gain_ffn}


highest = lax.Precision.HIGHEST
epsilon = 1e-05

@jax.custom_vjp
def lower_precision(v):
    return lax.optimization_barrier(v.astype(jnp.bfloat16)).astype(jnp.float32)

@jax.custom_vjp
def lower_precision_reverse(v):
    return v

def low_keep(v):
    return (lower_precision(v), None)

def low_pass(kept, grad):
    return (grad,)

def back_keep(v):
    return (v, None)

def back_low(kept, grad):
    return (lower_precision(grad),)
lower_precision.defvjp(low_keep, low_pass)
lower_precision_reverse.defvjp(back_keep, back_low)

def positions(lengths, grouped_row_block):
    lengths = lengths.astype(jnp.int32)
    finish = jnp.cumsum(lengths).astype(jnp.int32)
    token_index = jnp.arange(grouped_row_block, dtype=jnp.int32)
    passed = (token_index[:, None] >= finish[None, :]).astype(jnp.int32)
    segment = lax.optimization_barrier(jnp.sum(passed, axis=1)).astype(jnp.int32)
    token_position = (token_index - lax.optimization_barrier(jnp.sum(passed * lengths[None, :], axis=1))).astype(jnp.int32)
    return (segment, token_position)

def rotary_embed(heads, token_position, direction):
    half_width = heads.shape[-1] // 2
    frequency = 10000.0 ** (-2.0 * jnp.arange(half_width, dtype=jnp.float32) / heads.shape[-1])
    angles = token_position.astype(jnp.float32)[:, None] * frequency[None, :]
    cosines = jnp.cos(angles)[:, None, :]
    sines = direction * jnp.sin(angles)[:, None, :]
    front_half = heads[..., :half_width]
    back_half = heads[..., half_width:]
    return jnp.concatenate([front_half * cosines - back_half * sines, back_half * cosines + front_half * sines], axis=-1)

def norm_rows(hidden, gain_vec):
    return hidden * lax.rsqrt(lax.optimization_barrier(jnp.mean(hidden * hidden, axis=-1, keepdims=True)) + epsilon) * gain_vec

def matrix_multiply(left, right):
    return jnp.dot(left, right, precision=highest, preferred_element_type=jnp.float32)

def layer(hidden_in, params, segment, token_position):
    w_query, key_projection_weight, value_projection_weight, w_out, w_gate, w_up, w_down, gain_attn, gain_ffn = params
    grouped_row_block = hidden_in.shape[0]
    normalized_input = lower_precision(norm_rows(hidden_in, gain_attn))
    query_rows = lower_precision(rotary_embed(lower_precision_reverse(matrix_multiply(normalized_input, w_query)).reshape(grouped_row_block, QUERY_HEADS, HEAD_SIZE), token_position, 1.0))
    key_head_rows = lower_precision(rotary_embed(lower_precision_reverse(matrix_multiply(normalized_input, key_projection_weight)).reshape(grouped_row_block, KEY_VALUE_HEADS, HEAD_SIZE), token_position, 1.0))
    value_head_rows = lower_precision_reverse(lower_precision(matrix_multiply(normalized_input, value_projection_weight))).reshape(grouped_row_block, KEY_VALUE_HEADS, HEAD_SIZE)
    query_groups = query_rows.reshape(grouped_row_block, KEY_VALUE_HEADS, QUERY_HEADS // KEY_VALUE_HEADS, HEAD_SIZE)
    token_index = jnp.arange(grouped_row_block, dtype=jnp.int32)
    allowed = (segment[:, None] == segment[None, :]) & (token_index[:, None] >= token_index[None, :])
    raw_scores = jnp.einsum('qkgd,skd->kgqs', query_groups, key_head_rows, precision=highest) * 0.125
    scores = lower_precision_reverse(jnp.where(allowed[None, None], raw_scores, -1e+30))
    row_peak = lax.optimization_barrier(jnp.max(scores, axis=-1, keepdims=True))
    exponent = jnp.exp(scores - row_peak)
    soft_probs = lower_precision(exponent / lax.optimization_barrier(jnp.sum(exponent, axis=-1, keepdims=True)))
    mixed_heads = jnp.einsum('kgqs,skd->qkgd', soft_probs, value_head_rows, precision=highest).reshape(grouped_row_block, QUERY_HEADS * HEAD_SIZE)
    mixed_heads = lower_precision_reverse(lower_precision(mixed_heads))
    middle = hidden_in + lower_precision_reverse(matrix_multiply(mixed_heads, w_out))
    normed_ffn = lower_precision(norm_rows(middle, gain_ffn))
    gate_act = lower_precision_reverse(matrix_multiply(normed_ffn, w_gate))
    up_act = lower_precision_reverse(matrix_multiply(normed_ffn, w_up))
    inner_act = lower_precision(gate_act * jax.nn.sigmoid(gate_act) * up_act)
    return middle + lower_precision_reverse(matrix_multiply(inner_act, w_down))

def row_pass(row_input, row_probe, row_lengths, params):
    segment, token_position = positions(row_lengths, GROUP)
    first = lower_precision_reverse(lower_precision(layer(row_input, params, segment, token_position)) + row_probe)
    second = lower_precision(layer(first, params, segment, token_position))
    return (first, second)

def reference(ends, doc_lengths, w_query, key_projection_weight, value_projection_weight, w_out, w_gate, w_up, w_down, gain_attn, gain_ffn):
    row_count = MB * N_DP
    inputs = ends[0].astype(jnp.float32).reshape(row_count, GROUP, D)
    cotangent = ends[1].astype(jnp.float32).reshape(row_count, GROUP, D)
    lengths = doc_lengths.reshape(row_count, NDOC).astype(jnp.int32)
    params = tuple((weight.astype(jnp.float32) for weight in (w_query, key_projection_weight, value_projection_weight, w_out, w_gate, w_up, w_down, gain_attn, gain_ffn)))
    checked = jax.checkpoint(row_pass)

    def forward(input_rows, probe_rows, weights):

        def advance(carry, row_items):
            return (carry, checked(row_items[0], row_items[1], row_items[2], weights))
        unused, outputs = lax.scan(advance, jnp.zeros((), jnp.float32), (input_rows, probe_rows, lengths))
        return outputs
    probes = jnp.zeros_like(inputs)
    (first, second), pullback = jax.vjp(forward, inputs, probes, params)
    grad_inputs, grad_probes, grad_params = pullback((jnp.zeros_like(first), cotangent))
    acts = jnp.stack([first, second]).reshape(2, MB, TOKENS, D).astype(jnp.bfloat16)
    grads_in = jnp.stack([grad_inputs, grad_probes]).reshape(2, MB, TOKENS, D).astype(jnp.bfloat16)
    return (acts, grads_in, grad_params[0], grad_params[1], grad_params[2], grad_params[3], grad_params[4], grad_params[5], grad_params[6], grad_params[7], grad_params[8])
```

```python
import functools

import jax
import jax.numpy as jnp
from jax import lax
from jax.experimental import pallas as pl
from jax.experimental.pallas import tpu as pltpu
from jax.sharding import PartitionSpec as P

MESH = pl.DeviceIdType.MESH
QUERY_HEADS = 15
KEY_VALUE_HEADS = 5
HEAD_SIZE = 64
SHARE = QUERY_HEADS // KEY_VALUE_HEADS
RANKS = 4
epsilon = 1e-05
masked_fill = -1e30
F32 = jnp.float32
BF16 = jnp.bfloat16


def dot(left, right):
    return jnp.dot(left, right, preferred_element_type=F32)


def dot_rt(left, right):
    return lax.dot_general(left, right, (((1,), (1,)), ((), ())), preferred_element_type=F32)


def dot_lt(left, right):
    return lax.dot_general(left, right, (((0,), (0,)), ((), ())), preferred_element_type=F32)


def tiles(total, width):
    return [(at, min(width, total - at)) for at in range(0, total, width)]


def wide(block):
    missing = 128 - block.shape[1]
    if not missing:
        return block
    return jnp.concatenate([block, jnp.zeros((block.shape[0], missing), block.dtype)], axis=1)


def lanes(rows):
    return lax.broadcasted_iota(jnp.int32, (rows, 128), 1)


def half_turn(block):
    front = lanes(block.shape[0]) % HEAD_SIZE < HEAD_SIZE // 2
    return jnp.where(front, pltpu.roll(block, 96, 1), pltpu.roll(block, 32, 1))


def inverse_rms(hidden):
    return lax.rsqrt(jnp.mean(hidden * hidden, axis=-1, keepdims=True) + epsilon)


def layers_kernel(
    ends, cosines, sines, seg_keys, seg_mine, gains, wq_h, wkv_h, wo_h, wg_h, wu_h, wd_h,
    acts_o, grads_o, gain_o, nf_o, in_o, gg_o, gu_o, br_o, la_o, ra_o, nr_o, kvg_o,
    wq, wkv, wo, wg, wu, wd,
    act, go, middle, norm_ffn, fact_a, fact_b, inner, lm, qd, kv, o_raw,
    sum_acc, gm, gg, gu, br, ra, dq_raw, pds, dkv, dkv_in, gkv,
    w_sem, in_send, in_recv, kv_send, kv_recv, dk_send, dk_recv, out_send, out_recv,
    op_own, op_send, op_recv,
):
    section = lax.axis_index("section")
    dp = lax.axis_index("dp")
    ctx = lax.axis_index("ctx")
    micro = ctx // 2
    xbit = ctx % 2
    rank = 2 * section + xbit
    rows, width = act.shape[1], act.shape[2]
    ff = wg.shape[1]
    ff_half = ff // 2

    def device_of(r):
        return (r // 2, dp, 2 * micro + r % 2)

    partner = (1 - section, dp, ctx)

    loads = [
        pltpu.make_async_copy(h, v, w_sem.at[i])
        for i, (h, v) in enumerate(
            [(wkv_h, wkv), (wq_h, wq), (wo_h, wo), (wg_h, wg), (wu_h, wu), (wd_h, wd)]
        )
    ]
    kv[...] = jnp.zeros_like(kv)
    barrier = pltpu.get_barrier_semaphore()
    for step in range(1, 8):
        other = (4 * section + ctx + step) % 8
        pl.semaphore_signal(
            barrier, inc=1, device_id=(other // 4, dp, other % 4), device_id_type=MESH
        )
    pl.semaphore_wait(barrier, 7)

    def in_copy(block, into_x):
        dst = act.at[0] if into_x else go.at[2]
        slot = 0 if into_x else 1
        return (
            pltpu.make_async_copy(ends.at[0, block], dst, in_recv.at[slot]),
            pltpu.make_async_remote_copy(
                src_ref=ends.at[0, block],
                dst_ref=dst,
                send_sem=in_send.at[block],
                recv_sem=in_recv.at[slot],
                device_id=(ctx // 2, dp, 2 * block + xbit),
                device_id_type=MESH,
            ),
        )

    def in_mine(block):
        return (section == ctx // 2) & (ctx // 2 == block)

    for block in range(2):
        for into_x in (True, False):
            here = section == (0 if into_x else 1)
            local, remote = in_copy(block, into_x)

            @pl.when(here & in_mine(block))
            def _(local=local):
                local.start()

            @pl.when(here & jnp.logical_not(in_mine(block)))
            def _(remote=remote):
                remote.start()

    for load in loads:
        load.start()

    lane = lanes(rows)
    low = lane < HEAD_SIZE
    cos_q = cosines[...]
    sin_q = sines[...]
    gain_attn = gains[0:1, :]
    gain_ffn = gains[1:2, :]

    def mask():
        query_index = rank * rows + lax.broadcasted_iota(jnp.int32, (rows, RANKS * rows), 0)
        key_index = lax.broadcasted_iota(jnp.int32, (rows, RANKS * rows), 1)
        ok = (seg_mine[:, 0:1] == seg_keys[0:1, :]) & (query_index >= key_index)
        return jnp.where(ok, 0.0, masked_fill)

    def kv_rows(l, r):
        return kv.at[l, pl.ds(pl.multiple_of(r * rows, 16), rows)]

    def kv_copy(l, quarter, dst, slot):
        return pltpu.make_async_remote_copy(
            src_ref=kv_rows(l, quarter),
            dst_ref=kv_rows(l, quarter),
            send_sem=kv_send.at[l, slot],
            recv_sem=kv_recv.at[l, quarter],
            device_id=device_of(dst),
            device_id_type=MESH,
        )

    kv_plan = [(0, 0, 1, 0), (0, 0, 2, 1), (1, 1, 2, 0), (1, 1, 3, 1), (2, 2, 3, 0)]
    kv_relay = (1, 0, 3, 2)

    def kv_start(l):
        for sender, quarter, dst, slot in kv_plan:

            @pl.when(rank == sender)
            def _(quarter=quarter, dst=dst, slot=slot):
                kv_copy(l, quarter, dst, slot).start()

    def kv_finish(l):
        @pl.when(rank == 1)
        def _():
            kv_copy(l, 0, 3, 2).wait_recv()
            kv_copy(l, 0, 3, 2).start()

        for quarter, receivers in ((0, (2, 3)), (1, (2, 3)), (2, (3,))):
            for receiver in receivers:

                @pl.when(rank == receiver)
                def _(quarter=quarter):
                    kv_copy(l, quarter, 0, 0).wait_recv()

    def kv_sent(l):
        for sender, quarter, dst, slot in kv_plan + [kv_relay]:

            @pl.when(rank == sender)
            def _(quarter=quarter, dst=dst, slot=slot):
                kv_copy(l, quarter, dst, slot).wait_send()

    def out_copy(array, out, l, kind):
        home = 2 * section + xbit
        return (
            pltpu.make_async_copy(array, out.at[0, micro], out_recv.at[kind, micro]),
            pltpu.make_async_remote_copy(
                src_ref=array,
                dst_ref=out.at[0, micro],
                send_sem=out_send.at[kind, l],
                recv_sem=out_recv.at[kind, micro],
                device_id=(l, dp, home),
                device_id_type=MESH,
            ),
        )

    def out_mine(l):
        return (section == l) & (ctx == 2 * section + xbit)

    def out_start(array, out, l, kind):
        local, remote = out_copy(array, out, l, kind)

        @pl.when(out_mine(l))
        def _():
            local.start()

        @pl.when(jnp.logical_not(out_mine(l)))
        def _():
            remote.start()

    place = [pl.ds((2 * c + l) * rows, rows) for c in range(2) for l in range(2)]

    def op_rows(l):
        return pl.ds(pl.multiple_of((2 * section + l) * rows, 16), rows)

    def op_copy(kind, l, own):
        role = section if own else 1 - section
        half = pl.ds(pl.multiple_of(role * ff_half, 128), ff_half)
        src = [
            lambda: norm_ffn.at[l],
            lambda: inner.at[l],
            lambda: gg.at[:, half],
            lambda: gu.at[:, half],
            lambda: br.at[:, pl.ds(pl.multiple_of(role * 512, 128), 512)],
            lambda: lm.at[l, role],
            lambda: ra.at[role],
            lambda: lm.at[l, 0],
            lambda: gkv.at[:, pl.ds(pl.multiple_of(role * 256, 128), 384)],
        ][kind]()
        dst = [nf_o, in_o, gg_o, gu_o, br_o, la_o, ra_o, nr_o, kvg_o][kind].at[op_rows(l)]
        if own:
            return pltpu.make_async_copy(src, dst, op_own.at[kind, l])
        return pltpu.make_async_remote_copy(
            src_ref=src,
            dst_ref=dst,
            send_sem=op_send.at[kind, l],
            recv_sem=op_recv.at[kind, l],
            device_id=partner,
            device_id_type=MESH,
        )

    def op_start(kinds, l):
        for kind in kinds:
            op_copy(kind, l, True).start()
            op_copy(kind, l, False).start()

    def op_sent(kinds, l):
        for kind in kinds:
            op_copy(kind, l, True).wait()
            op_copy(kind, l, False).wait_send()

    @pl.when(section == 0)
    def _():
        for block in range(2):

            @pl.when(jnp.logical_not(in_mine(block)))
            def _(block=block):
                in_copy(block, True)[1].wait_send()

    @pl.when(section == 1)
    def _():
        for block in range(2):

            @pl.when(jnp.logical_not(in_mine(block)))
            def _(block=block):
                in_copy(block, False)[1].wait_send()

    in_copy(0, True)[1].wait_recv()
    loads[0].wait()

    def forward(l, carry):
        hidden = act[l].astype(F32)
        lm[l, 0] = (hidden * inverse_rms(hidden) * gain_attn).astype(BF16)
        cos_kv = jnp.where(low, cos_q, 1.0)
        sin_kv = jnp.where(low, sin_q, 0.0)
        mine = pl.ds(pl.multiple_of(rank * rows, 16), rows)
        for g in range(KEY_VALUE_HEADS):
            block = dot(lm[l, 0], wkv[:, 128 * g : 128 * g + 128])
            turned = block * cos_kv + half_turn(block) * sin_kv
            kv[l, mine, 128 * g : 128 * g + 128] = turned.astype(BF16)
        kv_start(l)

        @pl.when(l == 0)
        def _():
            loads[1].wait()

        for at, size in tiles(width, 256):
            product = dot(lm[l, 0], wq[:, at : at + size])
            for inside, part in tiles(size, 128):
                block = wide(product[:, inside : inside + part])
                turned = (block * cos_q + half_turn(block) * sin_q) * 0.125
                head = (at + inside) // HEAD_SIZE
                qd[l, head // SHARE, pl.ds(head % SHARE * rows, rows), :] = jnp.where(
                    low, turned, 0.0
                ).astype(BF16)
                head += 1
                if head < QUERY_HEADS:
                    qd[l, head // SHARE, pl.ds(head % SHARE * rows, rows), :] = jnp.where(
                        low, pltpu.roll(turned, 64, 1), 0.0
                    ).astype(BF16)
        kv_finish(l)
        allowed = mask()

        def heads(g, carry):
            kv_g = kv[l, :, pl.ds(pl.multiple_of(g * 128, 128), 128)]
            for i in range(SHARE):
                scores = dot_rt(qd[l, g, i * rows : (i + 1) * rows, :], kv_g) + allowed
                peak = jnp.max(scores, axis=-1, keepdims=True)
                exponent = jnp.exp(scores - peak)
                total = jnp.sum(exponent, axis=-1, keepdims=True)
                out = dot(exponent.astype(BF16), kv_g) / total
                o_raw[l, g * SHARE + i] = jnp.where(low, peak + jnp.log(total), out)
            return carry

        lax.fori_loop(0, KEY_VALUE_HEADS, heads, 0)
        for at, size in tiles(width, 128):
            head = at // HEAD_SIZE
            block = pltpu.roll(o_raw[l, head], 64, 1)
            if size == 128:
                block = jnp.where(low, block, o_raw[l, head + 1])
            lm[l, 1, :, at : at + size] = block[:, :size].astype(BF16)

        @pl.when(l == 0)
        def _():
            loads[2].wait()

        for at, size in tiles(width, 256):
            middle[l, :, at : at + size] = act[l, :, at : at + size].astype(F32) + dot(
                lm[l, 1], wo[:, at : at + size]
            )
        mid = middle[l]
        norm_ffn[l] = (mid * inverse_rms(mid) * gain_ffn).astype(BF16)

        @pl.when(l == 0)
        def _():
            loads[3].wait()
            loads[4].wait()

        def gates(j, carry):
            part = pl.ds(pl.multiple_of(j * 256, 256), 256)
            gate = dot(norm_ffn[l], wg[:, part])
            upper = dot(norm_ffn[l], wu[:, part])
            s = jax.nn.sigmoid(gate)
            swish = gate * s
            inner[l, :, part] = (swish * upper).astype(BF16)
            fact_a[l, :, part] = (upper * s * (1.0 + gate * (1.0 - s))).astype(BF16)
            fact_b[l, :, part] = swish.astype(BF16)
            return carry

        lax.fori_loop(0, ff // 256, gates, 0)

        @pl.when(l == 0)
        def _():
            loads[5].wait()

        for at, size in tiles(width, 256):
            act[l + 1, :, at : at + size] = (
                middle[l, :, at : at + size] + dot(inner[l], wd[:, at : at + size])
            ).astype(BF16)
        out_start(act.at[l + 1], acts_o, l, 0)
        op_start((0, 1, 7), l)
        kv_sent(l)
        return carry

    lax.fori_loop(0, 2, forward, 0)

    in_copy(0, False)[1].wait_recv()
    gain_o[...] = jnp.zeros_like(gain_o)
    br[...] = jnp.zeros_like(br)

    def dk_copy(l, src_quarter, count, dst, slot_in, slot):
        return pltpu.make_async_remote_copy(
            src_ref=dkv.at[pl.ds(src_quarter * rows, count * rows)],
            dst_ref=dkv_in.at[l, pl.ds(slot_in * rows, count * rows)],
            send_sem=dk_send.at[l, slot],
            recv_sem=dk_recv.at[l, slot_in],
            device_id=device_of(dst),
            device_id_type=MESH,
        )

    def backward(step, carry):
        l = 1 - step

        @pl.when(l == 0)
        def _():
            op_sent((2, 3, 4, 5, 6, 8), 1)

        branch = go[l + 1]
        br[:, :width] = branch
        op_start((4,), l)

        def gates(j, carry):
            part = pl.ds(pl.multiple_of(j * 256, 256), 256)
            grad_inner = dot_rt(go[l + 1], wd[part, :])
            gg[:, part] = (grad_inner * fact_a[l, :, part].astype(F32)).astype(BF16)
            gu[:, part] = (grad_inner * fact_b[l, :, part].astype(F32)).astype(BF16)
            return carry

        lax.fori_loop(0, ff // 256, gates, 0)
        op_start((2, 3), l)
        for at, size in tiles(width, 256):
            sum_acc[:, at : at + size] = dot_rt(gg[...], wg[at : at + size, :]) + dot_rt(
                gu[...], wu[at : at + size, :]
            )

        def norm_back(hidden, gain, row):
            upstream = sum_acc[...]
            scale = inverse_rms(hidden)
            weighted = upstream * gain
            inside = jnp.mean(weighted * hidden, axis=-1, keepdims=True)
            gain_o[row : row + 1, :] += jnp.sum(upstream * hidden * scale, axis=0, keepdims=True)
            return scale * weighted - hidden * (scale * scale * scale * inside)

        gm[...] = go[l + 1].astype(F32) + norm_back(middle[l], gain_ffn, 1)
        ra[1] = gm[...].astype(BF16)

        for at, size in tiles(width, 256):
            product = dot_rt(ra[1], wo[at : at + size, :])
            for inside, part in tiles(size, 128):
                block = wide(product[:, inside : inside + part])
                head = (at + inside) // HEAD_SIZE
                qd[l, head // SHARE, pl.ds((SHARE + head % SHARE) * rows, rows), :] = jnp.where(
                    low, 0.0, pltpu.roll(block, 64, 1)
                ).astype(BF16)
                head += 1
                if head < QUERY_HEADS:
                    qd[l, head // SHARE, pl.ds((SHARE + head % SHARE) * rows, rows), :] = (
                        jnp.where(low, 0.0, block).astype(BF16)
                    )
        allowed = mask()

        def heads(g, carry):
            kv_g = kv[l, :, pl.ds(pl.multiple_of(g * 128, 128), 128)]
            for i in range(SHARE):
                mine = slice(i * rows, (i + 1) * rows)
                other = slice((SHARE + i) * rows, (SHARE + i + 1) * rows)
                kept = o_raw[l, g * SHARE + i]
                log_total = kept[:, 0:1]
                scores = dot_rt(qd[l, g, mine, :], kv_g) + allowed
                probs = jnp.exp(scores - log_total)
                grad_out = qd[l, g, other, :]
                grad_probs = dot_rt(grad_out, kv_g)
                weight = jnp.sum(grad_out.astype(F32) * kept, axis=-1, keepdims=True)
                grad_scores = (probs * (grad_probs - weight)).astype(BF16)
                pds[mine, :] = grad_scores
                pds[other, :] = probs.astype(BF16)
                dq_raw[g * SHARE + i] = dot(grad_scores, kv_g)
            grad_kv = dot_lt(qd[l, g], pds[...])
            dkv[:, pl.ds(pl.multiple_of(g * 128, 128), 128)] = grad_kv.T.astype(BF16)
            return carry

        lax.fori_loop(0, KEY_VALUE_HEADS, heads, 0)

        @pl.when(rank == 3)
        def _():
            dk_copy(l, 2, 1, 2, 0, 0).start()
            dk_copy(l, 0, 2, 1, 0, 1).start()

        @pl.when(rank == 2)
        def _():
            dk_copy(l, 1, 1, 1, 2, 0).start()
            dk_copy(l, 0, 1, 0, 1, 1).start()

        @pl.when(rank == 1)
        def _():
            dk_copy(l, 0, 2, 1, 0, 0).wait_recv()
            dkv[:rows] = (dkv[:rows].astype(F32) + dkv_in[l, :rows].astype(F32)).astype(BF16)
            dk_copy(l, 0, 1, 0, 0, 0).start()

        for at, size in tiles(width, 128):
            head = at // HEAD_SIZE
            block = dq_raw[head]
            if size == 128:
                block = jnp.where(low, block, pltpu.roll(dq_raw[head + 1], 64, 1))
            turned = (block * cos_q - half_turn(block) * sin_q) * 0.125
            ra[0, :, at : at + size] = turned[:, :size].astype(BF16)
        op_start((5, 6), l)

        @pl.when(rank == 3)
        def _():
            dk_copy(l, 2, 1, 2, 0, 0).wait_send()
            dk_copy(l, 0, 2, 1, 0, 1).wait_send()

        @pl.when(rank == 2)
        def _():
            dk_copy(l, 0, 1, 2, 0, 0).wait_recv()
            dk_copy(l, 1, 1, 1, 2, 0).wait_send()
            dk_copy(l, 0, 1, 0, 1, 1).wait_send()
            dkv[2 * rows : 3 * rows] = (
                dkv[2 * rows : 3 * rows].astype(F32) + dkv_in[l, :rows].astype(F32)
            ).astype(BF16)

        @pl.when(rank == 1)
        def _():
            dk_copy(l, 0, 1, 2, 2, 0).wait_recv()
            dk_copy(l, 0, 1, 0, 0, 0).wait_send()
            dkv[rows : 2 * rows] = (
                dkv[rows : 2 * rows].astype(F32)
                + dkv_in[l, rows : 2 * rows].astype(F32)
                + dkv_in[l, 2 * rows :].astype(F32)
            ).astype(BF16)

        @pl.when(rank == 0)
        def _():
            dk_copy(l, 0, 1, 2, 0, 0).wait_recv()
            dk_copy(l, 0, 1, 2, 1, 0).wait_recv()
            dkv[:rows] = (
                dkv[:rows].astype(F32)
                + dkv_in[l, :rows].astype(F32)
                + dkv_in[l, rows : 2 * rows].astype(F32)
            ).astype(BF16)

        cos_kv = jnp.where(low, cos_q, 1.0)
        sin_kv = jnp.where(low, sin_q, 0.0)
        mine = pl.ds(pl.multiple_of(rank * rows, 16), rows)
        for g in range(KEY_VALUE_HEADS):
            part = slice(128 * g, 128 * g + 128)
            block = dkv[mine, part].astype(F32)
            gkv[:, part] = (block * cos_kv - half_turn(block) * sin_kv).astype(BF16)
        op_start((8,), l)
        for at, size in tiles(width, 256):
            sum_acc[:, at : at + size] = dot_rt(ra[0], wq[at : at + size, :]) + dot_rt(
                gkv[...], wkv[at : at + size, :]
            )
        go[l] = (gm[...] + norm_back(act[l].astype(F32), gain_attn, 0)).astype(BF16)
        out_start(go.at[l], grads_o, l, 1)
        return carry

    lax.fori_loop(0, 2, backward, 0)

    op_sent((2, 3, 4, 5, 6, 8), 0)
    for l in range(2):
        op_sent((0, 1, 7), l)
        for kind in range(9):
            op_copy(kind, l, False).wait_recv()
        for kind, out, array in ((0, acts_o, act.at[l + 1]), (1, grads_o, go.at[l])):

            @pl.when(jnp.logical_not(out_mine(l)))
            def _(l=l, kind=kind, out=out, array=array):
                out_copy(array, out, l, kind)[1].wait_send()

    for kind, out in ((0, acts_o), (1, grads_o)):
        for block in range(2):
            pltpu.make_async_copy(act.at[0], out.at[0, block], out_recv.at[kind, block]).wait()


def run_layers(ends, cosines, sines, seg_keys, seg_mine, gains, weights):
    micro_count, rows, width = ends.shape[1:]
    wq, wkv, wo, wg, wu, wd = weights
    ff = wg.shape[1]
    keys = RANKS * rows
    kv_width = wkv.shape[1]
    vmem, hbm = pl.BlockSpec(memory_space=pltpu.VMEM), pl.BlockSpec(memory_space=pl.ANY)
    op_rows = 4 * rows
    out = lambda *shape: jax.ShapeDtypeStruct(shape, BF16)
    dma = pltpu.SemaphoreType.DMA
    return pl.pallas_call(
        layers_kernel,
        out_shape=[
            out(*ends.shape),
            out(*ends.shape),
            jax.ShapeDtypeStruct((8, width), F32),
            out(op_rows, width),
            out(op_rows, ff),
            out(op_rows, ff // 2),
            out(op_rows, ff // 2),
            out(op_rows, 512),
            out(op_rows, width),
            out(op_rows, width),
            out(op_rows, width),
            out(op_rows, 384),
        ],
        in_specs=[hbm] + [vmem] * 5 + [hbm] * 6,
        out_specs=[hbm, hbm, vmem] + [hbm] * 9,
        scratch_shapes=[
            pltpu.VMEM(wq.shape, BF16),
            pltpu.VMEM(wkv.shape, BF16),
            pltpu.VMEM(wo.shape, BF16),
            pltpu.VMEM(wg.shape, BF16),
            pltpu.VMEM(wu.shape, BF16),
            pltpu.VMEM(wd.shape, BF16),
            pltpu.VMEM((3, rows, width), BF16),
            pltpu.VMEM((3, rows, width), BF16),
            pltpu.VMEM((2, rows, width), F32),
            pltpu.VMEM((2, rows, width), BF16),
            pltpu.VMEM((2, rows, ff), BF16),
            pltpu.VMEM((2, rows, ff), BF16),
            pltpu.VMEM((2, rows, ff), BF16),
            pltpu.VMEM((2, 2, rows, width), BF16),
            pltpu.VMEM((2, KEY_VALUE_HEADS, 2 * SHARE * rows, 128), BF16),
            pltpu.VMEM((2, keys, kv_width), BF16),
            pltpu.VMEM((2, QUERY_HEADS, rows, 128), F32),
            pltpu.VMEM((rows, width), F32),
            pltpu.VMEM((rows, width), F32),
            pltpu.VMEM((rows, ff), BF16),
            pltpu.VMEM((rows, ff), BF16),
            pltpu.VMEM((rows, 1024), BF16),
            pltpu.VMEM((2, rows, width), BF16),
            pltpu.VMEM((QUERY_HEADS, rows, 128), F32),
            pltpu.VMEM((2 * SHARE * rows, keys), BF16),
            pltpu.VMEM((keys, kv_width), BF16),
            pltpu.VMEM((2, 3 * rows, kv_width), BF16),
            pltpu.VMEM((rows, kv_width), BF16),
            dma((6,)),
            dma((2,)),
            dma((2,)),
            dma((2, 3)),
            dma((2, 3)),
            dma((2, 2)),
            dma((2, 3)),
            dma((2, 2)),
            dma((2, 2)),
            dma((9, 2)),
            dma((9, 2)),
            dma((9, 2)),
        ],
        compiler_params=pltpu.CompilerParams(
            collective_id=1, has_side_effects=True, vmem_limit_bytes=61 * 2**20
        ),
        name="layers",
    )(ends, cosines, sines, seg_keys, seg_mine, gains, wq, wkv, wo, wg, wu, wd)


def shards(
    ends,
    doc_lengths,
    w_query,
    key_projection_weight,
    value_projection_weight,
    w_out,
    w_gate,
    w_up,
    w_down,
    gain_attn,
    gain_ffn,
):
    rows, width = ends.shape[2:]
    section = lax.axis_index("section")
    ctx = lax.axis_index("ctx")
    row_tokens = rows * lax.axis_size("ctx")
    rank = 2 * section + ctx % 2
    lengths = lax.dynamic_index_in_dim(doc_lengths, ctx // 2, 0, keepdims=False)[0]

    def place(token_index):
        segment = jnp.zeros_like(token_index)
        start = jnp.zeros_like(token_index)
        finish = jnp.int32(0)
        for slot in range(lengths.shape[0]):
            finish = finish + lengths[slot]
            passed = (token_index >= finish).astype(jnp.int32)
            segment = segment + passed
            start = start + passed * lengths[slot]
        return segment, token_index - start

    seg_keys, _ = place(lax.broadcasted_iota(jnp.int32, (8, row_tokens), 1))
    seg_mine, token_position = place(
        rank * rows + lax.broadcasted_iota(jnp.int32, (rows, 128), 0)
    )
    lane = lax.broadcasted_iota(jnp.int32, (rows, 128), 1)
    half = HEAD_SIZE // 2
    frequency = 10000.0 ** (-2.0 * (lane % half).astype(F32) / HEAD_SIZE)
    angles = token_position.astype(F32) * frequency
    cosines = jnp.cos(angles)
    sines = jnp.where(lane % HEAD_SIZE < half, -1.0, 1.0) * jnp.sin(angles)
    w_kv = jnp.stack(
        [
            key_projection_weight.reshape(width, KEY_VALUE_HEADS, HEAD_SIZE),
            value_projection_weight.reshape(width, KEY_VALUE_HEADS, HEAD_SIZE),
        ],
        axis=2,
    ).reshape(width, 2 * KEY_VALUE_HEADS * HEAD_SIZE)
    gains = jnp.concatenate(
        [jnp.stack([gain_attn, gain_ffn]).astype(F32), jnp.zeros((6, width), F32)]
    )
    acts, grads_in, gain_sums, nf, inner, gg, gu, br, la, ra, nr, kvg = run_layers(
        ends,
        cosines,
        sines,
        seg_keys,
        seg_mine,
        gains,
        (w_query, w_kv, w_out, w_gate, w_up, w_down),
    )

    def reduced(left, right):
        total = lax.dot_general(
            left, right, (((0,), (0,)), ((), ())), preferred_element_type=F32
        ).astype(BF16)
        piece = lax.psum_scatter(total, "dp", scatter_dimension=0, tiled=True)
        return lax.psum(piece, "ctx")

    def both(piece, axis):
        return lax.all_gather(piece, "section", axis=axis, tiled=axis > 0).astype(F32)

    grad_gate = both(reduced(nf, gg), 1)
    grad_up = both(reduced(nf, gu), 1)
    grad_down = both(reduced(inner, br), 1)[:, :width]
    attn = both(reduced(la, ra), 0)
    kv_parts = both(reduced(nr, kvg), 0)
    kv_grad = jnp.concatenate([kv_parts[0], kv_parts[1][:, 128:]], axis=1).reshape(
        -1, KEY_VALUE_HEADS, 2, HEAD_SIZE
    )
    grad_key = kv_grad[:, :, 0].reshape(kv_grad.shape[0], -1)
    grad_value = kv_grad[:, :, 1].reshape(kv_grad.shape[0], -1)
    gain_sum = lax.psum(gain_sums[:2], ("section", "ctx"))
    gain_piece = lax.psum_scatter(gain_sum, "dp", scatter_dimension=1, tiled=True)
    return (
        acts,
        grads_in,
        attn[0],
        grad_key,
        grad_value,
        attn[1],
        grad_gate,
        grad_up,
        grad_down,
        gain_piece[0],
        gain_piece[1],
    )


def solution(mesh):
    return jax.shard_map(
        shards,
        mesh=mesh,
        in_specs=(P("section", None, ("dp", "ctx"), None), P(None, "dp", None)) + (P(),) * 9,
        out_specs=(P("section", None, ("dp", "ctx"), None),) * 2
        + (P("dp", None),) * 7
        + (P("dp"),) * 2,
        check_vma=False,
    )
```

```python
import jax
import jax.numpy as jnp
from jax import lax
from jax.experimental import pallas as pl
from jax.experimental.pallas import tpu as pltpu
from jax.sharding import PartitionSpec as P

MESH = pl.DeviceIdType.MESH
QUERY_HEADS = 15
KEY_VALUE_HEADS = 5
HEAD_SIZE = 64
SHARE = QUERY_HEADS // KEY_VALUE_HEADS
RANKS = 4
epsilon = 1e-05
masked_fill = -1e30
F32 = jnp.float32
BF16 = jnp.bfloat16


def dot(left, right):
    return jnp.dot(left, right, preferred_element_type=F32)


def dot_rt(left, right):
    return lax.dot_general(left, right, (((1,), (1,)), ((), ())), preferred_element_type=F32)


def dot_lt(left, right):
    return lax.dot_general(left, right, (((0,), (0,)), ((), ())), preferred_element_type=F32)


def tiles(total, width):
    return [(at, min(width, total - at)) for at in range(0, total, width)]


def wide(block):
    missing = 128 - block.shape[1]
    if not missing:
        return block
    return jnp.concatenate([block, jnp.zeros((block.shape[0], missing), block.dtype)], axis=1)


def lanes(rows):
    return lax.broadcasted_iota(jnp.int32, (rows, 128), 1)


def half_turn(block):
    front = lanes(block.shape[0]) % HEAD_SIZE < HEAD_SIZE // 2
    return jnp.where(front, pltpu.roll(block, 96, 1), pltpu.roll(block, 32, 1))


def inverse_rms(hidden):
    return lax.rsqrt(jnp.mean(hidden * hidden, axis=-1, keepdims=True) + epsilon)


def layers_kernel(
    ends, cosines, sines, seg_keys, seg_mine, gains, wq_h, wkv_h, wo_h, wg_h, wu_h, wd_h,
    acts_o, grads_o, gain_o, nf_o, in_o, gg_o, gu_o, br_o, la_o, ra_o, nr_o, kvg_o,
    wq, wkv, wo, wg, wu, wd,
    act, go, middle, norm_ffn, fact_a, fact_b, inner, lm, qd, kv, o_raw,
    sum_acc, gm, gg, gu, br, ra, dq_raw, pds, dkv, dkv_in, gkv,
    w_sem, in_send, in_recv, kv_send, kv_recv, dk_send, dk_recv, out_send, out_recv,
    op_own, op_send, op_recv,
):
    section = lax.axis_index("section")
    dp = lax.axis_index("dp")
    ctx = lax.axis_index("ctx")
    micro = ctx // 2
    xbit = ctx % 2
    rank = 2 * section + xbit
    rows, width = act.shape[1], act.shape[2]
    ff = wg.shape[1]
    ff_half = ff // 2

    def device_of(r):
        return (r // 2, dp, 2 * micro + r % 2)

    partner = (1 - section, dp, ctx)

    loads = [
        pltpu.make_async_copy(h, v, w_sem.at[i])
        for i, (h, v) in enumerate(
            [(wkv_h, wkv), (wq_h, wq), (wo_h, wo), (wg_h, wg), (wu_h, wu), (wd_h, wd)]
        )
    ]
    kv[...] = jnp.zeros_like(kv)
    barrier = pltpu.get_barrier_semaphore()
    for step in range(1, 8):
        other = (4 * section + ctx + step) % 8
        pl.semaphore_signal(
            barrier, inc=1, device_id=(other // 4, dp, other % 4), device_id_type=MESH
        )
    pl.semaphore_wait(barrier, 7)

    def in_copy(block, into_x):
        dst = act.at[0] if into_x else go.at[2]
        slot = 0 if into_x else 1
        return (
            pltpu.make_async_copy(ends.at[0, block], dst, in_recv.at[slot]),
            pltpu.make_async_remote_copy(
                src_ref=ends.at[0, block],
                dst_ref=dst,
                send_sem=in_send.at[block],
                recv_sem=in_recv.at[slot],
                device_id=(ctx // 2, dp, 2 * block + xbit),
                device_id_type=MESH,
            ),
        )

    def in_mine(block):
        return (section == ctx // 2) & (ctx // 2 == block)

    for block in range(2):
        for into_x in (True, False):
            here = section == (0 if into_x else 1)
            local, remote = in_copy(block, into_x)

            @pl.when(here & in_mine(block))
            def _(local=local):
                local.start()

            @pl.when(here & jnp.logical_not(in_mine(block)))
            def _(remote=remote):
                remote.start()

    for load in loads:
        load.start()

    lane = lanes(rows)
    low = lane < HEAD_SIZE
    cos_q = cosines[...]
    sin_q = sines[...]
    gain_attn = gains[0:1, :]
    gain_ffn = gains[1:2, :]

    def mask():
        query_index = rank * rows + lax.broadcasted_iota(jnp.int32, (rows, RANKS * rows), 0)
        key_index = lax.broadcasted_iota(jnp.int32, (rows, RANKS * rows), 1)
        ok = (seg_mine[:, 0:1] == seg_keys[0:1, :]) & (query_index >= key_index)
        return jnp.where(ok, 0.0, masked_fill)

    def kv_rows(l, r):
        return kv.at[l, pl.ds(pl.multiple_of(r * rows, 16), rows)]

    def kv_copy(l, quarter, dst, slot):
        return pltpu.make_async_remote_copy(
            src_ref=kv_rows(l, quarter),
            dst_ref=kv_rows(l, quarter),
            send_sem=kv_send.at[l, slot],
            recv_sem=kv_recv.at[l, quarter],
            device_id=device_of(dst),
            device_id_type=MESH,
        )

    kv_plan = [(0, 0, 1, 0), (0, 0, 2, 1), (1, 1, 2, 0), (1, 1, 3, 1), (2, 2, 3, 0)]
    kv_relay = (1, 0, 3, 2)

    def kv_start(l):
        for sender, quarter, dst, slot in kv_plan:

            @pl.when(rank == sender)
            def _(quarter=quarter, dst=dst, slot=slot):
                kv_copy(l, quarter, dst, slot).start()

    def kv_finish(l):
        @pl.when(rank == 1)
        def _():
            kv_copy(l, 0, 3, 2).wait_recv()
            kv_copy(l, 0, 3, 2).start()

        for quarter, receivers in ((0, (2, 3)), (1, (2, 3)), (2, (3,))):
            for receiver in receivers:

                @pl.when(rank == receiver)
                def _(quarter=quarter):
                    kv_copy(l, quarter, 0, 0).wait_recv()

    def kv_sent(l):
        for sender, quarter, dst, slot in kv_plan + [kv_relay]:

            @pl.when(rank == sender)
            def _(quarter=quarter, dst=dst, slot=slot):
                kv_copy(l, quarter, dst, slot).wait_send()

    def out_copy(array, out, l, kind):
        home = 2 * section + xbit
        return (
            pltpu.make_async_copy(array, out.at[0, micro], out_recv.at[kind, micro]),
            pltpu.make_async_remote_copy(
                src_ref=array,
                dst_ref=out.at[0, micro],
                send_sem=out_send.at[kind, l],
                recv_sem=out_recv.at[kind, micro],
                device_id=(l, dp, home),
                device_id_type=MESH,
            ),
        )

    def out_mine(l):
        return (section == l) & (ctx == 2 * section + xbit)

    def out_start(array, out, l, kind):
        local, remote = out_copy(array, out, l, kind)

        @pl.when(out_mine(l))
        def _():
            local.start()

        @pl.when(jnp.logical_not(out_mine(l)))
        def _():
            remote.start()

    place = [pl.ds((2 * c + l) * rows, rows) for c in range(2) for l in range(2)]

    def op_rows(l):
        return pl.ds(pl.multiple_of((2 * section + l) * rows, 16), rows)

    def op_copy(kind, l, own):
        role = section if own else 1 - section
        half = pl.ds(pl.multiple_of(role * ff_half, 128), ff_half)
        src = [
            lambda: norm_ffn.at[l],
            lambda: inner.at[l],
            lambda: gg.at[:, half],
            lambda: gu.at[:, half],
            lambda: br.at[:, pl.ds(pl.multiple_of(role * 512, 128), 512)],
            lambda: lm.at[l, role],
            lambda: ra.at[role],
            lambda: lm.at[l, 0],
            lambda: gkv.at[:, pl.ds(pl.multiple_of(role * 256, 128), 384)],
        ][kind]()
        dst = [nf_o, in_o, gg_o, gu_o, br_o, la_o, ra_o, nr_o, kvg_o][kind].at[op_rows(l)]
        if own:
            return pltpu.make_async_copy(src, dst, op_own.at[kind, l])
        return pltpu.make_async_remote_copy(
            src_ref=src,
            dst_ref=dst,
            send_sem=op_send.at[kind, l],
            recv_sem=op_recv.at[kind, l],
            device_id=partner,
            device_id_type=MESH,
        )

    def op_start(kinds, l):
        for kind in kinds:
            op_copy(kind, l, True).start()
            op_copy(kind, l, False).start()

    def op_sent(kinds, l):
        for kind in kinds:
            op_copy(kind, l, True).wait()
            op_copy(kind, l, False).wait_send()

    @pl.when(section == 0)
    def _():
        for block in range(2):

            @pl.when(jnp.logical_not(in_mine(block)))
            def _(block=block):
                in_copy(block, True)[1].wait_send()

    @pl.when(section == 1)
    def _():
        for block in range(2):

            @pl.when(jnp.logical_not(in_mine(block)))
            def _(block=block):
                in_copy(block, False)[1].wait_send()

    in_copy(0, True)[1].wait_recv()
    loads[0].wait()

    def forward(l, carry):
        hidden = act[l].astype(F32)
        lm[l, 0] = (hidden * inverse_rms(hidden) * gain_attn).astype(BF16)
        cos_kv = jnp.where(low, cos_q, 1.0)
        sin_kv = jnp.where(low, sin_q, 0.0)
        mine = pl.ds(pl.multiple_of(rank * rows, 16), rows)
        for g in range(KEY_VALUE_HEADS):
            block = dot(lm[l, 0], wkv[:, 128 * g : 128 * g + 128])
            turned = block * cos_kv + half_turn(block) * sin_kv
            kv[l, mine, 128 * g : 128 * g + 128] = turned.astype(BF16)
        kv_start(l)

        @pl.when(l == 0)
        def _():
            loads[1].wait()

        for at, size in tiles(width, 256):
            product = dot(lm[l, 0], wq[:, at : at + size])
            for inside, part in tiles(size, 128):
                block = wide(product[:, inside : inside + part])
                turned = (block * cos_q + half_turn(block) * sin_q) * 0.125
                head = (at + inside) // HEAD_SIZE
                qd[l, head // SHARE, pl.ds(head % SHARE * rows, rows), :] = jnp.where(
                    low, turned, 0.0
                ).astype(BF16)
                head += 1
                if head < QUERY_HEADS:
                    qd[l, head // SHARE, pl.ds(head % SHARE * rows, rows), :] = jnp.where(
                        low, pltpu.roll(turned, 64, 1), 0.0
                    ).astype(BF16)
        kv_finish(l)
        allowed = mask()

        def heads(g, carry):
            kv_g = kv[l, :, pl.ds(pl.multiple_of(g * 128, 128), 128)]
            for i in range(SHARE):
                scores = dot_rt(qd[l, g, i * rows : (i + 1) * rows, :], kv_g) + allowed
                peak = jnp.max(scores, axis=-1, keepdims=True)
                exponent = jnp.exp(scores - peak)
                total = jnp.sum(exponent, axis=-1, keepdims=True)
                out = dot(exponent.astype(BF16), kv_g) / total
                o_raw[l, g * SHARE + i] = jnp.where(low, peak + jnp.log(total), out)
            return carry

        lax.fori_loop(0, KEY_VALUE_HEADS, heads, 0)
        for at, size in tiles(width, 128):
            head = at // HEAD_SIZE
            block = pltpu.roll(o_raw[l, head], 64, 1)
            if size == 128:
                block = jnp.where(low, block, o_raw[l, head + 1])
            lm[l, 1, :, at : at + size] = block[:, :size].astype(BF16)

        @pl.when(l == 0)
        def _():
            loads[2].wait()

        for at, size in tiles(width, 256):
            middle[l, :, at : at + size] = act[l, :, at : at + size].astype(F32) + dot(
                lm[l, 1], wo[:, at : at + size]
            )
        mid = middle[l]
        norm_ffn[l] = (mid * inverse_rms(mid) * gain_ffn).astype(BF16)

        @pl.when(l == 0)
        def _():
            loads[3].wait()
            loads[4].wait()

        def gates(j, carry):
            part = pl.ds(pl.multiple_of(j * 256, 256), 256)
            gate = dot(norm_ffn[l], wg[:, part])
            upper = dot(norm_ffn[l], wu[:, part])
            s = jax.nn.sigmoid(gate)
            swish = gate * s
            inner[l, :, part] = (swish * upper).astype(BF16)
            fact_a[l, :, part] = (upper * s * (1.0 + gate * (1.0 - s))).astype(BF16)
            fact_b[l, :, part] = swish.astype(BF16)
            return carry

        lax.fori_loop(0, ff // 256, gates, 0)

        @pl.when(l == 0)
        def _():
            loads[5].wait()

        for at, size in tiles(width, 256):
            act[l + 1, :, at : at + size] = (
                middle[l, :, at : at + size] + dot(inner[l], wd[:, at : at + size])
            ).astype(BF16)
        out_start(act.at[l + 1], acts_o, l, 0)
        op_start((0, 1, 7), l)
        kv_sent(l)
        return carry

    lax.fori_loop(0, 2, forward, 0)

    in_copy(0, False)[1].wait_recv()
    gain_o[...] = jnp.zeros_like(gain_o)
    br[...] = jnp.zeros_like(br)

    def dk_copy(l, src_quarter, count, dst, slot_in, slot):
        return pltpu.make_async_remote_copy(
            src_ref=dkv.at[pl.ds(src_quarter * rows, count * rows)],
            dst_ref=dkv_in.at[l, pl.ds(slot_in * rows, count * rows)],
            send_sem=dk_send.at[l, slot],
            recv_sem=dk_recv.at[l, slot_in],
            device_id=device_of(dst),
            device_id_type=MESH,
        )

    def backward(step, carry):
        l = 1 - step

        @pl.when(l == 0)
        def _():
            op_sent((2, 3, 4, 5, 6, 8), 1)

        branch = go[l + 1]
        br[:, :width] = branch
        op_start((4,), l)

        def gates(j, carry):
            part = pl.ds(pl.multiple_of(j * 256, 256), 256)
            grad_inner = dot_rt(go[l + 1], wd[part, :])
            gg[:, part] = (grad_inner * fact_a[l, :, part].astype(F32)).astype(BF16)
            gu[:, part] = (grad_inner * fact_b[l, :, part].astype(F32)).astype(BF16)
            return carry

        lax.fori_loop(0, ff // 256, gates, 0)
        op_start((2, 3), l)
        for at, size in tiles(width, 256):
            sum_acc[:, at : at + size] = dot_rt(gg[...], wg[at : at + size, :]) + dot_rt(
                gu[...], wu[at : at + size, :]
            )

        def norm_back(hidden, gain, row):
            upstream = sum_acc[...]
            scale = inverse_rms(hidden)
            weighted = upstream * gain
            inside = jnp.mean(weighted * hidden, axis=-1, keepdims=True)
            gain_o[row : row + 1, :] += jnp.sum(upstream * hidden * scale, axis=0, keepdims=True)
            return scale * weighted - hidden * (scale * scale * scale * inside)

        gm[...] = go[l + 1].astype(F32) + norm_back(middle[l], gain_ffn, 1)
        ra[1] = gm[...].astype(BF16)

        for at, size in tiles(width, 256):
            product = dot_rt(ra[1], wo[at : at + size, :])
            for inside, part in tiles(size, 128):
                block = wide(product[:, inside : inside + part])
                head = (at + inside) // HEAD_SIZE
                qd[l, head // SHARE, pl.ds((SHARE + head % SHARE) * rows, rows), :] = jnp.where(
                    low, 0.0, pltpu.roll(block, 64, 1)
                ).astype(BF16)
                head += 1
                if head < QUERY_HEADS:
                    qd[l, head // SHARE, pl.ds((SHARE + head % SHARE) * rows, rows), :] = (
                        jnp.where(low, 0.0, block).astype(BF16)
                    )
        allowed = mask()

        def heads(g, carry):
            kv_g = kv[l, :, pl.ds(pl.multiple_of(g * 128, 128), 128)]
            for i in range(SHARE):
                mine = slice(i * rows, (i + 1) * rows)
                other = slice((SHARE + i) * rows, (SHARE + i + 1) * rows)
                kept = o_raw[l, g * SHARE + i]
                log_total = kept[:, 0:1]
                scores = dot_rt(qd[l, g, mine, :], kv_g) + allowed
                probs = jnp.exp(scores - log_total)
                grad_out = qd[l, g, other, :]
                grad_probs = dot_rt(grad_out, kv_g)
                weight = jnp.sum(grad_out.astype(F32) * kept, axis=-1, keepdims=True)
                grad_scores = (probs * (grad_probs - weight)).astype(BF16)
                pds[mine, :] = grad_scores
                pds[other, :] = probs.astype(BF16)
                dq_raw[g * SHARE + i] = dot(grad_scores, kv_g)
            grad_kv = dot_lt(qd[l, g], pds[...])
            dkv[:, pl.ds(pl.multiple_of(g * 128, 128), 128)] = grad_kv.T.astype(BF16)
            return carry

        lax.fori_loop(0, KEY_VALUE_HEADS, heads, 0)

        @pl.when(rank == 3)
        def _():
            dk_copy(l, 2, 1, 2, 0, 0).start()
            dk_copy(l, 0, 2, 1, 0, 1).start()

        @pl.when(rank == 2)
        def _():
            dk_copy(l, 1, 1, 1, 2, 0).start()
            dk_copy(l, 0, 1, 0, 1, 1).start()

        @pl.when(rank == 1)
        def _():
            dk_copy(l, 0, 2, 1, 0, 0).wait_recv()
            dkv[:rows] = (dkv[:rows].astype(F32) + dkv_in[l, :rows].astype(F32)).astype(BF16)
            dk_copy(l, 0, 1, 0, 0, 0).start()

        for at, size in tiles(width, 128):
            head = at // HEAD_SIZE
            block = dq_raw[head]
            if size == 128:
                block = jnp.where(low, block, pltpu.roll(dq_raw[head + 1], 64, 1))
            turned = (block * cos_q - half_turn(block) * sin_q) * 0.125
            ra[0, :, at : at + size] = turned[:, :size].astype(BF16)
        op_start((5, 6), l)

        @pl.when(rank == 3)
        def _():
            dk_copy(l, 2, 1, 2, 0, 0).wait_send()
            dk_copy(l, 0, 2, 1, 0, 1).wait_send()

        @pl.when(rank == 2)
        def _():
            dk_copy(l, 0, 1, 2, 0, 0).wait_recv()
            dk_copy(l, 1, 1, 1, 2, 0).wait_send()
            dk_copy(l, 0, 1, 0, 1, 1).wait_send()
            dkv[2 * rows : 3 * rows] = (
                dkv[2 * rows : 3 * rows].astype(F32) + dkv_in[l, :rows].astype(F32)
            ).astype(BF16)

        @pl.when(rank == 1)
        def _():
            dk_copy(l, 0, 1, 2, 2, 0).wait_recv()
            dk_copy(l, 0, 1, 0, 0, 0).wait_send()
            dkv[rows : 2 * rows] = (
                dkv[rows : 2 * rows].astype(F32)
                + dkv_in[l, rows : 2 * rows].astype(F32)
                + dkv_in[l, 2 * rows :].astype(F32)
            ).astype(BF16)

        @pl.when(rank == 0)
        def _():
            dk_copy(l, 0, 1, 2, 0, 0).wait_recv()
            dk_copy(l, 0, 1, 2, 1, 0).wait_recv()
            dkv[:rows] = (
                dkv[:rows].astype(F32)
                + dkv_in[l, :rows].astype(F32)
                + dkv_in[l, rows : 2 * rows].astype(F32)
            ).astype(BF16)

        cos_kv = jnp.where(low, cos_q, 1.0)
        sin_kv = jnp.where(low, sin_q, 0.0)
        mine = pl.ds(pl.multiple_of(rank * rows, 16), rows)
        for g in range(KEY_VALUE_HEADS):
            part = slice(128 * g, 128 * g + 128)
            block = dkv[mine, part].astype(F32)
            gkv[:, part] = (block * cos_kv - half_turn(block) * sin_kv).astype(BF16)
        op_start((8,), l)
        for at, size in tiles(width, 256):
            sum_acc[:, at : at + size] = dot_rt(ra[0], wq[at : at + size, :]) + dot_rt(
                gkv[...], wkv[at : at + size, :]
            )
        go[l] = (gm[...] + norm_back(act[l].astype(F32), gain_attn, 0)).astype(BF16)
        out_start(go.at[l], grads_o, l, 1)
        return carry

    lax.fori_loop(0, 2, backward, 0)

    op_sent((2, 3, 4, 5, 6, 8), 0)
    for l in range(2):
        op_sent((0, 1, 7), l)
        for kind in range(9):
            op_copy(kind, l, False).wait_recv()
        for kind, out, array in ((0, acts_o, act.at[l + 1]), (1, grads_o, go.at[l])):

            @pl.when(jnp.logical_not(out_mine(l)))
            def _(l=l, kind=kind, out=out, array=array):
                out_copy(array, out, l, kind)[1].wait_send()

    for kind, out in ((0, acts_o), (1, grads_o)):
        for block in range(2):
            pltpu.make_async_copy(act.at[0], out.at[0, block], out_recv.at[kind, block]).wait()


def run_layers(ends, cosines, sines, seg_keys, seg_mine, gains, weights):
    micro_count, rows, width = ends.shape[1:]
    wq, wkv, wo, wg, wu, wd = weights
    ff = wg.shape[1]
    keys = RANKS * rows
    kv_width = wkv.shape[1]
    vmem, hbm = pl.BlockSpec(memory_space=pltpu.VMEM), pl.BlockSpec(memory_space=pl.ANY)
    op_rows = 4 * rows
    out = lambda *shape: jax.ShapeDtypeStruct(shape, BF16)
    dma = pltpu.SemaphoreType.DMA
    return pl.pallas_call(
        layers_kernel,
        out_shape=[
            out(*ends.shape),
            out(*ends.shape),
            jax.ShapeDtypeStruct((8, width), F32),
            out(op_rows, width),
            out(op_rows, ff),
            out(op_rows, ff // 2),
            out(op_rows, ff // 2),
            out(op_rows, 512),
            out(op_rows, width),
            out(op_rows, width),
            out(op_rows, width),
            out(op_rows, 384),
        ],
        in_specs=[hbm] + [vmem] * 5 + [hbm] * 6,
        out_specs=[hbm, hbm, vmem] + [hbm] * 9,
        scratch_shapes=[
            pltpu.VMEM(wq.shape, BF16),
            pltpu.VMEM(wkv.shape, BF16),
            pltpu.VMEM(wo.shape, BF16),
            pltpu.VMEM(wg.shape, BF16),
            pltpu.VMEM(wu.shape, BF16),
            pltpu.VMEM(wd.shape, BF16),
            pltpu.VMEM((3, rows, width), BF16),
            pltpu.VMEM((3, rows, width), BF16),
            pltpu.VMEM((2, rows, width), F32),
            pltpu.VMEM((2, rows, width), BF16),
            pltpu.VMEM((2, rows, ff), BF16),
            pltpu.VMEM((2, rows, ff), BF16),
            pltpu.VMEM((2, rows, ff), BF16),
            pltpu.VMEM((2, 2, rows, width), BF16),
            pltpu.VMEM((2, KEY_VALUE_HEADS, 2 * SHARE * rows, 128), BF16),
            pltpu.VMEM((2, keys, kv_width), BF16),
            pltpu.VMEM((2, QUERY_HEADS, rows, 128), F32),
            pltpu.VMEM((rows, width), F32),
            pltpu.VMEM((rows, width), F32),
            pltpu.VMEM((rows, ff), BF16),
            pltpu.VMEM((rows, ff), BF16),
            pltpu.VMEM((rows, 1024), BF16),
            pltpu.VMEM((2, rows, width), BF16),
            pltpu.VMEM((QUERY_HEADS, rows, 128), F32),
            pltpu.VMEM((2 * SHARE * rows, keys), BF16),
            pltpu.VMEM((keys, kv_width), BF16),
            pltpu.VMEM((2, 3 * rows, kv_width), BF16),
            pltpu.VMEM((rows, kv_width), BF16),
            dma((6,)),
            dma((2,)),
            dma((2,)),
            dma((2, 3)),
            dma((2, 3)),
            dma((2, 2)),
            dma((2, 3)),
            dma((2, 2)),
            dma((2, 2)),
            dma((9, 2)),
            dma((9, 2)),
            dma((9, 2)),
        ],
        compiler_params=pltpu.CompilerParams(
            collective_id=1, has_side_effects=True, vmem_limit_bytes=61 * 2**20
        ),
        name="layers",
    )(ends, cosines, sines, seg_keys, seg_mine, gains, wq, wkv, wo, wg, wu, wd)


def sums_kernel(
    gain_sums, nf_h, in_h, gg_h, gu_h, br_h, la_h, ra_h, nr_h, kvg_h,
    q_o, out_o, kv_o, gain_o, gate_o, up_o, down_o,
    stage_a, stage_b, in_v, br_v, gg_v, gu_v, ra_v, kvg_v, nf_t, la_t, nr_t, in_t, gain_t,
    d_out, d_in, d_keep, d1_out, d1_in, d2_out, d2_in,
    f1_out, f1_in, f2_out, f2_in, f_keep, fz_in,
    t1_out, t1_in, t2_out, t2_in, t_keep, tz_in,
    d_all, f_all, t_all, gate_f, q_f, kv_f, gain_f, down_f,
    load, dz_s, dz_r, d1_s, d1_r, d2_s, d2_r, f1_s, f1_r, f2_s, f2_r, fz_s, fz_r,
    t1_s, t1_r, t2_s, t2_r, tz_s, tz_r, all_s, all_r, pair_r, write,
):
    section = lax.axis_index("section")
    z = lax.axis_index("dp")
    ctx = lax.axis_index("ctx")
    x, y = ctx % 2, ctx // 2
    x_next = (section, z, 2 * y + 1 - x)
    y_next = (section, z, 2 * (1 - y) + x)
    partner = (1 - section, z, ctx)
    depth = nf_h.shape[0]
    width = nf_h.shape[1]
    per = width // RANKS
    part = f_keep.shape[2]
    shift = per - part
    quarter = gg_v.shape[1] // 2
    deep = in_h.shape[1] // RANKS
    fine = deep // 2
    last = RANKS - 1

    def remote(src, dst, send, recv, device):
        return pltpu.make_async_remote_copy(
            src_ref=src, dst_ref=dst, send_sem=send, recv_sem=recv,
            device_id=device, device_id_type=MESH,
        )

    def some(start, size, unit=16):
        return pl.ds(pl.multiple_of(start, unit), size)

    loads = [
        pltpu.make_async_copy(h, v, load.at[i])
        for i, (h, v) in enumerate(
            [(in_h, in_v), (br_h, br_v), (nf_h, stage_a), (gg_h, gg_v), (gu_h, gu_v),
             (la_h, stage_b), (ra_h, ra_v), (kvg_h, kvg_v), (nr_h, stage_a)]
        )
    ]
    for copy in loads[:8]:
        copy.start()
    barrier = pltpu.get_barrier_semaphore()
    for device in (x_next, y_next, partner):
        pl.semaphore_signal(barrier, inc=1, device_id=device, device_id_type=MESH)
    inner_left = (z > 0).astype(jnp.int32)
    inner_right = (z < last).astype(jnp.int32)

    @pl.when(z > 0)
    def _():
        pl.semaphore_signal(barrier, inc=1, device_id=(section, z - 1, ctx), device_id_type=MESH)

    @pl.when(z < last)
    def _():
        pl.semaphore_signal(barrier, inc=1, device_id=(section, z + 1, ctx), device_id_type=MESH)

    pl.semaphore_wait(barrier, 3 + inner_left + inner_right)

    def turn(src, dst):
        for at, size in tiles(src.shape[1], 128):
            block = src[:, at : at + size]
            if size < 128:
                block = wide(block)
            dst[at : at + size, :] = block.T[:size]

    def z_way(t):
        up = (z < t).astype(jnp.int32)
        to = z + 2 * up - 1
        arrives = up * inner_left + (1 - up) * inner_right
        meets = (1 - up) * (t == z - 1).astype(jnp.int32)
        return (section, to, ctx), arrives, t * (1 - meets) + RANKS * meets

    def d_turn(k):
        is_ = lambda v: (z == v).astype(jnp.int32)
        order = ((3, 2, 1), (3, 0, 2), (0, 3, 1), (0, 1, 2))
        return sum(is_(v) * order[v][k] for v in range(RANKS))

    def d_block(t):
        for b in range(deep // 128):
            in_t[b * 128 : (b + 1) * 128, :] = in_v[:, some(t * deep + b * 128, 128, 128)].T

    def d_send(k, t, sub):
        device, _, slot = z_way(t)
        rows = pl.ds(sub * fine, fine)
        return remote(d_out.at[k, rows], d_in.at[slot, rows], dz_s.at[k, sub], dz_r.at[slot, sub], device)

    def d_step(k):
        t = d_turn(k)
        _, arrives, _ = z_way(t)
        d_block(t)
        for sub in range(2):
            rows = slice(sub * fine, (sub + 1) * fine)
            mine = dot(in_t[rows, :], br_v[...])

            @pl.when(arrives == 0)
            def _():
                d_out[k, rows, :] = mine.astype(BF16)

            @pl.when(arrives == 1)
            def _():
                remote(d_out.at[k, rows], d_in.at[t, rows], dz_s.at[k, sub], dz_r.at[t, sub], partner).wait_recv()
                d_out[k, rows, :] = (mine + d_in[t, rows, :].astype(F32)).astype(BF16)

            d_send(k, t, sub).start()

    def f_links(k):
        return (x_next, y_next, x, y) if k == 0 else (y_next, x_next, y, x)

    def f_right(k, column_half):
        src = gg_v if k == 0 else gu_v
        return src[:, some(column_half * quarter, quarter, 128)]

    def f1_copy(k, d):
        return remote(f1_out.at[k, d], f1_in.at[k, d], f1_s.at[k, d], f1_r.at[k, d], f_links(k)[0])

    def f2_copy(k, d):
        return remote(f2_out.at[k, d], f2_in.at[k, d], f2_s.at[k, d], f2_r.at[k, d], f_links(k)[1])

    def f1_step(d):
        for k in range(2):
            first = f_links(k)[2]
            left = nf_t[some(d * per, per), :]
            f1_out[k, d] = dot(left, f_right(k, 1 - first)).astype(BF16)
            f1_copy(k, d).start()

    def f2_step(d):
        for k in range(2):
            first, second = f_links(k)[2:]
            f1_copy(k, d).wait_recv()
            for mine in (False, True):
                at = (second if mine else 1 - second) * shift
                total = dot(nf_t[some(d * per + at, part), :], f_right(k, first)) + f1_in[
                    k, d, some(at, part), :
                ].astype(F32)
                if mine:
                    f_keep[k, d] = total.astype(BF16)
                else:
                    f2_out[k, d] = total.astype(BF16)
                    f2_copy(k, d).start()

    def t_links(d):
        x_first = (d < RANKS // 2).astype(jnp.int32)
        first, second = x_first * x + (1 - x_first) * y, x_first * y + (1 - x_first) * x
        to_x = (section, z, 2 * y + 1 - x)
        to_y = (section, z, 2 * (1 - y) + x)
        pick = lambda a, b: tuple(x_first * i + (1 - x_first) * j for i, j in zip(a, b))
        return pick(to_x, to_y), pick(to_y, to_x), first, second

    def t_product(row, count, add):
        mine = dot(la_t[some(row, count), :], ra_v[...])
        pairs = dot(nr_t[some(row, count), :], kvg_v[...])
        gains = gain_t[some(row, count), :]
        full = width // 128 * 128
        tail = jnp.concatenate([mine[:, full:], gains[:, width - full :]], axis=1)
        return [(0, add(mine[:, :full], 0)), (full, add(tail, full)), (full + 128, add(pairs, full + 128))]

    def t1_copy(d):
        return remote(t1_out.at[d], t1_in.at[d], t1_s.at[d], t1_r.at[d], t_links(d)[0])

    def t2_copy(d):
        return remote(t2_out.at[d], t2_in.at[d], t2_s.at[d], t2_r.at[d], t_links(d)[1])

    def t1_step(d):
        first = t_links(d)[2]
        for at, value in t_product(d * per + (1 - first) * shift, part, lambda v, at: v):
            t1_out[d, :, at : at + value.shape[1]] = value.astype(BF16)
        t1_copy(d).start()

    def t2_step(d):
        _, _, first, second = t_links(d)
        t1_copy(d).wait_recv()
        for mine in (False, True):
            row = (second if mine else 1 - second) * (part // 2)
            add = lambda v, at: v + t1_in[d, some(row, part // 2), at : at + v.shape[1]].astype(F32)
            dst = t_keep if mine else t2_out
            for at, value in t_product(d * per + first * shift + row, part // 2, add):
                dst[d, :, at : at + value.shape[1]] = value.astype(BF16)
            if not mine:
                t2_copy(d).start()

    def z_step(keep, second_in, z_in, send, recv, copy, d):
        copy.wait_recv()
        keep[d] = (keep[d].astype(F32) + second_in[d].astype(F32)).astype(BF16)

        @pl.when(z != d)
        def _():
            device, arrives, slot = z_way(d)

            @pl.when(arrives == 1)
            def _():
                remote(keep.at[d], z_in.at[d], send.at[d], recv.at[d], partner).wait_recv()
                keep[d] = (keep[d].astype(F32) + z_in[d].astype(F32)).astype(BF16)

            remote(keep.at[d], z_in.at[slot], send.at[d], recv.at[slot], device).start()

    def z_arrived(z_in, recv, src):
        @pl.when(z > 0)
        def _():
            remote(src, z_in.at[z], recv.at[z], recv.at[z], partner).wait_recv()

        @pl.when(z < last)
        def _():
            remote(src, z_in.at[RANKS], recv.at[RANKS], recv.at[RANKS], partner).wait_recv()

    def z_total(value, up, down):
        value = value + jnp.where(z > 0, up.astype(F32), 0.0)
        return value + jnp.where(z < last, down.astype(F32), 0.0)

    def places(x_first):
        a, b = (1, 0) if x_first is True else (0, 1) if x_first is False else (x_first, 1 - x_first)
        spot = lambda i, j: a * (2 * i + j) + b * (2 * j + i)
        return spot(x, y), spot(1 - x, y), spot(x, 1 - y), spot(1 - x, 1 - y)

    class Gather:
        def __init__(self, number, buffer, x_first):
            self.n, self.buffer = number, buffer
            self.own, self.over_x, self.over_y, self.across = places(x_first)
            rows = buffer.shape[2]
            cut = (rows // 2 + 15) // 16 * 16
            self.halves = (pl.ds(0, cut), pl.ds(cut, rows - cut))

        def whole(self, spot, slot, device):
            ref = self.buffer.at[section, spot]
            return remote(ref, ref, all_s.at[self.n, slot], all_r.at[self.n, slot], device)

        def relay(self, spot, half, device):
            ref = self.buffer.at[section, spot, self.halves[half]]
            return remote(ref, ref, all_s.at[self.n, 2 + half], all_r.at[self.n, 2 + half], device)

        def pair(self, core, spot, slot):
            ref = self.buffer.at[core, spot]
            return remote(ref, ref, all_s.at[self.n, 4 + slot], pair_r.at[self.n, spot], partner)

        def start(self):
            self.whole(self.own, 0, x_next).start()
            self.whole(self.own, 1, y_next).start()
            self.pair(section, self.own, 0).start()

        def middle(self):
            self.whole(self.over_x, 0, x_next).wait_recv()
            self.relay(self.over_x, 0, y_next).start()
            self.pair(section, self.over_x, 1).start()
            self.whole(self.over_y, 1, y_next).wait_recv()
            self.relay(self.over_y, 1, x_next).start()
            self.pair(section, self.over_y, 2).start()

        def finish(self):
            self.relay(self.across, 0, y_next).wait_recv()
            self.relay(self.across, 1, x_next).wait_recv()
            self.pair(section, self.across, 3).start()
            for spot in (self.own, self.over_x, self.over_y, self.across):
                self.pair(1 - section, spot, 0).wait_recv()

        def sent(self):
            self.whole(self.own, 0, x_next).wait_send()
            self.whole(self.own, 1, y_next).wait_send()
            self.relay(self.over_x, 0, y_next).wait_send()
            self.relay(self.over_y, 1, x_next).wait_send()
            for slot, spot in enumerate((self.own, self.over_x, self.over_y, self.across)):
                self.pair(section, spot, slot).wait_send()

    below = (z < RANKS // 2).astype(jnp.int32)
    gathers = [
        Gather(0, d_all.at[0], True),
        Gather(1, d_all.at[1], False),
        Gather(2, f_all.at[0], True),
        Gather(3, f_all.at[1], False),
        Gather(4, t_all, below),
    ]

    def in_order(i):
        odd = i % 2
        return (1 - odd) * (last - i // 2) + odd * (i // 2)

    def each(step):
        def body(i, carry):
            step(in_order(i))
            return carry

        lax.fori_loop(0, RANKS, body, 0)

    loads[0].wait()
    loads[1].wait()
    d_step(0)
    loads[2].wait()
    turn(stage_a, nf_t)
    loads[8].start()
    loads[3].wait()
    loads[4].wait()
    each(f1_step)
    d_step(1)
    loads[5].wait()
    turn(stage_b, la_t)
    loads[8].wait()
    turn(stage_a, nr_t)
    loads[6].wait()
    loads[7].wait()
    gain_rows = jnp.concatenate(
        [gain_sums[...], jnp.zeros((128 - gain_sums.shape[0], width), F32)], axis=0
    )
    for at, size in tiles(width, 128):
        block = wide(gain_rows[:, at : at + size]).T
        gain_t[at : at + size, :] = pltpu.roll(block, 64, 1)[:size]
    each(t1_step)
    d_step(2)
    each(f2_step)

    d_block(z)

    def d1_copy(h):
        return remote(d1_out.at[h], d1_in.at[h], d1_s.at[h], d1_r.at[h], f_links(h)[0])

    def d2_copy(h):
        return remote(d2_out.at[h], d2_in.at[h], d2_s.at[h], d2_r.at[h], f_links(h)[1])

    for h in range(2):
        rows = slice(h * fine, (h + 1) * fine)

        @pl.when(z > 0)
        def _():
            remote(d_out.at[0, rows], d_in.at[z, rows], dz_r.at[z, h], dz_r.at[z, h], partner).wait_recv()

        @pl.when(z < last)
        def _():
            remote(d_out.at[0, rows], d_in.at[RANKS, rows], dz_r.at[RANKS, h], dz_r.at[RANKS, h], partner).wait_recv()

        first = f_links(h)[2]
        for mine in (False, True):
            at = h * fine + (first if mine else 1 - first) * (fine // 2)
            span = some(at, fine // 2)
            total = z_total(dot(in_t[span, :], br_v[...]), d_in[z, span, :], d_in[RANKS, span, :])
            if mine:
                d_keep[h] = total
            else:
                d1_out[h] = total.astype(BF16)
                d1_copy(h).start()

    each(t2_step)
    each(lambda d: [
        z_step(f_keep.at[k], f2_in.at[k], fz_in.at[k], fz_s.at[k], fz_r.at[k], f2_copy(k, d), d)
        for k in range(2)
    ])
    for h in range(2):
        second = f_links(h)[3]
        d1_copy(h).wait_recv()
        for mine in (False, True):
            span = some((second if mine else 1 - second) * (fine // 4), fine // 4)
            total = d_keep[h, span, :] + d1_in[h, span, :].astype(F32)
            if mine:
                d_keep[h, : fine // 4, :] = total
            else:
                d2_out[h] = total.astype(BF16)
                d2_copy(h).start()
    each(lambda d: z_step(t_keep, t2_in, tz_in, tz_s, tz_r, t2_copy(d), d))
    for h in range(2):
        d2_copy(h).wait_recv()
        gathers[h].buffer[section, gathers[h].own] = (
            d_keep[h, : fine // 4, :] + d2_in[h].astype(F32)
        ).astype(BF16)
        gathers[h].start()
    for k in range(2):
        z_arrived(fz_in.at[k], fz_r.at[k], f_keep.at[k, 0])
        f_all[k, section, gathers[2 + k].own] = z_total(
            f_keep[k, z].astype(F32), fz_in[k, z], fz_in[k, RANKS]
        ).astype(BF16)
        gathers[2 + k].start()
    gathers[0].middle()
    gathers[1].middle()
    z_arrived(tz_in, tz_r, t_keep.at[0])
    t_all[section, gathers[4].own] = z_total(
        t_keep[z].astype(F32), tz_in[z], tz_in[RANKS]
    ).astype(BF16)
    gathers[4].start()
    gathers[2].middle()
    gathers[3].middle()

    half_columns = 2 * quarter
    gathers[0].finish()
    gathers[1].finish()
    for core in range(2):
        columns = slice(512 * core, min(512 * core + 512, width))
        for h in range(2):
            for spot in range(4):
                row = h * fine + spot * (fine // 4)
                down_f[row : row + fine // 4, columns] = d_all[h, core, spot][
                    :, : columns.stop - columns.start
                ].astype(F32)
    writes = [pltpu.make_async_copy(down_f, down_o, write.at[0])]
    writes[0].start()
    gathers[4].middle()
    for k in range(2):
        gathers[2 + k].finish()
        for core in range(2):
            for f in range(2):
                at = core * half_columns + f * quarter
                columns = slice(at, at + quarter)
                gate_f[k, :part, columns] = f_all[k, core, 2 * f].astype(F32)
                gate_f[k, part:, columns] = f_all[k, core, 2 * f + 1, part - shift :, :].astype(F32)
        writes.append(pltpu.make_async_copy(gate_f.at[k], (gate_o, up_o)[k], write.at[1 + k]))
        writes[-1].start()
    gathers[4].finish()
    t_rows = part // 2
    pairs_at = width // 128 * 128 + 128
    for core in range(2):
        for spot in range(4):
            row = spot % 2 * t_rows + spot // 2 * shift
            skip = part - shift if spot == 2 else 0
            span = slice(row + skip, row + t_rows)
            q_f[core, span, :] = t_all[core, spot, skip:, :width].astype(F32)
            kv_f[core, span, :] = t_all[core, spot, skip:, pairs_at:].astype(F32)
            gain = t_all[core, spot, skip:, pairs_at - 128 : pairs_at].astype(F32)
            gain_f[span, :] = gain if core == 0 else gain_f[span, :] + gain
    for i, (src, dst) in enumerate(
        [(q_f.at[0], q_o), (q_f.at[1], out_o), (kv_f, kv_o), (gain_f, gain_o)]
    ):
        writes.append(pltpu.make_async_copy(src, dst, write.at[3 + i]))
        writes[-1].start()

    for k in range(3):
        for sub in range(2):
            d_send(k, d_turn(k), sub).wait_send()
    for h in range(2):
        d1_copy(h).wait_send()
        d2_copy(h).wait_send()

    def sent(d):
        t1_copy(d).wait_send()
        t2_copy(d).wait_send()
        for k in range(2):
            f1_copy(k, d).wait_send()
            f2_copy(k, d).wait_send()

        @pl.when(z != d)
        def _():
            for keep, z_in, send in (
                (f_keep.at[0], fz_in.at[0], fz_s.at[0]),
                (f_keep.at[1], fz_in.at[1], fz_s.at[1]),
                (t_keep, tz_in, tz_s),
            ):
                remote(keep.at[d], z_in.at[d], send.at[d], send.at[d], partner).wait_send()

    each(sent)
    for gather in gathers:
        gather.sent()
    for copy in writes:
        copy.wait()


def run_sums(gain_sums, operands):
    nf, inner, gg, gu, br, la, ra, nr, kvg = operands
    depth, width = nf.shape
    ff, half = inner.shape[1], gg.shape[1]
    per, deep = width // RANKS, ff // RANKS
    part = (per // 2 + 15) // 16 * 16
    quarter, fine = half // 2, deep // 2
    columns = br.shape[1]
    wide_t = width // 128 * 128 + 128 + kvg.shape[1]
    vmem, hbm = pl.BlockSpec(memory_space=pltpu.VMEM), pl.BlockSpec(memory_space=pl.ANY)
    out = lambda *shape: jax.ShapeDtypeStruct(shape, F32)
    b = lambda *shape: pltpu.VMEM(shape, BF16)
    f = lambda *shape: pltpu.VMEM(shape, F32)
    sem = lambda *shape: pltpu.SemaphoreType.DMA(shape)
    return pl.pallas_call(
        sums_kernel,
        out_shape=[
            out(per, width), out(per, width), out(2, per, kvg.shape[1]), out(per, 128),
            out(per, ff), out(per, ff), out(deep, width),
        ],
        in_specs=[vmem] + [hbm] * 9,
        out_specs=[hbm] * 7,
        scratch_shapes=[
            b(depth, width), b(depth, width), b(depth, ff), b(depth, columns), b(depth, half), b(depth, half),
            b(depth, width), b(depth, kvg.shape[1]),
            b(width, depth), b(width, depth), b(width, depth), b(deep, depth), f(width, 128),
            b(3, deep, columns), b(5, deep, columns), f(2, fine // 2, columns),
            b(2, fine // 2, columns), b(2, fine // 2, columns), b(2, fine // 4, columns), b(2, fine // 4, columns),
            b(2, RANKS, per, quarter), b(2, RANKS, per, quarter),
            b(2, RANKS, part, quarter), b(2, RANKS, part, quarter), b(2, RANKS, part, quarter), b(2, 5, part, quarter),
            b(RANKS, part, wide_t), b(RANKS, part, wide_t),
            b(RANKS, part // 2, wide_t), b(RANKS, part // 2, wide_t), b(RANKS, part // 2, wide_t), b(5, part // 2, wide_t),
            b(2, 2, 4, fine // 4, columns), b(2, 2, 4, part, quarter), b(2, 4, part // 2, wide_t),
            f(2, per, ff), f(2, per, width), f(2, per, kvg.shape[1]), f(per, 128), f(deep, width),
            sem(9), sem(3, 2), sem(5, 2), sem(2), sem(2), sem(2), sem(2),
            sem(2, 4), sem(2, 4), sem(2, 4), sem(2, 4), sem(2, 4), sem(2, 5),
            sem(4), sem(4), sem(4), sem(4), sem(4), sem(5),
            sem(5, 8), sem(5, 4), sem(5, 4), sem(7),
        ],
        compiler_params=pltpu.CompilerParams(
            collective_id=2, has_side_effects=True, vmem_limit_bytes=61 * 2**20
        ),
        name="sums",
    )(gain_sums, *operands)


def sums_by_xla(gain_sums, operands):
    nf, inner, gg, gu, br, la, ra, nr, kvg = operands
    width = nf.shape[1]

    def reduced(left, right):
        total = dot_lt(left, right).astype(BF16)
        piece = lax.psum_scatter(total, "dp", scatter_dimension=0, tiled=True)
        return lax.psum(piece, "ctx")

    def both(piece, axis):
        return lax.all_gather(piece, "section", axis=axis, tiled=axis > 0).astype(F32)

    attn = both(reduced(la, ra), 0)
    gain_sum = lax.psum(gain_sums[:2], ("section", "ctx"))
    return (
        attn[0],
        attn[1],
        both(reduced(nr, kvg), 0),
        lax.psum_scatter(gain_sum, "dp", scatter_dimension=1, tiled=True),
        both(reduced(nf, gg), 1),
        both(reduced(nf, gu), 1),
        both(reduced(inner, br), 1)[:, :width],
    )


def shards(
    ends,
    doc_lengths,
    w_query,
    key_projection_weight,
    value_projection_weight,
    w_out,
    w_gate,
    w_up,
    w_down,
    gain_attn,
    gain_ffn,
):
    rows, width = ends.shape[2:]
    section = lax.axis_index("section")
    ctx = lax.axis_index("ctx")
    row_tokens = rows * lax.axis_size("ctx")
    rank = 2 * section + ctx % 2
    lengths = lax.dynamic_index_in_dim(doc_lengths, ctx // 2, 0, keepdims=False)[0]

    def place(token_index):
        segment = jnp.zeros_like(token_index)
        start = jnp.zeros_like(token_index)
        finish = jnp.int32(0)
        for slot in range(lengths.shape[0]):
            finish = finish + lengths[slot]
            passed = (token_index >= finish).astype(jnp.int32)
            segment = segment + passed
            start = start + passed * lengths[slot]
        return segment, token_index - start

    seg_keys, _ = place(lax.broadcasted_iota(jnp.int32, (8, row_tokens), 1))
    seg_mine, token_position = place(
        rank * rows + lax.broadcasted_iota(jnp.int32, (rows, 128), 0)
    )
    lane = lax.broadcasted_iota(jnp.int32, (rows, 128), 1)
    half = HEAD_SIZE // 2
    frequency = 10000.0 ** (-2.0 * (lane % half).astype(F32) / HEAD_SIZE)
    angles = token_position.astype(F32) * frequency
    cosines = jnp.cos(angles)
    sines = jnp.where(lane % HEAD_SIZE < half, -1.0, 1.0) * jnp.sin(angles)
    w_kv = jnp.stack(
        [
            key_projection_weight.reshape(width, KEY_VALUE_HEADS, HEAD_SIZE),
            value_projection_weight.reshape(width, KEY_VALUE_HEADS, HEAD_SIZE),
        ],
        axis=2,
    ).reshape(width, 2 * KEY_VALUE_HEADS * HEAD_SIZE)
    gains = jnp.concatenate(
        [jnp.stack([gain_attn, gain_ffn]).astype(F32), jnp.zeros((6, width), F32)]
    )
    acts, grads_in, gain_sums, nf, inner, gg, gu, br, la, ra, nr, kvg = run_layers(
        ends,
        cosines,
        sines,
        seg_keys,
        seg_mine,
        gains,
        (w_query, w_kv, w_out, w_gate, w_up, w_down),
    )

    operands = (nf, inner, gg, gu, br, la, ra, nr, kvg)
    fits = lax.axis_size("dp") == RANKS and width % 64 == 0 and inner.shape[1] % 1280 == 0
    if fits:
        grad_query, grad_out, kv_parts, gain_pieces, grad_gate, grad_up, grad_down = run_sums(
            gain_sums, operands
        )
        gain_at = width % 128
        gain_piece = gain_pieces[:, gain_at : gain_at + 2].T
    else:
        grad_query, grad_out, kv_parts, gain_piece, grad_gate, grad_up, grad_down = sums_by_xla(
            gain_sums, operands
        )
    kv_grad = jnp.concatenate([kv_parts[0], kv_parts[1][:, 128:]], axis=1).reshape(
        -1, KEY_VALUE_HEADS, 2, HEAD_SIZE
    )
    grad_key = kv_grad[:, :, 0].reshape(kv_grad.shape[0], -1)
    grad_value = kv_grad[:, :, 1].reshape(kv_grad.shape[0], -1)
    return (
        acts,
        grads_in,
        grad_query,
        grad_key,
        grad_value,
        grad_out,
        grad_gate,
        grad_up,
        grad_down,
        gain_piece[0],
        gain_piece[1],
    )


def solution(mesh):
    return jax.shard_map(
        shards,
        mesh=mesh,
        in_specs=(P("section", None, ("dp", "ctx"), None), P(None, "dp", None)) + (P(),) * 9,
        out_specs=(P("section", None, ("dp", "ctx"), None),) * 2
        + (P("dp", None),) * 7
        + (P("dp"),) * 2,
        check_vma=False,
    )
```

```python
import jax
import jax.numpy as jnp
import numpy as np
from jax import lax
from jax.experimental import pallas as pl
from jax.experimental.pallas import tpu as pltpu
from jax.sharding import PartitionSpec as P

MESH = pl.DeviceIdType.MESH
QUERY_HEADS = 15
KEY_VALUE_HEADS = 5
HEAD_SIZE = 64
SHARE = QUERY_HEADS // KEY_VALUE_HEADS
RANKS = 4
epsilon = 1e-05
masked_fill = -1e30
F32 = jnp.float32
BF16 = jnp.bfloat16


def dot(left, right):
    return jnp.dot(left, right, preferred_element_type=F32)


def dot_rt(left, right):
    return lax.dot_general(left, right, (((1,), (1,)), ((), ())), preferred_element_type=F32)


def dot_lt(left, right):
    return lax.dot_general(left, right, (((0,), (0,)), ((), ())), preferred_element_type=F32)


def tiles(total, width):
    return [(at, min(width, total - at)) for at in range(0, total, width)]


def wide(block):
    missing = 128 - block.shape[1]
    if not missing:
        return block
    return jnp.concatenate([block, jnp.zeros((block.shape[0], missing), block.dtype)], axis=1)


def lanes(rows):
    return lax.broadcasted_iota(jnp.int32, (rows, 128), 1)


def half_turn(block):
    front = lanes(block.shape[0]) % HEAD_SIZE < HEAD_SIZE // 2
    return jnp.where(front, pltpu.roll(block, 96, 1), pltpu.roll(block, 32, 1))


def inverse_rms(hidden):
    return lax.rsqrt(jnp.mean(hidden * hidden, axis=-1, keepdims=True) + epsilon)


def layers_kernel(
    lengths, ends, frequency, gain_a, gain_f, wq_h, wk_h, wv_h, wo_h, wg_h, wu_h, wd_h,
    acts_o, grads_o, gain_o, nf_o, in_o, gg_o, gu_o, br_o, la_o, ra_o, nr_o, kvg_o,
    wq, wkv, wo, wg, wu, wd,
    act, go, middle, norm_ffn, fact_a, fact_b, inner, lm, qd, kv, o_raw,
    sum_acc, gm, gg, gu, br, ra, dq_raw, pds, dkv, dkv_in, gkv, cos_sin, allowed_add,
    w_sem, kv_sem, in_send, in_recv, kv_send, kv_recv, dk_send, dk_recv, out_send, out_recv,
    op_own, op_send, op_recv,
):
    section = lax.axis_index("section")
    dp = lax.axis_index("dp")
    ctx = lax.axis_index("ctx")
    micro = ctx // 2
    xbit = ctx % 2
    rank = 2 * section + xbit
    rows, width = act.shape[1], act.shape[2]
    ff = wg.shape[1]
    ff_half = ff // 2

    def device_of(r):
        return (r // 2, dp, 2 * micro + r % 2)

    partner = (1 - section, dp, ctx)

    loads = [
        pltpu.make_async_copy(h, v, w_sem.at[i])
        for i, (h, v) in enumerate([(wq_h, wq), (wo_h, wo), (wg_h, wg), (wu_h, wu), (wd_h, wd)])
    ]
    kv_loads = [
        pltpu.make_async_copy(
            h.at[pl.ds(g * HEAD_SIZE, HEAD_SIZE)],
            wkv.at[pl.ds((2 * g + i) * HEAD_SIZE, HEAD_SIZE)],
            kv_sem.at[i, g],
        )
        for g in range(KEY_VALUE_HEADS)
        for i, h in enumerate((wk_h, wv_h))
    ]
    for load in kv_loads + loads:
        load.start()
    kv[...] = jnp.zeros_like(kv)
    barrier = pltpu.get_barrier_semaphore()
    for step in range(1, 8):
        other = (4 * section + ctx + step) % 8
        pl.semaphore_signal(
            barrier, inc=1, device_id=(other // 4, dp, other % 4), device_id_type=MESH
        )
    pl.semaphore_wait(barrier, 7)

    def in_copy(block, into_x):
        dst = act.at[0] if into_x else go.at[2]
        slot = 0 if into_x else 1
        return (
            pltpu.make_async_copy(ends.at[0, block], dst, in_recv.at[slot]),
            pltpu.make_async_remote_copy(
                src_ref=ends.at[0, block],
                dst_ref=dst,
                send_sem=in_send.at[block],
                recv_sem=in_recv.at[slot],
                device_id=(ctx // 2, dp, 2 * block + xbit),
                device_id_type=MESH,
            ),
        )

    def in_mine(block):
        return (section == ctx // 2) & (ctx // 2 == block)

    def in_start(into_x):
        here = section == (0 if into_x else 1)
        for block in range(2):

            @pl.when(here & in_mine(block))
            def _(block=block):
                in_copy(block, into_x)[0].start()

            @pl.when(here & jnp.logical_not(in_mine(block)))
            def _(block=block):
                in_copy(block, into_x)[1].start()

    in_start(True)

    lane = lanes(rows)
    low = lane < HEAD_SIZE
    gain_attn = gain_a[...].astype(F32)
    gain_ffn = gain_f[...].astype(F32)

    def place(token_index):
        segment = jnp.zeros_like(token_index)
        start = jnp.zeros_like(token_index)
        finish = jnp.int32(0)
        for slot in range(lengths.shape[2]):
            length = lengths[micro, 0, slot]
            finish = finish + length
            passed = (token_index >= finish).astype(jnp.int32)
            segment = segment + passed
            start = start + passed * length
        return segment, token_index - start

    seg_mine, position = place(rank * rows + lax.broadcasted_iota(jnp.int32, (rows, 128), 0))
    angles = position.astype(F32) * frequency[...]
    cos_sin[0] = jnp.cos(angles)
    cos_sin[1] = jnp.where(lane % HEAD_SIZE < HEAD_SIZE // 2, -1.0, 1.0) * jnp.sin(angles)
    key_index = lax.broadcasted_iota(jnp.int32, (1, RANKS * rows), 1)
    query_index = rank * rows + lax.broadcasted_iota(jnp.int32, (rows, 1), 0)
    allowed_add[...] = jnp.where(
        (seg_mine[:, 0:1] == place(key_index)[0]) & (query_index >= key_index), 0.0, masked_fill
    )

    def kv_rows(l, r):
        return kv.at[l, pl.ds(pl.multiple_of(r * rows, 16), rows)]

    def kv_copy(l, quarter, dst, slot):
        return pltpu.make_async_remote_copy(
            src_ref=kv_rows(l, quarter),
            dst_ref=kv_rows(l, quarter),
            send_sem=kv_send.at[l, slot],
            recv_sem=kv_recv.at[l, quarter],
            device_id=device_of(dst),
            device_id_type=MESH,
        )

    kv_plan = [(0, 0, 1, 0), (0, 0, 2, 1), (1, 1, 2, 0), (1, 1, 3, 1), (2, 2, 3, 0)]
    kv_relay = (1, 0, 3, 2)

    def kv_start(l):
        for sender, quarter, dst, slot in kv_plan:

            @pl.when(rank == sender)
            def _(quarter=quarter, dst=dst, slot=slot):
                kv_copy(l, quarter, dst, slot).start()

    def kv_finish(l):
        @pl.when(rank == 1)
        def _():
            kv_copy(l, 0, 3, 2).wait_recv()
            kv_copy(l, 0, 3, 2).start()

        for quarter, receivers in ((0, (2, 3)), (1, (2, 3)), (2, (3,))):
            for receiver in receivers:

                @pl.when(rank == receiver)
                def _(quarter=quarter):
                    kv_copy(l, quarter, 0, 0).wait_recv()

    def kv_sent(l):
        for sender, quarter, dst, slot in kv_plan + [kv_relay]:

            @pl.when(rank == sender)
            def _(quarter=quarter, dst=dst, slot=slot):
                kv_copy(l, quarter, dst, slot).wait_send()

    def out_copy(array, out, l, kind):
        home = 2 * section + xbit
        return (
            pltpu.make_async_copy(array, out.at[0, micro], out_recv.at[kind, micro]),
            pltpu.make_async_remote_copy(
                src_ref=array,
                dst_ref=out.at[0, micro],
                send_sem=out_send.at[kind, l],
                recv_sem=out_recv.at[kind, micro],
                device_id=(l, dp, home),
                device_id_type=MESH,
            ),
        )

    def out_mine(l):
        return (section == l) & (ctx == 2 * section + xbit)

    def out_start(array, out, l, kind):
        local, remote = out_copy(array, out, l, kind)

        @pl.when(out_mine(l))
        def _():
            local.start()

        @pl.when(jnp.logical_not(out_mine(l)))
        def _():
            remote.start()

    place = [pl.ds((2 * c + l) * rows, rows) for c in range(2) for l in range(2)]

    def op_rows(l):
        return pl.ds(pl.multiple_of((2 * section + l) * rows, 16), rows)

    def op_copy(kind, l, own):
        role = section if own else 1 - section
        half = pl.ds(pl.multiple_of(role * ff_half, 128), ff_half)
        src = [
            lambda: norm_ffn.at[l],
            lambda: inner.at[l],
            lambda: gg.at[:, half],
            lambda: gu.at[:, half],
            lambda: br.at[:, pl.ds(pl.multiple_of(role * 512, 128), 512)],
            lambda: lm.at[l, role],
            lambda: ra.at[role],
            lambda: lm.at[l, 0],
            lambda: gkv.at[:, pl.ds(pl.multiple_of(role * 256, 128), 384)],
        ][kind]()
        dst = [nf_o, in_o, gg_o, gu_o, br_o, la_o, ra_o, nr_o, kvg_o][kind].at[op_rows(l)]
        if own:
            return pltpu.make_async_copy(src, dst, op_own.at[kind, l])
        return pltpu.make_async_remote_copy(
            src_ref=src,
            dst_ref=dst,
            send_sem=op_send.at[kind, l],
            recv_sem=op_recv.at[kind, l],
            device_id=partner,
            device_id_type=MESH,
        )

    def op_start(kinds, l):
        for kind in kinds:
            op_copy(kind, l, True).start()
            op_copy(kind, l, False).start()

    def op_sent(kinds, l):
        for kind in kinds:
            op_copy(kind, l, True).wait()
            op_copy(kind, l, False).wait_send()

    in_copy(0, True)[1].wait_recv()
    for load in kv_loads:
        load.wait()

    def forward(l, carry):
        hidden = act[l].astype(F32)
        cos_q, sin_q = cos_sin[0], cos_sin[1]
        lm[l, 0] = (hidden * inverse_rms(hidden) * gain_attn).astype(BF16)
        cos_kv = jnp.where(low, cos_q, 1.0)
        sin_kv = jnp.where(low, sin_q, 0.0)
        mine = pl.ds(pl.multiple_of(rank * rows, 16), rows)
        for g in range(KEY_VALUE_HEADS):
            block = dot_rt(lm[l, 0], wkv[128 * g : 128 * g + 128, :])
            turned = block * cos_kv + half_turn(block) * sin_kv
            kv[l, mine, 128 * g : 128 * g + 128] = turned.astype(BF16)
        kv_start(l)

        @pl.when(l == 0)
        def _():
            loads[0].wait()
            in_start(False)

        for at, size in tiles(width, 256):
            product = dot(lm[l, 0], wq[:, at : at + size])
            for inside, part in tiles(size, 128):
                block = wide(product[:, inside : inside + part])
                turned = (block * cos_q + half_turn(block) * sin_q) * 0.125
                head = (at + inside) // HEAD_SIZE
                qd[l, head // SHARE, pl.ds(head % SHARE * rows, rows), :] = jnp.where(
                    low, turned, 0.0
                ).astype(BF16)
                head += 1
                if head < QUERY_HEADS:
                    qd[l, head // SHARE, pl.ds(head % SHARE * rows, rows), :] = jnp.where(
                        low, pltpu.roll(turned, 64, 1), 0.0
                    ).astype(BF16)
        kv_finish(l)
        allowed = allowed_add[...]
        cos_q, sin_q = cos_sin[0], cos_sin[1]

        def heads(g, carry):
            kv_g = kv[l, :, pl.ds(pl.multiple_of(g * 128, 128), 128)]
            for i in range(SHARE):
                scores = dot_rt(qd[l, g, i * rows : (i + 1) * rows, :], kv_g) + allowed
                peak = jnp.max(scores, axis=-1, keepdims=True)
                exponent = jnp.exp(scores - peak)
                total = jnp.sum(exponent, axis=-1, keepdims=True)
                out = dot(exponent.astype(BF16), kv_g) / total
                o_raw[l, g * SHARE + i] = jnp.where(low, peak + jnp.log(total), out)
            return carry

        lax.fori_loop(0, KEY_VALUE_HEADS, heads, 0)
        for at, size in tiles(width, 128):
            head = at // HEAD_SIZE
            block = pltpu.roll(o_raw[l, head], 64, 1)
            if size == 128:
                block = jnp.where(low, block, o_raw[l, head + 1])
            lm[l, 1, :, at : at + size] = block[:, :size].astype(BF16)

        @pl.when(l == 0)
        def _():
            loads[1].wait()

        for at, size in tiles(width, 256):
            middle[l, :, at : at + size] = act[l, :, at : at + size].astype(F32) + dot(
                lm[l, 1], wo[:, at : at + size]
            )
        mid = middle[l]
        norm_ffn[l] = (mid * inverse_rms(mid) * gain_ffn).astype(BF16)

        @pl.when(l == 0)
        def _():
            loads[2].wait()
            loads[3].wait()

        def gates(j, carry):
            part = pl.ds(pl.multiple_of(j * 256, 256), 256)
            gate = dot(norm_ffn[l], wg[:, part])
            upper = dot(norm_ffn[l], wu[:, part])
            s = jax.nn.sigmoid(gate)
            swish = gate * s
            inner[l, :, part] = (swish * upper).astype(BF16)
            fact_a[l, :, part] = (upper * s * (1.0 + gate * (1.0 - s))).astype(BF16)
            fact_b[l, :, part] = swish.astype(BF16)
            return carry

        lax.fori_loop(0, ff // 256, gates, 0)

        @pl.when(l == 0)
        def _():
            loads[4].wait()

        for at, size in tiles(width, 256):
            act[l + 1, :, at : at + size] = (
                middle[l, :, at : at + size] + dot_rt(inner[l], wd[at : at + size, :])
            ).astype(BF16)
        out_start(act.at[l + 1], acts_o, l, 0)
        op_start((0, 1, 7), l)
        kv_sent(l)
        return carry

    lax.fori_loop(0, 2, forward, 0)

    in_copy(0, False)[1].wait_recv()
    gain_o[...] = jnp.zeros_like(gain_o)
    br[...] = jnp.zeros_like(br)

    def dk_copy(l, src_quarter, count, dst, slot_in, slot):
        return pltpu.make_async_remote_copy(
            src_ref=dkv.at[pl.ds(src_quarter * rows, count * rows)],
            dst_ref=dkv_in.at[l, pl.ds(slot_in * rows, count * rows)],
            send_sem=dk_send.at[l, slot],
            recv_sem=dk_recv.at[l, slot_in],
            device_id=device_of(dst),
            device_id_type=MESH,
        )

    def backward(step, carry):
        l = 1 - step

        @pl.when(l == 0)
        def _():
            op_sent((2, 3, 4, 5, 6, 8), 1)

        branch = go[l + 1]
        br[:, :width] = branch
        op_start((4,), l)

        def gates(j, carry):
            part = pl.ds(pl.multiple_of(j * 256, 256), 256)
            grad_inner = dot(go[l + 1], wd[:, part])
            gg[:, part] = (grad_inner * fact_a[l, :, part].astype(F32)).astype(BF16)
            gu[:, part] = (grad_inner * fact_b[l, :, part].astype(F32)).astype(BF16)
            return carry

        lax.fori_loop(0, ff // 256, gates, 0)
        op_start((2, 3), l)
        for at, size in tiles(width, 256):
            sum_acc[:, at : at + size] = dot_rt(gg[...], wg[at : at + size, :]) + dot_rt(
                gu[...], wu[at : at + size, :]
            )

        def norm_back(hidden, gain, row):
            upstream = sum_acc[...]
            scale = inverse_rms(hidden)
            weighted = upstream * gain
            inside = jnp.mean(weighted * hidden, axis=-1, keepdims=True)
            gain_o[row : row + 1, :] += jnp.sum(upstream * hidden * scale, axis=0, keepdims=True)
            return scale * weighted - hidden * (scale * scale * scale * inside)

        gm[...] = go[l + 1].astype(F32) + norm_back(middle[l], gain_ffn, 1)
        ra[1] = gm[...].astype(BF16)

        for at, size in tiles(width, 256):
            product = dot_rt(ra[1], wo[at : at + size, :])
            for inside, part in tiles(size, 128):
                block = wide(product[:, inside : inside + part])
                head = (at + inside) // HEAD_SIZE
                qd[l, head // SHARE, pl.ds((SHARE + head % SHARE) * rows, rows), :] = jnp.where(
                    low, 0.0, pltpu.roll(block, 64, 1)
                ).astype(BF16)
                head += 1
                if head < QUERY_HEADS:
                    qd[l, head // SHARE, pl.ds((SHARE + head % SHARE) * rows, rows), :] = (
                        jnp.where(low, 0.0, block).astype(BF16)
                    )
        allowed = allowed_add[...]
        cos_q, sin_q = cos_sin[0], cos_sin[1]

        def heads(g, carry):
            kv_g = kv[l, :, pl.ds(pl.multiple_of(g * 128, 128), 128)]
            for i in range(SHARE):
                mine = slice(i * rows, (i + 1) * rows)
                other = slice((SHARE + i) * rows, (SHARE + i + 1) * rows)
                kept = o_raw[l, g * SHARE + i]
                log_total = kept[:, 0:1]
                scores = dot_rt(qd[l, g, mine, :], kv_g) + allowed
                probs = jnp.exp(scores - log_total)
                grad_out = qd[l, g, other, :]
                grad_probs = dot_rt(grad_out, kv_g)
                weight = jnp.sum(grad_out.astype(F32) * kept, axis=-1, keepdims=True)
                grad_scores = (probs * (grad_probs - weight)).astype(BF16)
                pds[mine, :] = grad_scores
                pds[other, :] = probs.astype(BF16)
                dq_raw[g * SHARE + i] = dot(grad_scores, kv_g)
            grad_kv = dot_lt(qd[l, g], pds[...])
            dkv[:, pl.ds(pl.multiple_of(g * 128, 128), 128)] = grad_kv.T.astype(BF16)
            return carry

        lax.fori_loop(0, KEY_VALUE_HEADS, heads, 0)

        @pl.when(rank == 3)
        def _():
            dk_copy(l, 2, 1, 2, 0, 0).start()
            dk_copy(l, 0, 2, 1, 0, 1).start()

        @pl.when(rank == 2)
        def _():
            dk_copy(l, 1, 1, 1, 2, 0).start()
            dk_copy(l, 0, 1, 0, 1, 1).start()

        @pl.when(rank == 1)
        def _():
            dk_copy(l, 0, 2, 1, 0, 0).wait_recv()
            dkv[:rows] = (dkv[:rows].astype(F32) + dkv_in[l, :rows].astype(F32)).astype(BF16)
            dk_copy(l, 0, 1, 0, 0, 0).start()

        for at, size in tiles(width, 128):
            head = at // HEAD_SIZE
            block = dq_raw[head]
            if size == 128:
                block = jnp.where(low, block, pltpu.roll(dq_raw[head + 1], 64, 1))
            turned = (block * cos_q - half_turn(block) * sin_q) * 0.125
            ra[0, :, at : at + size] = turned[:, :size].astype(BF16)
        op_start((5, 6), l)

        @pl.when(rank == 3)
        def _():
            dk_copy(l, 2, 1, 2, 0, 0).wait_send()
            dk_copy(l, 0, 2, 1, 0, 1).wait_send()

        @pl.when(rank == 2)
        def _():
            dk_copy(l, 0, 1, 2, 0, 0).wait_recv()
            dk_copy(l, 1, 1, 1, 2, 0).wait_send()
            dk_copy(l, 0, 1, 0, 1, 1).wait_send()
            dkv[2 * rows : 3 * rows] = (
                dkv[2 * rows : 3 * rows].astype(F32) + dkv_in[l, :rows].astype(F32)
            ).astype(BF16)

        @pl.when(rank == 1)
        def _():
            dk_copy(l, 0, 1, 2, 2, 0).wait_recv()
            dk_copy(l, 0, 1, 0, 0, 0).wait_send()
            dkv[rows : 2 * rows] = (
                dkv[rows : 2 * rows].astype(F32)
                + dkv_in[l, rows : 2 * rows].astype(F32)
                + dkv_in[l, 2 * rows :].astype(F32)
            ).astype(BF16)

        @pl.when(rank == 0)
        def _():
            dk_copy(l, 0, 1, 2, 0, 0).wait_recv()
            dk_copy(l, 0, 1, 2, 1, 0).wait_recv()
            dkv[:rows] = (
                dkv[:rows].astype(F32)
                + dkv_in[l, :rows].astype(F32)
                + dkv_in[l, rows : 2 * rows].astype(F32)
            ).astype(BF16)

        cos_kv = jnp.where(low, cos_q, 1.0)
        sin_kv = jnp.where(low, sin_q, 0.0)
        mine = pl.ds(pl.multiple_of(rank * rows, 16), rows)
        for g in range(KEY_VALUE_HEADS):
            part = slice(128 * g, 128 * g + 128)
            block = dkv[mine, part].astype(F32)
            gkv[:, part] = (block * cos_kv - half_turn(block) * sin_kv).astype(BF16)
        op_start((8,), l)
        for at, size in tiles(width, 256):
            sum_acc[:, at : at + size] = dot_rt(ra[0], wq[at : at + size, :]) + dot(
                gkv[...], wkv[:, at : at + size]
            )
        go[l] = (gm[...] + norm_back(act[l].astype(F32), gain_attn, 0)).astype(BF16)
        out_start(go.at[l], grads_o, l, 1)
        return carry

    lax.fori_loop(0, 2, backward, 0)

    @pl.when(section == 0)
    def _():
        for block in range(2):

            @pl.when(jnp.logical_not(in_mine(block)))
            def _(block=block):
                in_copy(block, True)[1].wait_send()

    @pl.when(section == 1)
    def _():
        for block in range(2):

            @pl.when(jnp.logical_not(in_mine(block)))
            def _(block=block):
                in_copy(block, False)[1].wait_send()

    op_sent((2, 3, 4, 5, 6, 8), 0)
    for l in range(2):
        op_sent((0, 1, 7), l)
        for kind in range(9):
            op_copy(kind, l, False).wait_recv()
        for kind, out, array in ((0, acts_o, act.at[l + 1]), (1, grads_o, go.at[l])):

            @pl.when(jnp.logical_not(out_mine(l)))
            def _(l=l, kind=kind, out=out, array=array):
                out_copy(array, out, l, kind)[1].wait_send()

    for kind, out in ((0, acts_o), (1, grads_o)):
        for block in range(2):
            pltpu.make_async_copy(act.at[0], out.at[0, block], out_recv.at[kind, block]).wait()


def run_layers(lengths, ends, frequency, gain_attn, gain_ffn, weights):
    micro_count, rows, width = ends.shape[1:]
    wq, wk, wv, wo, wg, wu, wd = weights
    ff = wg.shape[1]
    keys = RANKS * rows
    kv_width = 2 * wk.shape[0]
    vmem, hbm = pl.BlockSpec(memory_space=pltpu.VMEM), pl.BlockSpec(memory_space=pl.ANY)
    op_rows = 4 * rows
    out = lambda *shape: jax.ShapeDtypeStruct(shape, BF16)
    dma = pltpu.SemaphoreType.DMA
    return pl.pallas_call(
        layers_kernel,
        out_shape=[
            out(*ends.shape),
            out(*ends.shape),
            jax.ShapeDtypeStruct((8, width), F32),
            out(op_rows, width),
            out(op_rows, ff),
            out(op_rows, ff // 2),
            out(op_rows, ff // 2),
            out(op_rows, 512),
            out(op_rows, width),
            out(op_rows, width),
            out(op_rows, width),
            out(op_rows, 384),
        ],
        in_specs=[pl.BlockSpec(memory_space=pltpu.SMEM), hbm] + [vmem] * 3 + [hbm] * 7,
        out_specs=[hbm, hbm, vmem] + [hbm] * 9,
        scratch_shapes=[
            pltpu.VMEM(wq.shape, BF16),
            pltpu.VMEM((kv_width, width), BF16),
            pltpu.VMEM(wo.shape, BF16),
            pltpu.VMEM(wg.shape, BF16),
            pltpu.VMEM(wu.shape, BF16),
            pltpu.VMEM(wd.shape, BF16),
            pltpu.VMEM((3, rows, width), BF16),
            pltpu.VMEM((3, rows, width), BF16),
            pltpu.VMEM((2, rows, width), F32),
            pltpu.VMEM((2, rows, width), BF16),
            pltpu.VMEM((2, rows, ff), BF16),
            pltpu.VMEM((2, rows, ff), BF16),
            pltpu.VMEM((2, rows, ff), BF16),
            pltpu.VMEM((2, 2, rows, width), BF16),
            pltpu.VMEM((2, KEY_VALUE_HEADS, 2 * SHARE * rows, 128), BF16),
            pltpu.VMEM((2, keys, kv_width), BF16),
            pltpu.VMEM((2, QUERY_HEADS, rows, 128), F32),
            pltpu.VMEM((rows, width), F32),
            pltpu.VMEM((rows, width), F32),
            pltpu.VMEM((rows, ff), BF16),
            pltpu.VMEM((rows, ff), BF16),
            pltpu.VMEM((rows, 1024), BF16),
            pltpu.VMEM((2, rows, width), BF16),
            pltpu.VMEM((QUERY_HEADS, rows, 128), F32),
            pltpu.VMEM((2 * SHARE * rows, keys), BF16),
            pltpu.VMEM((keys, kv_width), BF16),
            pltpu.VMEM((2, 3 * rows, kv_width), BF16),
            pltpu.VMEM((rows, kv_width), BF16),
            pltpu.VMEM((2, rows, 128), F32),
            pltpu.VMEM((rows, keys), F32),
            dma((5,)),
            dma((2, KEY_VALUE_HEADS)),
            dma((2,)),
            dma((2,)),
            dma((2, 3)),
            dma((2, 3)),
            dma((2, 2)),
            dma((2, 3)),
            dma((2, 2)),
            dma((2, 2)),
            dma((9, 2)),
            dma((9, 2)),
            dma((9, 2)),
        ],
        compiler_params=pltpu.CompilerParams(
            collective_id=1, has_side_effects=True, vmem_limit_bytes=61 * 2**20
        ),
        name="layers",
    )(lengths, ends, frequency, gain_attn, gain_ffn, *weights)


def sums_kernel(
    gain_sums, nf_h, in_h, gg_h, gu_h, br_h, la_h, ra_h, nr_h, kvg_h,
    t_o, gate_o, up_o, down_o,
    stage_a, stage_b, in_v, br_v, gg_v, gu_v, ra_v, kvg_v, nf_t, la_t, nr_t, in_t, gain_t,
    d_out, d_in, d_keep, d1_out, d1_in, d2_out, d2_in,
    f1_out, f1_in, f2_out, f2_in, f_keep, fz_in,
    t1_out, t1_in, t2_out, t2_in, t_keep, tz_in,
    d_all, f_all, t_all,
    load, dz_s, dz_r, d1_s, d1_r, d2_s, d2_r, f1_s, f1_r, f2_s, f2_r, fz_s, fz_r,
    t1_s, t1_r, t2_s, t2_r, tz_s, tz_r, all_s, all_r, pair_r, write,
):
    section = lax.axis_index("section")
    z = lax.axis_index("dp")
    ctx = lax.axis_index("ctx")
    x, y = ctx % 2, ctx // 2
    x_next = (section, z, 2 * y + 1 - x)
    y_next = (section, z, 2 * (1 - y) + x)
    partner = (1 - section, z, ctx)
    depth = nf_h.shape[0]
    width = nf_h.shape[1]
    per = width // RANKS
    part = f_keep.shape[2]
    shift = per - part
    quarter = gg_v.shape[1] // 2
    deep = in_h.shape[1] // RANKS
    fine = deep // 2
    last = RANKS - 1

    def remote(src, dst, send, recv, device):
        return pltpu.make_async_remote_copy(
            src_ref=src, dst_ref=dst, send_sem=send, recv_sem=recv,
            device_id=device, device_id_type=MESH,
        )

    def some(start, size, unit=16):
        return pl.ds(pl.multiple_of(start, unit), size)

    loads = [
        pltpu.make_async_copy(h, v, load.at[i])
        for i, (h, v) in enumerate(
            [(in_h, in_v), (br_h, br_v), (nf_h, stage_a), (gg_h, gg_v), (gu_h, gu_v),
             (la_h, stage_b), (ra_h, ra_v), (kvg_h, kvg_v), (nr_h, stage_a)]
        )
    ]
    for copy in loads[:8]:
        copy.start()
    barrier = pltpu.get_barrier_semaphore()
    for device in (x_next, y_next, partner):
        pl.semaphore_signal(barrier, inc=1, device_id=device, device_id_type=MESH)
    inner_left = (z > 0).astype(jnp.int32)
    inner_right = (z < last).astype(jnp.int32)

    @pl.when(z > 0)
    def _():
        pl.semaphore_signal(barrier, inc=1, device_id=(section, z - 1, ctx), device_id_type=MESH)

    @pl.when(z < last)
    def _():
        pl.semaphore_signal(barrier, inc=1, device_id=(section, z + 1, ctx), device_id_type=MESH)

    pl.semaphore_wait(barrier, 3 + inner_left + inner_right)

    def turn(src, dst):
        for at, size in tiles(src.shape[1], 128):
            block = src[:, at : at + size]
            if size < 128:
                block = wide(block)
            dst[at : at + size, :] = block.T[:size]

    def z_way(t):
        up = (z < t).astype(jnp.int32)
        to = z + 2 * up - 1
        arrives = up * inner_left + (1 - up) * inner_right
        meets = (1 - up) * (t == z - 1).astype(jnp.int32)
        return (section, to, ctx), arrives, t * (1 - meets) + RANKS * meets

    def d_turn(k):
        is_ = lambda v: (z == v).astype(jnp.int32)
        order = ((3, 2, 1), (3, 0, 2), (0, 3, 1), (0, 1, 2))
        return sum(is_(v) * order[v][k] for v in range(RANKS))

    def d_block(t):
        for b in range(deep // 128):
            in_t[b * 128 : (b + 1) * 128, :] = in_v[:, some(t * deep + b * 128, 128, 128)].T

    def d_send(k, t, sub):
        device, _, slot = z_way(t)
        rows = pl.ds(sub * fine, fine)
        return remote(d_out.at[k, rows], d_in.at[slot, rows], dz_s.at[k, sub], dz_r.at[slot, sub], device)

    def d_step(k):
        t = d_turn(k)
        _, arrives, _ = z_way(t)
        d_block(t)
        for sub in range(2):
            rows = slice(sub * fine, (sub + 1) * fine)
            mine = dot(in_t[rows, :], br_v[...])

            @pl.when(arrives == 0)
            def _():
                d_out[k, rows, :] = mine.astype(BF16)

            @pl.when(arrives == 1)
            def _():
                remote(d_out.at[k, rows], d_in.at[t, rows], dz_s.at[k, sub], dz_r.at[t, sub], partner).wait_recv()
                d_out[k, rows, :] = (mine + d_in[t, rows, :].astype(F32)).astype(BF16)

            d_send(k, t, sub).start()

    def f_links(k):
        return (x_next, y_next, x, y) if k == 0 else (y_next, x_next, y, x)

    def f_right(k, column_half):
        src = gg_v if k == 0 else gu_v
        return src[:, some(column_half * quarter, quarter, 128)]

    def f1_copy(k, d):
        return remote(f1_out.at[k, d], f1_in.at[k, d], f1_s.at[k, d], f1_r.at[k, d], f_links(k)[0])

    def f2_copy(k, d):
        return remote(f2_out.at[k, d], f2_in.at[k, d], f2_s.at[k, d], f2_r.at[k, d], f_links(k)[1])

    def f1_step(d):
        for k in range(2):
            first = f_links(k)[2]
            left = nf_t[some(d * per, per), :]
            f1_out[k, d] = dot(left, f_right(k, 1 - first)).astype(BF16)
            f1_copy(k, d).start()

    def f2_step(d):
        for k in range(2):
            first, second = f_links(k)[2:]
            f1_copy(k, d).wait_recv()
            for mine in (False, True):
                at = (second if mine else 1 - second) * shift
                total = dot(nf_t[some(d * per + at, part), :], f_right(k, first)) + f1_in[
                    k, d, some(at, part), :
                ].astype(F32)
                if mine:
                    f_keep[k, d] = total.astype(BF16)
                else:
                    f2_out[k, d] = total.astype(BF16)
                    f2_copy(k, d).start()

    def t_links(d):
        x_first = (d < RANKS // 2).astype(jnp.int32)
        first, second = x_first * x + (1 - x_first) * y, x_first * y + (1 - x_first) * x
        to_x = (section, z, 2 * y + 1 - x)
        to_y = (section, z, 2 * (1 - y) + x)
        pick = lambda a, b: tuple(x_first * i + (1 - x_first) * j for i, j in zip(a, b))
        return pick(to_x, to_y), pick(to_y, to_x), first, second

    def t_product(row, count, add):
        mine = dot(la_t[some(row, count), :], ra_v[...])
        pairs = dot(nr_t[some(row, count), :], kvg_v[...])
        gains = gain_t[some(row, count), :]
        full = width // 128 * 128
        tail = jnp.concatenate([mine[:, full:], gains[:, width - full :]], axis=1)
        return [(0, add(mine[:, :full], 0)), (full, add(tail, full)), (full + 128, add(pairs, full + 128))]

    def t1_copy(d):
        return remote(t1_out.at[d], t1_in.at[d], t1_s.at[d], t1_r.at[d], t_links(d)[0])

    def t2_copy(d):
        return remote(t2_out.at[d], t2_in.at[d], t2_s.at[d], t2_r.at[d], t_links(d)[1])

    def t1_step(d):
        first = t_links(d)[2]
        for at, value in t_product(d * per + (1 - first) * shift, part, lambda v, at: v):
            t1_out[d, :, at : at + value.shape[1]] = value.astype(BF16)
        t1_copy(d).start()

    def t2_step(d):
        _, _, first, second = t_links(d)
        t1_copy(d).wait_recv()
        for mine in (False, True):
            row = (second if mine else 1 - second) * (part // 2)
            add = lambda v, at: v + t1_in[d, some(row, part // 2), at : at + v.shape[1]].astype(F32)
            dst = t_keep if mine else t2_out
            for at, value in t_product(d * per + first * shift + row, part // 2, add):
                dst[d, :, at : at + value.shape[1]] = value.astype(BF16)
            if not mine:
                t2_copy(d).start()

    def z_step(keep, second_in, z_in, send, recv, copy, d):
        copy.wait_recv()
        keep[d] = (keep[d].astype(F32) + second_in[d].astype(F32)).astype(BF16)

        @pl.when(z != d)
        def _():
            device, arrives, slot = z_way(d)

            @pl.when(arrives == 1)
            def _():
                remote(keep.at[d], z_in.at[d], send.at[d], recv.at[d], partner).wait_recv()
                keep[d] = (keep[d].astype(F32) + z_in[d].astype(F32)).astype(BF16)

            remote(keep.at[d], z_in.at[slot], send.at[d], recv.at[slot], device).start()

    def z_arrived(z_in, recv, src):
        @pl.when(z > 0)
        def _():
            remote(src, z_in.at[z], recv.at[z], recv.at[z], partner).wait_recv()

        @pl.when(z < last)
        def _():
            remote(src, z_in.at[RANKS], recv.at[RANKS], recv.at[RANKS], partner).wait_recv()

    def z_total(value, up, down):
        value = value + jnp.where(z > 0, up.astype(F32), 0.0)
        return value + jnp.where(z < last, down.astype(F32), 0.0)

    def places(x_first):
        a, b = (1, 0) if x_first is True else (0, 1) if x_first is False else (x_first, 1 - x_first)
        spot = lambda i, j: a * (2 * i + j) + b * (2 * j + i)
        return spot(x, y), spot(1 - x, y), spot(x, 1 - y), spot(1 - x, 1 - y)

    class Gather:
        def __init__(self, number, buffer, x_first):
            self.n, self.buffer = number, buffer
            self.own, self.over_x, self.over_y, self.across = places(x_first)
            rows = buffer.shape[2]
            cut = (rows // 2 + 15) // 16 * 16
            self.halves = (pl.ds(0, cut), pl.ds(cut, rows - cut))

        def whole(self, spot, slot, device):
            ref = self.buffer.at[section, spot]
            return remote(ref, ref, all_s.at[self.n, slot], all_r.at[self.n, slot], device)

        def relay(self, spot, half, device):
            ref = self.buffer.at[section, spot, self.halves[half]]
            return remote(ref, ref, all_s.at[self.n, 2 + half], all_r.at[self.n, 2 + half], device)

        def pair(self, core, spot, slot):
            ref = self.buffer.at[core, spot]
            return remote(ref, ref, all_s.at[self.n, 4 + slot], pair_r.at[self.n, spot], partner)

        def start(self):
            self.whole(self.own, 0, x_next).start()
            self.whole(self.own, 1, y_next).start()
            self.pair(section, self.own, 0).start()

        def middle(self):
            self.whole(self.over_x, 0, x_next).wait_recv()
            self.relay(self.over_x, 0, y_next).start()
            self.pair(section, self.over_x, 1).start()
            self.whole(self.over_y, 1, y_next).wait_recv()
            self.relay(self.over_y, 1, x_next).start()
            self.pair(section, self.over_y, 2).start()

        def finish(self):
            self.relay(self.across, 0, y_next).wait_recv()
            self.relay(self.across, 1, x_next).wait_recv()
            self.pair(section, self.across, 3).start()
            for spot in (self.own, self.over_x, self.over_y, self.across):
                self.pair(1 - section, spot, 0).wait_recv()

        def sent(self):
            self.whole(self.own, 0, x_next).wait_send()
            self.whole(self.own, 1, y_next).wait_send()
            self.relay(self.over_x, 0, y_next).wait_send()
            self.relay(self.over_y, 1, x_next).wait_send()
            for slot, spot in enumerate((self.own, self.over_x, self.over_y, self.across)):
                self.pair(section, spot, slot).wait_send()

    below = (z < RANKS // 2).astype(jnp.int32)
    gathers = [
        Gather(0, d_all.at[0], True),
        Gather(1, d_all.at[1], False),
        Gather(2, f_all.at[0], True),
        Gather(3, f_all.at[1], False),
        Gather(4, t_all, below),
    ]

    def in_order(i):
        odd = i % 2
        return (1 - odd) * (last - i // 2) + odd * (i // 2)

    def each(step):
        def body(i, carry):
            step(in_order(i))
            return carry

        lax.fori_loop(0, RANKS, body, 0)

    loads[0].wait()
    loads[1].wait()
    d_step(0)
    loads[2].wait()
    turn(stage_a, nf_t)
    loads[8].start()
    loads[3].wait()
    loads[4].wait()
    each(f1_step)
    d_step(1)
    loads[5].wait()
    turn(stage_b, la_t)
    loads[8].wait()
    turn(stage_a, nr_t)
    loads[6].wait()
    loads[7].wait()
    gain_rows = jnp.concatenate(
        [gain_sums[...], jnp.zeros((128 - gain_sums.shape[0], width), F32)], axis=0
    )
    for at, size in tiles(width, 128):
        block = wide(gain_rows[:, at : at + size]).T
        gain_t[at : at + size, :] = pltpu.roll(block, 64, 1)[:size]
    each(t1_step)
    d_step(2)
    each(f2_step)

    d_block(z)

    def d1_copy(h):
        return remote(d1_out.at[h], d1_in.at[h], d1_s.at[h], d1_r.at[h], f_links(h)[0])

    def d2_copy(h):
        return remote(d2_out.at[h], d2_in.at[h], d2_s.at[h], d2_r.at[h], f_links(h)[1])

    for h in range(2):
        rows = slice(h * fine, (h + 1) * fine)

        @pl.when(z > 0)
        def _():
            remote(d_out.at[0, rows], d_in.at[z, rows], dz_r.at[z, h], dz_r.at[z, h], partner).wait_recv()

        @pl.when(z < last)
        def _():
            remote(d_out.at[0, rows], d_in.at[RANKS, rows], dz_r.at[RANKS, h], dz_r.at[RANKS, h], partner).wait_recv()

        first = f_links(h)[2]
        for mine in (False, True):
            at = h * fine + (first if mine else 1 - first) * (fine // 2)
            span = some(at, fine // 2)
            total = z_total(dot(in_t[span, :], br_v[...]), d_in[z, span, :], d_in[RANKS, span, :])
            if mine:
                d_keep[h] = total
            else:
                d1_out[h] = total.astype(BF16)
                d1_copy(h).start()

    each(t2_step)
    each(lambda d: [
        z_step(f_keep.at[k], f2_in.at[k], fz_in.at[k], fz_s.at[k], fz_r.at[k], f2_copy(k, d), d)
        for k in range(2)
    ])
    for h in range(2):
        second = f_links(h)[3]
        d1_copy(h).wait_recv()
        for mine in (False, True):
            span = some((second if mine else 1 - second) * (fine // 4), fine // 4)
            total = d_keep[h, span, :] + d1_in[h, span, :].astype(F32)
            if mine:
                d_keep[h, : fine // 4, :] = total
            else:
                d2_out[h] = total.astype(BF16)
                d2_copy(h).start()
    each(lambda d: z_step(t_keep, t2_in, tz_in, tz_s, tz_r, t2_copy(d), d))
    for h in range(2):
        d2_copy(h).wait_recv()
        gathers[h].buffer[section, gathers[h].own] = (
            d_keep[h, : fine // 4, :] + d2_in[h].astype(F32)
        ).astype(BF16)
        gathers[h].start()
    for k in range(2):
        z_arrived(fz_in.at[k], fz_r.at[k], f_keep.at[k, 0])
        f_all[k, section, gathers[2 + k].own] = z_total(
            f_keep[k, z].astype(F32), fz_in[k, z], fz_in[k, RANKS]
        ).astype(BF16)
        gathers[2 + k].start()
    gathers[0].middle()
    gathers[1].middle()
    z_arrived(tz_in, tz_r, t_keep.at[0])
    t_all[section, gathers[4].own] = z_total(
        t_keep[z].astype(F32), tz_in[z], tz_in[RANKS]
    ).astype(BF16)
    gathers[4].start()
    gathers[2].middle()
    gathers[3].middle()

    writes = []

    def leave(src, dst):
        writes.append(pltpu.make_async_copy(src, dst, write.at[len(writes)]))
        writes[-1].start()

    for h in range(2):
        gathers[h].finish()
        for core in range(2):
            for spot in range(4):
                rows = pl.ds(h * fine + spot * (fine // 4), fine // 4)
                leave(d_all.at[h, core, spot], down_o.at[rows, pl.ds(core * br_v.shape[1], br_v.shape[1])])
    gathers[4].middle()
    for k in range(2):
        gathers[2 + k].finish()
        for core in range(2):
            for f in range(2):
                columns = pl.ds((2 * core + f) * quarter, quarter)
                out = (gate_o, up_o)[k]
                leave(f_all.at[k, core, 2 * f], out.at[pl.ds(0, part), columns])
                kept = pl.ds(part - shift, per - part)
                leave(f_all.at[k, core, 2 * f + 1, kept], out.at[pl.ds(part, per - part), columns])
    gathers[4].finish()
    t_rows = part // 2
    for core in range(2):
        for spot in range(4):
            row = spot % 2 * t_rows + spot // 2 * shift
            skip = part - shift if spot == 2 else 0
            kept = pl.ds(skip, t_rows - skip)
            leave(t_all.at[core, spot, kept], t_o.at[core, pl.ds(row + skip, t_rows - skip)])
    for k in range(3):
        for sub in range(2):
            d_send(k, d_turn(k), sub).wait_send()
    for h in range(2):
        d1_copy(h).wait_send()
        d2_copy(h).wait_send()

    def sent(d):
        t1_copy(d).wait_send()
        t2_copy(d).wait_send()
        for k in range(2):
            f1_copy(k, d).wait_send()
            f2_copy(k, d).wait_send()

        @pl.when(z != d)
        def _():
            for keep, z_in, send in (
                (f_keep.at[0], fz_in.at[0], fz_s.at[0]),
                (f_keep.at[1], fz_in.at[1], fz_s.at[1]),
                (t_keep, tz_in, tz_s),
            ):
                remote(keep.at[d], z_in.at[d], send.at[d], send.at[d], partner).wait_send()

    each(sent)
    for gather in gathers:
        gather.sent()
    for copy in writes:
        copy.wait()


def run_sums(gain_sums, operands):
    nf, inner, gg, gu, br, la, ra, nr, kvg = operands
    depth, width = nf.shape
    ff, half = inner.shape[1], gg.shape[1]
    per, deep = width // RANKS, ff // RANKS
    part = (per // 2 + 15) // 16 * 16
    quarter, fine = half // 2, deep // 2
    columns = br.shape[1]
    wide_t = width // 128 * 128 + 128 + kvg.shape[1]
    vmem, hbm = pl.BlockSpec(memory_space=pltpu.VMEM), pl.BlockSpec(memory_space=pl.ANY)
    out = lambda *shape: jax.ShapeDtypeStruct(shape, BF16)
    b = lambda *shape: pltpu.VMEM(shape, BF16)
    f = lambda *shape: pltpu.VMEM(shape, F32)
    sem = lambda *shape: pltpu.SemaphoreType.DMA(shape)
    return pl.pallas_call(
        sums_kernel,
        out_shape=[out(2, per, wide_t), out(per, ff), out(per, ff), out(deep, 2 * columns)],
        in_specs=[vmem] + [hbm] * 9,
        out_specs=[hbm] * 4,
        scratch_shapes=[
            b(depth, width), b(depth, width), b(depth, ff), b(depth, columns), b(depth, half), b(depth, half),
            b(depth, width), b(depth, kvg.shape[1]),
            b(width, depth), b(width, depth), b(width, depth), b(deep, depth), f(width, 128),
            b(3, deep, columns), b(5, deep, columns), f(2, fine // 2, columns),
            b(2, fine // 2, columns), b(2, fine // 2, columns), b(2, fine // 4, columns), b(2, fine // 4, columns),
            b(2, RANKS, per, quarter), b(2, RANKS, per, quarter),
            b(2, RANKS, part, quarter), b(2, RANKS, part, quarter), b(2, RANKS, part, quarter), b(2, 5, part, quarter),
            b(RANKS, part, wide_t), b(RANKS, part, wide_t),
            b(RANKS, part // 2, wide_t), b(RANKS, part // 2, wide_t), b(RANKS, part // 2, wide_t), b(5, part // 2, wide_t),
            b(2, 2, 4, fine // 4, columns), b(2, 2, 4, part, quarter), b(2, 4, part // 2, wide_t),
            sem(9), sem(3, 2), sem(5, 2), sem(2), sem(2), sem(2), sem(2),
            sem(2, 4), sem(2, 4), sem(2, 4), sem(2, 4), sem(2, 4), sem(2, 5),
            sem(4), sem(4), sem(4), sem(4), sem(4), sem(5),
            sem(5, 8), sem(5, 4), sem(5, 4), sem(40),
        ],
        compiler_params=pltpu.CompilerParams(
            collective_id=2, has_side_effects=True, vmem_limit_bytes=61 * 2**20
        ),
        name="sums",
    )(gain_sums, *operands)


def finish_kernel(
    acts_h, grads_h, t_h, gate_h, up_h, down_h,
    acts_o, grads_o, q_o, out_o, key_o, value_o, gain_o, gate_o, up_o, down_o,
    t_v, gate_v, down_v, q_f, kv_f, gate_f, down_f, load, store,
):
    width = q_f.shape[2]
    loads = [
        pltpu.make_async_copy(h, v, load.at[i])
        for i, (h, v) in enumerate(
            [(gate_h, gate_v.at[0]), (up_h, gate_v.at[1]), (down_h, down_v), (t_h, t_v)]
        )
    ]
    stores = [
        pltpu.make_async_copy(v, h, store.at[i])
        for i, (v, h) in enumerate(
            [(acts_h, acts_o), (grads_h, grads_o), (gate_f.at[0], gate_o), (gate_f.at[1], up_o),
             (down_f, down_o), (q_f.at[0], q_o), (q_f.at[1], out_o), (kv_f.at[0], key_o), (kv_f.at[1], value_o)]
        )
    ]
    for copy in loads + stores[:2]:
        copy.start()
    for k in range(2):
        loads[k].wait()
        gate_f[k] = gate_v[k].astype(F32)
        stores[2 + k].start()
    loads[2].wait()
    for at, size in tiles(width, 128):
        down_f[at : at + size, :] = down_v[:, at : at + 128].astype(F32).T[:size]
    stores[4].start()
    loads[3].wait()
    for core in range(2):
        q_f[core] = t_v[core, :, :width].astype(F32)
        stores[5 + core].start()
    pairs_at = width // 128 * 128 + 128
    half = KEY_VALUE_HEADS // 2 + 1
    for g in range(KEY_VALUE_HEADS):
        core = 0 if g < half else 1
        at = pairs_at + (g - core * (KEY_VALUE_HEADS - half)) * 128
        block = t_v[core, :, at : at + 128].astype(F32).T
        kv_f[0, g * HEAD_SIZE : (g + 1) * HEAD_SIZE, :] = block[:HEAD_SIZE]
        kv_f[1, g * HEAD_SIZE : (g + 1) * HEAD_SIZE, :] = block[HEAD_SIZE:]
    for copy in stores[7:]:
        copy.start()
    tail = slice(pairs_at - 128, pairs_at)
    both = t_v[0, :, tail].astype(F32) + t_v[1, :, tail].astype(F32)
    row = width % 128
    gain_o[...] = both.T[row : row + 8]
    for copy in stores:
        copy.wait()


def run_finish(acts, grads_in, t_sum, gate, up, down, width):
    per, ff = gate.shape
    vmem, hbm = pl.BlockSpec(memory_space=pltpu.VMEM), pl.BlockSpec(memory_space=pl.ANY)
    out = lambda *shape: jax.ShapeDtypeStruct(shape, F32)
    kv_rows = KEY_VALUE_HEADS * HEAD_SIZE
    return pl.pallas_call(
        finish_kernel,
        out_shape=[
            jax.ShapeDtypeStruct(acts.shape, BF16), jax.ShapeDtypeStruct(acts.shape, BF16),
            out(per, width), out(per, width), out(kv_rows, per), out(kv_rows, per), out(8, per),
            out(per, ff), out(per, ff), out(width, down.shape[0]),
        ],
        in_specs=[hbm] * 6,
        out_specs=[hbm] * 6 + [vmem] + [hbm] * 3,
        scratch_shapes=[
            pltpu.VMEM(t_sum.shape, BF16), pltpu.VMEM((2, per, ff), BF16), pltpu.VMEM(down.shape, BF16),
            pltpu.VMEM((2, per, width), F32), pltpu.VMEM((2, kv_rows, per), F32),
            pltpu.VMEM((2, per, ff), F32), pltpu.VMEM((width, down.shape[0]), F32),
            pltpu.SemaphoreType.DMA((4,)), pltpu.SemaphoreType.DMA((9,)),
        ],
        compiler_params=pltpu.CompilerParams(vmem_limit_bytes=40 * 2**20),
        name="finish",
    )(acts, grads_in, t_sum, gate, up, down)


def sums_by_xla(gain_sums, operands):
    nf, inner, gg, gu, br, la, ra, nr, kvg = operands
    width = nf.shape[1]

    def reduced(left, right):
        total = dot_lt(left, right).astype(BF16)
        piece = lax.psum_scatter(total, "dp", scatter_dimension=0, tiled=True)
        return lax.psum(piece, "ctx")

    def both(piece, axis):
        return lax.all_gather(piece, "section", axis=axis, tiled=axis > 0).astype(F32)

    attn = both(reduced(la, ra), 0)
    gain_sum = lax.psum(gain_sums[:2], ("section", "ctx"))
    return (
        attn[0],
        attn[1],
        both(reduced(nr, kvg), 0),
        lax.psum_scatter(gain_sum, "dp", scatter_dimension=1, tiled=True),
        both(reduced(nf, gg), 1),
        both(reduced(nf, gu), 1),
        both(reduced(inner, br), 1)[:, :width],
    )


def shards(
    ends,
    doc_lengths,
    w_query,
    key_projection_weight,
    value_projection_weight,
    w_out,
    w_gate,
    w_up,
    w_down,
    gain_attn,
    gain_ffn,
):
    width = ends.shape[3]
    half = HEAD_SIZE // 2
    turns = np.float32(10000.0) ** (
        np.float32(-2.0) * (np.arange(128) % half).astype(np.float32) / np.float32(HEAD_SIZE)
    )
    acts, grads_in, gain_sums, nf, inner, gg, gu, br, la, ra, nr, kvg = run_layers(
        doc_lengths,
        ends,
        jnp.asarray(turns.reshape(1, 128), F32),
        gain_attn.reshape(1, width),
        gain_ffn.reshape(1, width),
        (
            w_query,
            key_projection_weight.T,
            value_projection_weight.T,
            w_out,
            w_gate,
            w_up,
            w_down.T,
        ),
    )
    operands = (nf, inner, gg, gu, br, la, ra, nr, kvg)
    fits = lax.axis_size("dp") == RANKS and width % 64 == 0 and inner.shape[1] % 1280 == 0
    if fits:
        sums = run_sums(gain_sums, operands)
        acts, grads_in, grad_query, grad_out, grad_key, grad_value, gain_piece, grad_gate, grad_up, grad_down = (
            run_finish(acts, grads_in, *sums, width)
        )
        grad_key, grad_value, grad_down = grad_key.T, grad_value.T, grad_down.T
    else:
        grad_query, grad_out, kv_parts, gain_piece, grad_gate, grad_up, grad_down = sums_by_xla(
            gain_sums, operands
        )
        kv_grad = jnp.concatenate([kv_parts[0], kv_parts[1][:, 128:]], axis=1).reshape(
            -1, KEY_VALUE_HEADS, 2, HEAD_SIZE
        )
        grad_key = kv_grad[:, :, 0].reshape(kv_grad.shape[0], -1)
        grad_value = kv_grad[:, :, 1].reshape(kv_grad.shape[0], -1)
    return (
        acts,
        grads_in,
        grad_query,
        grad_key,
        grad_value,
        grad_out,
        grad_gate,
        grad_up,
        grad_down,
        gain_piece[0],
        gain_piece[1],
    )


def solution(mesh):
    return jax.shard_map(
        shards,
        mesh=mesh,
        in_specs=(P("section", None, ("dp", "ctx"), None), P(None, "dp", None)) + (P(),) * 9,
        out_specs=(P("section", None, ("dp", "ctx"), None),) * 2
        + (P("dp", None),) * 7
        + (P("dp"),) * 2,
        check_vma=False,
    )
```

```python
import jax
import jax.numpy as jnp
import numpy as np
from jax import lax
from jax.experimental import pallas as pl
from jax.experimental.pallas import tpu as pltpu
from jax.sharding import PartitionSpec as P

MESH = pl.DeviceIdType.MESH
QUERY_HEADS = 15
KEY_VALUE_HEADS = 5
HEAD_SIZE = 64
SHARE = QUERY_HEADS // KEY_VALUE_HEADS
RANKS = 4
epsilon = 1e-05
masked_fill = -1e30
F32 = jnp.float32
BF16 = jnp.bfloat16


def dot(left, right):
    return jnp.dot(left, right, preferred_element_type=F32)


def dot_rt(left, right):
    return lax.dot_general(left, right, (((1,), (1,)), ((), ())), preferred_element_type=F32)


def dot_lt(left, right):
    return lax.dot_general(left, right, (((0,), (0,)), ((), ())), preferred_element_type=F32)


def tiles(total, width):
    return [(at, min(width, total - at)) for at in range(0, total, width)]


def wide(block):
    missing = 128 - block.shape[1]
    if not missing:
        return block
    return jnp.concatenate([block, jnp.zeros((block.shape[0], missing), block.dtype)], axis=1)


def lanes(rows):
    return lax.broadcasted_iota(jnp.int32, (rows, 128), 1)


def half_turn(block):
    front = lanes(block.shape[0]) % HEAD_SIZE < HEAD_SIZE // 2
    return jnp.where(front, pltpu.roll(block, 96, 1), pltpu.roll(block, 32, 1))


def inverse_rms(hidden):
    return lax.rsqrt(jnp.mean(hidden * hidden, axis=-1, keepdims=True) + epsilon)


def half_turned(block, cosines, sines, direction):
    return block * cosines + direction * (half_turn(block) * sines)


def norm_back(hidden, gain, upstream):
    scale = inverse_rms(hidden)
    weighted = upstream * gain
    inside = jnp.mean(weighted * hidden, axis=-1, keepdims=True)
    gain_row = jnp.sum(upstream * hidden * scale, axis=0, keepdims=True)
    return scale * weighted - hidden * (scale * scale * scale * inside), gain_row


def start_if(condition, here, there):
    @pl.when(condition)
    def _():
        here().start()

    @pl.when(jnp.logical_not(condition))
    def _():
        there().start()


class AttentionBack:
    def __init__(
        self, rank, device_of, qd, kv, o_raw, allowed, cos_sin, ra, pds, dkv, dkv_in, gkv, send, recv
    ):
        self.rank, self.device_of = rank, device_of
        self.qd, self.kv, self.o_raw, self.allowed, self.cos_sin = qd, kv, o_raw, allowed, cos_sin
        self.ra, self.pds, self.dkv, self.dkv_in, self.gkv = ra, pds, dkv, dkv_in, gkv
        self.send_sem, self.recv_sem = send, recv
        self.rows, self.width = ra.shape[1:]

    def head(self, g):
        rows = self.rows
        kv_g = self.kv[g]
        for i in range(SHARE):
            mine = slice(i * rows, (i + 1) * rows)
            other = slice((SHARE + i) * rows, (SHARE + i + 1) * rows)
            kept = self.o_raw[g * SHARE + i]
            scores = dot_rt(self.qd[g, mine, :], kv_g) + self.allowed[...]
            probs = jnp.exp(scores - kept[:, 0:1])
            grad_out = self.qd[g, other, :]
            grad_probs = dot_rt(grad_out, kv_g)
            weight = jnp.sum(grad_out.astype(F32) * kept, axis=-1, keepdims=True)
            grad_scores = (probs * (grad_probs - weight)).astype(BF16)
            self.pds[mine, :] = grad_scores
            self.pds[other, :] = probs.astype(BF16)
            self.o_raw[g * SHARE + i] = dot(grad_scores, kv_g)
        grad_kv = dot_lt(self.qd[g], self.pds[...])
        self.dkv[g] = grad_kv.T.astype(BF16)
        self.send(g)

    def heads(self, first, last):
        def body(g, carry):
            self.head(g)

            @pl.when(g > 0)
            def _():
                self.relay(g - 1)

            return carry

        lax.fori_loop(first, last, body, 0)

    def copy(self, quarter, count, dst, slot_in, slot, g):
        rows = self.rows
        return pltpu.make_async_remote_copy(
            src_ref=self.dkv.at[g, pl.ds(quarter * rows, count * rows)],
            dst_ref=self.dkv_in.at[g, pl.ds(slot_in * rows, count * rows)],
            send_sem=self.send_sem.at[slot, g],
            recv_sem=self.recv_sem.at[slot_in, g],
            device_id=self.device_of(dst),
            device_id_type=MESH,
        )

    def add(self, quarter, slots, g):
        rows = self.rows
        span = slice(quarter * rows, (quarter + 1) * rows)
        total = self.dkv[g, span].astype(F32)
        for slot in slots:
            total = total + self.dkv_in[g, slot * rows : (slot + 1) * rows].astype(F32)
        self.dkv[g, span] = total.astype(BF16)

    def send(self, g):
        @pl.when(self.rank == 3)
        def _():
            self.copy(2, 1, 2, 0, 0, g).start()
            self.copy(0, 2, 1, 0, 1, g).start()

        @pl.when(self.rank == 2)
        def _():
            self.copy(1, 1, 1, 2, 0, g).start()
            self.copy(0, 1, 0, 1, 1, g).start()

    def relay(self, g):
        @pl.when(self.rank == 1)
        def _():
            self.copy(0, 2, 1, 0, 0, g).wait_recv()
            self.add(0, (0,), g)
            self.copy(0, 1, 0, 0, 0, g).start()

    def queries(self):
        for at, size in tiles(self.width, 128):
            head = at // HEAD_SIZE
            block = self.o_raw[head]
            if size == 128:
                low = lanes(self.rows) < HEAD_SIZE
                block = jnp.where(low, block, pltpu.roll(self.o_raw[head + 1], 64, 1))
            turned = half_turned(block, self.cos_sin[0], self.cos_sin[1], -1.0) * 0.125
            self.ra[0, :, at : at + size] = turned[:, :size].astype(BF16)

    def collect(self):
        low = lanes(self.rows) < HEAD_SIZE
        cosines = jnp.where(low, self.cos_sin[0], 1.0)
        sines = jnp.where(low, self.cos_sin[1], 0.0)
        mine = pl.ds(pl.multiple_of(self.rank * self.rows, 16), self.rows)
        for g in range(KEY_VALUE_HEADS):
            self.arrive(g)
            block = half_turned(self.dkv[g, mine, :].astype(F32), cosines, sines, -1.0)
            self.gkv[:, 128 * g : 128 * g + 128] = block.astype(BF16)

    def arrive(self, g):
        @pl.when(self.rank == 3)
        def _():
            self.copy(2, 1, 2, 0, 0, g).wait_send()
            self.copy(0, 2, 1, 0, 1, g).wait_send()

        @pl.when(self.rank == 2)
        def _():
            self.copy(0, 1, 2, 0, 0, g).wait_recv()
            self.copy(1, 1, 1, 2, 0, g).wait_send()
            self.copy(0, 1, 0, 1, 1, g).wait_send()
            self.add(2, (0,), g)

        @pl.when(self.rank == 1)
        def _():
            self.copy(0, 1, 2, 2, 0, g).wait_recv()
            self.copy(0, 1, 0, 0, 0, g).wait_send()
            self.add(1, (1, 2), g)

        @pl.when(self.rank == 0)
        def _():
            self.copy(0, 1, 2, 0, 0, g).wait_recv()
            self.copy(0, 1, 2, 1, 0, g).wait_recv()
            self.add(0, (0, 1), g)

    def project(self, total, wq, wkv):
        for at, size in tiles(self.width, 256):
            total[:, at : at + size] = dot_rt(self.ra[0], wq[at : at + size, :]) + dot(
                self.gkv[...], wkv[:, at : at + size]
            )


class OutCopy:
    def __init__(self, out, send, recv):
        self.section, self.dp, ctx = (lax.axis_index(a) for a in ("section", "dp", "ctx"))
        self.home = 2 * self.section + ctx % 2
        self.ctx, self.micro = ctx, ctx // 2
        self.out, self.send, self.recv = out, send, recv

    def here(self, l):
        return (self.section == l) & (self.ctx == self.home)

    def remote(self, array, l):
        return pltpu.make_async_remote_copy(
            src_ref=array,
            dst_ref=self.out.at[0, self.micro],
            send_sem=self.send.at[l],
            recv_sem=self.recv.at[self.micro],
            device_id=(l, self.dp, self.home),
            device_id_type=MESH,
        )

    def local(self, array):
        return pltpu.make_async_copy(array, self.out.at[0, self.micro], self.recv.at[self.micro])

    def start(self, array, l):
        start_if(self.here(l), lambda: self.local(array), lambda: self.remote(array, l))

    def sent(self, array, l):
        @pl.when(jnp.logical_not(self.here(l)))
        def _():
            self.remote(array, l).wait_send()

    def arrived(self, array):
        for block in range(2):
            pltpu.make_async_copy(array, self.out.at[0, block], self.recv.at[block]).wait()


def greet(barrier, dp):
    section, ctx = lax.axis_index("section"), lax.axis_index("ctx")
    for step in range(1, 8):
        other = (4 * section + ctx + step) % 8
        pl.semaphore_signal(
            barrier, inc=1, device_id=(other // 4, dp, other % 4), device_id_type=MESH
        )


def layers_kernel(complete, *refs):
    refs = list(refs)

    def take(count):
        taken = refs[:count]
        del refs[:count]
        return taken

    lengths, ends, frequency, gain_a, gain_f, wq_h, wk_h, wv_h, wo_h, wg_h, wu_h, wd_h = take(12)
    acts_o, grads_o, gain_o, nf_o, in_o, gg_o, gu_o, br_o, la_o, ra_o, nr_o, kvg_o = take(12)
    kept_o = [] if complete else take(7)
    wq, wkv, wo, wg, wu, wd = take(6)
    act, go, middle, norm_ffn, fact_a, fact_b, inner, lm, qd, kv, o_raw = take(11)
    sum_acc, gm, gg, gu, br, ra, pds, dkv, dkv_in, gkv, cos_sin, allowed_add, gain_v = take(13)
    w_sem, kv_sem, in_send, in_recv, kv_send, kv_recv, dk_send, dk_recv = take(8)
    act_send, act_recv, grad_send, grad_recv, op_own, op_send, op_recv, kept_sem = take(8)

    section = lax.axis_index("section")
    dp = lax.axis_index("dp")
    ctx = lax.axis_index("ctx")
    micro = ctx // 2
    xbit = ctx % 2
    rank = 2 * section + xbit
    rows, width = act.shape[1], act.shape[2]
    ff = wg.shape[1]
    ff_half = ff // 2

    def device_of(r):
        return (r // 2, dp, 2 * micro + r % 2)

    partner = (1 - section, dp, ctx)

    loads = [
        pltpu.make_async_copy(h, v, w_sem.at[i])
        for i, (h, v) in enumerate([(wq_h, wq), (wo_h, wo), (wg_h, wg), (wu_h, wu), (wd_h, wd)])
    ]
    kv_loads = [
        pltpu.make_async_copy(
            h.at[pl.ds(g * HEAD_SIZE, HEAD_SIZE)],
            wkv.at[pl.ds((2 * g + i) * HEAD_SIZE, HEAD_SIZE)],
            kv_sem.at[i, g],
        )
        for g in range(KEY_VALUE_HEADS)
        for i, h in enumerate((wk_h, wv_h))
    ]
    for load in kv_loads + loads:
        load.start()
    kv[...] = jnp.zeros_like(kv)
    barrier = pltpu.get_barrier_semaphore()
    greet(barrier, dp)
    pl.semaphore_wait(barrier, 7)

    def in_local(block, into_x):
        dst, slot = (act.at[0], 0) if into_x else (go.at[2], 1)
        return pltpu.make_async_copy(ends.at[0, block], dst, in_recv.at[slot])

    def in_remote(block, into_x):
        dst, slot = (act.at[0], 0) if into_x else (go.at[2], 1)
        return pltpu.make_async_remote_copy(
            src_ref=ends.at[0, block],
            dst_ref=dst,
            send_sem=in_send.at[block],
            recv_sem=in_recv.at[slot],
            device_id=(ctx // 2, dp, 2 * block + xbit),
            device_id_type=MESH,
        )

    def in_mine(block):
        return (section == ctx // 2) & (ctx // 2 == block)

    def in_start(into_x):
        @pl.when(section == (0 if into_x else 1))
        def _():
            for block in range(2):
                start_if(
                    in_mine(block),
                    lambda block=block: in_local(block, into_x),
                    lambda block=block: in_remote(block, into_x),
                )

    in_start(True)
    lane = lanes(rows)
    low = lane < HEAD_SIZE
    gain_attn = gain_a[...].astype(F32)
    gain_ffn = gain_f[...].astype(F32)

    def place(token_index):
        segment = jnp.zeros_like(token_index)
        start = jnp.zeros_like(token_index)
        finish = jnp.int32(0)
        for slot in range(lengths.shape[2]):
            length = lengths[micro, 0, slot]
            finish = finish + length
            passed = (token_index >= finish).astype(jnp.int32)
            segment = segment + passed
            start = start + passed * length
        return segment, token_index - start

    seg_mine, position = place(rank * rows + lax.broadcasted_iota(jnp.int32, (rows, 128), 0))
    angles = position.astype(F32) * frequency[...]
    cos_sin[0] = jnp.cos(angles)
    cos_sin[1] = jnp.where(lane % HEAD_SIZE < HEAD_SIZE // 2, -1.0, 1.0) * jnp.sin(angles)
    key_index = lax.broadcasted_iota(jnp.int32, (1, RANKS * rows), 1)
    query_index = rank * rows + lax.broadcasted_iota(jnp.int32, (rows, 1), 0)
    allowed_add[...] = jnp.where(
        (seg_mine[:, 0:1] == place(key_index)[0]) & (query_index >= key_index), 0.0, masked_fill
    )

    def kv_rows(l, r, g):
        return kv.at[l, g, pl.ds(r * rows, rows)]

    def kv_copy(l, quarter, dst, slot, g):
        return pltpu.make_async_remote_copy(
            src_ref=kv_rows(l, quarter, g),
            dst_ref=kv_rows(l, quarter, g),
            send_sem=kv_send.at[l, slot, g],
            recv_sem=kv_recv.at[l, quarter, g],
            device_id=device_of(dst),
            device_id_type=MESH,
        )

    kv_plan = [(0, 0, 1, 0), (0, 0, 2, 1), (1, 1, 2, 0), (1, 1, 3, 1), (2, 2, 3, 0)]
    kv_relay = (1, 0, 3, 2)

    def kv_start(l, g):
        for sender, quarter, dst, slot in kv_plan:

            @pl.when(rank == sender)
            def _(quarter=quarter, dst=dst, slot=slot):
                kv_copy(l, quarter, dst, slot, g).start()

    def kv_relayed(l, g):
        @pl.when(rank == 1)
        def _():
            kv_copy(l, 0, 3, 2, g).wait_recv()
            kv_copy(l, 0, 3, 2, g).start()

    def kv_finish(l, g):

        for quarter, receivers in ((0, (2, 3)), (1, (2, 3)), (2, (3,))):
            for receiver in receivers:

                @pl.when(rank == receiver)
                def _(quarter=quarter):
                    kv_copy(l, quarter, 0, 0, g).wait_recv()

    def kv_sent(l):
        for sender, quarter, dst, slot in kv_plan + [kv_relay]:

            @pl.when(rank == sender)
            def _(quarter=quarter, dst=dst, slot=slot):
                for g in range(KEY_VALUE_HEADS):
                    kv_copy(l, quarter, dst, slot, g).wait_send()

    acts_out = OutCopy(acts_o, act_send, act_recv)
    grads_out = OutCopy(grads_o, grad_send, grad_recv)

    def op_copy(kind, l, own):
        role = section if own else 1 - section
        half = pl.ds(pl.multiple_of(role * ff_half, 128), ff_half)
        src = [
            lambda: norm_ffn.at[l],
            lambda: inner.at[l],
            lambda: gg.at[:, half],
            lambda: gu.at[:, half],
            lambda: br.at[:, pl.ds(pl.multiple_of(role * 512, 128), 512)],
            lambda: lm.at[l, role],
            lambda: ra.at[role],
            lambda: lm.at[l, 0],
            lambda: gkv.at[:, pl.ds(pl.multiple_of(role * 256, 128), 384)],
        ][kind]()
        block = section if kind in (6, 8) and not complete else 2 * section + l
        dst = [nf_o, in_o, gg_o, gu_o, br_o, la_o, ra_o, nr_o, kvg_o][kind].at[
            pl.ds(pl.multiple_of(block * rows, 16), rows)
        ]
        if own:
            return pltpu.make_async_copy(src, dst, op_own.at[kind, l])
        return pltpu.make_async_remote_copy(
            src_ref=src,
            dst_ref=dst,
            send_sem=op_send.at[kind, l],
            recv_sem=op_recv.at[kind, l],
            device_id=partner,
            device_id_type=MESH,
        )

    def op_start(kinds, l):
        for kind in kinds:
            op_copy(kind, l, True).start()
            op_copy(kind, l, False).start()

    def op_sent(kinds, l):
        for kind in kinds:
            op_copy(kind, l, True).wait()
            op_copy(kind, l, False).wait_send()

    def kept_copy(i):
        src = [act.at[0], kv.at[0], o_raw.at[0], cos_sin, allowed_add, qd.at[0], gm][i]
        return pltpu.make_async_copy(src, kept_o[i], kept_sem.at[i])

    def kept_start(*which):
        if not complete:
            for i in which:
                kept_copy(i).start()

    in_remote(0, True).wait_recv()
    for load in kv_loads:
        load.wait()

    def forward(l, carry):
        hidden = act[l].astype(F32)
        cos_q, sin_q = cos_sin[0], cos_sin[1]
        lm[l, 0] = (hidden * inverse_rms(hidden) * gain_attn).astype(BF16)
        cos_kv = jnp.where(low, cos_q, 1.0)
        sin_kv = jnp.where(low, sin_q, 0.0)
        mine = pl.ds(pl.multiple_of(rank * rows, 16), rows)
        for g in range(KEY_VALUE_HEADS):
            block = dot_rt(lm[l, 0], wkv[128 * g : 128 * g + 128, :])
            turned = half_turned(block, cos_kv, sin_kv, 1.0)
            kv[l, g, mine, :] = turned.astype(BF16)
            kv_start(l, g)

        @pl.when(l == 0)
        def _():
            loads[0].wait()
            in_start(False)
            kept_start(0, 3, 4)

        for at, size in tiles(width, 256):
            product = dot(lm[l, 0], wq[:, at : at + size])
            for inside, part in tiles(size, 128):
                block = wide(product[:, inside : inside + part])
                turned = half_turned(block, cos_q, sin_q, 1.0) * 0.125
                head = (at + inside) // HEAD_SIZE
                qd[l, head // SHARE, pl.ds(head % SHARE * rows, rows), :] = jnp.where(
                    low, turned, 0.0
                ).astype(BF16)
                head += 1
                if head < QUERY_HEADS:
                    qd[l, head // SHARE, pl.ds(head % SHARE * rows, rows), :] = jnp.where(
                        low, pltpu.roll(turned, 64, 1), 0.0
                    ).astype(BF16)
        kv_relayed(l, 0)
        kv_finish(l, 0)

        def heads(g, carry):
            @pl.when(g < KEY_VALUE_HEADS - 1)
            def _():
                kv_relayed(l, g + 1)

            @pl.when(g > 0)
            def _():
                kv_finish(l, g)

            kv_g = kv[l, g]
            for i in range(SHARE):
                scores = dot_rt(qd[l, g, i * rows : (i + 1) * rows, :], kv_g) + allowed_add[...]
                peak = jnp.max(scores, axis=-1, keepdims=True)
                exponent = jnp.exp(scores - peak)
                total = jnp.sum(exponent, axis=-1, keepdims=True)
                out = dot(exponent.astype(BF16), kv_g) * (1.0 / total)
                o_raw[l, g * SHARE + i] = jnp.where(low, peak + jnp.log(total), out)
            return carry

        lax.fori_loop(0, KEY_VALUE_HEADS, heads, 0)

        @pl.when(l == 0)
        def _():
            kept_start(1, 2)
            loads[1].wait()

        for at, size in tiles(width, 128):
            head = at // HEAD_SIZE
            block = pltpu.roll(o_raw[l, head], 64, 1)
            if size == 128:
                block = jnp.where(low, block, o_raw[l, head + 1])
            lm[l, 1, :, at : at + size] = block[:, :size].astype(BF16)
        for at, size in tiles(width, 256):
            middle[l, :, at : at + size] = act[l, :, at : at + size].astype(F32) + dot(
                lm[l, 1], wo[:, at : at + size]
            )
        mid = middle[l]
        norm_ffn[l] = (mid * inverse_rms(mid) * gain_ffn).astype(BF16)
        op_start((0, 5, 7), l)

        @pl.when(l == 0)
        def _():
            loads[2].wait()
            loads[3].wait()

        def gates(j, carry):
            part = pl.ds(pl.multiple_of(j * 512, 512), 512)
            gate = dot(norm_ffn[l], wg[:, part])
            upper = dot(norm_ffn[l], wu[:, part])
            s = 0.5 * jnp.tanh(0.5 * gate) + 0.5
            swish = gate * s
            inner[l, :, part] = (swish * upper).astype(BF16)
            fact_a[l, :, part] = (upper * s * (1.0 + gate * (1.0 - s))).astype(BF16)
            fact_b[l, :, part] = swish.astype(BF16)
            return carry

        lax.fori_loop(0, ff // 512, gates, 0)

        @pl.when(l == 0)
        def _():
            loads[4].wait()

        op_start((1,), l)
        for at, size in tiles(width, 256):
            act[l + 1, :, at : at + size] = (
                middle[l, :, at : at + size] + dot_rt(inner[l], wd[at : at + size, :])
            ).astype(BF16)
        acts_out.start(act.at[l + 1], l)
        kv_sent(l)
        return carry

    lax.fori_loop(0, 2, forward, 0)

    in_remote(0, False).wait_recv()
    gain_v[...] = jnp.zeros_like(gain_v)
    br[...] = jnp.zeros_like(br)
    late = (6, 8)

    def backward(step, carry):
        l = 1 - step

        @pl.when(l == 0)
        def _():
            op_sent((2, 3, 4) + (late if complete else ()), 1)

        br[:, :width] = go[l + 1]
        op_start((4,), l)

        def gates(j, carry):
            part = pl.ds(pl.multiple_of(j * 512, 512), 512)
            grad_inner = dot(go[l + 1], wd[:, part])
            gg[:, part] = (grad_inner * fact_a[l, :, part].astype(F32)).astype(BF16)
            gu[:, part] = (grad_inner * fact_b[l, :, part].astype(F32)).astype(BF16)
            return carry

        lax.fori_loop(0, ff // 512, gates, 0)
        op_start((2, 3), l)
        for at, size in tiles(width, 256):
            sum_acc[:, at : at + size] = dot_rt(gg[...], wg[at : at + size, :]) + dot_rt(
                gu[...], wu[at : at + size, :]
            )
        grad, gain_row = norm_back(middle[l], gain_ffn, sum_acc[...])
        gain_v[1:2, :] += gain_row
        gm[...] = go[l + 1].astype(F32) + grad
        ra[1] = gm[...].astype(BF16)

        for at, size in tiles(width, 256):
            product = dot_rt(ra[1], wo[at : at + size, :])
            for inside, part in tiles(size, 128):
                block = wide(product[:, inside : inside + part])
                head = (at + inside) // HEAD_SIZE
                qd[l, head // SHARE, pl.ds((SHARE + head % SHARE) * rows, rows), :] = jnp.where(
                    low, 0.0, pltpu.roll(block, 64, 1)
                ).astype(BF16)
                head += 1
                if head < QUERY_HEADS:
                    qd[l, head // SHARE, pl.ds((SHARE + head % SHARE) * rows, rows), :] = (
                        jnp.where(low, 0.0, block).astype(BF16)
                    )

        def attention():
            back = AttentionBack(
                rank, device_of, qd.at[l], kv.at[l], o_raw.at[l], allowed_add, cos_sin, ra, pds,
                dkv, dkv_in.at[l] if complete else dkv_in, gkv,
                dk_send.at[l] if complete else dk_send, dk_recv.at[l] if complete else dk_recv,
            )
            back.heads(0, KEY_VALUE_HEADS)
            back.relay(KEY_VALUE_HEADS - 1)
            back.queries()
            op_start((6,), l)
            back.collect()
            op_start((8,), l)
            back.project(sum_acc, wq, wkv)
            grad, gain_row = norm_back(act[l].astype(F32), gain_attn, sum_acc[...])
            gain_v[0:1, :] += gain_row
            go[l] = (gm[...] + grad).astype(BF16)
            grads_out.start(go.at[l], l)

        if complete:
            attention()
        else:

            @pl.when(l == 1)
            def _():
                attention()

            @pl.when(l == 1)
            def _():
                op_sent(late, 1)

        return carry

    lax.fori_loop(0, 2, backward, 0)

    gain_copy = pltpu.make_async_copy(gain_v, gain_o, kept_sem.at[7])
    gain_copy.start()
    kept_start(5, 6)
    for into_x in (True, False):

        @pl.when(section == (0 if into_x else 1))
        def _(into_x=into_x):
            for block in range(2):

                @pl.when(jnp.logical_not(in_mine(block)))
                def _(block=block):
                    in_remote(block, into_x).wait_send()

    op_sent((2, 3, 4) + (late if complete else ()), 0)
    for l in range(2):
        op_sent((0, 1, 5, 7), l)
        for kind in range(9):
            if l == 1 or complete or kind not in late:
                op_copy(kind, l, False).wait_recv()
        acts_out.sent(act.at[l + 1], l)
        if l == 1 or complete:
            grads_out.sent(go.at[l], l)
    gain_copy.wait()
    acts_out.arrived(act.at[0])
    if complete:
        grads_out.arrived(act.at[0])
    else:

        @pl.when(section == 1)
        def _():
            grads_out.arrived(act.at[0])

        for i in range(len(kept_o)):
            kept_copy(i).wait()


def run_layers(lengths, ends, frequency, gain_attn, gain_ffn, weights, complete):
    micro_count, rows, width = ends.shape[1:]
    wq, wk, wv, wo, wg, wu, wd = weights
    ff = wg.shape[1]
    keys = RANKS * rows
    kv_width = 2 * wk.shape[0]
    vmem, hbm = pl.BlockSpec(memory_space=pltpu.VMEM), pl.BlockSpec(memory_space=pl.ANY)
    op_rows = 4 * rows
    late_rows = op_rows if complete else 2 * rows
    out = lambda *shape: jax.ShapeDtypeStruct(shape, BF16)
    out_f = lambda *shape: jax.ShapeDtypeStruct(shape, F32)
    dma = lambda *shape: pltpu.SemaphoreType.DMA(shape)
    kept = [
        out(rows, width),
        out(KEY_VALUE_HEADS, keys, 128),
        out_f(QUERY_HEADS, rows, 128),
        out_f(2, rows, 128),
        out_f(rows, keys),
        out(KEY_VALUE_HEADS, 2 * SHARE * rows, 128),
        out_f(rows, width),
    ]
    layers = (2,) if complete else ()
    return pl.pallas_call(
        lambda *refs: layers_kernel(complete, *refs),
        out_shape=[
            out(*ends.shape),
            out(*ends.shape),
            out_f(8, width),
            out(op_rows, width),
            out(op_rows, ff),
            out(op_rows, ff // 2),
            out(op_rows, ff // 2),
            out(op_rows, 512),
            out(op_rows, width),
            out(late_rows, width),
            out(op_rows, width),
            out(late_rows, 384),
        ]
        + ([] if complete else kept),
        in_specs=[pl.BlockSpec(memory_space=pltpu.SMEM), hbm] + [vmem] * 3 + [hbm] * 7,
        out_specs=[hbm] * (12 if complete else 19),
        scratch_shapes=[
            pltpu.VMEM(wq.shape, BF16),
            pltpu.VMEM((kv_width, width), BF16),
            pltpu.VMEM(wo.shape, BF16),
            pltpu.VMEM(wg.shape, BF16),
            pltpu.VMEM(wu.shape, BF16),
            pltpu.VMEM(wd.shape, BF16),
            pltpu.VMEM((3, rows, width), BF16),
            pltpu.VMEM((3, rows, width), BF16),
            pltpu.VMEM((2, rows, width), F32),
            pltpu.VMEM((2, rows, width), BF16),
            pltpu.VMEM((2, rows, ff), BF16),
            pltpu.VMEM((2, rows, ff), BF16),
            pltpu.VMEM((2, rows, ff), BF16),
            pltpu.VMEM((2, 2, rows, width), BF16),
            pltpu.VMEM((2, KEY_VALUE_HEADS, 2 * SHARE * rows, 128), BF16),
            pltpu.VMEM((2, KEY_VALUE_HEADS, keys, 128), BF16),
            pltpu.VMEM((2, QUERY_HEADS, rows, 128), F32),
            pltpu.VMEM((rows, width), F32),
            pltpu.VMEM((rows, width), F32),
            pltpu.VMEM((rows, ff), BF16),
            pltpu.VMEM((rows, ff), BF16),
            pltpu.VMEM((rows, 1024), BF16),
            pltpu.VMEM((2, rows, width), BF16),
            pltpu.VMEM((2 * SHARE * rows, keys), BF16),
            pltpu.VMEM((KEY_VALUE_HEADS, keys, 128), BF16),
            pltpu.VMEM(layers + (KEY_VALUE_HEADS, 3 * rows, 128), BF16),
            pltpu.VMEM((rows, kv_width), BF16),
            pltpu.VMEM((2, rows, 128), F32),
            pltpu.VMEM((rows, keys), F32),
            pltpu.VMEM((8, width), F32),
            dma(5),
            dma(2, KEY_VALUE_HEADS),
            dma(2),
            dma(2),
            dma(2, 3, KEY_VALUE_HEADS),
            dma(2, 3, KEY_VALUE_HEADS),
            dma(*layers, 2, KEY_VALUE_HEADS),
            dma(*layers, 3, KEY_VALUE_HEADS),
            dma(2),
            dma(2),
            dma(2),
            dma(2),
            dma(9, 2),
            dma(9, 2),
            dma(9, 2),
            dma(len(kept) + 1),
        ],
        compiler_params=pltpu.CompilerParams(
            collective_id=1, has_side_effects=True, vmem_limit_bytes=61 * 2**20
        ),
        name="layers",
    )(lengths, ends, frequency, gain_attn, gain_ffn, *weights)


def sums_kernel(*refs):
    refs = list(refs)

    def take(count):
        taken = refs[:count]
        del refs[:count]
        return taken

    gain_h, gain_a, nf_h, in_h, gg_h, gu_h, br_h, la_h, ra_h, nr_h, kvg_h = take(11)
    act_h, kv_h, o_h, cs_h, allowed_h, qd_h, gm_h, wq_h, wk_h, wv_h = take(10)
    grads_o, t_o, gate_o, up_o, down_o = take(5)
    stage, in_v, br_v, gg_v, gu_v, ra_v, kvg_v, nf_t, ln_t, in_t, gain_t = take(11)
    act, kv, o_raw, cos_sin, allowed, qd, gm, wq, wkv = take(9)
    go, ra, dkv, dkv_in, gkv, sum_acc, gain_rows = take(7)
    d_out, d_in, d_keep, d1_out, d1_in, d2_out, d2_in = take(7)
    f1_out, f1_in, f2_out, f2_in, f_keep, fz_in = take(6)
    t1_out, t1_in, t2_out, t2_in, t_keep, tz_in = take(6)
    d_all, f_all, t_all = take(3)
    load, kept_sem, w_sem, dk_s, dk_r, grad_s, grad_r, op_own, op_s, op_r = take(10)
    dz_s, dz_r, d1_s, d1_r, d2_s, d2_r, f1_s, f1_r, f2_s, f2_r, fz_s, fz_r = take(12)
    t1_s, t1_r, t2_s, t2_r, tz_s, tz_r, all_s, all_r, pair_r, write = take(10)

    section = lax.axis_index("section")
    z = lax.axis_index("dp")
    ctx = lax.axis_index("ctx")
    x, y = ctx % 2, ctx // 2
    rank = 2 * section + x
    x_next = (section, z, 2 * y + 1 - x)
    y_next = (section, z, 2 * (1 - y) + x)
    partner = (1 - section, z, ctx)
    rows = act.shape[0]
    width = nf_h.shape[1]
    per = width // RANKS
    part = f_keep.shape[2]
    shift = per - part
    quarter = gg_v.shape[1] // 2
    deep = in_t.shape[0]
    fine = deep // 2
    last = RANKS - 1
    edge = (z == 0) | (z == last)

    def at_edge(step):
        pl.when(edge)(step)

    def inside(step):
        pl.when(jnp.logical_not(edge))(step)

    def remote(src, dst, send, recv, device):
        return pltpu.make_async_remote_copy(
            src_ref=src, dst_ref=dst, send_sem=send, recv_sem=recv,
            device_id=device, device_id_type=MESH,
        )

    def some(start, size, unit=16):
        return pl.ds(pl.multiple_of(start, unit), size)

    gain_load = pltpu.make_async_copy(gain_h, gain_rows.at[pl.ds(0, gain_h.shape[0])], load.at[7])
    is_ = lambda v: (z == v).astype(jnp.int32)
    by_need = ((3, 2, 1), (3, 0, 2), (0, 3, 1), (0, 1, 2))
    by_turns = ((3, 2, 1), (3, 0, 2), (0, 3, 1), (0, 2, 1))

    def turn_of(k, order=by_need):
        return sum(is_(v) * order[v][k] for v in range(RANKS)) if k < last else z

    def in_load(k):
        return pltpu.make_async_copy(
            in_h.at[:, some(turn_of(k) * deep, deep, 128)], in_v, load.at[0]
        )

    loads = [None] + [
        pltpu.make_async_copy(h, v, load.at[1 + i])
        for i, (h, v) in enumerate(
            [(br_h, br_v), (nf_h, stage), (gg_h, gg_v), (gu_h, gu_v), (la_h, stage), (nr_h, stage)]
        )
    ]
    kept = [
        pltpu.make_async_copy(h, v, kept_sem.at[i])
        for i, (h, v) in enumerate(
            [(qd_h, qd), (kv_h, kv), (o_h, o_raw), (allowed_h, allowed), (cs_h, cos_sin),
             (gm_h, gm), (act_h, act)]
        )
    ]
    late = [
        pltpu.make_async_copy(h.at[pl.ds(c * rows, rows)], v.at[pl.ds((2 * c + 1) * rows, rows)], w_sem.at[i, c])
        for i, (h, v) in enumerate([(ra_h, ra_v), (kvg_h, kvg_v)])
        for c in range(2)
    ]
    weights = [pltpu.make_async_copy(wq_h, wq, w_sem.at[2, 0])] + [
        pltpu.make_async_copy(
            h.at[pl.ds(g * HEAD_SIZE, HEAD_SIZE)],
            wkv.at[pl.ds((2 * g + i) * HEAD_SIZE, HEAD_SIZE)],
            w_sem.at[3 + i, g],
        )
        for g in range(KEY_VALUE_HEADS)
        for i, h in enumerate((wk_h, wv_h))
    ]
    loads[2].start()
    loads[3].start()
    loads[4].start()
    gain_rows[...] = jnp.zeros_like(gain_rows)

    barrier = pltpu.get_barrier_semaphore()
    greet(barrier, z)
    not_first = (z > 0).astype(jnp.int32)
    not_last = (z < last).astype(jnp.int32)

    @pl.when(z > 0)
    def _():
        pl.semaphore_signal(barrier, inc=1, device_id=(section, z - 1, ctx), device_id_type=MESH)

    @pl.when(z < last)
    def _():
        pl.semaphore_signal(barrier, inc=1, device_id=(section, z + 1, ctx), device_id_type=MESH)

    def turn(src, dst, base=0):
        for at, size in tiles(src.shape[1], 128):
            block = src[:, at : at + size]
            if size < 128:
                block = wide(block)
            dst[base + at : base + at + size, :] = block.T[:size]

    def z_way(t):
        up = (z < t).astype(jnp.int32)
        to = z + 2 * up - 1
        arrives = up * not_first + (1 - up) * not_last
        meets = (1 - up) * (t == z - 1).astype(jnp.int32)
        return (section, to, ctx), arrives, t * (1 - meets) + RANKS * meets

    def d_block(k):
        in_load(k).wait()
        for b in range(deep // 128):
            in_t[b * 128 : (b + 1) * 128, :] = in_v[:, b * 128 : (b + 1) * 128].T
        if k < last:
            in_load(k + 1).start()

    def d_send(k, sub):
        device, _, slot = z_way(turn_of(k))
        span = pl.ds(sub * fine, fine)
        return remote(d_out.at[k, span], d_in.at[slot, span], dz_s.at[k, sub], dz_r.at[slot, sub], device)

    def d_step(k, sub):
        t = turn_of(k)
        _, arrives, _ = z_way(t)
        span = slice(sub * fine, (sub + 1) * fine)
        mine = dot(in_t[span, :], br_v[...])

        @pl.when(arrives == 0)
        def _():
            d_out[k, span, :] = mine.astype(BF16)

        @pl.when(arrives == 1)
        def _():
            remote(d_out.at[k, span], d_in.at[t, span], dz_s.at[k, sub], dz_r.at[t, sub], partner).wait_recv()
            d_out[k, span, :] = (mine + d_in[t, span, :].astype(F32)).astype(BF16)

        d_send(k, sub).start()

    def d_edge(k):
        @at_edge
        def _():
            d_block(k)
            d_step(k, 0)
            d_step(k, 1)

    def d_inside(k, sub):
        @inside
        def _():
            if sub == 0:
                d_block(k)
            d_step(k, sub)

    def f_links(k):
        return (x_next, y_next, x, y) if k == 0 else (y_next, x_next, y, x)

    def f_right(k, column_half):
        src = gg_v if k == 0 else gu_v
        return src[:, some(column_half * quarter, quarter, 128)]

    turns = (3, 0, 2, 1)

    def f1_copy(k, i):
        return remote(f1_out.at[k, i % 2], f1_in.at[k, turns[i]], f1_s.at[k, i % 2], f1_r.at[k, turns[i]], f_links(k)[0])

    def f2_copy(k, i):
        return remote(f2_out.at[k, i % 2], f2_in.at[k, turns[i]], f2_s.at[k, i % 2], f2_r.at[k, turns[i]], f_links(k)[1])

    def f1_step(i):
        for k in range(2):
            first = f_links(k)[2]
            value = dot(nf_t[turns[i] * per : (turns[i] + 1) * per, :], f_right(k, 1 - first))
            if i >= 2:
                f1_copy(k, i).wait_send()
            f1_out[k, i % 2] = value.astype(BF16)
            f1_copy(k, i).start()

    def f2_step(i):
        d = turns[i]
        for k in range(2):
            first, second = f_links(k)[2:]
            f1_copy(k, i).wait_recv()
            for mine in (False, True):
                at = (second if mine else 1 - second) * shift
                total = dot(nf_t[some(d * per + at, part), :], f_right(k, first)) + f1_in[
                    k, d, some(at, part), :
                ].astype(F32)
                if mine:
                    f_keep[k, d] = total.astype(BF16)
                else:
                    if i >= 2:
                        f2_copy(k, i).wait_send()
                    f2_out[k, i % 2] = total.astype(BF16)
                    f2_copy(k, i).start()

    def t_links(d):
        return (x_next, y_next, x, y) if d < RANKS // 2 else (y_next, x_next, y, x)

    def t_product(row, count, add):
        mine = dot(ln_t[some(row, count), :], ra_v[...])
        pairs = dot(ln_t[some(width + row, count), :], kvg_v[...])
        gains = gain_t[some(row, count), :]
        full = width // 128 * 128
        tail = jnp.concatenate([mine[:, full:], gains[:, width - full :]], axis=1)
        return [(0, add(mine[:, :full], 0)), (full, add(tail, full)), (full + 128, add(pairs, full + 128))]

    def t1_copy(d):
        return remote(t1_out.at[d], t1_in.at[d], t1_s.at[d], t1_r.at[d], t_links(d)[0])

    def t2_copy(d):
        return remote(t2_out.at[d], t2_in.at[d], t2_s.at[d], t2_r.at[d], t_links(d)[1])

    def t1_step(d):
        first = t_links(d)[2]
        for at, value in t_product(d * per + (1 - first) * shift, part, lambda v, at: v):
            t1_out[d, :, at : at + value.shape[1]] = value.astype(BF16)
        t1_copy(d).start()

    def t2_step(d):
        _, _, first, second = t_links(d)
        t1_copy(d).wait_recv()
        for mine in (False, True):
            row = (second if mine else 1 - second) * (part // 2)
            add = lambda v, at: v + t1_in[d, some(row, part // 2), at : at + v.shape[1]].astype(F32)
            dst = t_keep if mine else t2_out
            for at, value in t_product(d * per + first * shift + row, part // 2, add):
                dst[d, :, at : at + value.shape[1]] = value.astype(BF16)
            if not mine:
                t2_copy(d).start()

    class Line:
        def __init__(self, keep, second_in, z_in, send, recv):
            self.keep, self.second_in, self.z_in, self.send, self.recv = keep, second_in, z_in, send, recv

        def add(self, copy, d):
            copy.wait_recv()
            self.keep[d] = (self.keep[d].astype(F32) + self.second_in[d].astype(F32)).astype(BF16)

        def copy(self, k):
            d = turn_of(k, by_turns)
            device, _, slot = z_way(d)
            return remote(self.keep.at[d], self.z_in.at[slot], self.send.at[k], self.recv.at[slot], device)

        def step(self, k):
            d = turn_of(k, by_turns)
            _, arrives, _ = z_way(d)

            @pl.when(arrives == 1)
            def _():
                remote(self.keep.at[d], self.z_in.at[d], self.send.at[k], self.recv.at[d], partner).wait_recv()
                self.keep[d] = (self.keep[d].astype(F32) + self.z_in[d].astype(F32)).astype(BF16)

            self.copy(k).start()

        def total(self):
            for condition, slot in ((z > 0, z), (z < last, RANKS)):

                @pl.when(condition)
                def _(slot=slot):
                    remote(self.keep.at[0], self.z_in.at[slot], self.send.at[0], self.recv.at[slot], partner).wait_recv()

            value = self.keep[z].astype(F32)
            return z_total(value, self.z_in[z], self.z_in[RANKS])

    def z_total(value, up, down):
        value = value + jnp.where(z > 0, up.astype(F32), 0.0)
        return value + jnp.where(z < last, down.astype(F32), 0.0)

    lines = [
        Line(f_keep.at[k], f2_in.at[k], fz_in.at[k], fz_s.at[k], fz_r.at[k]) for k in range(2)
    ] + [Line(t_keep, t2_in, tz_in, tz_s, tz_r)]

    def f_add(i):
        for k in range(2):
            lines[k].add(f2_copy(k, i), turns[i])

    def z_steps(which, k, where):
        @where
        def _():
            for line in which:
                line.step(k)

    def places(x_first):
        a, b = (1, 0) if x_first is True else (0, 1) if x_first is False else (x_first, 1 - x_first)
        spot = lambda i, j: a * (2 * i + j) + b * (2 * j + i)
        return spot(x, y), spot(1 - x, y), spot(x, 1 - y), spot(1 - x, 1 - y)

    class Gather:
        def __init__(self, number, buffer, x_first):
            self.n, self.buffer = number, buffer
            self.own, self.over_x, self.over_y, self.across = places(x_first)
            size = buffer.shape[2]
            cut = (size // 2 + 15) // 16 * 16
            self.halves = (pl.ds(0, cut), pl.ds(cut, size - cut))

        def whole(self, spot, slot, device):
            ref = self.buffer.at[section, spot]
            return remote(ref, ref, all_s.at[self.n, slot], all_r.at[self.n, slot], device)

        def relay(self, spot, half, device):
            ref = self.buffer.at[section, spot, self.halves[half]]
            return remote(ref, ref, all_s.at[self.n, 2 + half], all_r.at[self.n, 2 + half], device)

        def pair(self, core, spot, slot):
            ref = self.buffer.at[core, spot]
            return remote(ref, ref, all_s.at[self.n, 4 + slot], pair_r.at[self.n, spot], partner)

        def start(self, value):
            self.buffer[section, self.own] = value.astype(BF16)
            self.whole(self.own, 0, x_next).start()
            self.whole(self.own, 1, y_next).start()
            self.pair(section, self.own, 0).start()

        def middle(self):
            self.whole(self.over_x, 0, x_next).wait_recv()
            self.relay(self.over_x, 0, y_next).start()
            self.pair(section, self.over_x, 1).start()
            self.whole(self.over_y, 1, y_next).wait_recv()
            self.relay(self.over_y, 1, x_next).start()
            self.pair(section, self.over_y, 2).start()

        def finish(self):
            self.relay(self.across, 0, y_next).wait_recv()
            self.relay(self.across, 1, x_next).wait_recv()
            self.pair(section, self.across, 3).start()
            for spot in (self.own, self.over_x, self.over_y, self.across):
                self.pair(1 - section, spot, 0).wait_recv()

        def sent(self):
            self.whole(self.own, 0, x_next).wait_send()
            self.whole(self.own, 1, y_next).wait_send()
            self.relay(self.over_x, 0, y_next).wait_send()
            self.relay(self.over_y, 1, x_next).wait_send()
            for slot, spot in enumerate((self.own, self.over_x, self.over_y, self.across)):
                self.pair(section, spot, slot).wait_send()

    below = (z < RANKS // 2).astype(jnp.int32)
    gathers = [
        Gather(0, d_all.at[0], True),
        Gather(1, d_all.at[1], False),
        Gather(2, f_all.at[0], True),
        Gather(3, f_all.at[1], False),
        Gather(4, t_all, below),
    ]

    def d1_copy(h):
        return remote(d1_out.at[h], d1_in.at[h], d1_s.at[h], d1_r.at[h], f_links(h)[0])

    def d2_copy(h):
        return remote(d2_out.at[h], d2_in.at[h], d2_s.at[h], d2_r.at[h], f_links(h)[1])

    def d_first(h):
        span = pl.ds(h * fine, fine)
        for condition, slot in ((z > 0, z), (z < last, RANKS)):

            @pl.when(condition)
            def _(slot=slot):
                remote(d_out.at[0, span], d_in.at[slot, span], dz_s.at[0, h], dz_r.at[slot, h], partner).wait_recv()

        first = f_links(h)[2]
        for mine in (False, True):
            at = h * fine + (first if mine else 1 - first) * (fine // 2)
            piece = some(at, fine // 2)
            total = z_total(dot(in_t[piece, :], br_v[...]), d_in[z, piece, :], d_in[RANKS, piece, :])
            if mine:
                d_keep[h] = total
            else:
                d1_out[h] = total.astype(BF16)
                d1_copy(h).start()

    def d_second(h):
        second = f_links(h)[3]
        d1_copy(h).wait_recv()
        for mine in (False, True):
            piece = some((second if mine else 1 - second) * (fine // 4), fine // 4)
            total = d_keep[h, piece, :] + d1_in[h, piece, :].astype(F32)
            if mine:
                d_keep[h, : fine // 4, :] = total
            else:
                d2_out[h] = total.astype(BF16)
                d2_copy(h).start()

    def d_gather(h):
        d2_copy(h).wait_recv()
        gathers[h].start(d_keep[h, : fine // 4, :] + d2_in[h].astype(F32))

    back = AttentionBack(
        rank, lambda r: (r // 2, z, 2 * y + r % 2), qd, kv, o_raw, allowed, cos_sin, ra,
        ln_t.at[pl.ds(0, 2 * SHARE * rows)], dkv, dkv_in, gkv, dk_s, dk_r,
    )
    grads_out = OutCopy(grads_o, grad_s, grad_r)

    def op_copy(kind, own):
        role = section if own else 1 - section
        src = ra.at[role] if kind == 0 else gkv.at[:, some(role * 256, 384, 128)]
        dst = (ra_v, kvg_v)[kind].at[some(2 * section * rows, rows)]
        if own:
            return pltpu.make_async_copy(src, dst, op_own.at[kind])
        return remote(src, dst, op_s.at[kind], op_r.at[kind], partner)

    def op_start(kind):
        op_copy(kind, True).start()
        op_copy(kind, False).start()

    def attention_end():
        back.collect()
        op_start(1)
        for copy in weights:
            copy.wait()
        kept[6].wait()
        back.project(sum_acc, wq, wkv)
        grad, gain_row = norm_back(act[...].astype(F32), gain_a[...].astype(F32), sum_acc[...])
        gain_load.wait()
        gain_rows[0:1, :] += gain_row
        go[...] = (gm[...] + grad).astype(BF16)
        grads_out.start(go, 0)

    def t_ready():
        loads[5].wait()
        turn(stage, ln_t)
        loads[6].start()
        block_of = lambda at, size: wide(gain_rows[:, at : at + size]).T
        for at, size in tiles(width, 128):
            gain_t[at : at + size, :] = pltpu.roll(block_of(at, size), 64, 1)[:size]
        loads[6].wait()
        turn(stage, ln_t, width)
        for copy in late:
            copy.wait()
        for kind in range(2):
            op_copy(kind, True).wait()
            op_copy(kind, False).wait_recv()

    loads[2].wait()
    turn(stage, nf_t)
    loads[3].wait()
    loads[4].wait()
    in_load(0).start()
    loads[1].start()
    for copy in kept + weights + late + [gain_load]:
        copy.start()
    pl.semaphore_wait(barrier, 7 + not_first + not_last)
    f1_step(0)
    loads[1].wait()
    d_edge(0)
    f1_step(1)
    d_edge(1)
    loads[5].start()
    for copy in kept[:6]:
        copy.wait()
    ra[1] = gm[...].astype(BF16)
    back.heads(0, 3)
    d_inside(0, 0)
    back.heads(3, KEY_VALUE_HEADS)
    back.relay(KEY_VALUE_HEADS - 1)
    f2_step(0)
    f1_step(2)
    back.queries()
    op_start(0)
    d_edge(2)
    d_inside(0, 1)
    f2_step(1)
    f1_step(3)
    attention_end()
    d_inside(1, 0)
    t_ready()
    d_inside(1, 1)
    f_add(0)
    f2_step(2)
    d_inside(2, 0)
    f_add(1)
    z_steps(lines[:2], 0, at_edge)
    f2_step(3)
    for d in (3, 0, 2, 1):
        t1_step(d)
    d_inside(2, 1)
    z_steps(lines[:2], 0, inside)
    f_add(2)
    z_steps(lines[:2], 1, at_edge)
    d_block(last)
    d_first(0)
    d_first(1)
    z_steps(lines[:2], 1, inside)
    f_add(3)
    z_steps(lines[:2], 2, at_edge)
    t2_step(3)
    t2_step(0)
    z_steps(lines[:2], 2, inside)
    d_second(0)
    d_second(1)
    gathers[2].start(lines[0].total())
    gathers[3].start(lines[1].total())
    t2_step(2)
    t2_step(1)
    for d in (3, 0):
        lines[2].add(t2_copy(d), d)
    z_steps(lines[2:], 0, at_edge)
    d_gather(0)
    d_gather(1)
    z_steps(lines[2:], 0, inside)
    for d in (2, 1):
        lines[2].add(t2_copy(d), d)
    z_steps(lines[2:], 1, at_edge)
    z_steps(lines[2:], 2, at_edge)
    z_steps(lines[2:], 1, inside)
    z_steps(lines[2:], 2, inside)
    gathers[2].middle()
    gathers[3].middle()
    gathers[0].middle()
    gathers[1].middle()
    gathers[4].start(lines[2].total())

    writes = []

    def leave(src, dst):
        writes.append(pltpu.make_async_copy(src, dst, write.at[len(writes)]))
        writes[-1].start()

    for k in range(2):
        gathers[2 + k].finish()
        for core in range(2):
            for f in range(2):
                columns = pl.ds((2 * core + f) * quarter, quarter)
                out = (gate_o, up_o)[k]
                leave(f_all.at[k, core, 2 * f], out.at[pl.ds(0, part), columns])
                rest = pl.ds(part - shift, per - part)
                leave(f_all.at[k, core, 2 * f + 1, rest], out.at[pl.ds(part, per - part), columns])
    gathers[4].middle()
    for h in range(2):
        gathers[h].finish()
        for core in range(2):
            for spot in range(4):
                span = pl.ds(h * fine + spot * (fine // 4), fine // 4)
                leave(d_all.at[h, core, spot], down_o.at[span, pl.ds(core * br_v.shape[1], br_v.shape[1])])
    gathers[4].finish()
    t_rows = part // 2
    for core in range(2):
        for spot in range(4):
            row = spot % 2 * t_rows + spot // 2 * shift
            skip = part - shift if spot == 2 else 0
            rest = pl.ds(skip, t_rows - skip)
            leave(t_all.at[core, spot, rest], t_o.at[core, pl.ds(row + skip, t_rows - skip)])

    for k in range(last):
        for sub in range(2):
            d_send(k, sub).wait_send()
        for line in lines:
            line.copy(k).wait_send()
    for h in range(2):
        d1_copy(h).wait_send()
        d2_copy(h).wait_send()
    for k in range(2):
        for i in (2, 3):
            f1_copy(k, i).wait_send()
            f2_copy(k, i).wait_send()
    for d in range(RANKS):
        t1_copy(d).wait_send()
        t2_copy(d).wait_send()
    for kind in range(2):
        op_copy(kind, False).wait_send()
    grads_out.sent(go, 0)

    @pl.when(section == 0)
    def _():
        grads_out.arrived(go)

    for gather in gathers:
        gather.sent()
    for copy in writes:
        copy.wait()


def run_sums(gain_sums, gain_attn, operands, kept, weights, ends_shape):
    nf, inner, gg, gu, br, la, ra, nr, kvg = operands
    act, kv, o_raw, cos_sin, allowed, qd, gm = kept
    depth, width = nf.shape
    rows = act.shape[0]
    ff, half = inner.shape[1], gg.shape[1]
    per, deep = width // RANKS, ff // RANKS
    part = (per // 2 + 15) // 16 * 16
    quarter, fine = half // 2, deep // 2
    columns = br.shape[1]
    wide_t = width // 128 * 128 + 128 + kvg.shape[1]
    vmem, hbm = pl.BlockSpec(memory_space=pltpu.VMEM), pl.BlockSpec(memory_space=pl.ANY)
    out = lambda *shape: jax.ShapeDtypeStruct(shape, BF16)
    b = lambda *shape: pltpu.VMEM(shape, BF16)
    f = lambda *shape: pltpu.VMEM(shape, F32)
    like = lambda a: pltpu.VMEM(a.shape, a.dtype)
    sem = lambda *shape: pltpu.SemaphoreType.DMA(shape)
    return pl.pallas_call(
        sums_kernel,
        out_shape=[
            out(*ends_shape), out(2, per, wide_t), out(per, ff), out(per, ff), out(deep, 2 * columns),
        ],
        in_specs=[hbm, vmem] + [hbm] * 19,
        out_specs=[hbm] * 5,
        scratch_shapes=[
            b(depth, width), b(depth, deep), b(depth, columns), b(depth, half), b(depth, half),
            b(depth, width), b(depth, kvg.shape[1]),
            b(width, depth), b(2 * width, depth), b(deep, depth), f(width, 128),
            like(act), like(kv), like(o_raw), like(cos_sin), like(allowed), like(qd), like(gm),
            like(weights[0]), b(2 * weights[1].shape[0], width),
            b(rows, width), b(2, rows, width), like(kv), b(KEY_VALUE_HEADS, 3 * rows, 128), b(rows, KEY_VALUE_HEADS * 128),
            f(rows, width), f(128, width),
            b(RANKS - 1, deep, columns), b(5, deep, columns), f(2, fine // 2, columns),
            b(2, fine // 2, columns), b(2, fine // 2, columns), b(2, fine // 4, columns), b(2, fine // 4, columns),
            b(2, 2, per, quarter), b(2, RANKS, per, quarter),
            b(2, 2, part, quarter), b(2, RANKS, part, quarter), b(2, RANKS, part, quarter), b(2, 5, part, quarter),
            b(RANKS, part, wide_t), b(RANKS, part, wide_t),
            b(RANKS, part // 2, wide_t), b(RANKS, part // 2, wide_t), b(RANKS, part // 2, wide_t), b(5, part // 2, wide_t),
            b(2, 2, 4, fine // 4, columns), b(2, 2, 4, part, quarter), b(2, 4, part // 2, wide_t),
            sem(8), sem(7), sem(5, KEY_VALUE_HEADS), sem(2, KEY_VALUE_HEADS), sem(3, KEY_VALUE_HEADS), sem(2), sem(2), sem(2), sem(2), sem(2),
            sem(3, 2), sem(5, 2), sem(2), sem(2), sem(2), sem(2),
            sem(2, 2), sem(2, 4), sem(2, 2), sem(2, 4), sem(2, 3), sem(2, 5),
            sem(4), sem(4), sem(4), sem(4), sem(3), sem(5),
            sem(5, 8), sem(5, 4), sem(5, 4), sem(40),
        ],
        compiler_params=pltpu.CompilerParams(
            collective_id=2, has_side_effects=True, vmem_limit_bytes=61 * 2**20
        ),
        name="sums",
    )(gain_sums, gain_attn, *operands, *kept, *weights)


def finish_kernel(
    acts_h, first_h, second_h, t_h, gate_h, up_h, down_h,
    acts_o, grads_o, q_o, out_o, key_o, value_o, gain_o, gate_o, up_o, down_o,
    t_v, gate_v, down_v, q_f, kv_f, gate_f, down_f, load, store,
):
    width = q_f.shape[2]
    loads = [
        pltpu.make_async_copy(h, v, load.at[i])
        for i, (h, v) in enumerate(
            [(gate_h, gate_v.at[0]), (up_h, gate_v.at[1]), (down_h, down_v), (t_h, t_v)]
        )
    ]
    stores = [
        pltpu.make_async_copy(v, h, store.at[i])
        for i, (v, h) in enumerate(
            [(acts_h, acts_o), (first_h, grads_o), (gate_f.at[0], gate_o), (gate_f.at[1], up_o),
             (down_f, down_o), (q_f.at[0], q_o), (q_f.at[1], out_o), (kv_f.at[0], key_o), (kv_f.at[1], value_o)]
        )
    ]
    section = lax.axis_index("section")
    for copy in loads + stores[:1]:
        copy.start()
    start_if(
        section == 0,
        lambda: pltpu.make_async_copy(first_h, grads_o, store.at[1]),
        lambda: pltpu.make_async_copy(second_h, grads_o, store.at[1]),
    )
    for k in range(2):
        loads[k].wait()
        gate_f[k] = gate_v[k].astype(F32)
        stores[2 + k].start()
    loads[2].wait()
    for at, size in tiles(width, 128):
        down_f[at : at + size, :] = down_v[:, at : at + 128].astype(F32).T[:size]
    stores[4].start()
    loads[3].wait()
    for core in range(2):
        q_f[core] = t_v[core, :, :width].astype(F32)
        stores[5 + core].start()
    pairs_at = width // 128 * 128 + 128
    half = KEY_VALUE_HEADS // 2 + 1
    for g in range(KEY_VALUE_HEADS):
        core = 0 if g < half else 1
        at = pairs_at + (g - core * (KEY_VALUE_HEADS - half)) * 128
        block = t_v[core, :, at : at + 128].astype(F32).T
        kv_f[0, g * HEAD_SIZE : (g + 1) * HEAD_SIZE, :] = block[:HEAD_SIZE]
        kv_f[1, g * HEAD_SIZE : (g + 1) * HEAD_SIZE, :] = block[HEAD_SIZE:]
    for copy in stores[7:]:
        copy.start()
    tail = slice(pairs_at - 128, pairs_at)
    both = t_v[0, :, tail].astype(F32) + t_v[1, :, tail].astype(F32)
    row = width % 128
    gain_o[...] = both.T[row : row + 8]
    for copy in stores:
        copy.wait()


def run_finish(acts, grads_first, grads_second, t_sum, gate, up, down, width):
    per, ff = gate.shape
    vmem, hbm = pl.BlockSpec(memory_space=pltpu.VMEM), pl.BlockSpec(memory_space=pl.ANY)
    out = lambda *shape: jax.ShapeDtypeStruct(shape, F32)
    kv_rows = KEY_VALUE_HEADS * HEAD_SIZE
    return pl.pallas_call(
        finish_kernel,
        out_shape=[
            jax.ShapeDtypeStruct(acts.shape, BF16), jax.ShapeDtypeStruct(acts.shape, BF16),
            out(per, width), out(per, width), out(kv_rows, per), out(kv_rows, per), out(8, per),
            out(per, ff), out(per, ff), out(width, down.shape[0]),
        ],
        in_specs=[hbm] * 7,
        out_specs=[hbm] * 6 + [vmem] + [hbm] * 3,
        scratch_shapes=[
            pltpu.VMEM(t_sum.shape, BF16), pltpu.VMEM((2, per, ff), BF16), pltpu.VMEM(down.shape, BF16),
            pltpu.VMEM((2, per, width), F32), pltpu.VMEM((2, kv_rows, per), F32),
            pltpu.VMEM((2, per, ff), F32), pltpu.VMEM((width, down.shape[0]), F32),
            pltpu.SemaphoreType.DMA((4,)), pltpu.SemaphoreType.DMA((9,)),
        ],
        compiler_params=pltpu.CompilerParams(vmem_limit_bytes=40 * 2**20),
        name="finish",
    )(acts, grads_first, grads_second, t_sum, gate, up, down)


def sums_by_xla(gain_sums, operands):
    nf, inner, gg, gu, br, la, ra, nr, kvg = operands
    width = nf.shape[1]

    def reduced(left, right):
        total = dot_lt(left, right).astype(BF16)
        piece = lax.psum_scatter(total, "dp", scatter_dimension=0, tiled=True)
        return lax.psum(piece, "ctx")

    def both(piece, axis):
        return lax.all_gather(piece, "section", axis=axis, tiled=axis > 0).astype(F32)

    attn = both(reduced(la, ra), 0)
    gain_sum = lax.psum(gain_sums[:2], ("section", "ctx"))
    return (
        attn[0],
        attn[1],
        both(reduced(nr, kvg), 0),
        lax.psum_scatter(gain_sum, "dp", scatter_dimension=1, tiled=True),
        both(reduced(nf, gg), 1),
        both(reduced(nf, gu), 1),
        both(reduced(inner, br), 1)[:, :width],
    )


def shards(
    ends,
    doc_lengths,
    w_query,
    key_projection_weight,
    value_projection_weight,
    w_out,
    w_gate,
    w_up,
    w_down,
    gain_attn,
    gain_ffn,
):
    width = ends.shape[3]
    half = HEAD_SIZE // 2
    turns = np.float32(10000.0) ** (
        np.float32(-2.0) * (np.arange(128) % half).astype(np.float32) / np.float32(HEAD_SIZE)
    )
    weights = (
        w_query,
        key_projection_weight.T,
        value_projection_weight.T,
        w_out,
        w_gate,
        w_up,
        w_down.T,
    )
    gain_row = gain_attn.reshape(1, width)
    ff = w_gate.shape[1]
    fits = lax.axis_size("dp") == RANKS and width % 64 == 0 and ff % 1280 == 0
    acts, grads_in, gain_sums, *kept = run_layers(
        doc_lengths,
        ends,
        jnp.asarray(turns.reshape(1, 128), F32),
        gain_row,
        gain_ffn.reshape(1, width),
        weights,
        not fits,
    )
    operands = kept[:9]
    if fits:
        grads_first, *sums = run_sums(
            gain_sums, gain_row, operands, kept[9:], weights[:3], ends.shape
        )
        acts, grads_in, grad_query, grad_out, grad_key, grad_value, gain_piece, grad_gate, grad_up, grad_down = (
            run_finish(acts, grads_first, grads_in, *sums, width)
        )
        grad_key, grad_value, grad_down = grad_key.T, grad_value.T, grad_down.T
    else:
        grad_query, grad_out, kv_parts, gain_piece, grad_gate, grad_up, grad_down = sums_by_xla(
            gain_sums, operands
        )
        kv_grad = jnp.concatenate([kv_parts[0], kv_parts[1][:, 128:]], axis=1).reshape(
            -1, KEY_VALUE_HEADS, 2, HEAD_SIZE
        )
        grad_key = kv_grad[:, :, 0].reshape(kv_grad.shape[0], -1)
        grad_value = kv_grad[:, :, 1].reshape(kv_grad.shape[0], -1)
    return (
        acts,
        grads_in,
        grad_query,
        grad_key,
        grad_value,
        grad_out,
        grad_gate,
        grad_up,
        grad_down,
        gain_piece[0],
        gain_piece[1],
    )


def solution(mesh):
    return jax.shard_map(
        shards,
        mesh=mesh,
        in_specs=(P("section", None, ("dp", "ctx"), None), P(None, "dp", None)) + (P(),) * 9,
        out_specs=(P("section", None, ("dp", "ctx"), None),) * 2
        + (P("dp", None),) * 7
        + (P("dp"),) * 2,
        check_vma=False,
    )
```

```python
import jax
import jax.numpy as jnp
import numpy as np
from jax import lax
from jax.experimental import pallas as pl
from jax.experimental.pallas import tpu as pltpu
from jax.sharding import PartitionSpec as P

MESH = pl.DeviceIdType.MESH
QUERY_HEADS = 15
KEY_VALUE_HEADS = 5
HEAD_SIZE = 64
SHARE = QUERY_HEADS // KEY_VALUE_HEADS
RANKS = 4
epsilon = 1e-05
masked_fill = -1e30
F32 = jnp.float32
BF16 = jnp.bfloat16


def dot(left, right):
    return jnp.dot(left, right, preferred_element_type=F32)


def dot_rt(left, right):
    return lax.dot_general(left, right, (((1,), (1,)), ((), ())), preferred_element_type=F32)


def dot_lt(left, right):
    return lax.dot_general(left, right, (((0,), (0,)), ((), ())), preferred_element_type=F32)


def tiles(total, width):
    return [(at, min(width, total - at)) for at in range(0, total, width)]


def wide(block):
    missing = 128 - block.shape[1]
    if not missing:
        return block
    return jnp.concatenate([block, jnp.zeros((block.shape[0], missing), block.dtype)], axis=1)


def lanes(rows):
    return lax.broadcasted_iota(jnp.int32, (rows, 128), 1)


def half_turn(block):
    front = lanes(block.shape[0]) % HEAD_SIZE < HEAD_SIZE // 2
    return jnp.where(front, pltpu.roll(block, 96, 1), pltpu.roll(block, 32, 1))


def inverse_rms(hidden):
    return lax.rsqrt(jnp.mean(hidden * hidden, axis=-1, keepdims=True) + epsilon)


def half_turned(block, cosines, sines, direction):
    return block * cosines + direction * (half_turn(block) * sines)


def norm_back(hidden, gain, upstream):
    scale = inverse_rms(hidden)
    weighted = upstream * gain
    inside = jnp.mean(weighted * hidden, axis=-1, keepdims=True)
    gain_row = jnp.sum(upstream * hidden * scale, axis=0, keepdims=True)
    return scale * weighted - hidden * (scale * scale * scale * inside), gain_row


def start_if(condition, here, there):
    @pl.when(condition)
    def _():
        here().start()

    @pl.when(jnp.logical_not(condition))
    def _():
        there().start()


class AttentionBack:
    def __init__(
        self, rank, device_of, qd, kv, o_raw, allowed, cos_sin, ra, pds, dkv, dkv_in, gkv, send, recv
    ):
        self.rank, self.device_of = rank, device_of
        self.qd, self.kv, self.o_raw, self.allowed, self.cos_sin = qd, kv, o_raw, allowed, cos_sin
        self.ra, self.pds, self.dkv, self.dkv_in, self.gkv = ra, pds, dkv, dkv_in, gkv
        self.send_sem, self.recv_sem = send, recv
        self.rows, self.width = ra.shape[1:]

    def head(self, g):
        rows = self.rows
        kv_g = self.kv[g]
        for i in range(SHARE):
            mine = slice(i * rows, (i + 1) * rows)
            other = slice((SHARE + i) * rows, (SHARE + i + 1) * rows)
            kept = self.o_raw[g * SHARE + i]
            scores = dot_rt(self.qd[g, mine, :], kv_g) + self.allowed[...]
            probs = jnp.exp(scores - kept[:, 0:1])
            grad_out = self.qd[g, other, :]
            grad_probs = dot_rt(grad_out, kv_g)
            weight = jnp.sum(grad_out.astype(F32) * kept, axis=-1, keepdims=True)
            grad_scores = (probs * (grad_probs - weight)).astype(BF16)
            self.pds[mine, :] = grad_scores
            self.pds[other, :] = probs.astype(BF16)
            self.o_raw[g * SHARE + i] = dot(grad_scores, kv_g)
        grad_kv = dot_lt(self.qd[g], self.pds[...])
        self.dkv[g] = grad_kv.T.astype(BF16)
        self.send(g)

    def heads(self, first, last):
        def body(g, carry):
            self.head(g)

            @pl.when(g > 0)
            def _():
                self.relay(g - 1)

            return carry

        lax.fori_loop(first, last, body, 0)

    def copy(self, quarter, count, dst, slot_in, slot, g):
        rows = self.rows
        return pltpu.make_async_remote_copy(
            src_ref=self.dkv.at[g, pl.ds(quarter * rows, count * rows)],
            dst_ref=self.dkv_in.at[g, pl.ds(slot_in * rows, count * rows)],
            send_sem=self.send_sem.at[slot, g],
            recv_sem=self.recv_sem.at[slot_in, g],
            device_id=self.device_of(dst),
            device_id_type=MESH,
        )

    def add(self, quarter, slots, g):
        rows = self.rows
        span = slice(quarter * rows, (quarter + 1) * rows)
        total = self.dkv[g, span].astype(F32)
        for slot in slots:
            total = total + self.dkv_in[g, slot * rows : (slot + 1) * rows].astype(F32)
        self.dkv[g, span] = total.astype(BF16)

    def send(self, g):
        @pl.when(self.rank == 3)
        def _():
            self.copy(2, 1, 2, 0, 0, g).start()
            self.copy(0, 2, 1, 0, 1, g).start()

        @pl.when(self.rank == 2)
        def _():
            self.copy(1, 1, 1, 2, 0, g).start()
            self.copy(0, 1, 0, 1, 1, g).start()

    def relay(self, g):
        @pl.when(self.rank == 1)
        def _():
            self.copy(0, 2, 1, 0, 0, g).wait_recv()
            self.add(0, (0,), g)
            self.copy(0, 1, 0, 0, 0, g).start()

    def queries(self):
        for at, size in tiles(self.width, 128):
            head = at // HEAD_SIZE
            block = self.o_raw[head]
            if size == 128:
                low = lanes(self.rows) < HEAD_SIZE
                block = jnp.where(low, block, pltpu.roll(self.o_raw[head + 1], 64, 1))
            turned = half_turned(block, self.cos_sin[0], self.cos_sin[1], -1.0) * 0.125
            self.ra[0, :, at : at + size] = turned[:, :size].astype(BF16)

    def collect(self):
        low = lanes(self.rows) < HEAD_SIZE
        cosines = jnp.where(low, self.cos_sin[0], 1.0)
        sines = jnp.where(low, self.cos_sin[1], 0.0)
        mine = pl.ds(pl.multiple_of(self.rank * self.rows, 16), self.rows)
        for g in range(KEY_VALUE_HEADS):
            self.arrive(g)
            block = half_turned(self.dkv[g, mine, :].astype(F32), cosines, sines, -1.0)
            self.gkv[:, 128 * g : 128 * g + 128] = block.astype(BF16)

    def arrive(self, g):
        @pl.when(self.rank == 3)
        def _():
            self.copy(2, 1, 2, 0, 0, g).wait_send()
            self.copy(0, 2, 1, 0, 1, g).wait_send()

        @pl.when(self.rank == 2)
        def _():
            self.copy(0, 1, 2, 0, 0, g).wait_recv()
            self.copy(1, 1, 1, 2, 0, g).wait_send()
            self.copy(0, 1, 0, 1, 1, g).wait_send()
            self.add(2, (0,), g)

        @pl.when(self.rank == 1)
        def _():
            self.copy(0, 1, 2, 2, 0, g).wait_recv()
            self.copy(0, 1, 0, 0, 0, g).wait_send()
            self.add(1, (1, 2), g)

        @pl.when(self.rank == 0)
        def _():
            self.copy(0, 1, 2, 0, 0, g).wait_recv()
            self.copy(0, 1, 2, 1, 0, g).wait_recv()
            self.add(0, (0, 1), g)

    def project(self, total, wq, wkv):
        for at, size in tiles(self.width, 256):
            total[:, at : at + size] = dot_rt(self.ra[0], wq[at : at + size, :]) + dot(
                self.gkv[...], wkv[:, at : at + size]
            )


class OutCopy:
    def __init__(self, out, send, recv):
        self.section, self.dp, ctx = (lax.axis_index(a) for a in ("section", "dp", "ctx"))
        self.home = 2 * self.section + ctx % 2
        self.ctx, self.micro = ctx, ctx // 2
        self.out, self.send, self.recv = out, send, recv

    def here(self, l):
        return (self.section == l) & (self.ctx == self.home)

    def remote(self, array, l):
        return pltpu.make_async_remote_copy(
            src_ref=array,
            dst_ref=self.out.at[0, self.micro],
            send_sem=self.send.at[l],
            recv_sem=self.recv.at[self.micro],
            device_id=(l, self.dp, self.home),
            device_id_type=MESH,
        )

    def local(self, array):
        return pltpu.make_async_copy(array, self.out.at[0, self.micro], self.recv.at[self.micro])

    def start(self, array, l):
        start_if(self.here(l), lambda: self.local(array), lambda: self.remote(array, l))

    def sent(self, array, l):
        @pl.when(jnp.logical_not(self.here(l)))
        def _():
            self.remote(array, l).wait_send()

    def arrived(self, array):
        for block in range(2):
            pltpu.make_async_copy(array, self.out.at[0, block], self.recv.at[block]).wait()


def greet(barrier, dp):
    section, ctx = lax.axis_index("section"), lax.axis_index("ctx")
    for step in range(1, 8):
        other = (4 * section + ctx + step) % 8
        pl.semaphore_signal(
            barrier, inc=1, device_id=(other // 4, dp, other % 4), device_id_type=MESH
        )


def layers_kernel(complete, *refs):
    refs = list(refs)

    def take(count):
        taken = refs[:count]
        del refs[:count]
        return taken

    lengths, ends, frequency, gain_a, gain_f, wq_h, wk_h, wv_h, wo_h, wg_h, wu_h, wd_h = take(12)
    acts_o, grads_o, gain_o, nf_o, in_o, gg_o, gu_o, br_o, la_o, ra_o, nr_o, kvg_o = take(12)
    kept_o = [] if complete else take(7)
    wq, wkv, wo, wg, wu, wd = take(6)
    act, go, middle, norm_ffn, fact_a, fact_b, inner, lm, qd, kv, o_raw = take(11)
    sum_acc, gm, gg, gu, br, ra, pds, dkv, dkv_in, gkv, cos_sin, allowed_add, gain_v = take(13)
    w_sem, kv_sem, in_send, in_recv, kv_send, kv_recv, dk_send, dk_recv = take(8)
    act_send, act_recv, grad_send, grad_recv, op_own, op_send, op_recv, kept_sem = take(8)

    section = lax.axis_index("section")
    dp = lax.axis_index("dp")
    ctx = lax.axis_index("ctx")
    micro = ctx // 2
    xbit = ctx % 2
    rank = 2 * section + xbit
    rows, width = act.shape[1], act.shape[2]
    ff = wg.shape[1]
    ff_half = ff // 2

    def device_of(r):
        return (r // 2, dp, 2 * micro + r % 2)

    partner = (1 - section, dp, ctx)

    loads = [
        pltpu.make_async_copy(h, v, w_sem.at[i])
        for i, (h, v) in enumerate([(wq_h, wq), (wo_h, wo), (wg_h, wg), (wu_h, wu), (wd_h, wd)])
    ]
    kv_loads = [
        pltpu.make_async_copy(
            h.at[pl.ds(g * HEAD_SIZE, HEAD_SIZE)],
            wkv.at[pl.ds((2 * g + i) * HEAD_SIZE, HEAD_SIZE)],
            kv_sem.at[i, g],
        )
        for g in range(KEY_VALUE_HEADS)
        for i, h in enumerate((wk_h, wv_h))
    ]
    for load in kv_loads + loads:
        load.start()
    kv[...] = jnp.zeros_like(kv)
    barrier = pltpu.get_barrier_semaphore()
    greet(barrier, dp)
    pl.semaphore_wait(barrier, 7)

    def in_local(block, into_x):
        dst, slot = (act.at[0], 0) if into_x else (go.at[2], 1)
        return pltpu.make_async_copy(ends.at[0, block], dst, in_recv.at[slot])

    def in_remote(block, into_x):
        dst, slot = (act.at[0], 0) if into_x else (go.at[2], 1)
        return pltpu.make_async_remote_copy(
            src_ref=ends.at[0, block],
            dst_ref=dst,
            send_sem=in_send.at[block],
            recv_sem=in_recv.at[slot],
            device_id=(ctx // 2, dp, 2 * block + xbit),
            device_id_type=MESH,
        )

    def in_mine(block):
        return (section == ctx // 2) & (ctx // 2 == block)

    def in_start(into_x):
        @pl.when(section == (0 if into_x else 1))
        def _():
            for block in range(2):
                start_if(
                    in_mine(block),
                    lambda block=block: in_local(block, into_x),
                    lambda block=block: in_remote(block, into_x),
                )

    in_start(True)
    lane = lanes(rows)
    low = lane < HEAD_SIZE
    gain_attn = gain_a[...].astype(F32).reshape(1, width)
    gain_ffn = gain_f[...].astype(F32).reshape(1, width)

    def place(token_index):
        segment = jnp.zeros_like(token_index)
        start = jnp.zeros_like(token_index)
        finish = jnp.int32(0)
        for slot in range(lengths.shape[2]):
            length = lengths[micro, 0, slot]
            finish = finish + length
            passed = (token_index >= finish).astype(jnp.int32)
            segment = segment + passed
            start = start + passed * length
        return segment, token_index - start

    seg_mine, position = place(rank * rows + lax.broadcasted_iota(jnp.int32, (rows, 128), 0))
    angles = position.astype(F32) * frequency[...]
    cos_sin[0] = jnp.cos(angles)
    cos_sin[1] = jnp.where(lane % HEAD_SIZE < HEAD_SIZE // 2, -1.0, 1.0) * jnp.sin(angles)
    key_index = lax.broadcasted_iota(jnp.int32, (1, RANKS * rows), 1)
    query_index = rank * rows + lax.broadcasted_iota(jnp.int32, (rows, 1), 0)
    allowed_add[...] = jnp.where(
        (seg_mine[:, 0:1] == place(key_index)[0]) & (query_index >= key_index), 0.0, masked_fill
    )

    def kv_rows(l, r, g):
        return kv.at[l, g, pl.ds(r * rows, rows)]

    def kv_copy(l, quarter, dst, slot, g):
        return pltpu.make_async_remote_copy(
            src_ref=kv_rows(l, quarter, g),
            dst_ref=kv_rows(l, quarter, g),
            send_sem=kv_send.at[l, slot, g],
            recv_sem=kv_recv.at[l, quarter, g],
            device_id=device_of(dst),
            device_id_type=MESH,
        )

    kv_plan = [(0, 0, 1, 0), (0, 0, 2, 1), (1, 1, 2, 0), (1, 1, 3, 1), (2, 2, 3, 0)]
    kv_relay = (1, 0, 3, 2)

    def kv_start(l, g):
        for sender, quarter, dst, slot in kv_plan:

            @pl.when(rank == sender)
            def _(quarter=quarter, dst=dst, slot=slot):
                kv_copy(l, quarter, dst, slot, g).start()

    def kv_relayed(l, g):
        @pl.when(rank == 1)
        def _():
            kv_copy(l, 0, 3, 2, g).wait_recv()
            kv_copy(l, 0, 3, 2, g).start()

    def kv_finish(l, g):

        for quarter, receivers in ((0, (2, 3)), (1, (2, 3)), (2, (3,))):
            for receiver in receivers:

                @pl.when(rank == receiver)
                def _(quarter=quarter):
                    kv_copy(l, quarter, 0, 0, g).wait_recv()

    def kv_sent(l):
        for sender, quarter, dst, slot in kv_plan + [kv_relay]:

            @pl.when(rank == sender)
            def _(quarter=quarter, dst=dst, slot=slot):
                for g in range(KEY_VALUE_HEADS):
                    kv_copy(l, quarter, dst, slot, g).wait_send()

    acts_out = OutCopy(acts_o, act_send, act_recv)
    grads_out = OutCopy(grads_o, grad_send, grad_recv)

    def op_copy(kind, l, own):
        role = section if own else 1 - section
        half = pl.ds(pl.multiple_of(role * ff_half, 128), ff_half)
        src = [
            lambda: norm_ffn.at[l],
            lambda: inner.at[l],
            lambda: gg.at[:, half],
            lambda: gu.at[:, half],
            lambda: br.at[:, pl.ds(pl.multiple_of(role * 512, 128), 512)],
            lambda: lm.at[l, role],
            lambda: ra.at[role],
            lambda: lm.at[l, 0],
            lambda: gkv.at[:, pl.ds(pl.multiple_of(role * 256, 128), 384)],
        ][kind]()
        block = section if kind in (6, 8) and not complete else 2 * section + l
        dst = [nf_o, in_o, gg_o, gu_o, br_o, la_o, ra_o, nr_o, kvg_o][kind].at[
            pl.ds(pl.multiple_of(block * rows, 16), rows)
        ]
        if own:
            return pltpu.make_async_copy(src, dst, op_own.at[kind, l])
        return pltpu.make_async_remote_copy(
            src_ref=src,
            dst_ref=dst,
            send_sem=op_send.at[kind, l],
            recv_sem=op_recv.at[kind, l],
            device_id=partner,
            device_id_type=MESH,
        )

    def op_start(kinds, l):
        for kind in kinds:
            op_copy(kind, l, True).start()
            op_copy(kind, l, False).start()

    def op_sent(kinds, l):
        for kind in kinds:
            op_copy(kind, l, True).wait()
            op_copy(kind, l, False).wait_send()

    def kept_copy(i):
        src = [act.at[0], kv.at[0], o_raw.at[0], cos_sin, allowed_add, qd.at[0], gm][i]
        return pltpu.make_async_copy(src, kept_o[i], kept_sem.at[i])

    def kept_start(*which):
        if not complete:
            for i in which:
                kept_copy(i).start()

    in_remote(0, True).wait_recv()
    for load in kv_loads:
        load.wait()

    def forward(l, carry):
        hidden = act[l].astype(F32)
        cos_q, sin_q = cos_sin[0], cos_sin[1]
        lm[l, 0] = (hidden * inverse_rms(hidden) * gain_attn).astype(BF16)
        cos_kv = jnp.where(low, cos_q, 1.0)
        sin_kv = jnp.where(low, sin_q, 0.0)
        mine = pl.ds(pl.multiple_of(rank * rows, 16), rows)
        for g in range(KEY_VALUE_HEADS):
            block = dot_rt(lm[l, 0], wkv[128 * g : 128 * g + 128, :])
            turned = half_turned(block, cos_kv, sin_kv, 1.0)
            kv[l, g, mine, :] = turned.astype(BF16)
            kv_start(l, g)

        @pl.when(l == 0)
        def _():
            loads[0].wait()
            in_start(False)
            kept_start(0, 3, 4)

        for at, size in tiles(width, 256):
            product = dot(lm[l, 0], wq[:, at : at + size])
            for inside, part in tiles(size, 128):
                block = wide(product[:, inside : inside + part])
                turned = half_turned(block, cos_q, sin_q, 1.0) * 0.125
                head = (at + inside) // HEAD_SIZE
                qd[l, head // SHARE, pl.ds(head % SHARE * rows, rows), :] = jnp.where(
                    low, turned, 0.0
                ).astype(BF16)
                head += 1
                if head < QUERY_HEADS:
                    qd[l, head // SHARE, pl.ds(head % SHARE * rows, rows), :] = jnp.where(
                        low, pltpu.roll(turned, 64, 1), 0.0
                    ).astype(BF16)
        kv_relayed(l, 0)
        kv_finish(l, 0)

        def heads(g, carry):
            @pl.when(g < KEY_VALUE_HEADS - 1)
            def _():
                kv_relayed(l, g + 1)

            @pl.when(g > 0)
            def _():
                kv_finish(l, g)

            kv_g = kv[l, g]
            for i in range(SHARE):
                scores = dot_rt(qd[l, g, i * rows : (i + 1) * rows, :], kv_g) + allowed_add[...]
                peak = jnp.max(scores, axis=-1, keepdims=True)
                exponent = jnp.exp(scores - peak)
                total = jnp.sum(exponent, axis=-1, keepdims=True)
                out = dot(exponent.astype(BF16), kv_g) * (1.0 / total)
                o_raw[l, g * SHARE + i] = jnp.where(low, peak + jnp.log(total), out)
            return carry

        lax.fori_loop(0, KEY_VALUE_HEADS, heads, 0)

        @pl.when(l == 0)
        def _():
            kept_start(1, 2)
            loads[1].wait()

        for at, size in tiles(width, 128):
            head = at // HEAD_SIZE
            block = pltpu.roll(o_raw[l, head], 64, 1)
            if size == 128:
                block = jnp.where(low, block, o_raw[l, head + 1])
            lm[l, 1, :, at : at + size] = block[:, :size].astype(BF16)
        for at, size in tiles(width, 256):
            middle[l, :, at : at + size] = act[l, :, at : at + size].astype(F32) + dot(
                lm[l, 1], wo[:, at : at + size]
            )
        mid = middle[l]
        norm_ffn[l] = (mid * inverse_rms(mid) * gain_ffn).astype(BF16)
        op_start((0, 5, 7), l)

        @pl.when(l == 0)
        def _():
            loads[2].wait()
            loads[3].wait()

        def gates(j, carry):
            part = pl.ds(pl.multiple_of(j * 512, 512), 512)
            gate = dot(norm_ffn[l], wg[:, part])
            upper = dot(norm_ffn[l], wu[:, part])
            s = 0.5 * jnp.tanh(0.5 * gate) + 0.5
            swish = gate * s
            inner[l, :, part] = (swish * upper).astype(BF16)
            fact_a[l, :, part] = (upper * s * (1.0 + gate * (1.0 - s))).astype(BF16)
            fact_b[l, :, part] = swish.astype(BF16)
            return carry

        lax.fori_loop(0, ff // 512, gates, 0)

        @pl.when(l == 0)
        def _():
            loads[4].wait()

        op_start((1,), l)
        for at, size in tiles(width, 256):
            act[l + 1, :, at : at + size] = (
                middle[l, :, at : at + size] + dot_rt(inner[l], wd[at : at + size, :])
            ).astype(BF16)
        acts_out.start(act.at[l + 1], l)
        kv_sent(l)
        return carry

    lax.fori_loop(0, 2, forward, 0)

    in_remote(0, False).wait_recv()
    gain_v[...] = jnp.zeros_like(gain_v)
    br[...] = jnp.zeros_like(br)
    late = (6, 8)

    def backward(step, carry):
        l = 1 - step

        @pl.when(l == 0)
        def _():
            op_sent((2, 3, 4) + (late if complete else ()), 1)

        br[:, :width] = go[l + 1]
        op_start((4,), l)

        def gates(j, carry):
            part = pl.ds(pl.multiple_of(j * 512, 512), 512)
            grad_inner = dot(go[l + 1], wd[:, part])
            gg[:, part] = (grad_inner * fact_a[l, :, part].astype(F32)).astype(BF16)
            gu[:, part] = (grad_inner * fact_b[l, :, part].astype(F32)).astype(BF16)
            return carry

        lax.fori_loop(0, ff // 512, gates, 0)
        op_start((2, 3), l)
        for at, size in tiles(width, 256):
            sum_acc[:, at : at + size] = dot_rt(gg[...], wg[at : at + size, :]) + dot_rt(
                gu[...], wu[at : at + size, :]
            )
        grad, gain_row = norm_back(middle[l], gain_ffn, sum_acc[...])
        gain_v[1:2, :] += gain_row
        gm[...] = go[l + 1].astype(F32) + grad
        ra[1] = gm[...].astype(BF16)

        for at, size in tiles(width, 256):
            product = dot_rt(ra[1], wo[at : at + size, :])
            for inside, part in tiles(size, 128):
                block = wide(product[:, inside : inside + part])
                head = (at + inside) // HEAD_SIZE
                qd[l, head // SHARE, pl.ds((SHARE + head % SHARE) * rows, rows), :] = jnp.where(
                    low, 0.0, pltpu.roll(block, 64, 1)
                ).astype(BF16)
                head += 1
                if head < QUERY_HEADS:
                    qd[l, head // SHARE, pl.ds((SHARE + head % SHARE) * rows, rows), :] = (
                        jnp.where(low, 0.0, block).astype(BF16)
                    )

        def attention():
            back = AttentionBack(
                rank, device_of, qd.at[l], kv.at[l], o_raw.at[l], allowed_add, cos_sin, ra, pds,
                dkv, dkv_in.at[l] if complete else dkv_in, gkv,
                dk_send.at[l] if complete else dk_send, dk_recv.at[l] if complete else dk_recv,
            )
            back.heads(0, KEY_VALUE_HEADS)
            back.relay(KEY_VALUE_HEADS - 1)
            back.queries()
            op_start((6,), l)
            back.collect()
            op_start((8,), l)
            back.project(sum_acc, wq, wkv)
            grad, gain_row = norm_back(act[l].astype(F32), gain_attn, sum_acc[...])
            gain_v[0:1, :] += gain_row
            go[l] = (gm[...] + grad).astype(BF16)
            grads_out.start(go.at[l], l)

        if complete:
            attention()
        else:

            @pl.when(l == 1)
            def _():
                attention()

            @pl.when(l == 1)
            def _():
                op_sent(late, 1)

        return carry

    lax.fori_loop(0, 2, backward, 0)

    gain_copy = pltpu.make_async_copy(gain_v, gain_o, kept_sem.at[7])
    gain_copy.start()
    kept_start(5, 6)
    for into_x in (True, False):

        @pl.when(section == (0 if into_x else 1))
        def _(into_x=into_x):
            for block in range(2):

                @pl.when(jnp.logical_not(in_mine(block)))
                def _(block=block):
                    in_remote(block, into_x).wait_send()

    op_sent((2, 3, 4) + (late if complete else ()), 0)
    for l in range(2):
        op_sent((0, 1, 5, 7), l)
        for kind in range(9):
            if l == 1 or complete or kind not in late:
                op_copy(kind, l, False).wait_recv()
        acts_out.sent(act.at[l + 1], l)
        if l == 1 or complete:
            grads_out.sent(go.at[l], l)
    gain_copy.wait()
    acts_out.arrived(act.at[0])
    if complete:
        grads_out.arrived(act.at[0])
    else:

        @pl.when(section == 1)
        def _():
            grads_out.arrived(act.at[0])

        for i in range(len(kept_o)):
            kept_copy(i).wait()


def run_layers(lengths, ends, frequency, gain_attn, gain_ffn, weights, complete):
    micro_count, rows, width = ends.shape[1:]
    wq, wk, wv, wo, wg, wu, wd = weights
    ff = wg.shape[1]
    keys = RANKS * rows
    kv_width = 2 * wk.shape[0]
    vmem, hbm = pl.BlockSpec(memory_space=pltpu.VMEM), pl.BlockSpec(memory_space=pl.ANY)
    op_rows = 4 * rows
    late_rows = op_rows if complete else 2 * rows
    out = lambda *shape: jax.ShapeDtypeStruct(shape, BF16)
    out_f = lambda *shape: jax.ShapeDtypeStruct(shape, F32)
    dma = lambda *shape: pltpu.SemaphoreType.DMA(shape)
    kept = [
        out(rows, width),
        out(KEY_VALUE_HEADS, keys, 128),
        out_f(QUERY_HEADS, rows, 128),
        out_f(2, rows, 128),
        out_f(rows, keys),
        out(KEY_VALUE_HEADS, 2 * SHARE * rows, 128),
        out_f(rows, width),
    ]
    layers = (2,) if complete else ()
    return pl.pallas_call(
        lambda *refs: layers_kernel(complete, *refs),
        out_shape=[
            out(*ends.shape),
            out(*ends.shape),
            out_f(8, width),
            out(op_rows, width),
            out(op_rows, ff),
            out(op_rows, ff // 2),
            out(op_rows, ff // 2),
            out(op_rows, 512),
            out(op_rows, width),
            out(late_rows, width),
            out(op_rows, width),
            out(late_rows, 384),
        ]
        + ([] if complete else kept),
        in_specs=[pl.BlockSpec(memory_space=pltpu.SMEM), hbm] + [vmem] * 3 + [hbm] * 7,
        out_specs=[hbm] * (12 if complete else 19),
        scratch_shapes=[
            pltpu.VMEM(wq.shape, BF16),
            pltpu.VMEM((kv_width, width), BF16),
            pltpu.VMEM(wo.shape, BF16),
            pltpu.VMEM(wg.shape, BF16),
            pltpu.VMEM(wu.shape, BF16),
            pltpu.VMEM(wd.shape, BF16),
            pltpu.VMEM((3, rows, width), BF16),
            pltpu.VMEM((3, rows, width), BF16),
            pltpu.VMEM((2, rows, width), F32),
            pltpu.VMEM((2, rows, width), BF16),
            pltpu.VMEM((2, rows, ff), BF16),
            pltpu.VMEM((2, rows, ff), BF16),
            pltpu.VMEM((2, rows, ff), BF16),
            pltpu.VMEM((2, 2, rows, width), BF16),
            pltpu.VMEM((2, KEY_VALUE_HEADS, 2 * SHARE * rows, 128), BF16),
            pltpu.VMEM((2, KEY_VALUE_HEADS, keys, 128), BF16),
            pltpu.VMEM((2, QUERY_HEADS, rows, 128), F32),
            pltpu.VMEM((rows, width), F32),
            pltpu.VMEM((rows, width), F32),
            pltpu.VMEM((rows, ff), BF16),
            pltpu.VMEM((rows, ff), BF16),
            pltpu.VMEM((rows, 1024), BF16),
            pltpu.VMEM((2, rows, width), BF16),
            pltpu.VMEM((2 * SHARE * rows, keys), BF16),
            pltpu.VMEM((KEY_VALUE_HEADS, keys, 128), BF16),
            pltpu.VMEM(layers + (KEY_VALUE_HEADS, 3 * rows, 128), BF16),
            pltpu.VMEM((rows, kv_width), BF16),
            pltpu.VMEM((2, rows, 128), F32),
            pltpu.VMEM((rows, keys), F32),
            pltpu.VMEM((8, width), F32),
            dma(5),
            dma(2, KEY_VALUE_HEADS),
            dma(2),
            dma(2),
            dma(2, 3, KEY_VALUE_HEADS),
            dma(2, 3, KEY_VALUE_HEADS),
            dma(*layers, 2, KEY_VALUE_HEADS),
            dma(*layers, 3, KEY_VALUE_HEADS),
            dma(2),
            dma(2),
            dma(2),
            dma(2),
            dma(9, 2),
            dma(9, 2),
            dma(9, 2),
            dma(len(kept) + 1),
        ],
        compiler_params=pltpu.CompilerParams(
            collective_id=1, has_side_effects=True, vmem_limit_bytes=61 * 2**20
        ),
        name="layers",
    )(lengths, ends, frequency, gain_attn, gain_ffn, *weights)


MIDDLE_ORDER = (
    "near1", "near0", "head0", "head1", "head2", "far1", "head3", "head4",
    "near3", "query0", "down0", "near2", "down1", "fadd1", "far0", "aend0",
    "tready0", "tnear2", "down2", "down3", "tnear0", "down4", "far3", "down5",
    "far2", "fadd0", "tfar0", "tnear3", "dfirst0", "tnear1", "fz0", "fadd3",
    "tfar3", "tadd0", "fadd2", "fz1", "dsecond0", "fz2", "tfar1", "tfar2",
    "tadd3", "tz0", "tadd1", "ftotal0", "dgather0", "tadd2", "tz1", "tz2",
    "fmiddle0", "ttotal0", "dmiddle0",
)
END_ORDER = (
    "near1", "head0", "near0", "down0", "far1", "head1", "down1", "down2",
    "head2", "head3", "head4", "near3", "down3", "far0", "fadd1", "down4",
    "query0", "near2", "aend0", "down5", "fadd0", "far3", "fz0", "tready0",
    "tnear3", "far2", "fadd3", "tnear0", "fz2", "tnear2", "fadd2", "fz1",
    "tnear1", "tfar3", "tfar0", "dfirst0", "tfar2", "tfar1", "tadd0", "tadd3",
    "tz0", "tadd1", "dsecond0", "tz2", "ftotal0", "tadd2", "tz1", "dgather0",
    "ttotal0", "fmiddle0", "dmiddle0",
)


def sums_kernel(*refs):
    refs = list(refs)

    def take(count):
        taken = refs[:count]
        del refs[:count]
        return taken

    gain_h, gain_a, nf_h, in_h, gg_h, gu_h, br_h, la_h, ra_h, nr_h, kvg_h = take(11)
    act_h, kv_h, o_h, cs_h, allowed_h, qd_h, gm_h, wq_h, wk_h, wv_h = take(10)
    grads_o, t_o, gate_o, up_o, down_o = take(5)
    stage, in_v, br_v, gg_v, gu_v, ra_v, kvg_v, nf_t, ln_t, in_t, gain_t = take(11)
    act, kv, o_raw, cos_sin, allowed, qd, gm, wq, wkv = take(9)
    go, ra, dkv, dkv_in, gkv, sum_acc, gain_rows = take(7)
    d_out, d_in, d_keep, d1_out, d1_in, d2_out, d2_in = take(7)
    f1_out, f1_in, f2_out, f2_in, f_keep, fz_in = take(6)
    t1_out, t1_in, t2_out, t2_in, t_keep, tz_in = take(6)
    d_all, f_all, t_all = take(3)
    load, kept_sem, w_sem, dk_s, dk_r, grad_s, grad_r, op_own, op_s, op_r = take(10)
    dz_s, dz_r, d1_s, d1_r, d2_s, d2_r, f1_s, f1_r, f2_s, f2_r, fz_s, fz_r = take(12)
    t1_s, t1_r, t2_s, t2_r, tz_s, tz_r, all_s, all_r, pair_r, write = take(10)

    section = lax.axis_index("section")
    z = lax.axis_index("dp")
    ctx = lax.axis_index("ctx")
    x, y = ctx % 2, ctx // 2
    rank = 2 * section + x
    x_next = (section, z, 2 * y + 1 - x)
    y_next = (section, z, 2 * (1 - y) + x)
    partner = (1 - section, z, ctx)
    rows = act.shape[0]
    width = nf_h.shape[1]
    per = width // RANKS
    part = f_keep.shape[2]
    shift = per - part
    quarter = gg_v.shape[1] // 2
    deep = in_t.shape[0]
    fine = deep // 2
    last = RANKS - 1
    edge = ((z == 0) | (z == last)).astype(jnp.int32)

    def pick(index, values):
        if isinstance(index, int):
            return values[index]
        return sum((index == i).astype(jnp.int32) * v for i, v in enumerate(values) if not (type(v) is int and v == 0))

    def remote(src, dst, send, recv, device):
        return pltpu.make_async_remote_copy(
            src_ref=src, dst_ref=dst, send_sem=send, recv_sem=recv,
            device_id=device, device_id_type=MESH,
        )

    def some(start, size, unit=16):
        return pl.ds(pl.multiple_of(start, unit), size)

    gain_load = pltpu.make_async_copy(gain_h, gain_rows.at[pl.ds(0, gain_h.shape[0])], load.at[7])
    by_need = ((3, 2, 1, 0), (3, 0, 2, 1), (0, 3, 1, 2), (0, 1, 2, 3))
    by_turns = ((3, 2, 1, 0), (3, 0, 2, 1), (0, 3, 1, 2), (0, 2, 1, 3))

    def turn_of(k, order=by_need):
        return pick(k, [pick(z, [row[i] for row in order]) for i in range(RANKS)])

    def in_load(k):
        return pltpu.make_async_copy(
            in_h.at[:, some(turn_of(k) * deep, deep, 128)], in_v, load.at[0]
        )

    loads = [None] + [
        pltpu.make_async_copy(h, v, load.at[1 + i])
        for i, (h, v) in enumerate(
            [(br_h, br_v), (nf_h, stage), (gg_h, gg_v), (gu_h, gu_v), (la_h, stage), (nr_h, stage)]
        )
    ]
    kept = [
        pltpu.make_async_copy(h, v, kept_sem.at[i])
        for i, (h, v) in enumerate(
            [(qd_h, qd), (kv_h, kv), (o_h, o_raw), (allowed_h, allowed), (cs_h, cos_sin),
             (gm_h, gm), (act_h, act)]
        )
    ]
    late = [
        pltpu.make_async_copy(h.at[pl.ds(c * rows, rows)], v.at[pl.ds((2 * c + 1) * rows, rows)], w_sem.at[i, c])
        for i, (h, v) in enumerate([(ra_h, ra_v), (kvg_h, kvg_v)])
        for c in range(2)
    ]
    weights = [pltpu.make_async_copy(wq_h, wq, w_sem.at[2, 0])] + [
        pltpu.make_async_copy(
            h.at[pl.ds(g * HEAD_SIZE, HEAD_SIZE)],
            wkv.at[pl.ds((2 * g + i) * HEAD_SIZE, HEAD_SIZE)],
            w_sem.at[3 + i, g],
        )
        for g in range(KEY_VALUE_HEADS)
        for i, h in enumerate((wk_h, wv_h))
    ]
    loads[2].start()
    loads[3].start()
    loads[4].start()
    gain_rows[...] = jnp.zeros_like(gain_rows)

    barrier = pltpu.get_barrier_semaphore()
    greet(barrier, z)
    not_first = (z > 0).astype(jnp.int32)
    not_last = (z < last).astype(jnp.int32)

    @pl.when(z > 0)
    def _():
        pl.semaphore_signal(barrier, inc=1, device_id=(section, z - 1, ctx), device_id_type=MESH)

    @pl.when(z < last)
    def _():
        pl.semaphore_signal(barrier, inc=1, device_id=(section, z + 1, ctx), device_id_type=MESH)

    def turn(src, dst, base=0):
        for at, size in tiles(src.shape[1], 128):
            block = src[:, at : at + size]
            if size < 128:
                block = wide(block)
            dst[base + at : base + at + size, :] = block.T[:size]

    def z_way(t):
        up = (z < t).astype(jnp.int32)
        to = z + 2 * up - 1
        arrives = up * not_first + (1 - up) * not_last
        meets = (1 - up) * (t == z - 1).astype(jnp.int32)
        return (section, to, ctx), arrives, t * (1 - meets) + RANKS * meets

    def d_block(k):
        in_load(k).wait()
        for b in range(deep // 128):
            in_t[b * 128 : (b + 1) * 128, :] = in_v[:, b * 128 : (b + 1) * 128].T

        if not isinstance(k, int):

            @pl.when(k < last)
            def _():
                in_load(k + 1).start()

    def d_send(k, sub):
        device, _, slot = z_way(turn_of(k))
        span = some(sub * fine, fine)
        return remote(d_out.at[k, span], d_in.at[slot, span], dz_s.at[k, sub], dz_r.at[slot, sub], device)

    def d_step(n):
        k, sub = n // 2, n % 2

        @pl.when(n == 0)
        def _():
            loads[1].wait()

        @pl.when(sub == 0)
        def _():
            d_block(k)

        t = turn_of(k)
        _, arrives, _ = z_way(t)
        span = some(sub * fine, fine)
        mine = dot(in_t[span, :], br_v[...])

        @pl.when(arrives == 0)
        def _():
            d_out[k, span, :] = mine.astype(BF16)

        @pl.when(arrives == 1)
        def _():
            remote(d_out.at[k, span], d_in.at[t, span], dz_s.at[k, sub], dz_r.at[t, sub], partner).wait_recv()
            d_out[k, span, :] = (mine + d_in[t, span, :].astype(F32)).astype(BF16)

        d_send(k, sub).start()

    def f_links(k):
        return (x_next, y_next, x, y) if k == 0 else (y_next, x_next, y, x)

    def f_right(k, column_half):
        src = gg_v if k == 0 else gu_v
        return src[:, some(column_half * quarter, quarter, 128)]

    turns = (3, 0, 2, 1)

    def f1_copy(k, i):
        d = pick(i, turns)
        return remote(f1_out.at[k, i % 2], f1_in.at[k, d], f1_s.at[k, i % 2], f1_r.at[k, d], f_links(k)[0])

    def f2_copy(k, i):
        d = pick(i, turns)
        return remote(f2_out.at[k, i % 2], f2_in.at[k, d], f2_s.at[k, i % 2], f2_r.at[k, d], f_links(k)[1])

    def f1_step(i):
        left = nf_t[some(pick(i, turns) * per, per), :]
        for k in range(2):
            value = dot(left, f_right(k, 1 - f_links(k)[2])).astype(BF16)

            @pl.when(i >= 2)
            def _():
                f1_copy(k, i).wait_send()

            f1_out[k, i % 2] = value
            f1_copy(k, i).start()

    def f2_step(i):
        d = pick(i, turns)
        for k in range(2):
            first, second = f_links(k)[2:]
            f1_copy(k, i).wait_recv()

            def total(which):
                return (
                    dot(nf_t[some(d * per + which * shift, part), :], f_right(k, first))
                    + f1_in[k, d, some(which * shift, part), :].astype(F32)
                ).astype(BF16)

            value = total(1 - second)

            @pl.when(i >= 2)
            def _():
                f2_copy(k, i).wait_send()

            f2_out[k, i % 2] = value
            f2_copy(k, i).start()
            f_keep[k, d] = total(second)

    def t_links(d):
        x_first = (d < RANKS // 2) * 1
        choose = lambda a, b: x_first * a + (1 - x_first) * b
        ways = [tuple(choose(a, b) for a, b in zip(*pair)) for pair in ((x_next[1:], y_next[1:]), (y_next[1:], x_next[1:]))]
        return (section, *ways[0]), (section, *ways[1]), choose(x, y), choose(y, x)

    def t_product(row, count, add, dst):
        full = width // 128 * 128
        mine = dot(ln_t[some(row, count), :], ra_v[...])
        dst[:, :full] = add(mine[:, :full], 0).astype(BF16)
        tail = jnp.concatenate([mine[:, full:], gain_t[some(row, count), width - full :]], axis=1)
        dst[:, full : full + 128] = add(tail, full).astype(BF16)
        pairs = dot(ln_t[some(width + row, count), :], kvg_v[...])
        dst[:, full + 128 :] = add(pairs, full + 128).astype(BF16)

    def t1_copy(d):
        return remote(t1_out.at[d], t1_in.at[d], t1_s.at[d], t1_r.at[d], t_links(d)[0])

    def t2_copy(d):
        return remote(t2_out.at[d], t2_in.at[d], t2_s.at[d], t2_r.at[d], t_links(d)[1])

    def t1_step(d):
        first = t_links(d)[2]
        t_product(d * per + (1 - first) * shift, part, lambda v, at: v, t1_out.at[d])
        t1_copy(d).start()

    def t2_step(d):
        _, _, first, second = t_links(d)
        t1_copy(d).wait_recv()
        for which, dst in ((1 - second, t2_out), (second, t_keep)):
            row = which * (part // 2)
            add = lambda v, at: v + t1_in[d, some(row, part // 2), at : at + v.shape[1]].astype(F32)
            t_product(d * per + first * shift + row, part // 2, add, dst.at[d])
            if dst is t2_out:
                t2_copy(d).start()

    class Line:
        def __init__(self, keep, second_in, z_in, send, recv):
            self.keep, self.second_in, self.z_in, self.send, self.recv = keep, second_in, z_in, send, recv

        def add(self, copy, d):
            copy.wait_recv()
            self.keep[d] = (self.keep[d].astype(F32) + self.second_in[d].astype(F32)).astype(BF16)

        def copy(self, k):
            d = turn_of(k, by_turns)
            device, _, slot = z_way(d)
            return remote(self.keep.at[d], self.z_in.at[slot], self.send.at[k], self.recv.at[slot], device)

        def step(self, k):
            d = turn_of(k, by_turns)
            _, arrives, _ = z_way(d)

            @pl.when(arrives == 1)
            def _():
                remote(self.keep.at[d], self.z_in.at[d], self.send.at[k], self.recv.at[d], partner).wait_recv()
                self.keep[d] = (self.keep[d].astype(F32) + self.z_in[d].astype(F32)).astype(BF16)

            self.copy(k).start()

        def total(self):
            for condition, slot in ((z > 0, z), (z < last, RANKS)):

                @pl.when(condition)
                def _(slot=slot):
                    remote(self.keep.at[0], self.z_in.at[slot], self.send.at[0], self.recv.at[slot], partner).wait_recv()

            value = self.keep[z].astype(F32)
            return z_total(value, self.z_in[z], self.z_in[RANKS])

    def z_total(value, up, down):
        value = value + jnp.where(z > 0, up.astype(F32), 0.0)
        return value + jnp.where(z < last, down.astype(F32), 0.0)

    lines = [
        Line(f_keep.at[k], f2_in.at[k], fz_in.at[k], fz_s.at[k], fz_r.at[k]) for k in range(2)
    ] + [Line(t_keep, t2_in, tz_in, tz_s, tz_r)]

    def f_add(i):
        for k in range(2):
            lines[k].add(f2_copy(k, i), pick(i, turns))

    def t_add(d):
        lines[2].add(t2_copy(d), d)

    def f_line(k):
        lines[0].step(k)
        lines[1].step(k)

    def places(x_first):
        a, b = (1, 0) if x_first is True else (0, 1) if x_first is False else (x_first, 1 - x_first)
        spot = lambda i, j: a * (2 * i + j) + b * (2 * j + i)
        return spot(x, y), spot(1 - x, y), spot(x, 1 - y), spot(1 - x, 1 - y)

    class Gather:
        def __init__(self, number, buffer, x_first):
            self.n, self.buffer = number, buffer
            self.own, self.over_x, self.over_y, self.across = places(x_first)
            size = buffer.shape[2]
            cut = (size // 2 + 15) // 16 * 16
            self.halves = (pl.ds(0, cut), pl.ds(cut, size - cut))

        def whole(self, spot, slot, device):
            ref = self.buffer.at[section, spot]
            return remote(ref, ref, all_s.at[self.n, slot], all_r.at[self.n, slot], device)

        def relay(self, spot, half, device):
            ref = self.buffer.at[section, spot, self.halves[half]]
            return remote(ref, ref, all_s.at[self.n, 2 + half], all_r.at[self.n, 2 + half], device)

        def pair(self, core, spot, slot):
            ref = self.buffer.at[core, spot]
            return remote(ref, ref, all_s.at[self.n, 4 + slot], pair_r.at[self.n, spot], partner)

        def start(self, value):
            self.buffer[section, self.own] = value.astype(BF16)
            self.whole(self.own, 0, x_next).start()
            self.whole(self.own, 1, y_next).start()
            self.pair(section, self.own, 0).start()

        def middle(self):
            self.whole(self.over_x, 0, x_next).wait_recv()
            self.relay(self.over_x, 0, y_next).start()
            self.pair(section, self.over_x, 1).start()
            self.whole(self.over_y, 1, y_next).wait_recv()
            self.relay(self.over_y, 1, x_next).start()
            self.pair(section, self.over_y, 2).start()

        def finish(self):
            self.relay(self.across, 0, y_next).wait_recv()
            self.relay(self.across, 1, x_next).wait_recv()
            self.pair(section, self.across, 3).start()
            for spot in (self.own, self.over_x, self.over_y, self.across):
                self.pair(1 - section, spot, 0).wait_recv()

        def sent(self):
            self.whole(self.own, 0, x_next).wait_send()
            self.whole(self.own, 1, y_next).wait_send()
            self.relay(self.over_x, 0, y_next).wait_send()
            self.relay(self.over_y, 1, x_next).wait_send()
            for slot, spot in enumerate((self.own, self.over_x, self.over_y, self.across)):
                self.pair(section, spot, slot).wait_send()

    below = (z < RANKS // 2).astype(jnp.int32)
    gathers = [
        Gather(0, d_all.at[0], True),
        Gather(1, d_all.at[1], False),
        Gather(2, f_all.at[0], True),
        Gather(3, f_all.at[1], False),
        Gather(4, t_all, below),
    ]

    def d1_copy(h):
        return remote(d1_out.at[h], d1_in.at[h], d1_s.at[h], d1_r.at[h], f_links(h)[0])

    def d2_copy(h):
        return remote(d2_out.at[h], d2_in.at[h], d2_s.at[h], d2_r.at[h], f_links(h)[1])

    def d_first(h):
        span = pl.ds(h * fine, fine)
        for condition, slot in ((z > 0, z), (z < last, RANKS)):

            @pl.when(condition)
            def _(slot=slot):
                remote(d_out.at[0, span], d_in.at[slot, span], dz_s.at[0, h], dz_r.at[slot, h], partner).wait_recv()

        first = f_links(h)[2]
        for mine in (False, True):
            at = h * fine + (first if mine else 1 - first) * (fine // 2)
            piece = some(at, fine // 2)
            total = z_total(dot(in_t[piece, :], br_v[...]), d_in[z, piece, :], d_in[RANKS, piece, :])
            if mine:
                d_keep[h] = total
            else:
                d1_out[h] = total.astype(BF16)
                d1_copy(h).start()

    def d_second(h):
        second = f_links(h)[3]
        d1_copy(h).wait_recv()
        for mine in (False, True):
            piece = some((second if mine else 1 - second) * (fine // 4), fine // 4)
            total = d_keep[h, piece, :] + d1_in[h, piece, :].astype(F32)
            if mine:
                d_keep[h, : fine // 4, :] = total
            else:
                d2_out[h] = total.astype(BF16)
                d2_copy(h).start()

    def d_gather(h):
        d2_copy(h).wait_recv()
        gathers[h].start(d_keep[h, : fine // 4, :] + d2_in[h].astype(F32))

    back = AttentionBack(
        rank, lambda r: (r // 2, z, 2 * y + r % 2), qd, kv, o_raw, allowed, cos_sin, ra,
        ln_t.at[pl.ds(0, 2 * SHARE * rows)], dkv, dkv_in, gkv, dk_s, dk_r,
    )
    grads_out = OutCopy(grads_o, grad_s, grad_r)

    def op_copy(kind, own):
        role = section if own else 1 - section
        src = ra.at[role] if kind == 0 else gkv.at[:, some(role * 256, 384, 128)]
        dst = (ra_v, kvg_v)[kind].at[some(2 * section * rows, rows)]
        if own:
            return pltpu.make_async_copy(src, dst, op_own.at[kind])
        return remote(src, dst, op_s.at[kind], op_r.at[kind], partner)

    def op_start(kind):
        op_copy(kind, True).start()
        op_copy(kind, False).start()

    def attention_end():
        back.collect()
        op_start(1)
        for copy in weights:
            copy.wait()
        kept[6].wait()
        back.project(sum_acc, wq, wkv)
        grad, gain_row = norm_back(act[...].astype(F32), gain_a[...].astype(F32).reshape(1, width), sum_acc[...])
        gain_load.wait()
        gain_rows[0:1, :] += gain_row
        go[...] = (gm[...] + grad).astype(BF16)
        grads_out.start(go, 0)

    def t_ready():
        loads[5].wait()
        turn(stage, ln_t)
        loads[6].start()
        block_of = lambda at, size: wide(gain_rows[:, at : at + size]).T
        for at, size in tiles(width, 128):
            gain_t[at : at + size, :] = pltpu.roll(block_of(at, size), 64, 1)[:size]
        loads[6].wait()
        turn(stage, ln_t, width)
        for copy in late:
            copy.wait()
        for kind in range(2):
            op_copy(kind, True).wait()
            op_copy(kind, False).wait_recv()

    def both(step):
        step(0)
        step(1)

    def head_step(g):
        @pl.when(g == 0)
        def _():
            for copy in kept[:6]:
                copy.wait()
            ra[1] = gm[...].astype(BF16)

        back.head(g)

        @pl.when(g > 0)
        def _():
            back.relay(g - 1)

    def queries_step():
        back.relay(KEY_VALUE_HEADS - 1)
        back.queries()
        op_start(0)

    def d_first_step():
        d_block(last)
        both(d_first)

    def f_total():
        both(lambda k: gathers[2 + k].start(lines[k].total()))

    actions = {
        "near": f1_step,
        "far": f2_step,
        "tnear": t1_step,
        "tfar": t2_step,
        "down": d_step,
        "head": head_step,
        "fadd": f_add,
        "fz": f_line,
        "tadd": t_add,
        "tz": lines[2].step,
        "query": lambda p: queries_step(),
        "aend": lambda p: attention_end(),
        "tready": lambda p: t_ready(),
        "dfirst": lambda p: d_first_step(),
        "dsecond": lambda p: both(d_second),
        "dgather": lambda p: both(d_gather),
        "ftotal": lambda p: f_total(),
        "ttotal": lambda p: gathers[4].start(lines[2].total()),
        "fmiddle": lambda p: both(lambda k: gathers[2 + k].middle()),
        "dmiddle": lambda p: both(lambda h: gathers[h].middle()),
    }
    names = list(actions)

    def codes(table):
        return [8 * names.index(step.rstrip("0123456789")) + int(step[-1]) for step in table]

    tables = [codes(MIDDLE_ORDER), codes(END_ORDER)]
    steps = max(len(t) for t in tables)

    loads[2].wait()
    turn(stage, nf_t)
    loads[3].wait()
    loads[4].wait()
    in_load(0).start()
    loads[1].start()
    for copy in kept + weights + late + [gain_load]:
        copy.start()
    pl.semaphore_wait(barrier, 7 + not_first + not_last)
    loads[5].start()

    def one(n, carry):
        code = (1 - edge) * pick(n, tables[0]) + edge * pick(n, tables[1])
        lax.switch(code // 8, list(actions.values()), code % 8)
        return carry

    lax.fori_loop(0, steps, one, 0)

    writes = []

    def leave(src, dst):
        writes.append(pltpu.make_async_copy(src, dst, write.at[len(writes)]))
        writes[-1].start()

    for k in range(2):
        gathers[2 + k].finish()
        for core in range(2):
            for f in range(2):
                columns = pl.ds((2 * core + f) * quarter, quarter)
                out = (gate_o, up_o)[k]
                leave(f_all.at[k, core, 2 * f], out.at[pl.ds(0, part), columns])
                rest = pl.ds(part - shift, per - part)
                leave(f_all.at[k, core, 2 * f + 1, rest], out.at[pl.ds(part, per - part), columns])
    gathers[4].middle()
    for h in range(2):
        gathers[h].finish()
        for core in range(2):
            for spot in range(4):
                span = pl.ds(h * fine + spot * (fine // 4), fine // 4)
                leave(d_all.at[h, core, spot], down_o.at[span, pl.ds(core * br_v.shape[1], br_v.shape[1])])
    gathers[4].finish()
    t_rows = part // 2
    for core in range(2):
        for spot in range(4):
            row = spot % 2 * t_rows + spot // 2 * shift
            skip = part - shift if spot == 2 else 0
            rest = pl.ds(skip, t_rows - skip)
            leave(t_all.at[core, spot, rest], t_o.at[core, pl.ds(row + skip, t_rows - skip)])

    for k in range(last):
        for sub in range(2):
            d_send(k, sub).wait_send()
        for line in lines:
            line.copy(k).wait_send()
    for h in range(2):
        d1_copy(h).wait_send()
        d2_copy(h).wait_send()
    for k in range(2):
        for i in (2, 3):
            f1_copy(k, i).wait_send()
            f2_copy(k, i).wait_send()
    for d in range(RANKS):
        t1_copy(d).wait_send()
        t2_copy(d).wait_send()
    for kind in range(2):
        op_copy(kind, False).wait_send()
    grads_out.sent(go, 0)

    @pl.when(section == 0)
    def _():
        grads_out.arrived(go)

    for gather in gathers:
        gather.sent()
    for copy in writes:
        copy.wait()


def run_sums(gain_sums, gain_attn, operands, kept, weights, ends_shape):
    nf, inner, gg, gu, br, la, ra, nr, kvg = operands
    act, kv, o_raw, cos_sin, allowed, qd, gm = kept
    depth, width = nf.shape
    rows = act.shape[0]
    ff, half = inner.shape[1], gg.shape[1]
    per, deep = width // RANKS, ff // RANKS
    part = (per // 2 + 15) // 16 * 16
    quarter, fine = half // 2, deep // 2
    columns = br.shape[1]
    wide_t = width // 128 * 128 + 128 + kvg.shape[1]
    vmem, hbm = pl.BlockSpec(memory_space=pltpu.VMEM), pl.BlockSpec(memory_space=pl.ANY)
    out = lambda *shape: jax.ShapeDtypeStruct(shape, BF16)
    b = lambda *shape: pltpu.VMEM(shape, BF16)
    f = lambda *shape: pltpu.VMEM(shape, F32)
    like = lambda a: pltpu.VMEM(a.shape, a.dtype)
    sem = lambda *shape: pltpu.SemaphoreType.DMA(shape)
    return pl.pallas_call(
        sums_kernel,
        out_shape=[
            out(*ends_shape), out(2, per, wide_t), out(per, ff), out(per, ff), out(deep, 2 * columns),
        ],
        in_specs=[hbm, vmem] + [hbm] * 19,
        out_specs=[hbm] * 5,
        scratch_shapes=[
            b(depth, width), b(depth, deep), b(depth, columns), b(depth, half), b(depth, half),
            b(depth, width), b(depth, kvg.shape[1]),
            b(width, depth), b(2 * width, depth), b(deep, depth), f(width, 128),
            like(act), like(kv), like(o_raw), like(cos_sin), like(allowed), like(qd), like(gm),
            like(weights[0]), b(2 * weights[1].shape[0], width),
            b(rows, width), b(2, rows, width), like(kv), b(KEY_VALUE_HEADS, 3 * rows, 128), b(rows, KEY_VALUE_HEADS * 128),
            f(rows, width), f(128, width),
            b(RANKS - 1, deep, columns), b(5, deep, columns), f(2, fine // 2, columns),
            b(2, fine // 2, columns), b(2, fine // 2, columns), b(2, fine // 4, columns), b(2, fine // 4, columns),
            b(2, 2, per, quarter), b(2, RANKS, per, quarter),
            b(2, 2, part, quarter), b(2, RANKS, part, quarter), b(2, RANKS, part, quarter), b(2, 5, part, quarter),
            b(RANKS, part, wide_t), b(RANKS, part, wide_t),
            b(RANKS, part // 2, wide_t), b(RANKS, part // 2, wide_t), b(RANKS, part // 2, wide_t), b(5, part // 2, wide_t),
            b(2, 2, 4, fine // 4, columns), b(2, 2, 4, part, quarter), b(2, 4, part // 2, wide_t),
            sem(8), sem(7), sem(5, KEY_VALUE_HEADS), sem(2, KEY_VALUE_HEADS), sem(3, KEY_VALUE_HEADS), sem(2), sem(2), sem(2), sem(2), sem(2),
            sem(3, 2), sem(5, 2), sem(2), sem(2), sem(2), sem(2),
            sem(2, 2), sem(2, 4), sem(2, 2), sem(2, 4), sem(2, 3), sem(2, 5),
            sem(4), sem(4), sem(4), sem(4), sem(3), sem(5),
            sem(5, 8), sem(5, 4), sem(5, 4), sem(40),
        ],
        compiler_params=pltpu.CompilerParams(
            collective_id=2, has_side_effects=True, vmem_limit_bytes=61 * 2**20
        ),
        name="sums",
    )(gain_sums, gain_attn, *operands, *kept, *weights)


def finish_kernel(
    acts_h, first_h, second_h, t_h, gate_h, up_h, down_h,
    acts_o, grads_o, q_o, out_o, key_o, value_o, gain_a, gain_f, gate_o, up_o, down_o,
    row_v, t_v, gate_v, down_v, q_f, kv_f, gate_f, down_f, load, store,
):
    width = q_f.shape[2]
    loads = [
        pltpu.make_async_copy(h, v, load.at[i])
        for i, (h, v) in enumerate(
            [(gate_h, gate_v.at[0]), (up_h, gate_v.at[1]), (down_h, down_v), (t_h, t_v), (acts_h, row_v.at[0])]
        )
    ]
    stores = [
        pltpu.make_async_copy(v, h, store.at[i])
        for i, (v, h) in enumerate(
            [(row_v.at[0], acts_o), (row_v.at[1], grads_o), (gate_f.at[0], gate_o), (gate_f.at[1], up_o),
             (down_f, down_o), (q_f.at[0], q_o), (q_f.at[1], out_o), (kv_f.at[0], key_o), (kv_f.at[1], value_o)]
        )
    ]
    section = lax.axis_index("section")
    for copy in loads:
        copy.start()
    start_if(
        section == 0,
        lambda: pltpu.make_async_copy(first_h, row_v.at[1], load.at[5]),
        lambda: pltpu.make_async_copy(second_h, row_v.at[1], load.at[5]),
    )
    for k in range(2):
        loads[k].wait()
        gate_f[k] = gate_v[k].astype(F32)
        stores[2 + k].start()
    loads[4].wait()
    stores[0].start()
    pltpu.make_async_copy(first_h, row_v.at[1], load.at[5]).wait()
    stores[1].start()
    loads[2].wait()
    for at, size in tiles(width, 128):
        down_f[at : at + size, :] = down_v[:, at : at + 128].astype(F32).T[:size]
    stores[4].start()
    loads[3].wait()
    for core in range(2):
        q_f[core] = t_v[core, :, :width].astype(F32)
        stores[5 + core].start()
    pairs_at = width // 128 * 128 + 128
    half = KEY_VALUE_HEADS // 2 + 1
    for g in range(KEY_VALUE_HEADS):
        core = 0 if g < half else 1
        at = pairs_at + (g - core * (KEY_VALUE_HEADS - half)) * 128
        block = t_v[core, :, at : at + 128].astype(F32).T
        kv_f[0, g * HEAD_SIZE : (g + 1) * HEAD_SIZE, :] = block[:HEAD_SIZE]
        kv_f[1, g * HEAD_SIZE : (g + 1) * HEAD_SIZE, :] = block[HEAD_SIZE:]
    for copy in stores[7:]:
        copy.start()
    tail = slice(pairs_at - 128, pairs_at)
    both = t_v[0, :, tail].astype(F32) + t_v[1, :, tail].astype(F32)
    row = width % 128
    gain_rows = both.T
    gain_a[...] = gain_rows[row]
    gain_f[...] = gain_rows[row + 1]
    for copy in stores:
        copy.wait()


def run_finish(acts, grads_first, grads_second, t_sum, gate, up, down, width):
    per, ff = gate.shape
    vmem, hbm = pl.BlockSpec(memory_space=pltpu.VMEM), pl.BlockSpec(memory_space=pl.ANY)
    out = lambda *shape: jax.ShapeDtypeStruct(shape, F32)
    kv_rows = KEY_VALUE_HEADS * HEAD_SIZE
    return pl.pallas_call(
        finish_kernel,
        out_shape=[
            jax.ShapeDtypeStruct(acts.shape, BF16), jax.ShapeDtypeStruct(acts.shape, BF16),
            out(per, width), out(per, width), out(kv_rows, per), out(kv_rows, per), out(per), out(per),
            out(per, ff), out(per, ff), out(width, down.shape[0]),
        ],
        in_specs=[hbm] * 7,
        out_specs=[hbm] * 6 + [vmem] * 2 + [hbm] * 3,
        scratch_shapes=[
            pltpu.VMEM((2, *acts.shape), BF16), pltpu.VMEM(t_sum.shape, BF16), pltpu.VMEM((2, per, ff), BF16), pltpu.VMEM(down.shape, BF16),
            pltpu.VMEM((2, per, width), F32), pltpu.VMEM((2, kv_rows, per), F32),
            pltpu.VMEM((2, per, ff), F32), pltpu.VMEM((width, down.shape[0]), F32),
            pltpu.SemaphoreType.DMA((6,)), pltpu.SemaphoreType.DMA((9,)),
        ],
        compiler_params=pltpu.CompilerParams(vmem_limit_bytes=61 * 2**20),
        name="finish",
    )(acts, grads_first, grads_second, t_sum, gate, up, down)


def sums_by_xla(gain_sums, operands):
    nf, inner, gg, gu, br, la, ra, nr, kvg = operands
    width = nf.shape[1]

    def reduced(left, right):
        total = dot_lt(left, right).astype(BF16)
        piece = lax.psum_scatter(total, "dp", scatter_dimension=0, tiled=True)
        return lax.psum(piece, "ctx")

    def both(piece, axis):
        return lax.all_gather(piece, "section", axis=axis, tiled=axis > 0).astype(F32)

    attn = both(reduced(la, ra), 0)
    gain_sum = lax.psum(gain_sums[:2], ("section", "ctx"))
    return (
        attn[0],
        attn[1],
        both(reduced(nr, kvg), 0),
        lax.psum_scatter(gain_sum, "dp", scatter_dimension=1, tiled=True),
        both(reduced(nf, gg), 1),
        both(reduced(nf, gu), 1),
        both(reduced(inner, br), 1)[:, :width],
    )


def shards(
    ends,
    doc_lengths,
    w_query,
    key_projection_weight,
    value_projection_weight,
    w_out,
    w_gate,
    w_up,
    w_down,
    gain_attn,
    gain_ffn,
):
    width = ends.shape[3]
    half = HEAD_SIZE // 2
    turns = np.float32(10000.0) ** (
        np.float32(-2.0) * (np.arange(128) % half).astype(np.float32) / np.float32(HEAD_SIZE)
    )
    weights = (
        w_query,
        key_projection_weight.T,
        value_projection_weight.T,
        w_out,
        w_gate,
        w_up,
        w_down.T,
    )
    ff = w_gate.shape[1]
    fits = lax.axis_size("dp") == RANKS and width % 64 == 0 and ff % 1280 == 0
    acts, grads_in, gain_sums, *kept = run_layers(
        doc_lengths,
        ends,
        jnp.asarray(turns.reshape(1, 128), F32),
        gain_attn,
        gain_ffn,
        weights,
        not fits,
    )
    operands = kept[:9]
    if fits:
        grads_first, *sums = run_sums(
            gain_sums, gain_attn, operands, kept[9:], weights[:3], ends.shape
        )
        acts, grads_in, grad_query, grad_out, grad_key, grad_value, *gain_piece, grad_gate, grad_up, grad_down = (
            run_finish(acts, grads_first, grads_in, *sums, width)
        )
        grad_key, grad_value, grad_down = grad_key.T, grad_value.T, grad_down.T
    else:
        grad_query, grad_out, kv_parts, gain_piece, grad_gate, grad_up, grad_down = sums_by_xla(
            gain_sums, operands
        )
        kv_grad = jnp.concatenate([kv_parts[0], kv_parts[1][:, 128:]], axis=1).reshape(
            -1, KEY_VALUE_HEADS, 2, HEAD_SIZE
        )
        grad_key = kv_grad[:, :, 0].reshape(kv_grad.shape[0], -1)
        grad_value = kv_grad[:, :, 1].reshape(kv_grad.shape[0], -1)
    return (
        acts,
        grads_in,
        grad_query,
        grad_key,
        grad_value,
        grad_out,
        grad_gate,
        grad_up,
        grad_down,
        gain_piece[0],
        gain_piece[1],
    )


def solution(mesh):
    return jax.shard_map(
        shards,
        mesh=mesh,
        in_specs=(P("section", None, ("dp", "ctx"), None), P(None, "dp", None)) + (P(),) * 9,
        out_specs=(P("section", None, ("dp", "ctx"), None),) * 2
        + (P("dp", None),) * 7
        + (P("dp"),) * 2,
        check_vma=False,
    )
```

```python
import jax
import jax.numpy as jnp
import numpy as np
from jax import lax
from jax.experimental import pallas as pl
from jax.experimental.pallas import tpu as pltpu
from jax.sharding import PartitionSpec as P

MESH = pl.DeviceIdType.MESH
QUERY_HEADS = 15
KEY_VALUE_HEADS = 5
HEAD_SIZE = 64
SHARE = QUERY_HEADS // KEY_VALUE_HEADS
RANKS = 4
epsilon = 1e-05
masked_fill = -1e30
F32 = jnp.float32
BF16 = jnp.bfloat16


def dot(left, right):
    return jnp.dot(left, right, preferred_element_type=F32)


def dot_rt(left, right):
    return lax.dot_general(left, right, (((1,), (1,)), ((), ())), preferred_element_type=F32)


def dot_lt(left, right):
    return lax.dot_general(left, right, (((0,), (0,)), ((), ())), preferred_element_type=F32)


def tiles(total, width):
    return [(at, min(width, total - at)) for at in range(0, total, width)]


def wide(block):
    missing = 128 - block.shape[1]
    if not missing:
        return block
    return jnp.concatenate([block, jnp.zeros((block.shape[0], missing), block.dtype)], axis=1)


def lanes(rows):
    return lax.broadcasted_iota(jnp.int32, (rows, 128), 1)


def half_turn(block):
    front = lanes(block.shape[0]) % HEAD_SIZE < HEAD_SIZE // 2
    return jnp.where(front, pltpu.roll(block, 96, 1), pltpu.roll(block, 32, 1))


def inverse_rms(hidden):
    return lax.rsqrt(jnp.mean(hidden * hidden, axis=-1, keepdims=True) + epsilon)


def half_turned(block, cosines, sines, direction):
    return block * cosines + direction * (half_turn(block) * sines)


def norm_back(hidden, gain, upstream):
    scale = inverse_rms(hidden)
    weighted = upstream * gain
    inside = jnp.mean(weighted * hidden, axis=-1, keepdims=True)
    gain_row = jnp.sum(upstream * hidden * scale, axis=0, keepdims=True)
    return scale * weighted - hidden * (scale * scale * scale * inside), gain_row


def start_if(condition, here, there):
    @pl.when(condition)
    def _():
        here().start()

    @pl.when(jnp.logical_not(condition))
    def _():
        there().start()


class AttentionBack:
    def __init__(
        self, rank, device_of, qd, kv, o_raw, allowed, cos_sin, ra, pds, dkv, dkv_in, gkv, send, recv
    ):
        self.rank, self.device_of = rank, device_of
        self.qd, self.kv, self.o_raw, self.allowed, self.cos_sin = qd, kv, o_raw, allowed, cos_sin
        self.ra, self.pds, self.dkv, self.dkv_in, self.gkv = ra, pds, dkv, dkv_in, gkv
        self.send_sem, self.recv_sem = send, recv
        self.rows, self.width = ra.shape[1:]

    def head(self, g):
        rows = self.rows
        kv_g = self.kv[g]
        mine = [slice(i * rows, (i + 1) * rows) for i in range(SHARE)]
        other = [slice((SHARE + i) * rows, (SHARE + i + 1) * rows) for i in range(SHARE)]
        all_scores = [dot_rt(self.qd[g, span, :], kv_g) + self.allowed[...] for span in mine]
        for i, scores in enumerate(all_scores):
            kept = self.o_raw[g * SHARE + i]
            probs = jnp.exp(scores - kept[:, 0:1])
            grad_out = self.qd[g, other[i], :]
            grad_probs = dot_rt(grad_out, kv_g)
            weight = jnp.sum(grad_out.astype(F32) * kept, axis=-1, keepdims=True)
            grad_scores = (probs * (grad_probs - weight)).astype(BF16)
            self.pds[mine[i], :] = grad_scores
            self.pds[other[i], :] = probs.astype(BF16)
            self.o_raw[g * SHARE + i] = dot(grad_scores, kv_g)
        grad_kv = dot_lt(self.qd[g], self.pds[...])
        self.dkv[g] = grad_kv.T.astype(BF16)
        self.send(g)

    def heads(self, first, last):
        def body(g, carry):
            self.head(g)

            @pl.when(g > 0)
            def _():
                self.relay(g - 1)

            return carry

        lax.fori_loop(first, last, body, 0)

    def copy(self, quarter, count, dst, slot_in, slot, g):
        rows = self.rows
        return pltpu.make_async_remote_copy(
            src_ref=self.dkv.at[g, pl.ds(quarter * rows, count * rows)],
            dst_ref=self.dkv_in.at[g, pl.ds(slot_in * rows, count * rows)],
            send_sem=self.send_sem.at[slot, g],
            recv_sem=self.recv_sem.at[slot_in, g],
            device_id=self.device_of(dst),
            device_id_type=MESH,
        )

    def add(self, quarter, slots, g):
        rows = self.rows
        span = slice(quarter * rows, (quarter + 1) * rows)
        total = self.dkv[g, span].astype(F32)
        for slot in slots:
            total = total + self.dkv_in[g, slot * rows : (slot + 1) * rows].astype(F32)
        self.dkv[g, span] = total.astype(BF16)

    def send(self, g):
        @pl.when(self.rank == 3)
        def _():
            self.copy(2, 1, 2, 0, 0, g).start()
            self.copy(0, 2, 1, 0, 1, g).start()

        @pl.when(self.rank == 2)
        def _():
            self.copy(1, 1, 1, 2, 0, g).start()
            self.copy(0, 1, 0, 1, 1, g).start()

    def relay(self, g):
        @pl.when(self.rank == 1)
        def _():
            self.copy(0, 2, 1, 0, 0, g).wait_recv()
            self.add(0, (0,), g)
            self.copy(0, 1, 0, 0, 0, g).start()

    def queries(self):
        for at, size in tiles(self.width, 128):
            head = at // HEAD_SIZE
            block = self.o_raw[head]
            if size == 128:
                low = lanes(self.rows) < HEAD_SIZE
                block = jnp.where(low, block, pltpu.roll(self.o_raw[head + 1], 64, 1))
            turned = half_turned(block, self.cos_sin[0], self.cos_sin[1], -1.0) * 0.125
            self.ra[0, :, at : at + size] = turned[:, :size].astype(BF16)

    def collect(self):
        low = lanes(self.rows) < HEAD_SIZE
        cosines = jnp.where(low, self.cos_sin[0], 1.0)
        sines = jnp.where(low, self.cos_sin[1], 0.0)
        mine = pl.ds(pl.multiple_of(self.rank * self.rows, 16), self.rows)
        for g in range(KEY_VALUE_HEADS):
            self.arrive(g)
            block = half_turned(self.dkv[g, mine, :].astype(F32), cosines, sines, -1.0)
            self.gkv[:, 128 * g : 128 * g + 128] = block.astype(BF16)

    def arrive(self, g):
        @pl.when(self.rank == 3)
        def _():
            self.copy(2, 1, 2, 0, 0, g).wait_send()
            self.copy(0, 2, 1, 0, 1, g).wait_send()

        @pl.when(self.rank == 2)
        def _():
            self.copy(0, 1, 2, 0, 0, g).wait_recv()
            self.copy(1, 1, 1, 2, 0, g).wait_send()
            self.copy(0, 1, 0, 1, 1, g).wait_send()
            self.add(2, (0,), g)

        @pl.when(self.rank == 1)
        def _():
            self.copy(0, 1, 2, 2, 0, g).wait_recv()
            self.copy(0, 1, 0, 0, 0, g).wait_send()
            self.add(1, (1, 2), g)

        @pl.when(self.rank == 0)
        def _():
            self.copy(0, 1, 2, 0, 0, g).wait_recv()
            self.copy(0, 1, 2, 1, 0, g).wait_recv()
            self.add(0, (0, 1), g)

    def project(self, total, wq, wkv):
        for at, size in tiles(self.width, 256):
            total[:, at : at + size] = dot_rt(self.ra[0], wq[at : at + size, :]) + dot(
                self.gkv[...], wkv[:, at : at + size]
            )


class OutCopy:
    def __init__(self, out, send, recv):
        self.section, self.dp, ctx = (lax.axis_index(a) for a in ("section", "dp", "ctx"))
        self.home = 2 * self.section + ctx % 2
        self.ctx, self.micro = ctx, ctx // 2
        self.out, self.send, self.recv = out, send, recv

    def here(self, l):
        return (self.section == l) & (self.ctx == self.home)

    def remote(self, array, l):
        return pltpu.make_async_remote_copy(
            src_ref=array,
            dst_ref=self.out.at[0, self.micro],
            send_sem=self.send.at[l],
            recv_sem=self.recv.at[self.micro],
            device_id=(l, self.dp, self.home),
            device_id_type=MESH,
        )

    def local(self, array):
        return pltpu.make_async_copy(array, self.out.at[0, self.micro], self.recv.at[self.micro])

    def start(self, array, l):
        start_if(self.here(l), lambda: self.local(array), lambda: self.remote(array, l))

    def sent(self, array, l):
        @pl.when(jnp.logical_not(self.here(l)))
        def _():
            self.remote(array, l).wait_send()

    def arrived(self, array):
        for block in range(2):
            pltpu.make_async_copy(array, self.out.at[0, block], self.recv.at[block]).wait()


def greet(barrier, dp):
    section, ctx = lax.axis_index("section"), lax.axis_index("ctx")
    for step in range(1, 8):
        other = (4 * section + ctx + step) % 8
        pl.semaphore_signal(
            barrier, inc=1, device_id=(other // 4, dp, other % 4), device_id_type=MESH
        )


def layers_kernel(complete, *refs):
    refs = list(refs)

    def take(count):
        taken = refs[:count]
        del refs[:count]
        return taken

    lengths, ends, frequency, gain_a, gain_f, wq_h, wk_h, wv_h, wo_h, wg_h, wu_h, wd_h = take(12)
    acts_o, grads_o, gain_o, nf_o, in_o, gg_o, gu_o, br_o, la_o, ra_o, nr_o, kvg_o = take(12)
    kept_o = [] if complete else take(7)
    wq, wkv, wo, wg, wu, wd = take(6)
    act, go, middle, norm_ffn, fact_a, fact_b, inner, lm, qd, kv, o_raw = take(11)
    sum_acc, gm, gg, gu, br, ra, pds, dkv, dkv_in, gkv, cos_sin, allowed_add, gain_v = take(13)
    w_sem, kv_sem, in_send, in_recv, kv_send, kv_recv, dk_send, dk_recv = take(8)
    act_send, act_recv, grad_send, grad_recv, op_own, op_send, op_recv, kept_sem = take(8)

    section = lax.axis_index("section")
    dp = lax.axis_index("dp")
    ctx = lax.axis_index("ctx")
    micro = ctx // 2
    xbit = ctx % 2
    rank = 2 * section + xbit
    rows, width = act.shape[1], act.shape[2]
    ff = wg.shape[1]
    ff_half = ff // 2

    def device_of(r):
        return (r // 2, dp, 2 * micro + r % 2)

    partner = (1 - section, dp, ctx)

    loads = [
        pltpu.make_async_copy(h, v, w_sem.at[i])
        for i, (h, v) in enumerate([(wq_h, wq), (wo_h, wo), (wg_h, wg), (wu_h, wu), (wd_h, wd)])
    ]
    kv_loads = [
        pltpu.make_async_copy(
            h.at[pl.ds(g * HEAD_SIZE, HEAD_SIZE)],
            wkv.at[pl.ds((2 * g + i) * HEAD_SIZE, HEAD_SIZE)],
            kv_sem.at[i, g],
        )
        for g in range(KEY_VALUE_HEADS)
        for i, h in enumerate((wk_h, wv_h))
    ]
    for load in kv_loads + loads:
        load.start()
    kv[...] = jnp.zeros_like(kv)
    barrier = pltpu.get_barrier_semaphore()
    greet(barrier, dp)
    pl.semaphore_wait(barrier, 7)

    def in_local(block, into_x):
        dst, slot = (act.at[0], 0) if into_x else (go.at[2], 1)
        return pltpu.make_async_copy(ends.at[0, block], dst, in_recv.at[slot])

    def in_remote(block, into_x):
        dst, slot = (act.at[0], 0) if into_x else (go.at[2], 1)
        return pltpu.make_async_remote_copy(
            src_ref=ends.at[0, block],
            dst_ref=dst,
            send_sem=in_send.at[block],
            recv_sem=in_recv.at[slot],
            device_id=(ctx // 2, dp, 2 * block + xbit),
            device_id_type=MESH,
        )

    def in_mine(block):
        return (section == ctx // 2) & (ctx // 2 == block)

    def in_start(into_x):
        @pl.when(section == (0 if into_x else 1))
        def _():
            for block in range(2):
                start_if(
                    in_mine(block),
                    lambda block=block: in_local(block, into_x),
                    lambda block=block: in_remote(block, into_x),
                )

    in_start(True)
    lane = lanes(rows)
    low = lane < HEAD_SIZE
    gain_attn = gain_a[...].astype(F32).reshape(1, width)
    gain_ffn = gain_f[...].astype(F32).reshape(1, width)

    def place(token_index):
        segment = jnp.zeros_like(token_index)
        start = jnp.zeros_like(token_index)
        finish = jnp.int32(0)
        for slot in range(lengths.shape[2]):
            length = lengths[micro, 0, slot]
            finish = finish + length
            passed = (token_index >= finish).astype(jnp.int32)
            segment = segment + passed
            start = start + passed * length
        return segment, token_index - start

    seg_mine, position = place(rank * rows + lax.broadcasted_iota(jnp.int32, (rows, 128), 0))
    angles = position.astype(F32) * frequency[...]
    cos_sin[0] = jnp.cos(angles)
    cos_sin[1] = jnp.where(lane % HEAD_SIZE < HEAD_SIZE // 2, -1.0, 1.0) * jnp.sin(angles)
    key_index = lax.broadcasted_iota(jnp.int32, (1, RANKS * rows), 1)
    query_index = rank * rows + lax.broadcasted_iota(jnp.int32, (rows, 1), 0)
    allowed_add[...] = jnp.where(
        (seg_mine[:, 0:1] == place(key_index)[0]) & (query_index >= key_index), 0.0, masked_fill
    )

    def kv_rows(l, r, g):
        return kv.at[l, g, pl.ds(pl.multiple_of(r * rows, 16), rows)]

    def kv_copy(l, quarter, dst, slot, g):
        return pltpu.make_async_remote_copy(
            src_ref=kv_rows(l, quarter, g),
            dst_ref=kv_rows(l, quarter, g),
            send_sem=kv_send.at[l, slot, g],
            recv_sem=kv_recv.at[l, quarter, g],
            device_id=device_of(dst),
            device_id_type=MESH,
        )

    def kv_start(l, g):
        @pl.when(rank < 3)
        def _():
            kv_copy(l, rank, rank + 1, 0, g).start()

        @pl.when(rank < 2)
        def _():
            kv_copy(l, rank, rank + 2, 1, g).start()

    def kv_relayed(l, g):
        @pl.when(rank == 1)
        def _():
            kv_copy(l, 0, 3, 2, g).wait_recv()
            kv_copy(l, 0, 3, 2, g).start()

    def kv_finish(l, g):
        @pl.when(rank >= 2)
        def _():
            kv_copy(l, 0, 0, 0, g).wait_recv()
            kv_copy(l, 1, 0, 0, g).wait_recv()

        @pl.when(rank == 3)
        def _():
            kv_copy(l, 2, 0, 0, g).wait_recv()

    def kv_sent(l):
        for senders, slot in ((3, 0), (2, 1)):

            @pl.when(rank < senders)
            def _(slot=slot):
                for g in range(KEY_VALUE_HEADS):
                    kv_copy(l, rank, rank + 1 + slot, slot, g).wait_send()

        @pl.when(rank == 1)
        def _():
            for g in range(KEY_VALUE_HEADS):
                kv_copy(l, 0, 3, 2, g).wait_send()

    acts_out = OutCopy(acts_o, act_send, act_recv)
    grads_out = OutCopy(grads_o, grad_send, grad_recv)

    def op_copy(kind, l, own):
        role = section if own else 1 - section
        half = pl.ds(pl.multiple_of(role * ff_half, 128), ff_half)
        src = [
            lambda: norm_ffn.at[l],
            lambda: inner.at[l],
            lambda: gg.at[:, half],
            lambda: gu.at[:, half],
            lambda: br.at[:, pl.ds(pl.multiple_of(role * 512, 128), 512)],
            lambda: lm.at[l, role],
            lambda: ra.at[role],
            lambda: lm.at[l, 0],
            lambda: gkv.at[:, pl.ds(pl.multiple_of(role * 256, 128), 384)],
        ][kind]()
        block = section if kind in (6, 8) and not complete else 2 * section + l
        dst = [nf_o, in_o, gg_o, gu_o, br_o, la_o, ra_o, nr_o, kvg_o][kind].at[
            pl.ds(pl.multiple_of(block * rows, 16), rows)
        ]
        if own:
            return pltpu.make_async_copy(src, dst, op_own.at[kind, l])
        return pltpu.make_async_remote_copy(
            src_ref=src,
            dst_ref=dst,
            send_sem=op_send.at[kind, l],
            recv_sem=op_recv.at[kind, l],
            device_id=partner,
            device_id_type=MESH,
        )

    def op_start(kinds, l):
        for kind in kinds:
            op_copy(kind, l, True).start()
            op_copy(kind, l, False).start()

    def op_sent(kinds, l):
        for kind in kinds:
            op_copy(kind, l, True).wait()
            op_copy(kind, l, False).wait_send()

    def kept_copy(i):
        src = [act.at[0], kv.at[0], o_raw.at[0], cos_sin, allowed_add, qd.at[0], gm][i]
        return pltpu.make_async_copy(src, kept_o[i], kept_sem.at[i])

    def kept_start(*which):
        if not complete:
            for i in which:
                kept_copy(i).start()

    in_remote(0, True).wait_recv()
    for load in kv_loads:
        load.wait()

    def forward(l, carry):
        hidden = act[l].astype(F32)
        cos_q, sin_q = cos_sin[0], cos_sin[1]
        lm[l, 0] = (hidden * inverse_rms(hidden) * gain_attn).astype(BF16)
        cos_kv = jnp.where(low, cos_q, 1.0)
        sin_kv = jnp.where(low, sin_q, 0.0)
        mine = pl.ds(pl.multiple_of(rank * rows, 16), rows)
        for g in range(KEY_VALUE_HEADS):
            block = dot_rt(lm[l, 0], wkv[128 * g : 128 * g + 128, :])
            turned = half_turned(block, cos_kv, sin_kv, 1.0)
            kv[l, g, mine, :] = turned.astype(BF16)
        for g in range(KEY_VALUE_HEADS):
            kv_start(l, g)

        @pl.when(l == 0)
        def _():
            loads[0].wait()
            in_start(False)
            kept_start(0, 3, 4)

        for at, size in tiles(width, 256):
            product = dot(lm[l, 0], wq[:, at : at + size])
            for inside, part in tiles(size, 128):
                block = wide(product[:, inside : inside + part])
                turned = half_turned(block, cos_q, sin_q, 1.0) * 0.125
                head = (at + inside) // HEAD_SIZE
                qd[l, head // SHARE, pl.ds(head % SHARE * rows, rows), :] = jnp.where(
                    low, turned, 0.0
                ).astype(BF16)
                head += 1
                if head < QUERY_HEADS:
                    qd[l, head // SHARE, pl.ds(head % SHARE * rows, rows), :] = jnp.where(
                        low, pltpu.roll(turned, 64, 1), 0.0
                    ).astype(BF16)
        kv_relayed(l, 0)
        kv_finish(l, 0)

        def heads(g, carry):
            @pl.when(g < KEY_VALUE_HEADS - 1)
            def _():
                kv_relayed(l, g + 1)

            @pl.when(g > 0)
            def _():
                kv_finish(l, g)

            kv_g = kv[l, g]
            all_scores = [
                dot_rt(qd[l, g, i * rows : (i + 1) * rows, :], kv_g) + allowed_add[...]
                for i in range(SHARE)
            ]
            for i, scores in enumerate(all_scores):
                peak = jnp.max(scores, axis=-1, keepdims=True)
                exponent = jnp.exp(scores - peak)
                total = jnp.sum(exponent, axis=-1, keepdims=True)
                out = dot(exponent.astype(BF16), kv_g) * (1.0 / total)
                o_raw[l, g * SHARE + i] = jnp.where(low, peak + jnp.log(total), out)
            return carry

        lax.fori_loop(0, KEY_VALUE_HEADS, heads, 0)

        @pl.when(l == 0)
        def _():
            kept_start(1, 2)
            loads[1].wait()

        for at, size in tiles(width, 128):
            head = at // HEAD_SIZE
            block = pltpu.roll(o_raw[l, head], 64, 1)
            if size == 128:
                block = jnp.where(low, block, o_raw[l, head + 1])
            lm[l, 1, :, at : at + size] = block[:, :size].astype(BF16)
        for at, size in tiles(width, 256):
            middle[l, :, at : at + size] = act[l, :, at : at + size].astype(F32) + dot(
                lm[l, 1], wo[:, at : at + size]
            )
        mid = middle[l]
        norm_ffn[l] = (mid * inverse_rms(mid) * gain_ffn).astype(BF16)
        op_start((0, 5, 7), l)

        @pl.when(l == 0)
        def _():
            loads[2].wait()
            loads[3].wait()

        def gates(j, carry):
            part = pl.ds(pl.multiple_of(j * 512, 512), 512)
            gate = dot(norm_ffn[l], wg[:, part])
            upper = dot(norm_ffn[l], wu[:, part])
            s = 0.5 * jnp.tanh(0.5 * gate) + 0.5
            swish = gate * s
            inner[l, :, part] = (swish * upper).astype(BF16)
            fact_a[l, :, part] = (upper * s * (1.0 + gate * (1.0 - s))).astype(BF16)
            fact_b[l, :, part] = swish.astype(BF16)
            return carry

        lax.fori_loop(0, ff // 512, gates, 0)

        @pl.when(l == 0)
        def _():
            loads[4].wait()

        op_start((1,), l)
        for at, size in tiles(width, 256):
            act[l + 1, :, at : at + size] = (
                middle[l, :, at : at + size] + dot_rt(inner[l], wd[at : at + size, :])
            ).astype(BF16)
        acts_out.start(act.at[l + 1], l)
        kv_sent(l)
        return carry

    lax.fori_loop(0, 2, forward, 0)

    in_remote(0, False).wait_recv()
    gain_v[...] = jnp.zeros_like(gain_v)
    br[...] = jnp.zeros_like(br)
    late = (6, 8)

    def backward(step, carry):
        l = 1 - step

        @pl.when(l == 0)
        def _():
            op_sent((2, 3, 4) + (late if complete else ()), 1)

        br[:, :width] = go[l + 1]
        op_start((4,), l)

        def gates(j, carry):
            part = pl.ds(pl.multiple_of(j * 512, 512), 512)
            grad_inner = dot(go[l + 1], wd[:, part])
            gg[:, part] = (grad_inner * fact_a[l, :, part].astype(F32)).astype(BF16)
            gu[:, part] = (grad_inner * fact_b[l, :, part].astype(F32)).astype(BF16)
            return carry

        lax.fori_loop(0, ff // 512, gates, 0)
        op_start((2, 3), l)
        for at, size in tiles(width, 256):
            sum_acc[:, at : at + size] = dot_rt(gg[...], wg[at : at + size, :]) + dot_rt(
                gu[...], wu[at : at + size, :]
            )
        grad, gain_row = norm_back(middle[l], gain_ffn, sum_acc[...])
        gain_v[1:2, :] += gain_row
        gm[...] = go[l + 1].astype(F32) + grad
        ra[1] = gm[...].astype(BF16)

        for at, size in tiles(width, 256):
            product = dot_rt(ra[1], wo[at : at + size, :])
            for inside, part in tiles(size, 128):
                block = wide(product[:, inside : inside + part])
                head = (at + inside) // HEAD_SIZE
                qd[l, head // SHARE, pl.ds((SHARE + head % SHARE) * rows, rows), :] = jnp.where(
                    low, 0.0, pltpu.roll(block, 64, 1)
                ).astype(BF16)
                head += 1
                if head < QUERY_HEADS:
                    qd[l, head // SHARE, pl.ds((SHARE + head % SHARE) * rows, rows), :] = (
                        jnp.where(low, 0.0, block).astype(BF16)
                    )

        def attention():
            back = AttentionBack(
                rank, device_of, qd.at[l], kv.at[l], o_raw.at[l], allowed_add, cos_sin, ra, pds,
                dkv, dkv_in.at[l] if complete else dkv_in, gkv,
                dk_send.at[l] if complete else dk_send, dk_recv.at[l] if complete else dk_recv,
            )
            back.heads(0, KEY_VALUE_HEADS)
            back.relay(KEY_VALUE_HEADS - 1)
            back.queries()
            op_start((6,), l)
            back.collect()
            op_start((8,), l)
            back.project(sum_acc, wq, wkv)
            grad, gain_row = norm_back(act[l].astype(F32), gain_attn, sum_acc[...])
            gain_v[0:1, :] += gain_row
            go[l] = (gm[...] + grad).astype(BF16)
            grads_out.start(go.at[l], l)

        if complete:
            attention()
        else:

            @pl.when(l == 1)
            def _():
                attention()

            @pl.when(l == 1)
            def _():
                op_sent(late, 1)

        return carry

    lax.fori_loop(0, 2, backward, 0)

    gain_copy = pltpu.make_async_copy(gain_v, gain_o, kept_sem.at[7])
    gain_copy.start()
    kept_start(5, 6)
    for into_x in (True, False):

        @pl.when(section == (0 if into_x else 1))
        def _(into_x=into_x):
            for block in range(2):

                @pl.when(jnp.logical_not(in_mine(block)))
                def _(block=block):
                    in_remote(block, into_x).wait_send()

    op_sent((2, 3, 4) + (late if complete else ()), 0)
    for l in range(2):
        op_sent((0, 1, 5, 7), l)
        for kind in range(9):
            if l == 1 or complete or kind not in late:
                op_copy(kind, l, False).wait_recv()
        acts_out.sent(act.at[l + 1], l)
        if l == 1 or complete:
            grads_out.sent(go.at[l], l)
    gain_copy.wait()
    acts_out.arrived(act.at[0])
    if complete:
        grads_out.arrived(act.at[0])
    else:

        @pl.when(section == 1)
        def _():
            grads_out.arrived(act.at[0])

        for i in range(len(kept_o)):
            kept_copy(i).wait()


def run_layers(lengths, ends, frequency, gain_attn, gain_ffn, weights, complete):
    micro_count, rows, width = ends.shape[1:]
    wq, wk, wv, wo, wg, wu, wd = weights
    ff = wg.shape[1]
    keys = RANKS * rows
    kv_width = 2 * wk.shape[0]
    vmem, hbm = pl.BlockSpec(memory_space=pltpu.VMEM), pl.BlockSpec(memory_space=pl.ANY)
    op_rows = 4 * rows
    late_rows = op_rows if complete else 2 * rows
    out = lambda *shape: jax.ShapeDtypeStruct(shape, BF16)
    out_f = lambda *shape: jax.ShapeDtypeStruct(shape, F32)
    dma = lambda *shape: pltpu.SemaphoreType.DMA(shape)
    kept = [
        out(rows, width),
        out(KEY_VALUE_HEADS, keys, 128),
        out_f(QUERY_HEADS, rows, 128),
        out_f(2, rows, 128),
        out_f(rows, keys),
        out(KEY_VALUE_HEADS, 2 * SHARE * rows, 128),
        out_f(rows, width),
    ]
    layers = (2,) if complete else ()
    return pl.pallas_call(
        lambda *refs: layers_kernel(complete, *refs),
        out_shape=[
            out(*ends.shape),
            out(*ends.shape),
            out_f(8, width),
            out(op_rows, width),
            out(op_rows, ff),
            out(op_rows, ff // 2),
            out(op_rows, ff // 2),
            out(op_rows, 512),
            out(op_rows, width),
            out(late_rows, width),
            out(op_rows, width),
            out(late_rows, 384),
        ]
        + ([] if complete else kept),
        in_specs=[pl.BlockSpec(memory_space=pltpu.SMEM), hbm] + [vmem] * 3 + [hbm] * 7,
        out_specs=[hbm] * (12 if complete else 19),
        scratch_shapes=[
            pltpu.VMEM(wq.shape, BF16),
            pltpu.VMEM((kv_width, width), BF16),
            pltpu.VMEM(wo.shape, BF16),
            pltpu.VMEM(wg.shape, BF16),
            pltpu.VMEM(wu.shape, BF16),
            pltpu.VMEM(wd.shape, BF16),
            pltpu.VMEM((3, rows, width), BF16),
            pltpu.VMEM((3, rows, width), BF16),
            pltpu.VMEM((2, rows, width), F32),
            pltpu.VMEM((2, rows, width), BF16),
            pltpu.VMEM((2, rows, ff), BF16),
            pltpu.VMEM((2, rows, ff), BF16),
            pltpu.VMEM((2, rows, ff), BF16),
            pltpu.VMEM((2, 2, rows, width), BF16),
            pltpu.VMEM((2, KEY_VALUE_HEADS, 2 * SHARE * rows, 128), BF16),
            pltpu.VMEM((2, KEY_VALUE_HEADS, keys, 128), BF16),
            pltpu.VMEM((2, QUERY_HEADS, rows, 128), F32),
            pltpu.VMEM((rows, width), F32),
            pltpu.VMEM((rows, width), F32),
            pltpu.VMEM((rows, ff), BF16),
            pltpu.VMEM((rows, ff), BF16),
            pltpu.VMEM((rows, 1024), BF16),
            pltpu.VMEM((2, rows, width), BF16),
            pltpu.VMEM((2 * SHARE * rows, keys), BF16),
            pltpu.VMEM((KEY_VALUE_HEADS, keys, 128), BF16),
            pltpu.VMEM(layers + (KEY_VALUE_HEADS, 3 * rows, 128), BF16),
            pltpu.VMEM((rows, kv_width), BF16),
            pltpu.VMEM((2, rows, 128), F32),
            pltpu.VMEM((rows, keys), F32),
            pltpu.VMEM((8, width), F32),
            dma(5),
            dma(2, KEY_VALUE_HEADS),
            dma(2),
            dma(2),
            dma(2, 3, KEY_VALUE_HEADS),
            dma(2, 3, KEY_VALUE_HEADS),
            dma(*layers, 2, KEY_VALUE_HEADS),
            dma(*layers, 3, KEY_VALUE_HEADS),
            dma(2),
            dma(2),
            dma(2),
            dma(2),
            dma(9, 2),
            dma(9, 2),
            dma(9, 2),
            dma(len(kept) + 1),
        ],
        compiler_params=pltpu.CompilerParams(
            collective_id=1, has_side_effects=True, vmem_limit_bytes=61 * 2**20
        ),
        name="layers",
    )(lengths, ends, frequency, gain_attn, gain_ffn, *weights)


MIDDLE_ORDER = (
    "near1", "near0", "head0", "head1", "head2", "far1", "head3", "head4",
    "near3", "query0", "down0", "near2", "down1", "fadd1", "far0", "aend0",
    "tready0", "tnear2", "down2", "down3", "tnear0", "down4", "far3", "down5",
    "far2", "fadd0", "tfar0", "tnear3", "dfirst0", "tnear1", "fz0", "fadd3",
    "tfar3", "tadd0", "fadd2", "fz1", "dsecond0", "fz2", "tfar1", "tfar2",
    "tadd3", "tz0", "tadd1", "ftotal0", "dgather0", "tadd2", "tz1", "tz2",
    "fmiddle0", "ttotal0", "dmiddle0",
)
END_ORDER = (
    "near1", "head0", "near0", "down0", "far1", "head1", "down1", "down2",
    "head2", "head3", "head4", "near3", "down3", "far0", "fadd1", "down4",
    "query0", "near2", "aend0", "down5", "fadd0", "far3", "fz0", "tready0",
    "tnear3", "far2", "fadd3", "tnear0", "fz2", "tnear2", "fadd2", "fz1",
    "tnear1", "tfar3", "tfar0", "dfirst0", "tfar2", "tfar1", "tadd0", "tadd3",
    "tz0", "tadd1", "dsecond0", "tz2", "ftotal0", "tadd2", "tz1", "dgather0",
    "ttotal0", "fmiddle0", "dmiddle0",
)


def sums_kernel(*refs):
    refs = list(refs)

    def take(count):
        taken = refs[:count]
        del refs[:count]
        return taken

    gain_h, gain_a, nf_h, in_h, gg_h, gu_h, br_h, la_h, ra_h, nr_h, kvg_h = take(11)
    act_h, kv_h, o_h, cs_h, allowed_h, qd_h, gm_h, wq_h, wk_h, wv_h = take(10)
    grads_o, t_o, gate_o, up_o, down_o = take(5)
    stage, in_v, br_v, gg_v, gu_v, ra_v, kvg_v, nf_t, ln_t, in_t, gain_t = take(11)
    act, kv, o_raw, cos_sin, allowed, qd, gm, wq, wkv = take(9)
    go, ra, dkv, dkv_in, gkv, sum_acc, gain_rows = take(7)
    d_out, d_in, d_keep, d1_out, d1_in, d2_out, d2_in = take(7)
    f1_out, f1_in, f2_out, f2_in, f_keep, fz_in = take(6)
    t1_out, t1_in, t2_out, t2_in, t_keep, tz_in = take(6)
    d_all, f_all, t_all = take(3)
    load, kept_sem, w_sem, dk_s, dk_r, grad_s, grad_r, op_own, op_s, op_r = take(10)
    dz_s, dz_r, d1_s, d1_r, d2_s, d2_r, f1_s, f1_r, f2_s, f2_r, fz_s, fz_r = take(12)
    t1_s, t1_r, t2_s, t2_r, tz_s, tz_r, all_s, all_r, pair_r, write = take(10)

    section = lax.axis_index("section")
    z = lax.axis_index("dp")
    ctx = lax.axis_index("ctx")
    x, y = ctx % 2, ctx // 2
    rank = 2 * section + x
    x_next = (section, z, 2 * y + 1 - x)
    y_next = (section, z, 2 * (1 - y) + x)
    partner = (1 - section, z, ctx)
    rows = act.shape[0]
    width = nf_h.shape[1]
    per = width // RANKS
    part = f_keep.shape[2]
    shift = per - part
    quarter = gg_v.shape[1] // 2
    deep = in_t.shape[0]
    fine = deep // 2
    last = RANKS - 1
    edge = ((z == 0) | (z == last)).astype(jnp.int32)

    def pick(index, values):
        if isinstance(index, int):
            return values[index]
        return sum((index == i).astype(jnp.int32) * v for i, v in enumerate(values) if not (type(v) is int and v == 0))

    def remote(src, dst, send, recv, device):
        return pltpu.make_async_remote_copy(
            src_ref=src, dst_ref=dst, send_sem=send, recv_sem=recv,
            device_id=device, device_id_type=MESH,
        )

    def some(start, size, unit=16):
        return pl.ds(pl.multiple_of(start, unit), size)

    gain_load = pltpu.make_async_copy(gain_h, gain_rows.at[pl.ds(0, gain_h.shape[0])], load.at[7])
    by_need = ((3, 2, 1, 0), (3, 0, 2, 1), (0, 3, 1, 2), (0, 1, 2, 3))
    by_turns = ((3, 2, 1, 0), (3, 0, 2, 1), (0, 3, 1, 2), (0, 2, 1, 3))

    def turn_of(k, order=by_need):
        return pick(k, [pick(z, [row[i] for row in order]) for i in range(RANKS)])

    def in_load(k):
        return pltpu.make_async_copy(
            in_h.at[:, some(turn_of(k) * deep, deep, 128)], in_v, load.at[0]
        )

    loads = [None] + [
        pltpu.make_async_copy(h, v, load.at[1 + i])
        for i, (h, v) in enumerate(
            [(br_h, br_v), (nf_h, stage), (gg_h, gg_v), (gu_h, gu_v), (la_h, stage), (nr_h, stage)]
        )
    ]
    kept = [
        pltpu.make_async_copy(h, v, kept_sem.at[i])
        for i, (h, v) in enumerate(
            [(qd_h, qd), (kv_h, kv), (o_h, o_raw), (allowed_h, allowed), (cs_h, cos_sin),
             (gm_h, gm), (act_h, act)]
        )
    ]
    late = [
        pltpu.make_async_copy(h.at[pl.ds(c * rows, rows)], v.at[pl.ds((2 * c + 1) * rows, rows)], w_sem.at[i, c])
        for i, (h, v) in enumerate([(ra_h, ra_v), (kvg_h, kvg_v)])
        for c in range(2)
    ]
    weights = [pltpu.make_async_copy(wq_h, wq, w_sem.at[2, 0])] + [
        pltpu.make_async_copy(
            h.at[pl.ds(g * HEAD_SIZE, HEAD_SIZE)],
            wkv.at[pl.ds((2 * g + i) * HEAD_SIZE, HEAD_SIZE)],
            w_sem.at[3 + i, g],
        )
        for g in range(KEY_VALUE_HEADS)
        for i, h in enumerate((wk_h, wv_h))
    ]
    loads[2].start()
    loads[3].start()
    loads[4].start()
    gain_rows[...] = jnp.zeros_like(gain_rows)

    barrier = pltpu.get_barrier_semaphore()
    greet(barrier, z)
    not_first = (z > 0).astype(jnp.int32)
    not_last = (z < last).astype(jnp.int32)

    @pl.when(z > 0)
    def _():
        pl.semaphore_signal(barrier, inc=1, device_id=(section, z - 1, ctx), device_id_type=MESH)

    @pl.when(z < last)
    def _():
        pl.semaphore_signal(barrier, inc=1, device_id=(section, z + 1, ctx), device_id_type=MESH)

    def turn(src, dst, base=0):
        for at, size in tiles(src.shape[1], 128):
            block = src[:, at : at + size]
            if size < 128:
                block = wide(block)
            dst[base + at : base + at + size, :] = block.T[:size]

    def z_way(t):
        up = (z < t).astype(jnp.int32)
        to = z + 2 * up - 1
        arrives = up * not_first + (1 - up) * not_last
        meets = (1 - up) * (t == z - 1).astype(jnp.int32)
        return (section, to, ctx), arrives, t * (1 - meets) + RANKS * meets

    def d_block(k):
        in_load(k).wait()
        for b in range(deep // 128):
            in_t[b * 128 : (b + 1) * 128, :] = in_v[:, b * 128 : (b + 1) * 128].T

        if not isinstance(k, int):

            @pl.when(k < last)
            def _():
                in_load(k + 1).start()

    def d_send(k, sub):
        device, _, slot = z_way(turn_of(k))
        span = some(sub * fine, fine)
        return remote(d_out.at[k, span], d_in.at[slot, span], dz_s.at[k, sub], dz_r.at[slot, sub], device)

    def d_step(n):
        k, sub = n // 2, n % 2

        @pl.when(n == 0)
        def _():
            loads[1].wait()

        @pl.when(sub == 0)
        def _():
            d_block(k)

        t = turn_of(k)
        _, arrives, _ = z_way(t)
        span = some(sub * fine, fine)
        mine = dot(in_t[span, :], br_v[...])

        @pl.when(arrives == 0)
        def _():
            d_out[k, span, :] = mine.astype(BF16)

        @pl.when(arrives == 1)
        def _():
            remote(d_out.at[k, span], d_in.at[t, span], dz_s.at[k, sub], dz_r.at[t, sub], partner).wait_recv()
            d_out[k, span, :] = (mine + d_in[t, span, :].astype(F32)).astype(BF16)

        d_send(k, sub).start()

    def f_links(k):
        return (x_next, y_next, x, y) if k == 0 else (y_next, x_next, y, x)

    def f_right(k, column_half):
        src = gg_v if k == 0 else gu_v
        return src[:, some(column_half * quarter, quarter, 128)]

    turns = (3, 0, 2, 1)

    def f1_copy(k, i):
        d = pick(i, turns)
        return remote(f1_out.at[k, i % 2], f1_in.at[k, d], f1_s.at[k, i % 2], f1_r.at[k, d], f_links(k)[0])

    def f2_copy(k, i):
        d = pick(i, turns)
        return remote(f2_out.at[k, i % 2], f2_in.at[k, d], f2_s.at[k, i % 2], f2_r.at[k, d], f_links(k)[1])

    def f1_step(i):
        left = nf_t[some(pick(i, turns) * per, per), :]
        for k in range(2):
            value = dot(left, f_right(k, 1 - f_links(k)[2])).astype(BF16)

            @pl.when(i >= 2)
            def _():
                f1_copy(k, i).wait_send()

            f1_out[k, i % 2] = value
            f1_copy(k, i).start()

    def f2_step(i):
        d = pick(i, turns)
        for k in range(2):
            first, second = f_links(k)[2:]
            f1_copy(k, i).wait_recv()

            def total(which):
                return (
                    dot(nf_t[some(d * per + which * shift, part), :], f_right(k, first))
                    + f1_in[k, d, some(which * shift, part), :].astype(F32)
                ).astype(BF16)

            value = total(1 - second)

            @pl.when(i >= 2)
            def _():
                f2_copy(k, i).wait_send()

            f2_out[k, i % 2] = value
            f2_copy(k, i).start()
            f_keep[k, d] = total(second)

    def t_links(d):
        x_first = (d < RANKS // 2) * 1
        choose = lambda a, b: x_first * a + (1 - x_first) * b
        ways = [tuple(choose(a, b) for a, b in zip(*pair)) for pair in ((x_next[1:], y_next[1:]), (y_next[1:], x_next[1:]))]
        return (section, *ways[0]), (section, *ways[1]), choose(x, y), choose(y, x)

    def t_product(row, count, add, dst):
        full = width // 128 * 128
        mine = dot(ln_t[some(row, count), :], ra_v[...])
        dst[:, :full] = add(mine[:, :full], 0).astype(BF16)
        tail = jnp.concatenate([mine[:, full:], gain_t[some(row, count), width - full :]], axis=1)
        dst[:, full : full + 128] = add(tail, full).astype(BF16)
        pairs = dot(ln_t[some(width + row, count), :], kvg_v[...])
        dst[:, full + 128 :] = add(pairs, full + 128).astype(BF16)

    def t1_copy(d):
        return remote(t1_out.at[d], t1_in.at[d], t1_s.at[d], t1_r.at[d], t_links(d)[0])

    def t2_copy(d):
        return remote(t2_out.at[d], t2_in.at[d], t2_s.at[d], t2_r.at[d], t_links(d)[1])

    def t1_step(d):
        first = t_links(d)[2]
        t_product(d * per + (1 - first) * shift, part, lambda v, at: v, t1_out.at[d])
        t1_copy(d).start()

    def t2_step(d):
        _, _, first, second = t_links(d)
        t1_copy(d).wait_recv()
        for which, dst in ((1 - second, t2_out), (second, t_keep)):
            row = which * (part // 2)
            add = lambda v, at: v + t1_in[d, some(row, part // 2), at : at + v.shape[1]].astype(F32)
            t_product(d * per + first * shift + row, part // 2, add, dst.at[d])
            if dst is t2_out:
                t2_copy(d).start()

    class Line:
        def __init__(self, keep, second_in, z_in, send, recv):
            self.keep, self.second_in, self.z_in, self.send, self.recv = keep, second_in, z_in, send, recv

        def add(self, copy, d):
            copy.wait_recv()
            self.keep[d] = (self.keep[d].astype(F32) + self.second_in[d].astype(F32)).astype(BF16)

        def copy(self, k):
            d = turn_of(k, by_turns)
            device, _, slot = z_way(d)
            return remote(self.keep.at[d], self.z_in.at[slot], self.send.at[k], self.recv.at[slot], device)

        def step(self, k):
            d = turn_of(k, by_turns)
            _, arrives, _ = z_way(d)

            @pl.when(arrives == 1)
            def _():
                remote(self.keep.at[d], self.z_in.at[d], self.send.at[k], self.recv.at[d], partner).wait_recv()
                self.keep[d] = (self.keep[d].astype(F32) + self.z_in[d].astype(F32)).astype(BF16)

            self.copy(k).start()

        def total(self):
            for condition, slot in ((z > 0, z), (z < last, RANKS)):

                @pl.when(condition)
                def _(slot=slot):
                    remote(self.keep.at[0], self.z_in.at[slot], self.send.at[0], self.recv.at[slot], partner).wait_recv()

            value = self.keep[z].astype(F32)
            return z_total(value, self.z_in[z], self.z_in[RANKS])

    def z_total(value, up, down):
        value = value + jnp.where(z > 0, up.astype(F32), 0.0)
        return value + jnp.where(z < last, down.astype(F32), 0.0)

    lines = [
        Line(f_keep.at[k], f2_in.at[k], fz_in.at[k], fz_s.at[k], fz_r.at[k]) for k in range(2)
    ] + [Line(t_keep, t2_in, tz_in, tz_s, tz_r)]

    def f_add(i):
        for k in range(2):
            lines[k].add(f2_copy(k, i), pick(i, turns))

    def t_add(d):
        lines[2].add(t2_copy(d), d)

    def f_line(k):
        lines[0].step(k)
        lines[1].step(k)

    def places(x_first):
        a, b = (1, 0) if x_first is True else (0, 1) if x_first is False else (x_first, 1 - x_first)
        spot = lambda i, j: a * (2 * i + j) + b * (2 * j + i)
        return spot(x, y), spot(1 - x, y), spot(x, 1 - y), spot(1 - x, 1 - y)

    class Gather:
        def __init__(self, number, buffer, x_first):
            self.n, self.buffer = number, buffer
            self.own, self.over_x, self.over_y, self.across = places(x_first)
            size = buffer.shape[2]
            cut = (size // 2 + 15) // 16 * 16
            self.halves = (pl.ds(0, cut), pl.ds(cut, size - cut))

        def whole(self, spot, slot, device):
            ref = self.buffer.at[section, spot]
            return remote(ref, ref, all_s.at[self.n, slot], all_r.at[self.n, slot], device)

        def relay(self, spot, half, device):
            ref = self.buffer.at[section, spot, self.halves[half]]
            return remote(ref, ref, all_s.at[self.n, 2 + half], all_r.at[self.n, 2 + half], device)

        def pair(self, core, spot, slot):
            ref = self.buffer.at[core, spot]
            return remote(ref, ref, all_s.at[self.n, 4 + slot], pair_r.at[self.n, spot], partner)

        def start(self, value):
            self.buffer[section, self.own] = value.astype(BF16)
            self.whole(self.own, 0, x_next).start()
            self.whole(self.own, 1, y_next).start()
            self.pair(section, self.own, 0).start()

        def middle(self):
            self.whole(self.over_x, 0, x_next).wait_recv()
            self.relay(self.over_x, 0, y_next).start()
            self.pair(section, self.over_x, 1).start()
            self.whole(self.over_y, 1, y_next).wait_recv()
            self.relay(self.over_y, 1, x_next).start()
            self.pair(section, self.over_y, 2).start()

        def finish(self):
            self.relay(self.across, 0, y_next).wait_recv()
            self.relay(self.across, 1, x_next).wait_recv()
            self.pair(section, self.across, 3).start()
            for spot in (self.own, self.over_x, self.over_y, self.across):
                self.pair(1 - section, spot, 0).wait_recv()

        def sent(self):
            self.whole(self.own, 0, x_next).wait_send()
            self.whole(self.own, 1, y_next).wait_send()
            self.relay(self.over_x, 0, y_next).wait_send()
            self.relay(self.over_y, 1, x_next).wait_send()
            for slot, spot in enumerate((self.own, self.over_x, self.over_y, self.across)):
                self.pair(section, spot, slot).wait_send()

    below = (z < RANKS // 2).astype(jnp.int32)
    gathers = [
        Gather(0, d_all.at[0], True),
        Gather(1, d_all.at[1], False),
        Gather(2, f_all.at[0], True),
        Gather(3, f_all.at[1], False),
        Gather(4, t_all, below),
    ]

    def d1_copy(h):
        return remote(d1_out.at[h], d1_in.at[h], d1_s.at[h], d1_r.at[h], f_links(h)[0])

    def d2_copy(h):
        return remote(d2_out.at[h], d2_in.at[h], d2_s.at[h], d2_r.at[h], f_links(h)[1])

    def d_first(h):
        span = pl.ds(h * fine, fine)
        for condition, slot in ((z > 0, z), (z < last, RANKS)):

            @pl.when(condition)
            def _(slot=slot):
                remote(d_out.at[0, span], d_in.at[slot, span], dz_s.at[0, h], dz_r.at[slot, h], partner).wait_recv()

        first = f_links(h)[2]
        for mine in (False, True):
            at = h * fine + (first if mine else 1 - first) * (fine // 2)
            piece = some(at, fine // 2)
            total = z_total(dot(in_t[piece, :], br_v[...]), d_in[z, piece, :], d_in[RANKS, piece, :])
            if mine:
                d_keep[h] = total
            else:
                d1_out[h] = total.astype(BF16)
                d1_copy(h).start()

    def d_second(h):
        second = f_links(h)[3]
        d1_copy(h).wait_recv()
        for mine in (False, True):
            piece = some((second if mine else 1 - second) * (fine // 4), fine // 4)
            total = d_keep[h, piece, :] + d1_in[h, piece, :].astype(F32)
            if mine:
                d_keep[h, : fine // 4, :] = total
            else:
                d2_out[h] = total.astype(BF16)
                d2_copy(h).start()

    def d_gather(h):
        d2_copy(h).wait_recv()
        gathers[h].start(d_keep[h, : fine // 4, :] + d2_in[h].astype(F32))

    back = AttentionBack(
        rank, lambda r: (r // 2, z, 2 * y + r % 2), qd, kv, o_raw, allowed, cos_sin, ra,
        ln_t.at[pl.ds(0, 2 * SHARE * rows)], dkv, dkv_in, gkv, dk_s, dk_r,
    )
    grads_out = OutCopy(grads_o, grad_s, grad_r)

    def op_copy(kind, own):
        role = section if own else 1 - section
        src = ra.at[role] if kind == 0 else gkv.at[:, some(role * 256, 384, 128)]
        dst = (ra_v, kvg_v)[kind].at[some(2 * section * rows, rows)]
        if own:
            return pltpu.make_async_copy(src, dst, op_own.at[kind])
        return remote(src, dst, op_s.at[kind], op_r.at[kind], partner)

    def op_start(kind):
        op_copy(kind, True).start()
        op_copy(kind, False).start()

    def attention_end():
        back.collect()
        op_start(1)
        for copy in weights:
            copy.wait()
        kept[6].wait()
        back.project(sum_acc, wq, wkv)
        grad, gain_row = norm_back(act[...].astype(F32), gain_a[...].astype(F32).reshape(1, width), sum_acc[...])
        gain_load.wait()
        gain_rows[0:1, :] += gain_row
        go[...] = (gm[...] + grad).astype(BF16)
        grads_out.start(go, 0)

    def t_ready():
        loads[5].wait()
        turn(stage, ln_t)
        loads[6].start()
        block_of = lambda at, size: wide(gain_rows[:, at : at + size]).T
        for at, size in tiles(width, 128):
            gain_t[at : at + size, :] = pltpu.roll(block_of(at, size), 64, 1)[:size]
        loads[6].wait()
        turn(stage, ln_t, width)
        for copy in late:
            copy.wait()
        for kind in range(2):
            op_copy(kind, True).wait()
            op_copy(kind, False).wait_recv()

    def both(step):
        step(0)
        step(1)

    def head_step(g):
        @pl.when(g == 0)
        def _():
            for copy in kept[:6]:
                copy.wait()
            ra[1] = gm[...].astype(BF16)

        back.head(g)

        @pl.when(g > 0)
        def _():
            back.relay(g - 1)

    def queries_step():
        back.relay(KEY_VALUE_HEADS - 1)
        back.queries()
        op_start(0)

    def d_first_step():
        d_block(last)
        both(d_first)

    def f_total():
        both(lambda k: gathers[2 + k].start(lines[k].total()))

    actions = {
        "near": f1_step,
        "far": f2_step,
        "tnear": t1_step,
        "tfar": t2_step,
        "down": d_step,
        "head": head_step,
        "fadd": f_add,
        "fz": f_line,
        "tadd": t_add,
        "tz": lines[2].step,
        "query": lambda p: queries_step(),
        "aend": lambda p: attention_end(),
        "tready": lambda p: t_ready(),
        "dfirst": lambda p: d_first_step(),
        "dsecond": lambda p: both(d_second),
        "dgather": lambda p: both(d_gather),
        "ftotal": lambda p: f_total(),
        "ttotal": lambda p: gathers[4].start(lines[2].total()),
        "fmiddle": lambda p: both(lambda k: gathers[2 + k].middle()),
        "dmiddle": lambda p: both(lambda h: gathers[h].middle()),
    }
    names = list(actions)

    def codes(table):
        return [8 * names.index(step.rstrip("0123456789")) + int(step[-1]) for step in table]

    tables = [codes(MIDDLE_ORDER), codes(END_ORDER)]
    steps = max(len(t) for t in tables)

    loads[2].wait()
    turn(stage, nf_t)
    loads[3].wait()
    loads[4].wait()
    in_load(0).start()
    loads[1].start()
    for copy in kept + weights + late + [gain_load]:
        copy.start()
    pl.semaphore_wait(barrier, 7 + not_first + not_last)
    loads[5].start()

    def one(n, carry):
        code = (1 - edge) * pick(n, tables[0]) + edge * pick(n, tables[1])
        lax.switch(code // 8, list(actions.values()), code % 8)
        return carry

    lax.fori_loop(0, steps, one, 0)

    writes = []

    def leave(src, dst):
        writes.append(pltpu.make_async_copy(src, dst, write.at[len(writes)]))
        writes[-1].start()

    for k in range(2):
        gathers[2 + k].finish()
        for core in range(2):
            for f in range(2):
                columns = pl.ds((2 * core + f) * quarter, quarter)
                out = (gate_o, up_o)[k]
                leave(f_all.at[k, core, 2 * f], out.at[pl.ds(0, part), columns])
                rest = pl.ds(part - shift, per - part)
                leave(f_all.at[k, core, 2 * f + 1, rest], out.at[pl.ds(part, per - part), columns])
    gathers[4].middle()
    for h in range(2):
        gathers[h].finish()
        for core in range(2):
            for spot in range(4):
                span = pl.ds(h * fine + spot * (fine // 4), fine // 4)
                leave(d_all.at[h, core, spot], down_o.at[span, pl.ds(core * br_v.shape[1], br_v.shape[1])])
    gathers[4].finish()
    t_rows = part // 2
    for core in range(2):
        for spot in range(4):
            row = spot % 2 * t_rows + spot // 2 * shift
            skip = part - shift if spot == 2 else 0
            rest = pl.ds(skip, t_rows - skip)
            leave(t_all.at[core, spot, rest], t_o.at[core, pl.ds(row + skip, t_rows - skip)])

    for k in range(last):
        for sub in range(2):
            d_send(k, sub).wait_send()
        for line in lines:
            line.copy(k).wait_send()
    for h in range(2):
        d1_copy(h).wait_send()
        d2_copy(h).wait_send()
    for k in range(2):
        for i in (2, 3):
            f1_copy(k, i).wait_send()
            f2_copy(k, i).wait_send()
    for d in range(RANKS):
        t1_copy(d).wait_send()
        t2_copy(d).wait_send()
    for kind in range(2):
        op_copy(kind, False).wait_send()
    grads_out.sent(go, 0)

    @pl.when(section == 0)
    def _():
        grads_out.arrived(go)

    for gather in gathers:
        gather.sent()
    for copy in writes:
        copy.wait()


def run_sums(gain_sums, gain_attn, operands, kept, weights, ends_shape):
    nf, inner, gg, gu, br, la, ra, nr, kvg = operands
    act, kv, o_raw, cos_sin, allowed, qd, gm = kept
    depth, width = nf.shape
    rows = act.shape[0]
    ff, half = inner.shape[1], gg.shape[1]
    per, deep = width // RANKS, ff // RANKS
    part = (per // 2 + 15) // 16 * 16
    quarter, fine = half // 2, deep // 2
    columns = br.shape[1]
    wide_t = width // 128 * 128 + 128 + kvg.shape[1]
    vmem, hbm = pl.BlockSpec(memory_space=pltpu.VMEM), pl.BlockSpec(memory_space=pl.ANY)
    out = lambda *shape: jax.ShapeDtypeStruct(shape, BF16)
    b = lambda *shape: pltpu.VMEM(shape, BF16)
    f = lambda *shape: pltpu.VMEM(shape, F32)
    like = lambda a: pltpu.VMEM(a.shape, a.dtype)
    sem = lambda *shape: pltpu.SemaphoreType.DMA(shape)
    return pl.pallas_call(
        sums_kernel,
        out_shape=[
            out(*ends_shape), out(2, per, wide_t), out(per, ff), out(per, ff), out(deep, 2 * columns),
        ],
        in_specs=[hbm, vmem] + [hbm] * 19,
        out_specs=[hbm] * 5,
        scratch_shapes=[
            b(depth, width), b(depth, deep), b(depth, columns), b(depth, half), b(depth, half),
            b(depth, width), b(depth, kvg.shape[1]),
            b(width, depth), b(2 * width, depth), b(deep, depth), f(width, 128),
            like(act), like(kv), like(o_raw), like(cos_sin), like(allowed), like(qd), like(gm),
            like(weights[0]), b(2 * weights[1].shape[0], width),
            b(rows, width), b(2, rows, width), like(kv), b(KEY_VALUE_HEADS, 3 * rows, 128), b(rows, KEY_VALUE_HEADS * 128),
            f(rows, width), f(128, width),
            b(RANKS - 1, deep, columns), b(5, deep, columns), f(2, fine // 2, columns),
            b(2, fine // 2, columns), b(2, fine // 2, columns), b(2, fine // 4, columns), b(2, fine // 4, columns),
            b(2, 2, per, quarter), b(2, RANKS, per, quarter),
            b(2, 2, part, quarter), b(2, RANKS, part, quarter), b(2, RANKS, part, quarter), b(2, 5, part, quarter),
            b(RANKS, part, wide_t), b(RANKS, part, wide_t),
            b(RANKS, part // 2, wide_t), b(RANKS, part // 2, wide_t), b(RANKS, part // 2, wide_t), b(5, part // 2, wide_t),
            b(2, 2, 4, fine // 4, columns), b(2, 2, 4, part, quarter), b(2, 4, part // 2, wide_t),
            sem(8), sem(7), sem(5, KEY_VALUE_HEADS), sem(2, KEY_VALUE_HEADS), sem(3, KEY_VALUE_HEADS), sem(2), sem(2), sem(2), sem(2), sem(2),
            sem(3, 2), sem(5, 2), sem(2), sem(2), sem(2), sem(2),
            sem(2, 2), sem(2, 4), sem(2, 2), sem(2, 4), sem(2, 3), sem(2, 5),
            sem(4), sem(4), sem(4), sem(4), sem(3), sem(5),
            sem(5, 8), sem(5, 4), sem(5, 4), sem(40),
        ],
        compiler_params=pltpu.CompilerParams(
            collective_id=2, has_side_effects=True, vmem_limit_bytes=61 * 2**20
        ),
        name="sums",
    )(gain_sums, gain_attn, *operands, *kept, *weights)


def finish_kernel(
    acts_h, first_h, second_h, t_h, gate_h, up_h, down_h,
    acts_o, grads_o, q_o, out_o, key_o, value_o, gain_a, gain_f, gate_o, up_o, down_o,
    row_v, t_v, gate_v, down_v, q_f, kv_f, gate_f, down_f, load, store,
):
    width = q_f.shape[2]
    loads = [
        pltpu.make_async_copy(h, v, load.at[i])
        for i, (h, v) in enumerate(
            [(gate_h, gate_v.at[0]), (up_h, gate_v.at[1]), (down_h, down_v), (t_h, t_v), (acts_h, row_v.at[0])]
        )
    ]
    stores = [
        pltpu.make_async_copy(v, h, store.at[i])
        for i, (v, h) in enumerate(
            [(row_v.at[0], acts_o), (row_v.at[1], grads_o), (gate_f.at[0], gate_o), (gate_f.at[1], up_o),
             (down_f, down_o), (q_f.at[0], q_o), (q_f.at[1], out_o), (kv_f.at[0], key_o), (kv_f.at[1], value_o)]
        )
    ]
    section = lax.axis_index("section")
    for copy in loads:
        copy.start()
    start_if(
        section == 0,
        lambda: pltpu.make_async_copy(first_h, row_v.at[1], load.at[5]),
        lambda: pltpu.make_async_copy(second_h, row_v.at[1], load.at[5]),
    )
    for k in range(2):
        loads[k].wait()
        gate_f[k] = gate_v[k].astype(F32)
        stores[2 + k].start()
    loads[4].wait()
    stores[0].start()
    pltpu.make_async_copy(first_h, row_v.at[1], load.at[5]).wait()
    stores[1].start()
    loads[2].wait()
    for at, size in tiles(width, 128):
        down_f[at : at + size, :] = down_v[:, at : at + 128].astype(F32).T[:size]
    stores[4].start()
    loads[3].wait()
    for core in range(2):
        q_f[core] = t_v[core, :, :width].astype(F32)
        stores[5 + core].start()
    pairs_at = width // 128 * 128 + 128
    half = KEY_VALUE_HEADS // 2 + 1
    for g in range(KEY_VALUE_HEADS):
        core = 0 if g < half else 1
        at = pairs_at + (g - core * (KEY_VALUE_HEADS - half)) * 128
        block = t_v[core, :, at : at + 128].astype(F32).T
        kv_f[0, g * HEAD_SIZE : (g + 1) * HEAD_SIZE, :] = block[:HEAD_SIZE]
        kv_f[1, g * HEAD_SIZE : (g + 1) * HEAD_SIZE, :] = block[HEAD_SIZE:]
    for copy in stores[7:]:
        copy.start()
    tail = slice(pairs_at - 128, pairs_at)
    both = t_v[0, :, tail].astype(F32) + t_v[1, :, tail].astype(F32)
    row = width % 128
    gain_rows = both.T
    gain_a[...] = gain_rows[row]
    gain_f[...] = gain_rows[row + 1]
    for copy in stores:
        copy.wait()


def run_finish(acts, grads_first, grads_second, t_sum, gate, up, down, width):
    per, ff = gate.shape
    vmem, hbm = pl.BlockSpec(memory_space=pltpu.VMEM), pl.BlockSpec(memory_space=pl.ANY)
    out = lambda *shape: jax.ShapeDtypeStruct(shape, F32)
    kv_rows = KEY_VALUE_HEADS * HEAD_SIZE
    return pl.pallas_call(
        finish_kernel,
        out_shape=[
            jax.ShapeDtypeStruct(acts.shape, BF16), jax.ShapeDtypeStruct(acts.shape, BF16),
            out(per, width), out(per, width), out(kv_rows, per), out(kv_rows, per), out(per), out(per),
            out(per, ff), out(per, ff), out(width, down.shape[0]),
        ],
        in_specs=[hbm] * 7,
        out_specs=[hbm] * 6 + [vmem] * 2 + [hbm] * 3,
        scratch_shapes=[
            pltpu.VMEM((2, *acts.shape), BF16), pltpu.VMEM(t_sum.shape, BF16), pltpu.VMEM((2, per, ff), BF16), pltpu.VMEM(down.shape, BF16),
            pltpu.VMEM((2, per, width), F32), pltpu.VMEM((2, kv_rows, per), F32),
            pltpu.VMEM((2, per, ff), F32), pltpu.VMEM((width, down.shape[0]), F32),
            pltpu.SemaphoreType.DMA((6,)), pltpu.SemaphoreType.DMA((9,)),
        ],
        compiler_params=pltpu.CompilerParams(vmem_limit_bytes=61 * 2**20),
        name="finish",
    )(acts, grads_first, grads_second, t_sum, gate, up, down)


def sums_by_xla(gain_sums, operands):
    nf, inner, gg, gu, br, la, ra, nr, kvg = operands
    width = nf.shape[1]

    def reduced(left, right):
        total = dot_lt(left, right).astype(BF16)
        piece = lax.psum_scatter(total, "dp", scatter_dimension=0, tiled=True)
        return lax.psum(piece, "ctx")

    def both(piece, axis):
        return lax.all_gather(piece, "section", axis=axis, tiled=axis > 0).astype(F32)

    attn = both(reduced(la, ra), 0)
    gain_sum = lax.psum(gain_sums[:2], ("section", "ctx"))
    return (
        attn[0],
        attn[1],
        both(reduced(nr, kvg), 0),
        lax.psum_scatter(gain_sum, "dp", scatter_dimension=1, tiled=True),
        both(reduced(nf, gg), 1),
        both(reduced(nf, gu), 1),
        both(reduced(inner, br), 1)[:, :width],
    )


def shards(
    ends,
    doc_lengths,
    w_query,
    key_projection_weight,
    value_projection_weight,
    w_out,
    w_gate,
    w_up,
    w_down,
    gain_attn,
    gain_ffn,
):
    width = ends.shape[3]
    half = HEAD_SIZE // 2
    turns = np.float32(10000.0) ** (
        np.float32(-2.0) * (np.arange(128) % half).astype(np.float32) / np.float32(HEAD_SIZE)
    )
    weights = (
        w_query,
        key_projection_weight.T,
        value_projection_weight.T,
        w_out,
        w_gate,
        w_up,
        w_down.T,
    )
    ff = w_gate.shape[1]
    fits = lax.axis_size("dp") == RANKS and width % 64 == 0 and ff % 1280 == 0
    acts, grads_in, gain_sums, *kept = run_layers(
        doc_lengths,
        ends,
        jnp.asarray(turns.reshape(1, 128), F32),
        gain_attn,
        gain_ffn,
        weights,
        not fits,
    )
    operands = kept[:9]
    if fits:
        grads_first, *sums = run_sums(
            gain_sums, gain_attn, operands, kept[9:], weights[:3], ends.shape
        )
        acts, grads_in, grad_query, grad_out, grad_key, grad_value, *gain_piece, grad_gate, grad_up, grad_down = (
            run_finish(acts, grads_first, grads_in, *sums, width)
        )
        grad_key, grad_value, grad_down = grad_key.T, grad_value.T, grad_down.T
    else:
        grad_query, grad_out, kv_parts, gain_piece, grad_gate, grad_up, grad_down = sums_by_xla(
            gain_sums, operands
        )
        kv_grad = jnp.concatenate([kv_parts[0], kv_parts[1][:, 128:]], axis=1).reshape(
            -1, KEY_VALUE_HEADS, 2, HEAD_SIZE
        )
        grad_key = kv_grad[:, :, 0].reshape(kv_grad.shape[0], -1)
        grad_value = kv_grad[:, :, 1].reshape(kv_grad.shape[0], -1)
    return (
        acts,
        grads_in,
        grad_query,
        grad_key,
        grad_value,
        grad_out,
        grad_gate,
        grad_up,
        grad_down,
        gain_piece[0],
        gain_piece[1],
    )


def solution(mesh):
    return jax.shard_map(
        shards,
        mesh=mesh,
        in_specs=(P("section", None, ("dp", "ctx"), None), P(None, "dp", None)) + (P(),) * 9,
        out_specs=(P("section", None, ("dp", "ctx"), None),) * 2
        + (P("dp", None),) * 7
        + (P("dp"),) * 2,
        check_vma=False,
    )
```

```python
import jax
import jax.numpy as jnp
import numpy as np
from jax import lax
from jax.experimental import pallas as pl
from jax.experimental.pallas import tpu as pltpu
from jax.sharding import PartitionSpec as P

MESH = pl.DeviceIdType.MESH
QUERY_HEADS = 15
KEY_VALUE_HEADS = 5
HEAD_SIZE = 64
SHARE = QUERY_HEADS // KEY_VALUE_HEADS
RANKS = 4
epsilon = 1e-05
masked_fill = -1e30
F32 = jnp.float32
BF16 = jnp.bfloat16


def dot(left, right):
    return jnp.dot(left, right, preferred_element_type=F32)


def dot_rt(left, right):
    return lax.dot_general(left, right, (((1,), (1,)), ((), ())), preferred_element_type=F32)


def dot_lt(left, right):
    return lax.dot_general(left, right, (((0,), (0,)), ((), ())), preferred_element_type=F32)


def tiles(total, width):
    return [(at, min(width, total - at)) for at in range(0, total, width)]


def wide(block):
    missing = 128 - block.shape[1]
    if not missing:
        return block
    return jnp.concatenate([block, jnp.zeros((block.shape[0], missing), block.dtype)], axis=1)


def lanes(rows):
    return lax.broadcasted_iota(jnp.int32, (rows, 128), 1)


def half_turn(block):
    front = lanes(block.shape[0]) % HEAD_SIZE < HEAD_SIZE // 2
    return jnp.where(front, pltpu.roll(block, 96, 1), pltpu.roll(block, 32, 1))


def inverse_rms(hidden):
    return lax.rsqrt(jnp.mean(hidden * hidden, axis=-1, keepdims=True) + epsilon)


def half_turned(block, cosines, sines, direction):
    return block * cosines + direction * (half_turn(block) * sines)


def norm_back(hidden, gain, upstream):
    scale = inverse_rms(hidden)
    weighted = upstream * gain
    inside = jnp.mean(weighted * hidden, axis=-1, keepdims=True)
    gain_row = jnp.sum(upstream * hidden * scale, axis=0, keepdims=True)
    return scale * weighted - hidden * (scale * scale * scale * inside), gain_row


def start_if(condition, here, there):
    @pl.when(condition)
    def _():
        here().start()

    @pl.when(jnp.logical_not(condition))
    def _():
        there().start()


class AttentionBack:
    def __init__(
        self, rank, device_of, qd, kv, o_raw, allowed, cos_sin, ra, pds, dkv, dkv_in, gkv, send, recv
    ):
        self.rank, self.device_of = rank, device_of
        self.qd, self.kv, self.o_raw, self.allowed, self.cos_sin = qd, kv, o_raw, allowed, cos_sin
        self.ra, self.pds, self.dkv, self.dkv_in, self.gkv = ra, pds, dkv, dkv_in, gkv
        self.send_sem, self.recv_sem = send, recv
        self.rows, self.width = ra.shape[1:]

    def head(self, g):
        rows = self.rows
        kv_g = self.kv[g]
        mine = [slice(i * rows, (i + 1) * rows) for i in range(SHARE)]
        other = [slice((SHARE + i) * rows, (SHARE + i + 1) * rows) for i in range(SHARE)]
        all_scores = [dot_rt(self.qd[g, span, :], kv_g) + self.allowed[...] for span in mine]
        for i, scores in enumerate(all_scores):
            kept = self.o_raw[g * SHARE + i]
            probs = jnp.exp(scores - kept[:, 0:1])
            grad_out = self.qd[g, other[i], :]
            grad_probs = dot_rt(grad_out, kv_g)
            weight = jnp.sum(grad_out.astype(F32) * kept, axis=-1, keepdims=True)
            grad_scores = (probs * (grad_probs - weight)).astype(BF16)
            self.pds[mine[i], :] = grad_scores
            self.pds[other[i], :] = probs.astype(BF16)
            self.o_raw[g * SHARE + i] = dot(grad_scores, kv_g)
        grad_kv = dot_lt(self.qd[g], self.pds[...])
        self.dkv[g] = grad_kv.T.astype(BF16)
        self.send(g)

    def heads(self, first, last):
        def body(g, carry):
            self.head(g)

            @pl.when(g > 0)
            def _():
                self.relay(g - 1)

            return carry

        lax.fori_loop(first, last, body, 0)

    def copy(self, quarter, count, dst, slot_in, slot, g):
        rows = self.rows
        return pltpu.make_async_remote_copy(
            src_ref=self.dkv.at[g, pl.ds(quarter * rows, count * rows)],
            dst_ref=self.dkv_in.at[g, pl.ds(slot_in * rows, count * rows)],
            send_sem=self.send_sem.at[slot, g],
            recv_sem=self.recv_sem.at[slot_in, g],
            device_id=self.device_of(dst),
            device_id_type=MESH,
        )

    def add(self, quarter, slots, g):
        rows = self.rows
        span = slice(quarter * rows, (quarter + 1) * rows)
        total = self.dkv[g, span].astype(F32)
        for slot in slots:
            total = total + self.dkv_in[g, slot * rows : (slot + 1) * rows].astype(F32)
        self.dkv[g, span] = total.astype(BF16)

    def send(self, g):
        @pl.when(self.rank == 3)
        def _():
            self.copy(2, 1, 2, 0, 0, g).start()
            self.copy(0, 2, 1, 0, 1, g).start()

        @pl.when(self.rank == 2)
        def _():
            self.copy(1, 1, 1, 2, 0, g).start()
            self.copy(0, 1, 0, 1, 1, g).start()

    def relay(self, g):
        @pl.when(self.rank == 1)
        def _():
            self.copy(0, 2, 1, 0, 0, g).wait_recv()
            self.add(0, (0,), g)
            self.copy(0, 1, 0, 0, 0, g).start()

    def queries(self):
        for at, size in tiles(self.width, 128):
            head = at // HEAD_SIZE
            block = self.o_raw[head]
            if size == 128:
                low = lanes(self.rows) < HEAD_SIZE
                block = jnp.where(low, block, pltpu.roll(self.o_raw[head + 1], 64, 1))
            turned = half_turned(block, self.cos_sin[0], self.cos_sin[1], -1.0) * 0.125
            self.ra[0, :, at : at + size] = turned[:, :size].astype(BF16)

    def collect(self):
        low = lanes(self.rows) < HEAD_SIZE
        cosines = jnp.where(low, self.cos_sin[0], 1.0)
        sines = jnp.where(low, self.cos_sin[1], 0.0)
        mine = pl.ds(pl.multiple_of(self.rank * self.rows, 16), self.rows)
        for g in range(KEY_VALUE_HEADS):
            self.arrive(g)
            block = half_turned(self.dkv[g, mine, :].astype(F32), cosines, sines, -1.0)
            self.gkv[:, 128 * g : 128 * g + 128] = block.astype(BF16)

    def arrive(self, g):
        @pl.when(self.rank == 3)
        def _():
            self.copy(2, 1, 2, 0, 0, g).wait_send()
            self.copy(0, 2, 1, 0, 1, g).wait_send()

        @pl.when(self.rank == 2)
        def _():
            self.copy(0, 1, 2, 0, 0, g).wait_recv()
            self.copy(1, 1, 1, 2, 0, g).wait_send()
            self.copy(0, 1, 0, 1, 1, g).wait_send()
            self.add(2, (0,), g)

        @pl.when(self.rank == 1)
        def _():
            self.copy(0, 1, 2, 2, 0, g).wait_recv()
            self.copy(0, 1, 0, 0, 0, g).wait_send()
            self.add(1, (1, 2), g)

        @pl.when(self.rank == 0)
        def _():
            self.copy(0, 1, 2, 0, 0, g).wait_recv()
            self.copy(0, 1, 2, 1, 0, g).wait_recv()
            self.add(0, (0, 1), g)

    def project(self, total, wq, wkv):
        for at, size in tiles(self.width, 256):
            total[:, at : at + size] = dot_rt(self.ra[0], wq[at : at + size, :]) + dot(
                self.gkv[...], wkv[:, at : at + size]
            )


class OutCopy:
    def __init__(self, out, send, recv):
        self.section, self.dp, ctx = (lax.axis_index(a) for a in ("section", "dp", "ctx"))
        self.home = 2 * self.section + ctx % 2
        self.ctx, self.micro = ctx, ctx // 2
        self.out, self.send, self.recv = out, send, recv

    def here(self, l):
        return (self.section == l) & (self.ctx == self.home)

    def remote(self, array, l):
        return pltpu.make_async_remote_copy(
            src_ref=array,
            dst_ref=self.out.at[0, self.micro],
            send_sem=self.send.at[l],
            recv_sem=self.recv.at[self.micro],
            device_id=(l, self.dp, self.home),
            device_id_type=MESH,
        )

    def local(self, array):
        return pltpu.make_async_copy(array, self.out.at[0, self.micro], self.recv.at[self.micro])

    def start(self, array, l):
        start_if(self.here(l), lambda: self.local(array), lambda: self.remote(array, l))

    def sent(self, array, l):
        @pl.when(jnp.logical_not(self.here(l)))
        def _():
            self.remote(array, l).wait_send()

    def arrived(self, array):
        for block in range(2):
            pltpu.make_async_copy(array, self.out.at[0, block], self.recv.at[block]).wait()


def greet(barrier, dp):
    section, ctx = lax.axis_index("section"), lax.axis_index("ctx")
    for step in range(1, 8):
        other = (4 * section + ctx + step) % 8
        pl.semaphore_signal(
            barrier, inc=1, device_id=(other // 4, dp, other % 4), device_id_type=MESH
        )


def layers_kernel(complete, *refs):
    refs = list(refs)

    def take(count):
        taken = refs[:count]
        del refs[:count]
        return taken

    lengths, ends, frequency, gain_a, gain_f, wq_h, wk_h, wv_h, wo_h, wg_h, wu_h, wd_h = take(12)
    acts_o, grads_o, gain_o, nf_o, in_o, gg_o, gu_o, br_o, la_o, ra_o, nr_o, kvg_o = take(12)
    kept_o = [] if complete else take(7)
    wq, wkv, wo, wg, wu, wd = take(6)
    act, go, middle, norm_ffn, fact_a, fact_b, inner, lm, qd, kv, o_raw = take(11)
    sum_acc, gm, gg, gu, br, ra, pds, dkv, dkv_in, gkv, cos_sin, allowed_add, gain_v = take(13)
    w_sem, kv_sem, in_send, in_recv, kv_send, kv_recv, dk_send, dk_recv = take(8)
    act_send, act_recv, grad_send, grad_recv, op_own, op_send, op_recv, kept_sem = take(8)

    section = lax.axis_index("section")
    dp = lax.axis_index("dp")
    ctx = lax.axis_index("ctx")
    micro = ctx // 2
    xbit = ctx % 2
    rank = 2 * section + xbit
    rows, width = act.shape[1], act.shape[2]
    ff = wg.shape[1]
    ff_half = ff // 2

    def device_of(r):
        return (r // 2, dp, 2 * micro + r % 2)

    partner = (1 - section, dp, ctx)

    loads = [
        pltpu.make_async_copy(h, v, w_sem.at[i])
        for i, (h, v) in enumerate([(wq_h, wq), (wo_h, wo), (wg_h, wg), (wu_h, wu), (wd_h, wd)])
    ]
    kv_loads = [
        pltpu.make_async_copy(
            h.at[pl.ds(g * HEAD_SIZE, HEAD_SIZE)],
            wkv.at[pl.ds((2 * g + i) * HEAD_SIZE, HEAD_SIZE)],
            kv_sem.at[i, g],
        )
        for g in range(KEY_VALUE_HEADS)
        for i, h in enumerate((wk_h, wv_h))
    ]
    for load in kv_loads + loads:
        load.start()
    kv[...] = jnp.zeros_like(kv)
    barrier = pltpu.get_barrier_semaphore()
    greet(barrier, dp)
    pl.semaphore_wait(barrier, 7)

    def in_local(block, into_x):
        dst, slot = (act.at[0], 0) if into_x else (go.at[2], 1)
        return pltpu.make_async_copy(ends.at[0, block], dst, in_recv.at[slot])

    def in_remote(block, into_x):
        dst, slot = (act.at[0], 0) if into_x else (go.at[2], 1)
        return pltpu.make_async_remote_copy(
            src_ref=ends.at[0, block],
            dst_ref=dst,
            send_sem=in_send.at[block],
            recv_sem=in_recv.at[slot],
            device_id=(ctx // 2, dp, 2 * block + xbit),
            device_id_type=MESH,
        )

    def in_mine(block):
        return (section == ctx // 2) & (ctx // 2 == block)

    def in_start(into_x):
        @pl.when(section == (0 if into_x else 1))
        def _():
            for block in range(2):
                start_if(
                    in_mine(block),
                    lambda block=block: in_local(block, into_x),
                    lambda block=block: in_remote(block, into_x),
                )

    in_start(True)
    lane = lanes(rows)
    low = lane < HEAD_SIZE
    gain_attn = gain_a[...].astype(F32).reshape(1, width)
    gain_ffn = gain_f[...].astype(F32).reshape(1, width)

    def place(token_index):
        segment = jnp.zeros_like(token_index)
        start = jnp.zeros_like(token_index)
        finish = jnp.int32(0)
        for slot in range(lengths.shape[2]):
            length = lengths[micro, 0, slot]
            finish = finish + length
            passed = (token_index >= finish).astype(jnp.int32)
            segment = segment + passed
            start = start + passed * length
        return segment, token_index - start

    seg_mine, position = place(rank * rows + lax.broadcasted_iota(jnp.int32, (rows, 128), 0))
    angles = position.astype(F32) * frequency[...]
    cos_sin[0] = jnp.cos(angles)
    cos_sin[1] = jnp.where(lane % HEAD_SIZE < HEAD_SIZE // 2, -1.0, 1.0) * jnp.sin(angles)
    key_index = lax.broadcasted_iota(jnp.int32, (1, RANKS * rows), 1)
    query_index = rank * rows + lax.broadcasted_iota(jnp.int32, (rows, 1), 0)
    allowed_add[...] = jnp.where(
        (seg_mine[:, 0:1] == place(key_index)[0]) & (query_index >= key_index), 0.0, masked_fill
    )

    def kv_rows(l, r, g):
        return kv.at[l, g, pl.ds(pl.multiple_of(r * rows, 16), rows)]

    def kv_copy(l, quarter, dst, slot, g):
        return pltpu.make_async_remote_copy(
            src_ref=kv_rows(l, quarter, g),
            dst_ref=kv_rows(l, quarter, g),
            send_sem=kv_send.at[l, slot, g],
            recv_sem=kv_recv.at[l, quarter, g],
            device_id=device_of(dst),
            device_id_type=MESH,
        )

    def kv_start(l, g):
        @pl.when(rank < 3)
        def _():
            kv_copy(l, rank, rank + 1, 0, g).start()

        @pl.when(rank < 2)
        def _():
            kv_copy(l, rank, rank + 2, 1, g).start()

    def kv_relayed(l, g):
        @pl.when(rank == 1)
        def _():
            kv_copy(l, 0, 3, 2, g).wait_recv()
            kv_copy(l, 0, 3, 2, g).start()

    def kv_finish(l, g):
        @pl.when(rank >= 2)
        def _():
            kv_copy(l, 0, 0, 0, g).wait_recv()
            kv_copy(l, 1, 0, 0, g).wait_recv()

        @pl.when(rank == 3)
        def _():
            kv_copy(l, 2, 0, 0, g).wait_recv()

    def kv_sent(l):
        for senders, slot in ((3, 0), (2, 1)):

            @pl.when(rank < senders)
            def _(slot=slot):
                for g in range(KEY_VALUE_HEADS):
                    kv_copy(l, rank, rank + 1 + slot, slot, g).wait_send()

        @pl.when(rank == 1)
        def _():
            for g in range(KEY_VALUE_HEADS):
                kv_copy(l, 0, 3, 2, g).wait_send()

    acts_out = OutCopy(acts_o, act_send, act_recv)
    grads_out = OutCopy(grads_o, grad_send, grad_recv)

    def op_copy(kind, l, own):
        role = section if own else 1 - section
        half = pl.ds(pl.multiple_of(role * ff_half, 128), ff_half)
        src = [
            lambda: norm_ffn.at[l],
            lambda: inner.at[l],
            lambda: gg.at[:, half],
            lambda: gu.at[:, half],
            lambda: br.at[:, pl.ds(pl.multiple_of(role * 512, 128), 512)],
            lambda: lm.at[l, role],
            lambda: ra.at[role],
            lambda: lm.at[l, 0],
            lambda: gkv.at[:, pl.ds(pl.multiple_of(role * 256, 128), 384)],
        ][kind]()
        block = section if kind in (6, 8) and not complete else 2 * section + l
        dst = [nf_o, in_o, gg_o, gu_o, br_o, la_o, ra_o, nr_o, kvg_o][kind].at[
            pl.ds(pl.multiple_of(block * rows, 16), rows)
        ]
        if own:
            return pltpu.make_async_copy(src, dst, op_own.at[kind, l])
        return pltpu.make_async_remote_copy(
            src_ref=src,
            dst_ref=dst,
            send_sem=op_send.at[kind, l],
            recv_sem=op_recv.at[kind, l],
            device_id=partner,
            device_id_type=MESH,
        )

    def op_start(kinds, l):
        for kind in kinds:
            op_copy(kind, l, True).start()
            op_copy(kind, l, False).start()

    def op_sent(kinds, l):
        for kind in kinds:
            op_copy(kind, l, True).wait()
            op_copy(kind, l, False).wait_send()

    def kept_copy(i):
        if i == 7:
            part = pl.ds(0, SHARE * rows)
            return pltpu.make_async_copy(qd.at[0, :, part], kept_o[5].at[:, part], kept_sem.at[8])
        if i == 5:
            part = pl.ds(SHARE * rows, SHARE * rows)
            return pltpu.make_async_copy(qd.at[0, :, part], kept_o[5].at[:, part], kept_sem.at[5])
        src = [act.at[0], kv.at[0], o_raw.at[0], cos_sin, allowed_add, None, gm][i]
        return pltpu.make_async_copy(src, kept_o[i], kept_sem.at[i])

    def kept_start(*which):
        if not complete:
            for i in which:
                kept_copy(i).start()

    in_remote(0, True).wait_recv()
    for load in kv_loads:
        load.wait()

    def forward(l, carry):
        hidden = act[l].astype(F32)
        cos_q, sin_q = cos_sin[0], cos_sin[1]
        lm[l, 0] = (hidden * inverse_rms(hidden) * gain_attn).astype(BF16)
        cos_kv = jnp.where(low, cos_q, 1.0)
        sin_kv = jnp.where(low, sin_q, 0.0)
        mine = pl.ds(pl.multiple_of(rank * rows, 16), rows)
        for g in range(KEY_VALUE_HEADS):
            block = dot_rt(lm[l, 0], wkv[128 * g : 128 * g + 128, :])
            turned = half_turned(block, cos_kv, sin_kv, 1.0)
            kv[l, g, mine, :] = turned.astype(BF16)
        for g in range(KEY_VALUE_HEADS):
            kv_start(l, g)

        @pl.when(l == 0)
        def _():
            loads[0].wait()
            in_start(False)
            kept_start(0, 3, 4)

        for at, size in tiles(width, 256):
            product = dot(lm[l, 0], wq[:, at : at + size])
            for inside, part in tiles(size, 128):
                block = wide(product[:, inside : inside + part])
                turned = half_turned(block, cos_q, sin_q, 1.0) * 0.125
                head = (at + inside) // HEAD_SIZE
                qd[l, head // SHARE, pl.ds(head % SHARE * rows, rows), :] = jnp.where(
                    low, turned, 0.0
                ).astype(BF16)
                head += 1
                if head < QUERY_HEADS:
                    qd[l, head // SHARE, pl.ds(head % SHARE * rows, rows), :] = jnp.where(
                        low, pltpu.roll(turned, 64, 1), 0.0
                    ).astype(BF16)
        kv_relayed(l, 0)
        kv_finish(l, 0)

        def heads(g, carry):
            @pl.when(g < KEY_VALUE_HEADS - 1)
            def _():
                kv_relayed(l, g + 1)

            @pl.when(g > 0)
            def _():
                kv_finish(l, g)

            kv_g = kv[l, g]
            all_scores = [
                dot_rt(qd[l, g, i * rows : (i + 1) * rows, :], kv_g) + allowed_add[...]
                for i in range(SHARE)
            ]
            for i, scores in enumerate(all_scores):
                peak = jnp.max(scores, axis=-1, keepdims=True)
                exponent = jnp.exp(scores - peak)
                total = jnp.sum(exponent, axis=-1, keepdims=True)
                out = dot(exponent.astype(BF16), kv_g) * (1.0 / total)
                o_raw[l, g * SHARE + i] = jnp.where(low, peak + jnp.log(total), out)
            return carry

        lax.fori_loop(0, KEY_VALUE_HEADS, heads, 0)

        @pl.when(l == 0)
        def _():
            kept_start(1, 2, 7)
            loads[1].wait()

        for at, size in tiles(width, 128):
            head = at // HEAD_SIZE
            block = pltpu.roll(o_raw[l, head], 64, 1)
            if size == 128:
                block = jnp.where(low, block, o_raw[l, head + 1])
            lm[l, 1, :, at : at + size] = block[:, :size].astype(BF16)
        for at, size in tiles(width, 256):
            middle[l, :, at : at + size] = act[l, :, at : at + size].astype(F32) + dot(
                lm[l, 1], wo[:, at : at + size]
            )
        mid = middle[l]
        norm_ffn[l] = (mid * inverse_rms(mid) * gain_ffn).astype(BF16)
        op_start((0, 5, 7), l)

        @pl.when(l == 0)
        def _():
            loads[2].wait()
            loads[3].wait()

        def gates(j, carry):
            part = pl.ds(pl.multiple_of(j * 1280, 128), 1280)
            gate = dot(norm_ffn[l], wg[:, part])
            upper = dot(norm_ffn[l], wu[:, part])
            s = 0.5 * jnp.tanh(0.5 * gate) + 0.5
            swish = gate * s
            inner[l, :, part] = (swish * upper).astype(BF16)
            fact_a[l, :, part] = (upper * s * (1.0 + gate * (1.0 - s))).astype(BF16)
            fact_b[l, :, part] = swish.astype(BF16)
            return carry

        lax.fori_loop(0, ff // 1280, gates, 0)

        @pl.when(l == 0)
        def _():
            loads[4].wait()

        op_start((1,), l)
        for at, size in tiles(width, 256):
            act[l + 1, :, at : at + size] = (
                middle[l, :, at : at + size] + dot_rt(inner[l], wd[at : at + size, :])
            ).astype(BF16)
        acts_out.start(act.at[l + 1], l)
        kv_sent(l)
        return carry

    lax.fori_loop(0, 2, forward, 0)

    in_remote(0, False).wait_recv()
    gain_v[...] = jnp.zeros_like(gain_v)
    br[...] = jnp.zeros_like(br)
    late = (6, 8)

    def backward(step, carry):
        l = 1 - step

        @pl.when(l == 0)
        def _():
            op_sent((2, 3, 4) + (late if complete else ()), 1)

        br[:, :width] = go[l + 1]
        op_start((4,), l)

        def gates(j, carry):
            part = pl.ds(pl.multiple_of(j * 1280, 128), 1280)
            grad_inner = dot(go[l + 1], wd[:, part])
            gg[:, part] = (grad_inner * fact_a[l, :, part].astype(F32)).astype(BF16)
            gu[:, part] = (grad_inner * fact_b[l, :, part].astype(F32)).astype(BF16)
            return carry

        lax.fori_loop(0, ff // 1280, gates, 0)
        op_start((2, 3), l)
        for at, size in tiles(width, 256):
            sum_acc[:, at : at + size] = dot_rt(gg[...], wg[at : at + size, :]) + dot_rt(
                gu[...], wu[at : at + size, :]
            )
        grad, gain_row = norm_back(middle[l], gain_ffn, sum_acc[...])
        gain_v[1:2, :] += gain_row
        gm[...] = go[l + 1].astype(F32) + grad
        ra[1] = gm[...].astype(BF16)

        @pl.when(l == 0)
        def _():
            kept_start(6)

        for at, size in tiles(width, 256):
            product = dot_rt(ra[1], wo[at : at + size, :])
            for inside, part in tiles(size, 128):
                block = wide(product[:, inside : inside + part])
                head = (at + inside) // HEAD_SIZE
                qd[l, head // SHARE, pl.ds((SHARE + head % SHARE) * rows, rows), :] = jnp.where(
                    low, 0.0, pltpu.roll(block, 64, 1)
                ).astype(BF16)
                head += 1
                if head < QUERY_HEADS:
                    qd[l, head // SHARE, pl.ds((SHARE + head % SHARE) * rows, rows), :] = (
                        jnp.where(low, 0.0, block).astype(BF16)
                    )

        def attention():
            back = AttentionBack(
                rank, device_of, qd.at[l], kv.at[l], o_raw.at[l], allowed_add, cos_sin, ra, pds,
                dkv, dkv_in.at[l] if complete else dkv_in, gkv,
                dk_send.at[l] if complete else dk_send, dk_recv.at[l] if complete else dk_recv,
            )
            back.heads(0, KEY_VALUE_HEADS)
            back.relay(KEY_VALUE_HEADS - 1)
            back.queries()
            op_start((6,), l)
            back.collect()
            op_start((8,), l)
            back.project(sum_acc, wq, wkv)
            grad, gain_row = norm_back(act[l].astype(F32), gain_attn, sum_acc[...])
            gain_v[0:1, :] += gain_row
            go[l] = (gm[...] + grad).astype(BF16)
            grads_out.start(go.at[l], l)

        if complete:
            attention()
        else:

            @pl.when(l == 1)
            def _():
                attention()

            @pl.when(l == 1)
            def _():
                op_sent(late, 1)

        return carry

    lax.fori_loop(0, 2, backward, 0)

    gain_copy = pltpu.make_async_copy(gain_v, gain_o, kept_sem.at[7])
    gain_copy.start()
    kept_start(5)
    for into_x in (True, False):

        @pl.when(section == (0 if into_x else 1))
        def _(into_x=into_x):
            for block in range(2):

                @pl.when(jnp.logical_not(in_mine(block)))
                def _(block=block):
                    in_remote(block, into_x).wait_send()

    op_sent((2, 3, 4) + (late if complete else ()), 0)
    for l in range(2):
        op_sent((0, 1, 5, 7), l)
        for kind in range(9):
            if l == 1 or complete or kind not in late:
                op_copy(kind, l, False).wait_recv()
        acts_out.sent(act.at[l + 1], l)
        if l == 1 or complete:
            grads_out.sent(go.at[l], l)
    gain_copy.wait()
    acts_out.arrived(act.at[0])
    if complete:
        grads_out.arrived(act.at[0])
    else:

        @pl.when(section == 1)
        def _():
            grads_out.arrived(act.at[0])

        for i in range(len(kept_o) + 1):
            kept_copy(i).wait()


def run_layers(lengths, ends, frequency, gain_attn, gain_ffn, weights, complete):
    micro_count, rows, width = ends.shape[1:]
    wq, wk, wv, wo, wg, wu, wd = weights
    ff = wg.shape[1]
    keys = RANKS * rows
    kv_width = 2 * wk.shape[0]
    vmem, hbm = pl.BlockSpec(memory_space=pltpu.VMEM), pl.BlockSpec(memory_space=pl.ANY)
    op_rows = 4 * rows
    late_rows = op_rows if complete else 2 * rows
    out = lambda *shape: jax.ShapeDtypeStruct(shape, BF16)
    out_f = lambda *shape: jax.ShapeDtypeStruct(shape, F32)
    dma = lambda *shape: pltpu.SemaphoreType.DMA(shape)
    kept = [
        out(rows, width),
        out(KEY_VALUE_HEADS, keys, 128),
        out_f(QUERY_HEADS, rows, 128),
        out_f(2, rows, 128),
        out_f(rows, keys),
        out(KEY_VALUE_HEADS, 2 * SHARE * rows, 128),
        out_f(rows, width),
    ]
    layers = (2,) if complete else ()
    return pl.pallas_call(
        lambda *refs: layers_kernel(complete, *refs),
        out_shape=[
            out(*ends.shape),
            out(*ends.shape),
            out_f(8, width),
            out(op_rows, width),
            out(op_rows, ff),
            out(op_rows, ff // 2),
            out(op_rows, ff // 2),
            out(op_rows, 512),
            out(op_rows, width),
            out(late_rows, width),
            out(op_rows, width),
            out(late_rows, 384),
        ]
        + ([] if complete else kept),
        in_specs=[pl.BlockSpec(memory_space=pltpu.SMEM), hbm] + [vmem] * 3 + [hbm] * 7,
        out_specs=[hbm] * (12 if complete else 19),
        scratch_shapes=[
            pltpu.VMEM(wq.shape, BF16),
            pltpu.VMEM((kv_width, width), BF16),
            pltpu.VMEM(wo.shape, BF16),
            pltpu.VMEM(wg.shape, BF16),
            pltpu.VMEM(wu.shape, BF16),
            pltpu.VMEM(wd.shape, BF16),
            pltpu.VMEM((3, rows, width), BF16),
            pltpu.VMEM((3, rows, width), BF16),
            pltpu.VMEM((2, rows, width), F32),
            pltpu.VMEM((2, rows, width), BF16),
            pltpu.VMEM((2, rows, ff), BF16),
            pltpu.VMEM((2, rows, ff), BF16),
            pltpu.VMEM((2, rows, ff), BF16),
            pltpu.VMEM((2, 2, rows, width), BF16),
            pltpu.VMEM((2, KEY_VALUE_HEADS, 2 * SHARE * rows, 128), BF16),
            pltpu.VMEM((2, KEY_VALUE_HEADS, keys, 128), BF16),
            pltpu.VMEM((2, QUERY_HEADS, rows, 128), F32),
            pltpu.VMEM((rows, width), F32),
            pltpu.VMEM((rows, width), F32),
            pltpu.VMEM((rows, ff), BF16),
            pltpu.VMEM((rows, ff), BF16),
            pltpu.VMEM((rows, 1024), BF16),
            pltpu.VMEM((2, rows, width), BF16),
            pltpu.VMEM((2 * SHARE * rows, keys), BF16),
            pltpu.VMEM((KEY_VALUE_HEADS, keys, 128), BF16),
            pltpu.VMEM(layers + (KEY_VALUE_HEADS, 3 * rows, 128), BF16),
            pltpu.VMEM((rows, kv_width), BF16),
            pltpu.VMEM((2, rows, 128), F32),
            pltpu.VMEM((rows, keys), F32),
            pltpu.VMEM((8, width), F32),
            dma(5),
            dma(2, KEY_VALUE_HEADS),
            dma(2),
            dma(2),
            dma(2, 3, KEY_VALUE_HEADS),
            dma(2, 3, KEY_VALUE_HEADS),
            dma(*layers, 2, KEY_VALUE_HEADS),
            dma(*layers, 3, KEY_VALUE_HEADS),
            dma(2),
            dma(2),
            dma(2),
            dma(2),
            dma(9, 2),
            dma(9, 2),
            dma(9, 2),
            dma(len(kept) + 2),
        ],
        compiler_params=pltpu.CompilerParams(
            collective_id=1, has_side_effects=True, vmem_limit_bytes=61 * 2**20
        ),
        name="layers",
    )(lengths, ends, frequency, gain_attn, gain_ffn, *weights)


MIDDLE_ORDER = (
    "near1", "head0", "head1", "head2", "head3", "near3", "down0", "head4",
    "down1", "far1", "query0", "near0", "far3", "near2", "aend0", "tready0",
    "far0", "fadd1", "down2", "fadd3", "tnear3", "tnear1", "down3", "down4",
    "far2", "fadd0", "down5", "fz0", "tnear0", "tnear2", "fadd2", "dfirst0",
    "tfar3", "fz1", "tfar0", "tfar2", "fz2", "tfar1", "tadd0", "dsecond0",
    "ftotal0", "tadd2", "tadd3", "dgather0", "tz0", "tz1", "tadd1", "tz2",
    "fmiddle0", "ttotal0", "dmiddle0",
)
END_ORDER = (
    "near0", "down0", "head0", "head1", "down1", "near1", "head2", "head3",
    "head4", "far0", "near3", "down2", "query0", "far1", "down3", "down4",
    "near2", "aend0", "fadd0", "tready0", "down5", "fadd1", "fz0", "tnear3",
    "far3", "far2", "tnear0", "fadd3", "fz2", "tnear2", "fadd2", "tnear1",
    "fz1", "tfar3", "tfar0", "dfirst0", "tadd0", "tfar2", "tfar1", "tadd3",
    "tz0", "dsecond0", "tadd1", "tz2", "ftotal0", "tadd2", "tz1", "dgather0",
    "fmiddle0", "ttotal0", "dmiddle0",
)


def sums_kernel(*refs):
    refs = list(refs)

    def take(count):
        taken = refs[:count]
        del refs[:count]
        return taken

    gain_h, gain_a, nf_h, in_h, gg_h, gu_h, br_h, la_h, ra_h, nr_h, kvg_h = take(11)
    act_h, kv_h, o_h, cs_h, allowed_h, qd_h, gm_h, wq_h, wk_h, wv_h = take(10)
    grads_o, t_o, gate_o, up_o, down_o = take(5)
    stage, in_v, br_v, gg_v, gu_v, ra_v, kvg_v, nf_t, ln_t, in_t, gain_t = take(11)
    act, kv, o_raw, cos_sin, allowed, qd, gm, wq, wkv = take(9)
    go, ra, dkv, dkv_in, gkv, sum_acc, gain_rows = take(7)
    d_out, d_in, d_keep, d1_out, d1_in, d2_out, d2_in = take(7)
    f1_out, f1_in, f2_out, f2_in, f_keep, fz_in = take(6)
    t1_out, t1_in, t2_out, t2_in, t_keep, tz_in = take(6)
    d_all, f_all, t_all = take(3)
    load, kept_sem, w_sem, dk_s, dk_r, grad_s, grad_r, op_own, op_s, op_r = take(10)
    dz_s, dz_r, d1_s, d1_r, d2_s, d2_r, f1_s, f1_r, f2_s, f2_r, fz_s, fz_r = take(12)
    t1_s, t1_r, t2_s, t2_r, tz_s, tz_r, all_s, all_r, pair_r, write = take(10)

    section = lax.axis_index("section")
    z = lax.axis_index("dp")
    ctx = lax.axis_index("ctx")
    x, y = ctx % 2, ctx // 2
    rank = 2 * section + x
    x_next = (section, z, 2 * y + 1 - x)
    y_next = (section, z, 2 * (1 - y) + x)
    partner = (1 - section, z, ctx)
    rows = act.shape[0]
    width = nf_h.shape[1]
    per = width // RANKS
    part = f_keep.shape[2]
    shift = per - part
    quarter = gg_v.shape[1] // 2
    deep = in_t.shape[0]
    fine = deep // 2
    last = RANKS - 1
    edge = ((z == 0) | (z == last)).astype(jnp.int32)

    def pick(index, values):
        if isinstance(index, int):
            return values[index]
        return sum((index == i).astype(jnp.int32) * v for i, v in enumerate(values) if not (type(v) is int and v == 0))

    def remote(src, dst, send, recv, device):
        return pltpu.make_async_remote_copy(
            src_ref=src, dst_ref=dst, send_sem=send, recv_sem=recv,
            device_id=device, device_id_type=MESH,
        )

    def some(start, size, unit=16):
        return pl.ds(pl.multiple_of(start, unit), size)

    gain_load = pltpu.make_async_copy(gain_h, gain_rows.at[pl.ds(0, gain_h.shape[0])], load.at[9])
    by_need = ((3, 2, 1, 0), (3, 0, 2, 1), (0, 3, 1, 2), (0, 1, 2, 3))
    by_turns = ((3, 2, 1, 0), (3, 0, 2, 1), (0, 3, 1, 2), (0, 2, 1, 3))

    def turn_of(k, order=by_need):
        return pick(k, [pick(z, [row[i] for row in order]) for i in range(RANKS)])

    def in_load(k):
        return pltpu.make_async_copy(
            in_h.at[:, some(turn_of(k) * deep, deep, 128)], in_v, load.at[0]
        )

    loads = [None] + [
        pltpu.make_async_copy(h, v, load.at[1 + i])
        for i, (h, v) in enumerate(
            [(br_h, br_v), (nf_h, stage), (la_h, stage), (nr_h, stage)]
        )
    ]
    halves = [
        [
            pltpu.make_async_copy(h.at[:, span], v.at[:, span], load.at[slot + 2 * own])
            for h, v, first, slot in ((gg_h, gg_v, x, 5), (gu_h, gu_v, y, 6))
            for span in (some((own * first + (1 - own) * (1 - first)) * quarter, quarter, 128),)
        ]
        for own in range(2)
    ]
    kept = [
        pltpu.make_async_copy(h, v, kept_sem.at[i])
        for i, (h, v) in enumerate(
            [(qd_h, qd), (kv_h, kv), (o_h, o_raw), (allowed_h, allowed), (cs_h, cos_sin),
             (gm_h, gm), (act_h, act)]
        )
    ]
    late = [
        pltpu.make_async_copy(h.at[pl.ds(c * rows, rows)], v.at[pl.ds((2 * c + 1) * rows, rows)], w_sem.at[i, c])
        for i, (h, v) in enumerate([(ra_h, ra_v), (kvg_h, kvg_v)])
        for c in range(2)
    ]
    weights = [pltpu.make_async_copy(wq_h, wq, w_sem.at[2, 0])] + [
        pltpu.make_async_copy(
            h.at[pl.ds(g * HEAD_SIZE, HEAD_SIZE)],
            wkv.at[pl.ds((2 * g + i) * HEAD_SIZE, HEAD_SIZE)],
            w_sem.at[3 + i, g],
        )
        for g in range(KEY_VALUE_HEADS)
        for i, h in enumerate((wk_h, wv_h))
    ]
    loads[2].start()
    for copy in halves[0]:
        copy.start()
    gain_rows[...] = jnp.zeros_like(gain_rows)

    barrier = pltpu.get_barrier_semaphore()
    greet(barrier, z)
    not_first = (z > 0).astype(jnp.int32)
    not_last = (z < last).astype(jnp.int32)

    @pl.when(z > 0)
    def _():
        pl.semaphore_signal(barrier, inc=1, device_id=(section, z - 1, ctx), device_id_type=MESH)

    @pl.when(z < last)
    def _():
        pl.semaphore_signal(barrier, inc=1, device_id=(section, z + 1, ctx), device_id_type=MESH)

    def turn(src, dst, base=0):
        for at, size in tiles(src.shape[1], 128):
            block = src[:, at : at + size]
            if size < 128:
                block = wide(block)
            dst[base + at : base + at + size, :] = block.T[:size]

    def z_way(t):
        up = (z < t).astype(jnp.int32)
        to = z + 2 * up - 1
        arrives = up * not_first + (1 - up) * not_last
        meets = (1 - up) * (t == z - 1).astype(jnp.int32)
        return (section, to, ctx), arrives, t * (1 - meets) + RANKS * meets

    def d_block(k):
        in_load(k).wait()
        for b in range(deep // 128):
            in_t[b * 128 : (b + 1) * 128, :] = in_v[:, b * 128 : (b + 1) * 128].T

        if not isinstance(k, int):

            @pl.when(k < last)
            def _():
                in_load(k + 1).start()

    def d_send(k, sub):
        device, _, slot = z_way(turn_of(k))
        span = some(sub * fine, fine)
        return remote(d_out.at[k, span], d_in.at[slot, span], dz_s.at[k, sub], dz_r.at[slot, sub], device)

    def d_step(n):
        k, sub = n // 2, n % 2

        @pl.when(n == 0)
        def _():
            loads[1].wait()

        @pl.when(sub == 0)
        def _():
            d_block(k)

        t = turn_of(k)
        _, arrives, _ = z_way(t)
        span = some(sub * fine, fine)
        mine = dot(in_t[span, :], br_v[...])

        @pl.when(arrives == 0)
        def _():
            d_out[k, span, :] = mine.astype(BF16)

        @pl.when(arrives == 1)
        def _():
            remote(d_out.at[k, span], d_in.at[t, span], dz_s.at[k, sub], dz_r.at[t, sub], partner).wait_recv()
            d_out[k, span, :] = (mine + d_in[t, span, :].astype(F32)).astype(BF16)

        d_send(k, sub).start()

    def f_links(k):
        return (x_next, y_next, x, y) if k == 0 else (y_next, x_next, y, x)

    def f_right(k, column_half):
        src = gg_v if k == 0 else gu_v
        return src[:, some(column_half * quarter, quarter, 128)]

    turns = (3, 0, 2, 1)

    def f1_copy(k, i):
        d = pick(i, turns)
        return remote(f1_out.at[k, i % 2], f1_in.at[k, d], f1_s.at[k, i % 2], f1_r.at[k, d], f_links(k)[0])

    def f2_copy(k, i):
        d = pick(i, turns)
        return remote(f2_out.at[k, i % 2], f2_in.at[k, d], f2_s.at[k, i % 2], f2_r.at[k, d], f_links(k)[1])

    def f1_step(i):
        left = nf_t[some(pick(i, turns) * per, per), :]
        for k in range(2):
            value = dot(left, f_right(k, 1 - f_links(k)[2])).astype(BF16)

            @pl.when(i >= 2)
            def _():
                f1_copy(k, i).wait_send()

            f1_out[k, i % 2] = value
            f1_copy(k, i).start()

    def f2_step(i):
        d = pick(i, turns)
        for k in range(2):
            first, second = f_links(k)[2:]
            f1_copy(k, i).wait_recv()

            def total(which):
                return (
                    dot(nf_t[some(d * per + which * shift, part), :], f_right(k, first))
                    + f1_in[k, d, some(which * shift, part), :].astype(F32)
                ).astype(BF16)

            value = total(1 - second)

            @pl.when(i >= 2)
            def _():
                f2_copy(k, i).wait_send()

            f2_out[k, i % 2] = value
            f2_copy(k, i).start()
            f_keep[k, d] = total(second)

    def t_links(d):
        x_first = (d < RANKS // 2) * 1
        choose = lambda a, b: x_first * a + (1 - x_first) * b
        ways = [tuple(choose(a, b) for a, b in zip(*pair)) for pair in ((x_next[1:], y_next[1:]), (y_next[1:], x_next[1:]))]
        return (section, *ways[0]), (section, *ways[1]), choose(x, y), choose(y, x)

    def t_product(row, count, add, dst):
        full = width // 128 * 128
        mine = dot(ln_t[some(row, count), :], ra_v[...])
        dst[:, :full] = add(mine[:, :full], 0).astype(BF16)
        tail = jnp.concatenate([mine[:, full:], gain_t[some(row, count), width - full :]], axis=1)
        dst[:, full : full + 128] = add(tail, full).astype(BF16)
        pairs = dot(ln_t[some(width + row, count), :], kvg_v[...])
        dst[:, full + 128 :] = add(pairs, full + 128).astype(BF16)

    def t1_copy(d):
        return remote(t1_out.at[d], t1_in.at[d], t1_s.at[d], t1_r.at[d], t_links(d)[0])

    def t2_copy(d):
        return remote(t2_out.at[d], t2_in.at[d], t2_s.at[d], t2_r.at[d], t_links(d)[1])

    def t1_step(d):
        first = t_links(d)[2]
        t_product(d * per + (1 - first) * shift, part, lambda v, at: v, t1_out.at[d])
        t1_copy(d).start()

    def t2_step(d):
        _, _, first, second = t_links(d)
        t1_copy(d).wait_recv()
        for which, dst in ((1 - second, t2_out), (second, t_keep)):
            row = which * (part // 2)
            add = lambda v, at: v + t1_in[d, some(row, part // 2), at : at + v.shape[1]].astype(F32)
            t_product(d * per + first * shift + row, part // 2, add, dst.at[d])
            if dst is t2_out:
                t2_copy(d).start()

    class Line:
        def __init__(self, keep, second_in, z_in, send, recv):
            self.keep, self.second_in, self.z_in, self.send, self.recv = keep, second_in, z_in, send, recv

        def add(self, copy, d):
            copy.wait_recv()
            self.keep[d] = (self.keep[d].astype(F32) + self.second_in[d].astype(F32)).astype(BF16)

        def copy(self, k):
            d = turn_of(k, by_turns)
            device, _, slot = z_way(d)
            return remote(self.keep.at[d], self.z_in.at[slot], self.send.at[k], self.recv.at[slot], device)

        def step(self, k):
            d = turn_of(k, by_turns)
            _, arrives, _ = z_way(d)

            @pl.when(arrives == 1)
            def _():
                remote(self.keep.at[d], self.z_in.at[d], self.send.at[k], self.recv.at[d], partner).wait_recv()
                self.keep[d] = (self.keep[d].astype(F32) + self.z_in[d].astype(F32)).astype(BF16)

            self.copy(k).start()

        def total(self):
            for condition, slot in ((z > 0, z), (z < last, RANKS)):

                @pl.when(condition)
                def _(slot=slot):
                    remote(self.keep.at[0], self.z_in.at[slot], self.send.at[0], self.recv.at[slot], partner).wait_recv()

            value = self.keep[z].astype(F32)
            return z_total(value, self.z_in[z], self.z_in[RANKS])

    def z_total(value, up, down):
        value = value + jnp.where(z > 0, up.astype(F32), 0.0)
        return value + jnp.where(z < last, down.astype(F32), 0.0)

    lines = [
        Line(f_keep.at[k], f2_in.at[k], fz_in.at[k], fz_s.at[k], fz_r.at[k]) for k in range(2)
    ] + [Line(t_keep, t2_in, tz_in, tz_s, tz_r)]

    def f_add(i):
        for k in range(2):
            lines[k].add(f2_copy(k, i), pick(i, turns))

    def t_add(d):
        lines[2].add(t2_copy(d), d)

    def f_line(k):
        lines[0].step(k)
        lines[1].step(k)

    def places(x_first):
        a, b = (1, 0) if x_first is True else (0, 1) if x_first is False else (x_first, 1 - x_first)
        spot = lambda i, j: a * (2 * i + j) + b * (2 * j + i)
        return spot(x, y), spot(1 - x, y), spot(x, 1 - y), spot(1 - x, 1 - y)

    class Gather:
        def __init__(self, number, buffer, x_first):
            self.n, self.buffer = number, buffer
            self.own, self.over_x, self.over_y, self.across = places(x_first)
            size = buffer.shape[2]
            cut = (size // 2 + 15) // 16 * 16
            self.halves = (pl.ds(0, cut), pl.ds(cut, size - cut))

        def whole(self, spot, slot, device):
            ref = self.buffer.at[section, spot]
            return remote(ref, ref, all_s.at[self.n, slot], all_r.at[self.n, slot], device)

        def relay(self, spot, half, device):
            ref = self.buffer.at[section, spot, self.halves[half]]
            return remote(ref, ref, all_s.at[self.n, 2 + half], all_r.at[self.n, 2 + half], device)

        def pair(self, core, spot, slot):
            ref = self.buffer.at[core, spot]
            return remote(ref, ref, all_s.at[self.n, 4 + slot], pair_r.at[self.n, spot], partner)

        def start(self, value):
            self.buffer[section, self.own] = value.astype(BF16)
            self.whole(self.own, 0, x_next).start()
            self.whole(self.own, 1, y_next).start()
            self.pair(section, self.own, 0).start()

        def middle(self):
            self.whole(self.over_x, 0, x_next).wait_recv()
            self.relay(self.over_x, 0, y_next).start()
            self.pair(section, self.over_x, 1).start()
            self.whole(self.over_y, 1, y_next).wait_recv()
            self.relay(self.over_y, 1, x_next).start()
            self.pair(section, self.over_y, 2).start()

        def finish(self):
            self.relay(self.across, 0, y_next).wait_recv()
            self.relay(self.across, 1, x_next).wait_recv()
            self.pair(section, self.across, 3).start()
            for spot in (self.own, self.over_x, self.over_y, self.across):
                self.pair(1 - section, spot, 0).wait_recv()

        def sent(self):
            self.whole(self.own, 0, x_next).wait_send()
            self.whole(self.own, 1, y_next).wait_send()
            self.relay(self.over_x, 0, y_next).wait_send()
            self.relay(self.over_y, 1, x_next).wait_send()
            for slot, spot in enumerate((self.own, self.over_x, self.over_y, self.across)):
                self.pair(section, spot, slot).wait_send()

    below = (z < RANKS // 2).astype(jnp.int32)
    gathers = [
        Gather(0, d_all.at[0], True),
        Gather(1, d_all.at[1], False),
        Gather(2, f_all.at[0], True),
        Gather(3, f_all.at[1], False),
        Gather(4, t_all, below),
    ]

    def d1_copy(h):
        return remote(d1_out.at[h], d1_in.at[h], d1_s.at[h], d1_r.at[h], f_links(h)[0])

    def d2_copy(h):
        return remote(d2_out.at[h], d2_in.at[h], d2_s.at[h], d2_r.at[h], f_links(h)[1])

    def d_first(h):
        span = pl.ds(h * fine, fine)
        for condition, slot in ((z > 0, z), (z < last, RANKS)):

            @pl.when(condition)
            def _(slot=slot):
                remote(d_out.at[0, span], d_in.at[slot, span], dz_s.at[0, h], dz_r.at[slot, h], partner).wait_recv()

        first = f_links(h)[2]
        for mine in (False, True):
            at = h * fine + (first if mine else 1 - first) * (fine // 2)
            piece = some(at, fine // 2)
            total = z_total(dot(in_t[piece, :], br_v[...]), d_in[z, piece, :], d_in[RANKS, piece, :])
            if mine:
                d_keep[h] = total
            else:
                d1_out[h] = total.astype(BF16)
                d1_copy(h).start()

    def d_second(h):
        second = f_links(h)[3]
        d1_copy(h).wait_recv()
        for mine in (False, True):
            piece = some((second if mine else 1 - second) * (fine // 4), fine // 4)
            total = d_keep[h, piece, :] + d1_in[h, piece, :].astype(F32)
            if mine:
                d_keep[h, : fine // 4, :] = total
            else:
                d2_out[h] = total.astype(BF16)
                d2_copy(h).start()

    def d_gather(h):
        d2_copy(h).wait_recv()
        gathers[h].start(d_keep[h, : fine // 4, :] + d2_in[h].astype(F32))

    back = AttentionBack(
        rank, lambda r: (r // 2, z, 2 * y + r % 2), qd, kv, o_raw, allowed, cos_sin, ra,
        ln_t.at[pl.ds(0, 2 * SHARE * rows)], dkv, dkv_in, gkv, dk_s, dk_r,
    )
    grads_out = OutCopy(grads_o, grad_s, grad_r)

    def op_copy(kind, own):
        role = section if own else 1 - section
        src = ra.at[role] if kind == 0 else gkv.at[:, some(role * 256, 384, 128)]
        dst = (ra_v, kvg_v)[kind].at[some(2 * section * rows, rows)]
        if own:
            return pltpu.make_async_copy(src, dst, op_own.at[kind])
        return remote(src, dst, op_s.at[kind], op_r.at[kind], partner)

    def op_start(kind):
        op_copy(kind, True).start()
        op_copy(kind, False).start()

    def attention_end():
        back.collect()
        op_start(1)
        for copy in weights:
            copy.wait()
        kept[6].wait()
        back.project(sum_acc, wq, wkv)
        grad, gain_row = norm_back(act[...].astype(F32), gain_a[...].astype(F32).reshape(1, width), sum_acc[...])
        gain_load.wait()
        gain_rows[0:1, :] += gain_row
        go[...] = (gm[...] + grad).astype(BF16)
        grads_out.start(go, 0)

    def t_ready():
        loads[3].wait()
        turn(stage, ln_t)
        loads[4].start()
        block_of = lambda at, size: wide(gain_rows[:, at : at + size]).T
        for at, size in tiles(width, 128):
            gain_t[at : at + size, :] = pltpu.roll(block_of(at, size), 64, 1)[:size]
        loads[4].wait()
        turn(stage, ln_t, width)
        for copy in late:
            copy.wait()
        for kind in range(2):
            op_copy(kind, True).wait()
            op_copy(kind, False).wait_recv()

    def both(step):
        step(0)
        step(1)

    def head_step(g):
        @pl.when(g == 0)
        def _():
            for copy in halves[1] + kept[:6]:
                copy.wait()
            ra[1] = gm[...].astype(BF16)

        back.head(g)

        @pl.when(g > 0)
        def _():
            back.relay(g - 1)

    def queries_step():
        back.relay(KEY_VALUE_HEADS - 1)
        back.queries()
        op_start(0)

    def d_first_step():
        d_block(last)
        both(d_first)

    def f_total():
        both(lambda k: gathers[2 + k].start(lines[k].total()))

    actions = {
        "near": f1_step,
        "far": f2_step,
        "tnear": t1_step,
        "tfar": t2_step,
        "down": d_step,
        "head": head_step,
        "fadd": f_add,
        "fz": f_line,
        "tadd": t_add,
        "tz": lines[2].step,
        "query": lambda p: queries_step(),
        "aend": lambda p: attention_end(),
        "tready": lambda p: t_ready(),
        "dfirst": lambda p: d_first_step(),
        "dsecond": lambda p: both(d_second),
        "dgather": lambda p: both(d_gather),
        "ftotal": lambda p: f_total(),
        "ttotal": lambda p: gathers[4].start(lines[2].total()),
        "fmiddle": lambda p: both(lambda k: gathers[2 + k].middle()),
        "dmiddle": lambda p: both(lambda h: gathers[h].middle()),
    }
    names = list(actions)

    def codes(table):
        return [8 * names.index(step.rstrip("0123456789")) + int(step[-1]) for step in table]

    tables = [codes(MIDDLE_ORDER), codes(END_ORDER)]
    steps = max(len(t) for t in tables)

    loads[2].wait()
    turn(stage, nf_t)
    for copy in halves[0]:
        copy.wait()
    in_load(0).start()
    loads[1].start()
    for copy in halves[1] + kept + weights + late + [gain_load]:
        copy.start()
    pl.semaphore_wait(barrier, 7 + not_first + not_last)
    loads[3].start()

    def one(n, carry):
        code = (1 - edge) * pick(n, tables[0]) + edge * pick(n, tables[1])
        lax.switch(code // 8, list(actions.values()), code % 8)
        return carry

    lax.fori_loop(0, steps, one, 0)

    writes = []

    def leave(src, dst):
        writes.append(pltpu.make_async_copy(src, dst, write.at[len(writes)]))
        writes[-1].start()

    for k in range(2):
        gathers[2 + k].finish()
        for core in range(2):
            for f in range(2):
                columns = pl.ds((2 * core + f) * quarter, quarter)
                out = (gate_o, up_o)[k]
                leave(f_all.at[k, core, 2 * f], out.at[pl.ds(0, part), columns])
                rest = pl.ds(part - shift, per - part)
                leave(f_all.at[k, core, 2 * f + 1, rest], out.at[pl.ds(part, per - part), columns])
    gathers[4].middle()
    for h in range(2):
        gathers[h].finish()
        for core in range(2):
            for spot in range(4):
                span = pl.ds(h * fine + spot * (fine // 4), fine // 4)
                leave(d_all.at[h, core, spot], down_o.at[span, pl.ds(core * br_v.shape[1], br_v.shape[1])])
    gathers[4].finish()
    t_rows = part // 2
    for core in range(2):
        for spot in range(4):
            row = spot % 2 * t_rows + spot // 2 * shift
            skip = part - shift if spot == 2 else 0
            rest = pl.ds(skip, t_rows - skip)
            leave(t_all.at[core, spot, rest], t_o.at[core, pl.ds(row + skip, t_rows - skip)])

    for k in range(last):
        for sub in range(2):
            d_send(k, sub).wait_send()
        for line in lines:
            line.copy(k).wait_send()
    for h in range(2):
        d1_copy(h).wait_send()
        d2_copy(h).wait_send()
    for k in range(2):
        for i in (2, 3):
            f1_copy(k, i).wait_send()
            f2_copy(k, i).wait_send()
    for d in range(RANKS):
        t1_copy(d).wait_send()
        t2_copy(d).wait_send()
    for kind in range(2):
        op_copy(kind, False).wait_send()
    grads_out.sent(go, 0)

    @pl.when(section == 0)
    def _():
        grads_out.arrived(go)

    for gather in gathers:
        gather.sent()
    for copy in writes:
        copy.wait()


def run_sums(gain_sums, gain_attn, operands, kept, weights, ends_shape):
    nf, inner, gg, gu, br, la, ra, nr, kvg = operands
    act, kv, o_raw, cos_sin, allowed, qd, gm = kept
    depth, width = nf.shape
    rows = act.shape[0]
    ff, half = inner.shape[1], gg.shape[1]
    per, deep = width // RANKS, ff // RANKS
    part = (per // 2 + 15) // 16 * 16
    quarter, fine = half // 2, deep // 2
    columns = br.shape[1]
    wide_t = width // 128 * 128 + 128 + kvg.shape[1]
    vmem, hbm = pl.BlockSpec(memory_space=pltpu.VMEM), pl.BlockSpec(memory_space=pl.ANY)
    out = lambda *shape: jax.ShapeDtypeStruct(shape, BF16)
    b = lambda *shape: pltpu.VMEM(shape, BF16)
    f = lambda *shape: pltpu.VMEM(shape, F32)
    like = lambda a: pltpu.VMEM(a.shape, a.dtype)
    sem = lambda *shape: pltpu.SemaphoreType.DMA(shape)
    return pl.pallas_call(
        sums_kernel,
        out_shape=[
            out(*ends_shape), out(2, per, wide_t), out(per, ff), out(per, ff), out(deep, 2 * columns),
        ],
        in_specs=[hbm, vmem] + [hbm] * 19,
        out_specs=[hbm] * 5,
        scratch_shapes=[
            b(depth, width), b(depth, deep), b(depth, columns), b(depth, half), b(depth, half),
            b(depth, width), b(depth, kvg.shape[1]),
            b(width, depth), b(2 * width, depth), b(deep, depth), f(width, 128),
            like(act), like(kv), like(o_raw), like(cos_sin), like(allowed), like(qd), like(gm),
            like(weights[0]), b(2 * weights[1].shape[0], width),
            b(rows, width), b(2, rows, width), like(kv), b(KEY_VALUE_HEADS, 3 * rows, 128), b(rows, KEY_VALUE_HEADS * 128),
            f(rows, width), f(128, width),
            b(RANKS - 1, deep, columns), b(5, deep, columns), f(2, fine // 2, columns),
            b(2, fine // 2, columns), b(2, fine // 2, columns), b(2, fine // 4, columns), b(2, fine // 4, columns),
            b(2, 2, per, quarter), b(2, RANKS, per, quarter),
            b(2, 2, part, quarter), b(2, RANKS, part, quarter), b(2, RANKS, part, quarter), b(2, 5, part, quarter),
            b(RANKS, part, wide_t), b(RANKS, part, wide_t),
            b(RANKS, part // 2, wide_t), b(RANKS, part // 2, wide_t), b(RANKS, part // 2, wide_t), b(5, part // 2, wide_t),
            b(2, 2, 4, fine // 4, columns), b(2, 2, 4, part, quarter), b(2, 4, part // 2, wide_t),
            sem(10), sem(7), sem(5, KEY_VALUE_HEADS), sem(2, KEY_VALUE_HEADS), sem(3, KEY_VALUE_HEADS), sem(2), sem(2), sem(2), sem(2), sem(2),
            sem(3, 2), sem(5, 2), sem(2), sem(2), sem(2), sem(2),
            sem(2, 2), sem(2, 4), sem(2, 2), sem(2, 4), sem(2, 3), sem(2, 5),
            sem(4), sem(4), sem(4), sem(4), sem(3), sem(5),
            sem(5, 8), sem(5, 4), sem(5, 4), sem(40),
        ],
        compiler_params=pltpu.CompilerParams(
            collective_id=2, has_side_effects=True, vmem_limit_bytes=61 * 2**20
        ),
        name="sums",
    )(gain_sums, gain_attn, *operands, *kept, *weights)


def finish_kernel(
    acts_h, first_h, second_h, t_h, gate_h, up_h, down_h,
    acts_o, grads_o, q_o, out_o, key_o, value_o, gain_a, gain_f, gate_o, up_o, down_o,
    row_v, t_v, gate_v, down_v, q_f, kv_f, gate_f, down_f, load, store,
):
    width = q_f.shape[2]
    loads = [
        pltpu.make_async_copy(h, v, load.at[i])
        for i, (h, v) in enumerate(
            [(gate_h, gate_v.at[0]), (up_h, gate_v.at[1]), (down_h, down_v), (t_h, t_v), (acts_h, row_v.at[0])]
        )
    ]
    stores = [
        pltpu.make_async_copy(v, h, store.at[i])
        for i, (v, h) in enumerate(
            [(row_v.at[0], acts_o), (row_v.at[1], grads_o), (gate_f.at[0], gate_o), (gate_f.at[1], up_o),
             (down_f, down_o), (q_f.at[0], q_o), (q_f.at[1], out_o), (kv_f.at[0], key_o), (kv_f.at[1], value_o)]
        )
    ]
    section = lax.axis_index("section")
    for copy in loads:
        copy.start()
    start_if(
        section == 0,
        lambda: pltpu.make_async_copy(first_h, row_v.at[1], load.at[5]),
        lambda: pltpu.make_async_copy(second_h, row_v.at[1], load.at[5]),
    )
    for k in range(2):
        loads[k].wait()
        gate_f[k] = gate_v[k].astype(F32)
        stores[2 + k].start()
    loads[4].wait()
    stores[0].start()
    pltpu.make_async_copy(first_h, row_v.at[1], load.at[5]).wait()
    stores[1].start()
    loads[2].wait()
    for at, size in tiles(width, 128):
        down_f[at : at + size, :] = down_v[:, at : at + 128].astype(F32).T[:size]
    stores[4].start()
    loads[3].wait()
    for core in range(2):
        q_f[core] = t_v[core, :, :width].astype(F32)
        stores[5 + core].start()
    pairs_at = width // 128 * 128 + 128
    half = KEY_VALUE_HEADS // 2 + 1
    for g in range(KEY_VALUE_HEADS):
        core = 0 if g < half else 1
        at = pairs_at + (g - core * (KEY_VALUE_HEADS - half)) * 128
        block = t_v[core, :, at : at + 128].astype(F32).T
        kv_f[0, g * HEAD_SIZE : (g + 1) * HEAD_SIZE, :] = block[:HEAD_SIZE]
        kv_f[1, g * HEAD_SIZE : (g + 1) * HEAD_SIZE, :] = block[HEAD_SIZE:]
    for copy in stores[7:]:
        copy.start()
    tail = slice(pairs_at - 128, pairs_at)
    both = t_v[0, :, tail].astype(F32) + t_v[1, :, tail].astype(F32)
    row = width % 128
    gain_rows = both.T
    gain_a[...] = gain_rows[row]
    gain_f[...] = gain_rows[row + 1]
    for copy in stores:
        copy.wait()


def run_finish(acts, grads_first, grads_second, t_sum, gate, up, down, width):
    per, ff = gate.shape
    vmem, hbm = pl.BlockSpec(memory_space=pltpu.VMEM), pl.BlockSpec(memory_space=pl.ANY)
    out = lambda *shape: jax.ShapeDtypeStruct(shape, F32)
    kv_rows = KEY_VALUE_HEADS * HEAD_SIZE
    return pl.pallas_call(
        finish_kernel,
        out_shape=[
            jax.ShapeDtypeStruct(acts.shape, BF16), jax.ShapeDtypeStruct(acts.shape, BF16),
            out(per, width), out(per, width), out(kv_rows, per), out(kv_rows, per), out(per), out(per),
            out(per, ff), out(per, ff), out(width, down.shape[0]),
        ],
        in_specs=[hbm] * 7,
        out_specs=[hbm] * 6 + [vmem] * 2 + [hbm] * 3,
        scratch_shapes=[
            pltpu.VMEM((2, *acts.shape), BF16), pltpu.VMEM(t_sum.shape, BF16), pltpu.VMEM((2, per, ff), BF16), pltpu.VMEM(down.shape, BF16),
            pltpu.VMEM((2, per, width), F32), pltpu.VMEM((2, kv_rows, per), F32),
            pltpu.VMEM((2, per, ff), F32), pltpu.VMEM((width, down.shape[0]), F32),
            pltpu.SemaphoreType.DMA((6,)), pltpu.SemaphoreType.DMA((9,)),
        ],
        compiler_params=pltpu.CompilerParams(vmem_limit_bytes=61 * 2**20),
        name="finish",
    )(acts, grads_first, grads_second, t_sum, gate, up, down)


def sums_by_xla(gain_sums, operands):
    nf, inner, gg, gu, br, la, ra, nr, kvg = operands
    width = nf.shape[1]

    def reduced(left, right):
        total = dot_lt(left, right).astype(BF16)
        piece = lax.psum_scatter(total, "dp", scatter_dimension=0, tiled=True)
        return lax.psum(piece, "ctx")

    def both(piece, axis):
        return lax.all_gather(piece, "section", axis=axis, tiled=axis > 0).astype(F32)

    attn = both(reduced(la, ra), 0)
    gain_sum = lax.psum(gain_sums[:2], ("section", "ctx"))
    return (
        attn[0],
        attn[1],
        both(reduced(nr, kvg), 0),
        lax.psum_scatter(gain_sum, "dp", scatter_dimension=1, tiled=True),
        both(reduced(nf, gg), 1),
        both(reduced(nf, gu), 1),
        both(reduced(inner, br), 1)[:, :width],
    )


def shards(
    ends,
    doc_lengths,
    w_query,
    key_projection_weight,
    value_projection_weight,
    w_out,
    w_gate,
    w_up,
    w_down,
    gain_attn,
    gain_ffn,
):
    width = ends.shape[3]
    half = HEAD_SIZE // 2
    turns = np.float32(10000.0) ** (
        np.float32(-2.0) * (np.arange(128) % half).astype(np.float32) / np.float32(HEAD_SIZE)
    )
    weights = (
        w_query,
        key_projection_weight.T,
        value_projection_weight.T,
        w_out,
        w_gate,
        w_up,
        w_down.T,
    )
    ff = w_gate.shape[1]
    fits = lax.axis_size("dp") == RANKS and width % 64 == 0 and ff % 1280 == 0
    acts, grads_in, gain_sums, *kept = run_layers(
        doc_lengths,
        ends,
        jnp.asarray(turns.reshape(1, 128), F32),
        gain_attn,
        gain_ffn,
        weights,
        not fits,
    )
    operands = kept[:9]
    if fits:
        grads_first, *sums = run_sums(
            gain_sums, gain_attn, operands, kept[9:], weights[:3], ends.shape
        )
        acts, grads_in, grad_query, grad_out, grad_key, grad_value, *gain_piece, grad_gate, grad_up, grad_down = (
            run_finish(acts, grads_first, grads_in, *sums, width)
        )
        grad_key, grad_value, grad_down = grad_key.T, grad_value.T, grad_down.T
    else:
        grad_query, grad_out, kv_parts, gain_piece, grad_gate, grad_up, grad_down = sums_by_xla(
            gain_sums, operands
        )
        kv_grad = jnp.concatenate([kv_parts[0], kv_parts[1][:, 128:]], axis=1).reshape(
            -1, KEY_VALUE_HEADS, 2, HEAD_SIZE
        )
        grad_key = kv_grad[:, :, 0].reshape(kv_grad.shape[0], -1)
        grad_value = kv_grad[:, :, 1].reshape(kv_grad.shape[0], -1)
    return (
        acts,
        grads_in,
        grad_query,
        grad_key,
        grad_value,
        grad_out,
        grad_gate,
        grad_up,
        grad_down,
        gain_piece[0],
        gain_piece[1],
    )


def solution(mesh):
    return jax.shard_map(
        shards,
        mesh=mesh,
        in_specs=(P("section", None, ("dp", "ctx"), None), P(None, "dp", None)) + (P(),) * 9,
        out_specs=(P("section", None, ("dp", "ctx"), None),) * 2
        + (P("dp", None),) * 7
        + (P("dp"),) * 2,
        check_vma=False,
    )
```

```python
import jax
import jax.numpy as jnp
import numpy as np
from jax import lax
from jax.experimental import pallas as pl
from jax.experimental.pallas import tpu as pltpu
from jax.sharding import PartitionSpec as P

MESH = pl.DeviceIdType.MESH
QUERY_HEADS = 15
KEY_VALUE_HEADS = 5
HEAD_SIZE = 64
SHARE = QUERY_HEADS // KEY_VALUE_HEADS
RANKS = 4
epsilon = 1e-05
masked_fill = -1e30
F32 = jnp.float32
BF16 = jnp.bfloat16


def dot(left, right):
    return jnp.dot(left, right, preferred_element_type=F32)


def dot_rt(left, right):
    return lax.dot_general(left, right, (((1,), (1,)), ((), ())), preferred_element_type=F32)


def dot_lt(left, right):
    return lax.dot_general(left, right, (((0,), (0,)), ((), ())), preferred_element_type=F32)


def tiles(total, width):
    return [(at, min(width, total - at)) for at in range(0, total, width)]


def wide(block):
    missing = 128 - block.shape[1]
    if not missing:
        return block
    return jnp.concatenate([block, jnp.zeros((block.shape[0], missing), block.dtype)], axis=1)


def lanes(rows):
    return lax.broadcasted_iota(jnp.int32, (rows, 128), 1)


def half_turn(block):
    front = lanes(block.shape[0]) % HEAD_SIZE < HEAD_SIZE // 2
    return jnp.where(front, pltpu.roll(block, 96, 1), pltpu.roll(block, 32, 1))


def inverse_rms(hidden):
    return lax.rsqrt(jnp.mean(hidden * hidden, axis=-1, keepdims=True) + epsilon)


def half_turned(block, cosines, sines, direction):
    return block * cosines + direction * (half_turn(block) * sines)


def norm_back(hidden, gain, upstream):
    scale = inverse_rms(hidden)
    weighted = upstream * gain
    inside = jnp.mean(weighted * hidden, axis=-1, keepdims=True)
    gain_row = jnp.sum(upstream * hidden * scale, axis=0, keepdims=True)
    return scale * weighted - hidden * (scale * scale * scale * inside), gain_row


def start_if(condition, here, there):
    @pl.when(condition)
    def _():
        here().start()

    @pl.when(jnp.logical_not(condition))
    def _():
        there().start()


class AttentionBack:
    def __init__(
        self, rank, device_of, qd, kv, o_raw, allowed, cos_sin, ra, pds, dkv, dkv_in, gkv, send, recv
    ):
        self.rank, self.device_of = rank, device_of
        self.qd, self.kv, self.o_raw, self.allowed, self.cos_sin = qd, kv, o_raw, allowed, cos_sin
        self.ra, self.pds, self.dkv, self.dkv_in, self.gkv = ra, pds, dkv, dkv_in, gkv
        self.send_sem, self.recv_sem = send, recv
        self.rows, self.width = ra.shape[1:]

    def head(self, g):
        rows = self.rows
        kv_g = self.kv[g]
        mine = [slice(i * rows, (i + 1) * rows) for i in range(SHARE)]
        other = [slice((SHARE + i) * rows, (SHARE + i + 1) * rows) for i in range(SHARE)]
        all_scores = [dot_rt(self.qd[g, span, :], kv_g) + self.allowed[...] for span in mine]
        for i, scores in enumerate(all_scores):
            kept = self.o_raw[g * SHARE + i]
            probs = jnp.exp(scores - kept[:, 0:1])
            grad_out = self.qd[g, other[i], :]
            grad_probs = dot_rt(grad_out, kv_g)
            weight = jnp.sum(grad_out.astype(F32) * kept, axis=-1, keepdims=True)
            grad_scores = (probs * (grad_probs - weight)).astype(BF16)
            self.pds[mine[i], :] = grad_scores
            self.pds[other[i], :] = probs.astype(BF16)
            self.o_raw[g * SHARE + i] = dot(grad_scores, kv_g)
        grad_kv = dot_lt(self.qd[g], self.pds[...])
        self.dkv[g] = grad_kv.T.astype(BF16)
        self.send(g)

    def heads(self, first, last):
        def body(g, carry):
            self.head(g)

            @pl.when(g > 0)
            def _():
                self.relay(g - 1)

            return carry

        lax.fori_loop(first, last, body, 0)

    def copy(self, quarter, count, dst, slot_in, slot, g):
        rows = self.rows
        return pltpu.make_async_remote_copy(
            src_ref=self.dkv.at[g, pl.ds(quarter * rows, count * rows)],
            dst_ref=self.dkv_in.at[g, pl.ds(slot_in * rows, count * rows)],
            send_sem=self.send_sem.at[slot, g],
            recv_sem=self.recv_sem.at[slot_in, g],
            device_id=self.device_of(dst),
            device_id_type=MESH,
        )

    def add(self, quarter, slots, g):
        rows = self.rows
        span = slice(quarter * rows, (quarter + 1) * rows)
        total = self.dkv[g, span].astype(F32)
        for slot in slots:
            total = total + self.dkv_in[g, slot * rows : (slot + 1) * rows].astype(F32)
        self.dkv[g, span] = total.astype(BF16)

    def send(self, g):
        @pl.when(self.rank == 3)
        def _():
            self.copy(2, 1, 2, 0, 0, g).start()
            self.copy(0, 2, 1, 0, 1, g).start()

        @pl.when(self.rank == 2)
        def _():
            self.copy(1, 1, 1, 2, 0, g).start()
            self.copy(0, 1, 0, 1, 1, g).start()

    def relay(self, g):
        @pl.when(self.rank == 1)
        def _():
            self.copy(0, 2, 1, 0, 0, g).wait_recv()
            self.add(0, (0,), g)
            self.copy(0, 1, 0, 0, 0, g).start()

    def queries(self):
        for at, size in tiles(self.width, 128):
            head = at // HEAD_SIZE
            block = self.o_raw[head]
            if size == 128:
                low = lanes(self.rows) < HEAD_SIZE
                block = jnp.where(low, block, pltpu.roll(self.o_raw[head + 1], 64, 1))
            turned = half_turned(block, self.cos_sin[0], self.cos_sin[1], -1.0) * 0.125
            self.ra[0, :, at : at + size] = turned[:, :size].astype(BF16)

    def collect(self):
        low = lanes(self.rows) < HEAD_SIZE
        cosines = jnp.where(low, self.cos_sin[0], 1.0)
        sines = jnp.where(low, self.cos_sin[1], 0.0)
        mine = pl.ds(pl.multiple_of(self.rank * self.rows, 16), self.rows)
        for g in range(KEY_VALUE_HEADS):
            self.arrive(g)
            block = half_turned(self.dkv[g, mine, :].astype(F32), cosines, sines, -1.0)
            self.gkv[:, 128 * g : 128 * g + 128] = block.astype(BF16)

    def arrive(self, g):
        @pl.when(self.rank == 3)
        def _():
            self.copy(2, 1, 2, 0, 0, g).wait_send()
            self.copy(0, 2, 1, 0, 1, g).wait_send()

        @pl.when(self.rank == 2)
        def _():
            self.copy(0, 1, 2, 0, 0, g).wait_recv()
            self.copy(1, 1, 1, 2, 0, g).wait_send()
            self.copy(0, 1, 0, 1, 1, g).wait_send()
            self.add(2, (0,), g)

        @pl.when(self.rank == 1)
        def _():
            self.copy(0, 1, 2, 2, 0, g).wait_recv()
            self.copy(0, 1, 0, 0, 0, g).wait_send()
            self.add(1, (1, 2), g)

        @pl.when(self.rank == 0)
        def _():
            self.copy(0, 1, 2, 0, 0, g).wait_recv()
            self.copy(0, 1, 2, 1, 0, g).wait_recv()
            self.add(0, (0, 1), g)

    def project(self, total, wq, wkv):
        for at, size in tiles(self.width, 256):
            total[:, at : at + size] = dot_rt(self.ra[0], wq[at : at + size, :]) + dot(
                self.gkv[...], wkv[:, at : at + size]
            )


class OutCopy:
    def __init__(self, out, send, recv):
        self.section, self.dp, ctx = (lax.axis_index(a) for a in ("section", "dp", "ctx"))
        self.home = 2 * self.section + ctx % 2
        self.ctx, self.micro = ctx, ctx // 2
        self.out, self.send, self.recv = out, send, recv

    def here(self, l):
        return (self.section == l) & (self.ctx == self.home)

    def remote(self, array, l):
        return pltpu.make_async_remote_copy(
            src_ref=array,
            dst_ref=self.out.at[0, self.micro],
            send_sem=self.send.at[l],
            recv_sem=self.recv.at[self.micro],
            device_id=(l, self.dp, self.home),
            device_id_type=MESH,
        )

    def local(self, array):
        return pltpu.make_async_copy(array, self.out.at[0, self.micro], self.recv.at[self.micro])

    def start(self, array, l):
        start_if(self.here(l), lambda: self.local(array), lambda: self.remote(array, l))

    def sent(self, array, l):
        @pl.when(jnp.logical_not(self.here(l)))
        def _():
            self.remote(array, l).wait_send()

    def arrived(self, array):
        for block in range(2):
            pltpu.make_async_copy(array, self.out.at[0, block], self.recv.at[block]).wait()


def greet(barrier, dp):
    section, ctx = lax.axis_index("section"), lax.axis_index("ctx")
    for step in range(1, 8):
        other = (4 * section + ctx + step) % 8
        pl.semaphore_signal(
            barrier, inc=1, device_id=(other // 4, dp, other % 4), device_id_type=MESH
        )


def layers_kernel(complete, *refs):
    refs = list(refs)

    def take(count):
        taken = refs[:count]
        del refs[:count]
        return taken

    lengths, ends, frequency, gain_a, gain_f, wq_h, wk_h, wv_h, wo_h, wg_h, wu_h, wd_h = take(12)
    acts_o, grads_o, gain_o, nf_o, in_o, gg_o, gu_o, br_o, la_o, ra_o, nr_o, kvg_o = take(12)
    kept_o = [] if complete else take(7)
    wq, wkv, wo, wg, wu, wd = take(6)
    act, go, middle, norm_ffn, fact_a, fact_b, inner, lm, qd, kv, o_raw = take(11)
    sum_acc, gm, gg, gu, br, ra, pds, dkv, dkv_in, gkv, cos_sin, allowed_add, gain_v = take(13)
    w_sem, kv_sem, in_send, in_recv, kv_send, kv_recv, dk_send, dk_recv = take(8)
    act_send, act_recv, grad_send, grad_recv, op_own, op_send, op_recv, kept_sem = take(8)

    section = lax.axis_index("section")
    dp = lax.axis_index("dp")
    ctx = lax.axis_index("ctx")
    micro = ctx // 2
    xbit = ctx % 2
    rank = 2 * section + xbit
    rows, width = act.shape[1], act.shape[2]
    ff = wg.shape[1]
    ff_half = ff // 2

    def device_of(r):
        return (r // 2, dp, 2 * micro + r % 2)

    partner = (1 - section, dp, ctx)

    loads = [
        pltpu.make_async_copy(h, v, w_sem.at[i])
        for i, (h, v) in enumerate([(wq_h, wq), (wo_h, wo), (wg_h, wg), (wu_h, wu), (wd_h, wd)])
    ]
    kv_loads = [
        pltpu.make_async_copy(
            h.at[pl.ds(g * HEAD_SIZE, HEAD_SIZE)],
            wkv.at[pl.ds((2 * g + i) * HEAD_SIZE, HEAD_SIZE)],
            kv_sem.at[i, g],
        )
        for g in range(KEY_VALUE_HEADS)
        for i, h in enumerate((wk_h, wv_h))
    ]
    for load in kv_loads + loads:
        load.start()
    kv[...] = jnp.zeros_like(kv)
    barrier = pltpu.get_barrier_semaphore()
    greet(barrier, dp)
    pl.semaphore_wait(barrier, 7)

    def in_local(block, into_x):
        dst, slot = (act.at[0], 0) if into_x else (go.at[2], 1)
        return pltpu.make_async_copy(ends.at[0, block], dst, in_recv.at[slot])

    def in_remote(block, into_x):
        dst, slot = (act.at[0], 0) if into_x else (go.at[2], 1)
        return pltpu.make_async_remote_copy(
            src_ref=ends.at[0, block],
            dst_ref=dst,
            send_sem=in_send.at[block],
            recv_sem=in_recv.at[slot],
            device_id=(ctx // 2, dp, 2 * block + xbit),
            device_id_type=MESH,
        )

    def in_mine(block):
        return (section == ctx // 2) & (ctx // 2 == block)

    def in_start(into_x):
        @pl.when(section == (0 if into_x else 1))
        def _():
            for block in range(2):
                start_if(
                    in_mine(block),
                    lambda block=block: in_local(block, into_x),
                    lambda block=block: in_remote(block, into_x),
                )

    in_start(True)
    lane = lanes(rows)
    low = lane < HEAD_SIZE
    gain_attn = gain_a[...].astype(F32).reshape(1, width)
    gain_ffn = gain_f[...].astype(F32).reshape(1, width)

    def place(token_index):
        segment = jnp.zeros_like(token_index)
        start = jnp.zeros_like(token_index)
        finish = jnp.int32(0)
        for slot in range(lengths.shape[2]):
            length = lengths[micro, 0, slot]
            finish = finish + length
            passed = (token_index >= finish).astype(jnp.int32)
            segment = segment + passed
            start = start + passed * length
        return segment, token_index - start

    seg_mine, position = place(rank * rows + lax.broadcasted_iota(jnp.int32, (rows, 128), 0))
    angles = position.astype(F32) * frequency[...]
    cos_sin[0] = jnp.cos(angles)
    cos_sin[1] = jnp.where(lane % HEAD_SIZE < HEAD_SIZE // 2, -1.0, 1.0) * jnp.sin(angles)
    key_index = lax.broadcasted_iota(jnp.int32, (1, RANKS * rows), 1)
    query_index = rank * rows + lax.broadcasted_iota(jnp.int32, (rows, 1), 0)
    allowed_add[...] = jnp.where(
        (seg_mine[:, 0:1] == place(key_index)[0]) & (query_index >= key_index), 0.0, masked_fill
    )

    def kv_rows(l, r, g):
        return kv.at[l, g, pl.ds(pl.multiple_of(r * rows, 16), rows)]

    def kv_copy(l, quarter, dst, slot, g):
        return pltpu.make_async_remote_copy(
            src_ref=kv_rows(l, quarter, g),
            dst_ref=kv_rows(l, quarter, g),
            send_sem=kv_send.at[l, slot, g],
            recv_sem=kv_recv.at[l, quarter, g],
            device_id=device_of(dst),
            device_id_type=MESH,
        )

    def kv_start(l, g):
        @pl.when(rank < 3)
        def _():
            kv_copy(l, rank, rank + 1, 0, g).start()

        @pl.when(rank < 2)
        def _():
            kv_copy(l, rank, rank + 2, 1, g).start()

    def kv_relayed(l, g):
        @pl.when(rank == 1)
        def _():
            kv_copy(l, 0, 3, 2, g).wait_recv()
            kv_copy(l, 0, 3, 2, g).start()

    def kv_finish(l, g):
        @pl.when(rank >= 2)
        def _():
            kv_copy(l, 0, 0, 0, g).wait_recv()
            kv_copy(l, 1, 0, 0, g).wait_recv()

        @pl.when(rank == 3)
        def _():
            kv_copy(l, 2, 0, 0, g).wait_recv()

    def kv_sent(l):
        for senders, slot in ((3, 0), (2, 1)):

            @pl.when(rank < senders)
            def _(slot=slot):
                for g in range(KEY_VALUE_HEADS):
                    kv_copy(l, rank, rank + 1 + slot, slot, g).wait_send()

        @pl.when(rank == 1)
        def _():
            for g in range(KEY_VALUE_HEADS):
                kv_copy(l, 0, 3, 2, g).wait_send()

    acts_out = OutCopy(acts_o, act_send, act_recv)
    grads_out = OutCopy(grads_o, grad_send, grad_recv)

    def op_copy(kind, l, own):
        role = section if own else 1 - section
        half = pl.ds(pl.multiple_of(role * ff_half, 128), ff_half)
        src = [
            lambda: norm_ffn.at[l],
            lambda: inner.at[l],
            lambda: gg.at[:, half],
            lambda: gu.at[:, half],
            lambda: br.at[:, pl.ds(pl.multiple_of(role * 512, 128), 512)],
            lambda: lm.at[l, role],
            lambda: ra.at[role],
            lambda: lm.at[l, 0],
            lambda: gkv.at[:, pl.ds(pl.multiple_of(role * 256, 128), 384)],
        ][kind]()
        block = section if kind in (6, 8) and not complete else 2 * section + l
        dst = [nf_o, in_o, gg_o, gu_o, br_o, la_o, ra_o, nr_o, kvg_o][kind].at[
            pl.ds(pl.multiple_of(block * rows, 16), rows)
        ]
        if own:
            return pltpu.make_async_copy(src, dst, op_own.at[kind, l])
        return pltpu.make_async_remote_copy(
            src_ref=src,
            dst_ref=dst,
            send_sem=op_send.at[kind, l],
            recv_sem=op_recv.at[kind, l],
            device_id=partner,
            device_id_type=MESH,
        )

    def op_start(kinds, l):
        for kind in kinds:
            op_copy(kind, l, True).start()
            op_copy(kind, l, False).start()

    def op_sent(kinds, l):
        for kind in kinds:
            op_copy(kind, l, True).wait()
            op_copy(kind, l, False).wait_send()

    def kept_copy(i):
        if i == 7:
            part = pl.ds(0, SHARE * rows)
            return pltpu.make_async_copy(qd.at[0, :, part], kept_o[5].at[:, part], kept_sem.at[8])
        if i == 5:
            part = pl.ds(SHARE * rows, SHARE * rows)
            return pltpu.make_async_copy(qd.at[0, :, part], kept_o[5].at[:, part], kept_sem.at[5])
        src = [act.at[0], kv.at[0], o_raw.at[0], cos_sin, allowed_add, None, gm][i]
        return pltpu.make_async_copy(src, kept_o[i], kept_sem.at[i])

    def kept_start(*which):
        if not complete:
            for i in which:
                kept_copy(i).start()

    in_remote(0, True).wait_recv()
    for load in kv_loads:
        load.wait()

    def forward(l, carry):
        hidden = act[l].astype(F32)
        cos_q, sin_q = cos_sin[0], cos_sin[1]
        lm[l, 0] = (hidden * inverse_rms(hidden) * gain_attn).astype(BF16)
        cos_kv = jnp.where(low, cos_q, 1.0)
        sin_kv = jnp.where(low, sin_q, 0.0)
        mine = pl.ds(pl.multiple_of(rank * rows, 16), rows)
        for g in range(KEY_VALUE_HEADS):
            block = dot_rt(lm[l, 0], wkv[128 * g : 128 * g + 128, :])
            turned = half_turned(block, cos_kv, sin_kv, 1.0)
            kv[l, g, mine, :] = turned.astype(BF16)
        for g in range(KEY_VALUE_HEADS):
            kv_start(l, g)

        @pl.when(l == 0)
        def _():
            loads[0].wait()
            in_start(False)
            kept_start(0, 3, 4)

        for at, size in tiles(width, 256):
            product = dot(lm[l, 0], wq[:, at : at + size])
            for inside, part in tiles(size, 128):
                block = wide(product[:, inside : inside + part])
                turned = half_turned(block, cos_q, sin_q, 1.0) * 0.125
                head = (at + inside) // HEAD_SIZE
                qd[l, head // SHARE, pl.ds(head % SHARE * rows, rows), :] = jnp.where(
                    low, turned, 0.0
                ).astype(BF16)
                head += 1
                if head < QUERY_HEADS:
                    qd[l, head // SHARE, pl.ds(head % SHARE * rows, rows), :] = jnp.where(
                        low, pltpu.roll(turned, 64, 1), 0.0
                    ).astype(BF16)
        kv_relayed(l, 0)
        kv_finish(l, 0)

        def heads(g, carry):
            @pl.when(g < KEY_VALUE_HEADS - 1)
            def _():
                kv_relayed(l, g + 1)

            @pl.when(g > 0)
            def _():
                kv_finish(l, g)

            kv_g = kv[l, g]
            all_scores = [
                dot_rt(qd[l, g, i * rows : (i + 1) * rows, :], kv_g) + allowed_add[...]
                for i in range(SHARE)
            ]
            for i, scores in enumerate(all_scores):
                peak = jnp.max(scores, axis=-1, keepdims=True)
                exponent = jnp.exp(scores - peak)
                total = jnp.sum(exponent, axis=-1, keepdims=True)
                out = dot(exponent.astype(BF16), kv_g) * (1.0 / total)
                o_raw[l, g * SHARE + i] = jnp.where(low, peak + jnp.log(total), out)
            return carry

        lax.fori_loop(0, KEY_VALUE_HEADS, heads, 0)

        @pl.when(l == 0)
        def _():
            kept_start(1, 2, 7)
            loads[1].wait()

        for at, size in tiles(width, 128):
            head = at // HEAD_SIZE
            block = pltpu.roll(o_raw[l, head], 64, 1)
            if size == 128:
                block = jnp.where(low, block, o_raw[l, head + 1])
            lm[l, 1, :, at : at + size] = block[:, :size].astype(BF16)
        for at, size in tiles(width, 256):
            middle[l, :, at : at + size] = act[l, :, at : at + size].astype(F32) + dot(
                lm[l, 1], wo[:, at : at + size]
            )
        mid = middle[l]
        norm_ffn[l] = (mid * inverse_rms(mid) * gain_ffn).astype(BF16)
        op_start((0, 5, 7), l)

        @pl.when(l == 0)
        def _():
            loads[2].wait()
            loads[3].wait()

        def gates(j, carry):
            part = pl.ds(pl.multiple_of(j * 1280, 128), 1280)
            gate = dot(norm_ffn[l], wg[:, part])
            upper = dot(norm_ffn[l], wu[:, part])
            s = 0.5 * jnp.tanh(0.5 * gate) + 0.5
            swish = gate * s
            inner[l, :, part] = (swish * upper).astype(BF16)
            fact_a[l, :, part] = (upper * s * (1.0 + gate * (1.0 - s))).astype(BF16)
            fact_b[l, :, part] = swish.astype(BF16)
            return carry

        lax.fori_loop(0, ff // 1280, gates, 0)

        @pl.when(l == 0)
        def _():
            loads[4].wait()

        op_start((1,), l)
        for at, size in tiles(width, 256):
            act[l + 1, :, at : at + size] = (
                middle[l, :, at : at + size] + dot_rt(inner[l], wd[at : at + size, :])
            ).astype(BF16)
        acts_out.start(act.at[l + 1], l)
        kv_sent(l)
        return carry

    lax.fori_loop(0, 2, forward, 0)

    in_remote(0, False).wait_recv()
    gain_v[...] = jnp.zeros_like(gain_v)
    br[...] = jnp.zeros_like(br)
    late = (6, 8)

    def backward(step, carry):
        l = 1 - step

        @pl.when(l == 0)
        def _():
            op_sent((2, 3, 4) + (late if complete else ()), 1)

        br[:, :width] = go[l + 1]
        op_start((4,), l)

        def gates(j, carry):
            part = pl.ds(pl.multiple_of(j * 1280, 128), 1280)
            grad_inner = dot(go[l + 1], wd[:, part])
            gg[:, part] = (grad_inner * fact_a[l, :, part].astype(F32)).astype(BF16)
            gu[:, part] = (grad_inner * fact_b[l, :, part].astype(F32)).astype(BF16)
            return carry

        lax.fori_loop(0, ff // 1280, gates, 0)
        op_start((2, 3), l)
        for at, size in tiles(width, 256):
            sum_acc[:, at : at + size] = dot_rt(gg[...], wg[at : at + size, :]) + dot_rt(
                gu[...], wu[at : at + size, :]
            )
        grad, gain_row = norm_back(middle[l], gain_ffn, sum_acc[...])
        gain_v[1:2, :] += gain_row
        gm[...] = go[l + 1].astype(F32) + grad
        ra[1] = gm[...].astype(BF16)

        @pl.when(l == 0)
        def _():
            kept_start(6)

        for at, size in tiles(width, 256):
            product = dot_rt(ra[1], wo[at : at + size, :])
            for inside, part in tiles(size, 128):
                block = wide(product[:, inside : inside + part])
                head = (at + inside) // HEAD_SIZE
                qd[l, head // SHARE, pl.ds((SHARE + head % SHARE) * rows, rows), :] = jnp.where(
                    low, 0.0, pltpu.roll(block, 64, 1)
                ).astype(BF16)
                head += 1
                if head < QUERY_HEADS:
                    qd[l, head // SHARE, pl.ds((SHARE + head % SHARE) * rows, rows), :] = (
                        jnp.where(low, 0.0, block).astype(BF16)
                    )

        def attention():
            back = AttentionBack(
                rank, device_of, qd.at[l], kv.at[l], o_raw.at[l], allowed_add, cos_sin, ra, pds,
                dkv, dkv_in.at[l] if complete else dkv_in, gkv,
                dk_send.at[l] if complete else dk_send, dk_recv.at[l] if complete else dk_recv,
            )
            back.heads(0, KEY_VALUE_HEADS)
            back.relay(KEY_VALUE_HEADS - 1)
            back.queries()
            op_start((6,), l)
            back.collect()
            op_start((8,), l)
            back.project(sum_acc, wq, wkv)
            grad, gain_row = norm_back(act[l].astype(F32), gain_attn, sum_acc[...])
            gain_v[0:1, :] += gain_row
            go[l] = (gm[...] + grad).astype(BF16)
            grads_out.start(go.at[l], l)

        if complete:
            attention()
        else:

            @pl.when(l == 1)
            def _():
                attention()

            @pl.when(l == 1)
            def _():
                op_sent(late, 1)

        return carry

    lax.fori_loop(0, 2, backward, 0)

    gain_copy = pltpu.make_async_copy(gain_v, gain_o, kept_sem.at[7])
    gain_copy.start()
    kept_start(5)
    for into_x in (True, False):

        @pl.when(section == (0 if into_x else 1))
        def _(into_x=into_x):
            for block in range(2):

                @pl.when(jnp.logical_not(in_mine(block)))
                def _(block=block):
                    in_remote(block, into_x).wait_send()

    op_sent((2, 3, 4) + (late if complete else ()), 0)
    for l in range(2):
        op_sent((0, 1, 5, 7), l)
        for kind in range(9):
            if l == 1 or complete or kind not in late:
                op_copy(kind, l, False).wait_recv()
        acts_out.sent(act.at[l + 1], l)
        if l == 1 or complete:
            grads_out.sent(go.at[l], l)
    gain_copy.wait()
    acts_out.arrived(act.at[0])
    if complete:
        grads_out.arrived(act.at[0])
    else:

        @pl.when(section == 1)
        def _():
            grads_out.arrived(act.at[0])

        for i in range(len(kept_o) + 1):
            kept_copy(i).wait()


def run_layers(lengths, ends, frequency, gain_attn, gain_ffn, weights, complete):
    micro_count, rows, width = ends.shape[1:]
    wq, wk, wv, wo, wg, wu, wd = weights
    ff = wg.shape[1]
    keys = RANKS * rows
    kv_width = 2 * wk.shape[0]
    vmem, hbm = pl.BlockSpec(memory_space=pltpu.VMEM), pl.BlockSpec(memory_space=pl.ANY)
    op_rows = 4 * rows
    late_rows = op_rows if complete else 2 * rows
    out = lambda *shape: jax.ShapeDtypeStruct(shape, BF16)
    out_f = lambda *shape: jax.ShapeDtypeStruct(shape, F32)
    dma = lambda *shape: pltpu.SemaphoreType.DMA(shape)
    kept = [
        out(rows, width),
        out(KEY_VALUE_HEADS, keys, 128),
        out_f(QUERY_HEADS, rows, 128),
        out_f(2, rows, 128),
        out_f(rows, keys),
        out(KEY_VALUE_HEADS, 2 * SHARE * rows, 128),
        out_f(rows, width),
    ]
    layers = (2,) if complete else ()
    return pl.pallas_call(
        lambda *refs: layers_kernel(complete, *refs),
        out_shape=[
            out(*ends.shape),
            out(*ends.shape),
            out_f(8, width),
            out(op_rows, width),
            out(op_rows, ff),
            out(op_rows, ff // 2),
            out(op_rows, ff // 2),
            out(op_rows, 512),
            out(op_rows, width),
            out(late_rows, width),
            out(op_rows, width),
            out(late_rows, 384),
        ]
        + ([] if complete else kept),
        in_specs=[pl.BlockSpec(memory_space=pltpu.SMEM), hbm] + [vmem] * 3 + [hbm] * 7,
        out_specs=[hbm] * (12 if complete else 19),
        scratch_shapes=[
            pltpu.VMEM(wq.shape, BF16),
            pltpu.VMEM((kv_width, width), BF16),
            pltpu.VMEM(wo.shape, BF16),
            pltpu.VMEM(wg.shape, BF16),
            pltpu.VMEM(wu.shape, BF16),
            pltpu.VMEM(wd.shape, BF16),
            pltpu.VMEM((3, rows, width), BF16),
            pltpu.VMEM((3, rows, width), BF16),
            pltpu.VMEM((2, rows, width), F32),
            pltpu.VMEM((2, rows, width), BF16),
            pltpu.VMEM((2, rows, ff), BF16),
            pltpu.VMEM((2, rows, ff), BF16),
            pltpu.VMEM((2, rows, ff), BF16),
            pltpu.VMEM((2, 2, rows, width), BF16),
            pltpu.VMEM((2, KEY_VALUE_HEADS, 2 * SHARE * rows, 128), BF16),
            pltpu.VMEM((2, KEY_VALUE_HEADS, keys, 128), BF16),
            pltpu.VMEM((2, QUERY_HEADS, rows, 128), F32),
            pltpu.VMEM((rows, width), F32),
            pltpu.VMEM((rows, width), F32),
            pltpu.VMEM((rows, ff), BF16),
            pltpu.VMEM((rows, ff), BF16),
            pltpu.VMEM((rows, 1024), BF16),
            pltpu.VMEM((2, rows, width), BF16),
            pltpu.VMEM((2 * SHARE * rows, keys), BF16),
            pltpu.VMEM((KEY_VALUE_HEADS, keys, 128), BF16),
            pltpu.VMEM(layers + (KEY_VALUE_HEADS, 3 * rows, 128), BF16),
            pltpu.VMEM((rows, kv_width), BF16),
            pltpu.VMEM((2, rows, 128), F32),
            pltpu.VMEM((rows, keys), F32),
            pltpu.VMEM((8, width), F32),
            dma(5),
            dma(2, KEY_VALUE_HEADS),
            dma(2),
            dma(2),
            dma(2, 3, KEY_VALUE_HEADS),
            dma(2, 3, KEY_VALUE_HEADS),
            dma(*layers, 2, KEY_VALUE_HEADS),
            dma(*layers, 3, KEY_VALUE_HEADS),
            dma(2),
            dma(2),
            dma(2),
            dma(2),
            dma(9, 2),
            dma(9, 2),
            dma(9, 2),
            dma(len(kept) + 2),
        ],
        compiler_params=pltpu.CompilerParams(
            collective_id=1, has_side_effects=True, vmem_limit_bytes=61 * 2**20
        ),
        name="layers",
    )(lengths, ends, frequency, gain_attn, gain_ffn, *weights)


MIDDLE_ORDER = (
    "near1", "head0", "head1", "head2", "head3", "near3", "down0", "head4",
    "down1", "far1", "query0", "near0", "far3", "near2", "aend0", "tready0",
    "far0", "fadd1", "down2", "fadd3", "tnear3", "tnear1", "down3", "down4",
    "far2", "fadd0", "down5", "fz0", "tnear0", "tnear2", "fadd2", "dfirst0",
    "tfar3", "fz1", "tfar0", "tfar2", "fz2", "tfar1", "tadd0", "dsecond0",
    "ftotal0", "tadd2", "tadd3", "dgather0", "tz0", "tz1", "tadd1", "tz2",
    "fmiddle0", "ttotal0", "dmiddle0",
)
END_ORDER = (
    "near0", "down0", "head0", "head1", "down1", "near1", "head2", "head3",
    "head4", "far0", "near3", "down2", "query0", "far1", "down3", "down4",
    "near2", "aend0", "fadd0", "tready0", "down5", "fadd1", "fz0", "tnear3",
    "far3", "far2", "tnear0", "fadd3", "fz2", "tnear2", "fadd2", "tnear1",
    "fz1", "tfar3", "tfar0", "dfirst0", "tadd0", "tfar2", "tfar1", "tadd3",
    "tz0", "dsecond0", "tadd1", "tz2", "ftotal0", "tadd2", "tz1", "dgather0",
    "fmiddle0", "ttotal0", "dmiddle0",
)


def sums_kernel(*refs):
    refs = list(refs)

    def take(count):
        taken = refs[:count]
        del refs[:count]
        return taken

    gain_h, gain_a, nf_h, in_h, gg_h, gu_h, br_h, la_h, ra_h, nr_h, kvg_h = take(11)
    act_h, kv_h, o_h, cs_h, allowed_h, qd_h, gm_h, wq_h, wk_h, wv_h = take(10)
    grads_o, t_o, gate_o, up_o, down_o = take(5)
    stage, in_v, br_v, gg_v, gu_v, ra_v, kvg_v, nf_t, ln_t, in_t, gain_t = take(11)
    act, kv, o_raw, cos_sin, allowed, qd, gm, wq, wkv = take(9)
    go, ra, dkv, dkv_in, gkv, sum_acc, gain_rows = take(7)
    d_out, d_in, d_keep, d1_out, d1_in, d2_out, d2_in = take(7)
    f1_out, f1_in, f2_out, f2_in, f_keep, fz_in = take(6)
    t1_out, t1_in, t2_out, t2_in, t_keep, tz_in = take(6)
    d_all, f_all, t_all = take(3)
    load, kept_sem, w_sem, dk_s, dk_r, grad_s, grad_r, op_own, op_s, op_r = take(10)
    dz_s, dz_r, d1_s, d1_r, d2_s, d2_r, f1_s, f1_r, f2_s, f2_r, fz_s, fz_r = take(12)
    t1_s, t1_r, t2_s, t2_r, tz_s, tz_r, all_s, all_r, pair_r, write = take(10)

    section = lax.axis_index("section")
    z = lax.axis_index("dp")
    ctx = lax.axis_index("ctx")
    x, y = ctx % 2, ctx // 2
    rank = 2 * section + x
    x_next = (section, z, 2 * y + 1 - x)
    y_next = (section, z, 2 * (1 - y) + x)
    partner = (1 - section, z, ctx)
    rows = act.shape[0]
    width = nf_h.shape[1]
    per = width // RANKS
    part = f_keep.shape[2]
    shift = per - part
    quarter = gg_v.shape[1] // 2
    deep = in_t.shape[0]
    fine = deep // 2
    last = RANKS - 1
    edge = ((z == 0) | (z == last)).astype(jnp.int32)

    def pick(index, values):
        if isinstance(index, int):
            return values[index]
        return sum((index == i).astype(jnp.int32) * v for i, v in enumerate(values) if not (type(v) is int and v == 0))

    def remote(src, dst, send, recv, device):
        return pltpu.make_async_remote_copy(
            src_ref=src, dst_ref=dst, send_sem=send, recv_sem=recv,
            device_id=device, device_id_type=MESH,
        )

    def some(start, size, unit=16):
        return pl.ds(pl.multiple_of(start, unit), size)

    gain_load = pltpu.make_async_copy(gain_h, gain_rows.at[pl.ds(0, gain_h.shape[0])], load.at[9])
    by_need = ((3, 2, 1, 0), (3, 0, 2, 1), (0, 3, 1, 2), (0, 1, 2, 3))
    by_turns = ((3, 2, 1, 0), (3, 0, 2, 1), (0, 3, 1, 2), (0, 2, 1, 3))

    def turn_of(k, order=by_need):
        return pick(k, [pick(z, [row[i] for row in order]) for i in range(RANKS)])

    def in_load(k):
        return pltpu.make_async_copy(
            in_h.at[:, some(turn_of(k) * deep, deep, 128)], in_v, load.at[0]
        )

    loads = [None] + [
        pltpu.make_async_copy(h, v, load.at[1 + i])
        for i, (h, v) in enumerate(
            [(br_h, br_v), (nf_h, stage), (la_h, stage), (nr_h, stage)]
        )
    ]
    halves = [
        [
            pltpu.make_async_copy(h.at[:, span], v.at[:, span], load.at[slot + 2 * own])
            for h, v, first, slot in ((gg_h, gg_v, x, 5), (gu_h, gu_v, y, 6))
            for span in (some((own * first + (1 - own) * (1 - first)) * quarter, quarter, 128),)
        ]
        for own in range(2)
    ]
    kept = [
        pltpu.make_async_copy(h, v, kept_sem.at[i])
        for i, (h, v) in enumerate(
            [(qd_h, qd), (kv_h, kv), (o_h, o_raw), (allowed_h, allowed), (cs_h, cos_sin),
             (gm_h, gm), (act_h, act)]
        )
    ]
    late = [
        pltpu.make_async_copy(h.at[pl.ds(c * rows, rows)], v.at[pl.ds((2 * c + 1) * rows, rows)], w_sem.at[i, c])
        for i, (h, v) in enumerate([(ra_h, ra_v), (kvg_h, kvg_v)])
        for c in range(2)
    ]
    weights = [pltpu.make_async_copy(wq_h, wq, w_sem.at[2, 0])] + [
        pltpu.make_async_copy(
            h.at[pl.ds(g * HEAD_SIZE, HEAD_SIZE)],
            wkv.at[pl.ds((2 * g + i) * HEAD_SIZE, HEAD_SIZE)],
            w_sem.at[3 + i, g],
        )
        for g in range(KEY_VALUE_HEADS)
        for i, h in enumerate((wk_h, wv_h))
    ]
    loads[2].start()
    for copy in halves[0]:
        copy.start()
    gain_rows[...] = jnp.zeros_like(gain_rows)

    barrier = pltpu.get_barrier_semaphore()
    greet(barrier, z)
    not_first = (z > 0).astype(jnp.int32)
    not_last = (z < last).astype(jnp.int32)

    @pl.when(z > 0)
    def _():
        pl.semaphore_signal(barrier, inc=1, device_id=(section, z - 1, ctx), device_id_type=MESH)

    @pl.when(z < last)
    def _():
        pl.semaphore_signal(barrier, inc=1, device_id=(section, z + 1, ctx), device_id_type=MESH)

    def turn(src, dst, base=0):
        for at, size in tiles(src.shape[1], 128):
            block = src[:, at : at + size]
            if size < 128:
                block = wide(block)
            dst[base + at : base + at + size, :] = block.T[:size]

    def z_way(t):
        up = (z < t).astype(jnp.int32)
        to = z + 2 * up - 1
        arrives = up * not_first + (1 - up) * not_last
        meets = (1 - up) * (t == z - 1).astype(jnp.int32)
        return (section, to, ctx), arrives, t * (1 - meets) + RANKS * meets

    def d_block(k):
        in_load(k).wait()
        for b in range(deep // 128):
            in_t[b * 128 : (b + 1) * 128, :] = in_v[:, b * 128 : (b + 1) * 128].T

        if not isinstance(k, int):

            @pl.when(k < last)
            def _():
                in_load(k + 1).start()

    def d_send(k, sub):
        device, _, slot = z_way(turn_of(k))
        span = some(sub * fine, fine)
        return remote(d_out.at[k, span], d_in.at[slot, span], dz_s.at[k, sub], dz_r.at[slot, sub], device)

    def d_step(n):
        k, sub = n // 2, n % 2

        @pl.when(n == 0)
        def _():
            loads[1].wait()

        @pl.when(sub == 0)
        def _():
            d_block(k)

        t = turn_of(k)
        _, arrives, _ = z_way(t)
        span = some(sub * fine, fine)
        mine = dot(in_t[span, :], br_v[...])

        @pl.when(arrives == 0)
        def _():
            d_out[k, span, :] = mine.astype(BF16)

        @pl.when(arrives == 1)
        def _():
            remote(d_out.at[k, span], d_in.at[t, span], dz_s.at[k, sub], dz_r.at[t, sub], partner).wait_recv()
            d_out[k, span, :] = (mine + d_in[t, span, :].astype(F32)).astype(BF16)

        d_send(k, sub).start()

    def f_links(k):
        return (x_next, y_next, x, y) if k == 0 else (y_next, x_next, y, x)

    def f_right(k, column_half):
        src = gg_v if k == 0 else gu_v
        return src[:, some(column_half * quarter, quarter, 128)]

    turns = (3, 0, 2, 1)

    def f1_copy(k, i):
        d = pick(i, turns)
        return remote(f1_out.at[k, i % 2], f1_in.at[k, d], f1_s.at[k, i % 2], f1_r.at[k, d], f_links(k)[0])

    def f2_copy(k, i):
        d = pick(i, turns)
        return remote(f2_out.at[k, i % 2], f2_in.at[k, d], f2_s.at[k, i % 2], f2_r.at[k, d], f_links(k)[1])

    def f1_step(i):
        left = nf_t[some(pick(i, turns) * per, per), :]
        for k in range(2):
            value = dot(left, f_right(k, 1 - f_links(k)[2])).astype(BF16)

            @pl.when(i >= 2)
            def _():
                f1_copy(k, i).wait_send()

            f1_out[k, i % 2] = value
            f1_copy(k, i).start()

    def f2_step(i):
        d = pick(i, turns)
        for k in range(2):
            first, second = f_links(k)[2:]
            f1_copy(k, i).wait_recv()

            def total(which):
                return (
                    dot(nf_t[some(d * per + which * shift, part), :], f_right(k, first))
                    + f1_in[k, d, some(which * shift, part), :].astype(F32)
                ).astype(BF16)

            value = total(1 - second)

            @pl.when(i >= 2)
            def _():
                f2_copy(k, i).wait_send()

            f2_out[k, i % 2] = value
            f2_copy(k, i).start()
            f_keep[k, d] = total(second)

    def t_links(d):
        x_first = (d < RANKS // 2) * 1
        choose = lambda a, b: x_first * a + (1 - x_first) * b
        ways = [tuple(choose(a, b) for a, b in zip(*pair)) for pair in ((x_next[1:], y_next[1:]), (y_next[1:], x_next[1:]))]
        return (section, *ways[0]), (section, *ways[1]), choose(x, y), choose(y, x)

    def t_product(row, count, add, dst):
        full = width // 128 * 128
        mine = dot(ln_t[some(row, count), :], ra_v[...])
        dst[:, :full] = add(mine[:, :full], 0).astype(BF16)
        tail = jnp.concatenate([mine[:, full:], gain_t[some(row, count), width - full :]], axis=1)
        dst[:, full : full + 128] = add(tail, full).astype(BF16)
        pairs = dot(ln_t[some(width + row, count), :], kvg_v[...])
        dst[:, full + 128 :] = add(pairs, full + 128).astype(BF16)

    def t1_copy(d):
        return remote(t1_out.at[d], t1_in.at[d], t1_s.at[d], t1_r.at[d], t_links(d)[0])

    def t2_copy(d):
        return remote(t2_out.at[d], t2_in.at[d], t2_s.at[d], t2_r.at[d], t_links(d)[1])

    def t1_step(d):
        first = t_links(d)[2]
        t_product(d * per + (1 - first) * shift, part, lambda v, at: v, t1_out.at[d])
        t1_copy(d).start()

    def t2_step(d):
        _, _, first, second = t_links(d)
        t1_copy(d).wait_recv()
        for which, dst in ((1 - second, t2_out), (second, t_keep)):
            row = which * (part // 2)
            add = lambda v, at: v + t1_in[d, some(row, part // 2), at : at + v.shape[1]].astype(F32)
            t_product(d * per + first * shift + row, part // 2, add, dst.at[d])
            if dst is t2_out:
                t2_copy(d).start()

    class Line:
        def __init__(self, keep, second_in, z_in, send, recv):
            self.keep, self.second_in, self.z_in, self.send, self.recv = keep, second_in, z_in, send, recv

        def add(self, copy, d):
            copy.wait_recv()
            self.keep[d] = (self.keep[d].astype(F32) + self.second_in[d].astype(F32)).astype(BF16)

        def copy(self, k):
            d = turn_of(k, by_turns)
            device, _, slot = z_way(d)
            return remote(self.keep.at[d], self.z_in.at[slot], self.send.at[k], self.recv.at[slot], device)

        def step(self, k):
            d = turn_of(k, by_turns)
            _, arrives, _ = z_way(d)

            @pl.when(arrives == 1)
            def _():
                remote(self.keep.at[d], self.z_in.at[d], self.send.at[k], self.recv.at[d], partner).wait_recv()
                self.keep[d] = (self.keep[d].astype(F32) + self.z_in[d].astype(F32)).astype(BF16)

            self.copy(k).start()

        def total(self):
            for condition, slot in ((z > 0, z), (z < last, RANKS)):

                @pl.when(condition)
                def _(slot=slot):
                    remote(self.keep.at[0], self.z_in.at[slot], self.send.at[0], self.recv.at[slot], partner).wait_recv()

            value = self.keep[z].astype(F32)
            return z_total(value, self.z_in[z], self.z_in[RANKS])

    def z_total(value, up, down):
        value = value + jnp.where(z > 0, up.astype(F32), 0.0)
        return value + jnp.where(z < last, down.astype(F32), 0.0)

    lines = [
        Line(f_keep.at[k], f2_in.at[k], fz_in.at[k], fz_s.at[k], fz_r.at[k]) for k in range(2)
    ] + [Line(t_keep, t2_in, tz_in, tz_s, tz_r)]

    def f_add(i):
        for k in range(2):
            lines[k].add(f2_copy(k, i), pick(i, turns))

    def t_add(d):
        lines[2].add(t2_copy(d), d)

    def f_line(k):
        lines[0].step(k)
        lines[1].step(k)

    def places(x_first):
        a, b = (1, 0) if x_first is True else (0, 1) if x_first is False else (x_first, 1 - x_first)
        spot = lambda i, j: a * (2 * i + j) + b * (2 * j + i)
        return spot(x, y), spot(1 - x, y), spot(x, 1 - y), spot(1 - x, 1 - y)

    class Gather:
        def __init__(self, number, buffer, x_first):
            self.n, self.buffer = number, buffer
            self.own, self.over_x, self.over_y, self.across = places(x_first)
            size = buffer.shape[2]
            cut = (size // 2 + 15) // 16 * 16
            self.halves = (pl.ds(0, cut), pl.ds(cut, size - cut))

        def whole(self, spot, slot, device):
            ref = self.buffer.at[section, spot]
            return remote(ref, ref, all_s.at[self.n, slot], all_r.at[self.n, slot], device)

        def relay(self, spot, half, device):
            ref = self.buffer.at[section, spot, self.halves[half]]
            return remote(ref, ref, all_s.at[self.n, 2 + half], all_r.at[self.n, 2 + half], device)

        def pair(self, core, spot, slot):
            ref = self.buffer.at[core, spot]
            return remote(ref, ref, all_s.at[self.n, 4 + slot], pair_r.at[self.n, spot], partner)

        def start(self, value):
            self.buffer[section, self.own] = value.astype(BF16)
            self.whole(self.own, 0, x_next).start()
            self.whole(self.own, 1, y_next).start()
            self.pair(section, self.own, 0).start()

        def middle(self):
            self.whole(self.over_x, 0, x_next).wait_recv()
            self.relay(self.over_x, 0, y_next).start()
            self.pair(section, self.over_x, 1).start()
            self.whole(self.over_y, 1, y_next).wait_recv()
            self.relay(self.over_y, 1, x_next).start()
            self.pair(section, self.over_y, 2).start()

        def finish(self):
            self.relay(self.across, 0, y_next).wait_recv()
            self.relay(self.across, 1, x_next).wait_recv()
            self.pair(section, self.across, 3).start()
            for spot in (self.own, self.over_x, self.over_y, self.across):
                self.pair(1 - section, spot, 0).wait_recv()

        def sent(self):
            self.whole(self.own, 0, x_next).wait_send()
            self.whole(self.own, 1, y_next).wait_send()
            self.relay(self.over_x, 0, y_next).wait_send()
            self.relay(self.over_y, 1, x_next).wait_send()
            for slot, spot in enumerate((self.own, self.over_x, self.over_y, self.across)):
                self.pair(section, spot, slot).wait_send()

    below = (z < RANKS // 2).astype(jnp.int32)
    gathers = [
        Gather(0, d_all.at[0], True),
        Gather(1, d_all.at[1], False),
        Gather(2, f_all.at[0], True),
        Gather(3, f_all.at[1], False),
        Gather(4, t_all, below),
    ]

    def d1_copy(h):
        return remote(d1_out.at[h], d1_in.at[h], d1_s.at[h], d1_r.at[h], f_links(h)[0])

    def d2_copy(h):
        return remote(d2_out.at[h], d2_in.at[h], d2_s.at[h], d2_r.at[h], f_links(h)[1])

    def d_first(h):
        span = pl.ds(h * fine, fine)
        for condition, slot in ((z > 0, z), (z < last, RANKS)):

            @pl.when(condition)
            def _(slot=slot):
                remote(d_out.at[0, span], d_in.at[slot, span], dz_s.at[0, h], dz_r.at[slot, h], partner).wait_recv()

        first = f_links(h)[2]
        for mine in (False, True):
            at = h * fine + (first if mine else 1 - first) * (fine // 2)
            piece = some(at, fine // 2)
            total = z_total(dot(in_t[piece, :], br_v[...]), d_in[z, piece, :], d_in[RANKS, piece, :])
            if mine:
                d_keep[h] = total
            else:
                d1_out[h] = total.astype(BF16)
                d1_copy(h).start()

    def d_second(h):
        second = f_links(h)[3]
        d1_copy(h).wait_recv()
        for mine in (False, True):
            piece = some((second if mine else 1 - second) * (fine // 4), fine // 4)
            total = d_keep[h, piece, :] + d1_in[h, piece, :].astype(F32)
            if mine:
                d_keep[h, : fine // 4, :] = total
            else:
                d2_out[h] = total.astype(BF16)
                d2_copy(h).start()

    def d_gather(h):
        d2_copy(h).wait_recv()
        gathers[h].start(d_keep[h, : fine // 4, :] + d2_in[h].astype(F32))

    back = AttentionBack(
        rank, lambda r: (r // 2, z, 2 * y + r % 2), qd, kv, o_raw, allowed, cos_sin, ra,
        ln_t.at[pl.ds(0, 2 * SHARE * rows)], dkv, dkv_in, gkv, dk_s, dk_r,
    )
    grads_out = OutCopy(grads_o, grad_s, grad_r)

    def op_copy(kind, own):
        role = section if own else 1 - section
        src = ra.at[role] if kind == 0 else gkv.at[:, some(role * 256, 384, 128)]
        dst = (ra_v, kvg_v)[kind].at[some(2 * section * rows, rows)]
        if own:
            return pltpu.make_async_copy(src, dst, op_own.at[kind])
        return remote(src, dst, op_s.at[kind], op_r.at[kind], partner)

    def op_start(kind):
        op_copy(kind, True).start()
        op_copy(kind, False).start()

    def attention_end():
        back.collect()
        op_start(1)
        for copy in weights:
            copy.wait()
        kept[6].wait()
        back.project(sum_acc, wq, wkv)
        grad, gain_row = norm_back(act[...].astype(F32), gain_a[...].astype(F32).reshape(1, width), sum_acc[...])
        gain_load.wait()
        gain_rows[0:1, :] += gain_row
        go[...] = (gm[...] + grad).astype(BF16)
        grads_out.start(go, 0)

    def t_ready():
        loads[3].wait()
        turn(stage, ln_t)
        loads[4].start()
        block_of = lambda at, size: wide(gain_rows[:, at : at + size]).T
        for at, size in tiles(width, 128):
            gain_t[at : at + size, :] = pltpu.roll(block_of(at, size), 64, 1)[:size]
        loads[4].wait()
        turn(stage, ln_t, width)
        for copy in late:
            copy.wait()
        for kind in range(2):
            op_copy(kind, True).wait()
            op_copy(kind, False).wait_recv()

    def both(step):
        step(0)
        step(1)

    def head_step(g):
        @pl.when(g == 0)
        def _():
            for copy in halves[1] + kept[:6]:
                copy.wait()
            ra[1] = gm[...].astype(BF16)

        back.head(g)

        @pl.when(g > 0)
        def _():
            back.relay(g - 1)

    def queries_step():
        back.relay(KEY_VALUE_HEADS - 1)
        back.queries()
        op_start(0)

    def d_first_step():
        d_block(last)
        both(d_first)

    def f_total():
        both(lambda k: gathers[2 + k].start(lines[k].total()))

    actions = {
        "near": f1_step,
        "far": f2_step,
        "tnear": t1_step,
        "tfar": t2_step,
        "down": d_step,
        "head": head_step,
        "fadd": f_add,
        "fz": f_line,
        "tadd": t_add,
        "tz": lines[2].step,
        "query": lambda p: queries_step(),
        "aend": lambda p: attention_end(),
        "tready": lambda p: t_ready(),
        "dfirst": lambda p: d_first_step(),
        "dsecond": lambda p: both(d_second),
        "dgather": lambda p: both(d_gather),
        "ftotal": lambda p: f_total(),
        "ttotal": lambda p: gathers[4].start(lines[2].total()),
        "fmiddle": lambda p: both(lambda k: gathers[2 + k].middle()),
        "dmiddle": lambda p: both(lambda h: gathers[h].middle()),
    }
    names = list(actions)

    def codes(table):
        return [8 * names.index(step.rstrip("0123456789")) + int(step[-1]) for step in table]

    tables = [codes(MIDDLE_ORDER), codes(END_ORDER)]
    steps = max(len(t) for t in tables)

    loads[2].wait()
    turn(stage, nf_t)
    for copy in halves[0]:
        copy.wait()
    in_load(0).start()
    loads[1].start()
    for copy in halves[1] + kept + weights + late + [gain_load]:
        copy.start()
    pl.semaphore_wait(barrier, 7 + not_first + not_last)
    loads[3].start()

    def one(n, carry):
        code = (1 - edge) * pick(n, tables[0]) + edge * pick(n, tables[1])
        lax.switch(code // 8, list(actions.values()), code % 8)
        return carry

    lax.fori_loop(0, steps, one, 0)

    writes = []

    def leave(src, dst):
        writes.append(pltpu.make_async_copy(src, dst, write.at[len(writes)]))
        writes[-1].start()

    for k in range(2):
        gathers[2 + k].finish()
        for core in range(2):
            for f in range(2):
                columns = pl.ds((2 * core + f) * quarter, quarter)
                out = (gate_o, up_o)[k]
                leave(f_all.at[k, core, 2 * f], out.at[pl.ds(0, part), columns])
                rest = pl.ds(part - shift, per - part)
                leave(f_all.at[k, core, 2 * f + 1, rest], out.at[pl.ds(part, per - part), columns])
    gathers[4].middle()
    for h in range(2):
        gathers[h].finish()
        for core in range(2):
            for spot in range(4):
                span = pl.ds(h * fine + spot * (fine // 4), fine // 4)
                leave(d_all.at[h, core, spot], down_o.at[span, pl.ds(core * br_v.shape[1], br_v.shape[1])])
    gathers[4].finish()
    t_rows = part // 2
    for core in range(2):
        for spot in range(4):
            row = spot % 2 * t_rows + spot // 2 * shift
            skip = part - shift if spot == 2 else 0
            rest = pl.ds(skip, t_rows - skip)
            leave(t_all.at[core, spot, rest], t_o.at[core, pl.ds(row + skip, t_rows - skip)])

    for k in range(last):
        for sub in range(2):
            d_send(k, sub).wait_send()
        for line in lines:
            line.copy(k).wait_send()
    for h in range(2):
        d1_copy(h).wait_send()
        d2_copy(h).wait_send()
    for k in range(2):
        for i in (2, 3):
            f1_copy(k, i).wait_send()
            f2_copy(k, i).wait_send()
    for d in range(RANKS):
        t1_copy(d).wait_send()
        t2_copy(d).wait_send()
    for kind in range(2):
        op_copy(kind, False).wait_send()
    grads_out.sent(go, 0)

    @pl.when(section == 0)
    def _():
        grads_out.arrived(go)

    for gather in gathers:
        gather.sent()
    for copy in writes:
        copy.wait()


def run_sums(gain_sums, gain_attn, operands, kept, weights, ends_shape):
    nf, inner, gg, gu, br, la, ra, nr, kvg = operands
    act, kv, o_raw, cos_sin, allowed, qd, gm = kept
    depth, width = nf.shape
    rows = act.shape[0]
    ff, half = inner.shape[1], gg.shape[1]
    per, deep = width // RANKS, ff // RANKS
    part = (per // 2 + 15) // 16 * 16
    quarter, fine = half // 2, deep // 2
    columns = br.shape[1]
    wide_t = width // 128 * 128 + 128 + kvg.shape[1]
    vmem, hbm = pl.BlockSpec(memory_space=pltpu.VMEM), pl.BlockSpec(memory_space=pl.ANY)
    out = lambda *shape: jax.ShapeDtypeStruct(shape, BF16)
    b = lambda *shape: pltpu.VMEM(shape, BF16)
    f = lambda *shape: pltpu.VMEM(shape, F32)
    like = lambda a: pltpu.VMEM(a.shape, a.dtype)
    sem = lambda *shape: pltpu.SemaphoreType.DMA(shape)
    return pl.pallas_call(
        sums_kernel,
        out_shape=[
            out(*ends_shape), out(2, per, wide_t), out(per, ff), out(per, ff), out(deep, 2 * columns),
        ],
        in_specs=[hbm, vmem] + [hbm] * 19,
        out_specs=[hbm] * 5,
        scratch_shapes=[
            b(depth, width), b(depth, deep), b(depth, columns), b(depth, half), b(depth, half),
            b(depth, width), b(depth, kvg.shape[1]),
            b(width, depth), b(2 * width, depth), b(deep, depth), f(width, 128),
            like(act), like(kv), like(o_raw), like(cos_sin), like(allowed), like(qd), like(gm),
            like(weights[0]), b(2 * weights[1].shape[0], width),
            b(rows, width), b(2, rows, width), like(kv), b(KEY_VALUE_HEADS, 3 * rows, 128), b(rows, KEY_VALUE_HEADS * 128),
            f(rows, width), f(128, width),
            b(RANKS - 1, deep, columns), b(5, deep, columns), f(2, fine // 2, columns),
            b(2, fine // 2, columns), b(2, fine // 2, columns), b(2, fine // 4, columns), b(2, fine // 4, columns),
            b(2, 2, per, quarter), b(2, RANKS, per, quarter),
            b(2, 2, part, quarter), b(2, RANKS, part, quarter), b(2, RANKS, part, quarter), b(2, 5, part, quarter),
            b(RANKS, part, wide_t), b(RANKS, part, wide_t),
            b(RANKS, part // 2, wide_t), b(RANKS, part // 2, wide_t), b(RANKS, part // 2, wide_t), b(5, part // 2, wide_t),
            b(2, 2, 4, fine // 4, columns), b(2, 2, 4, part, quarter), b(2, 4, part // 2, wide_t),
            sem(10), sem(7), sem(5, KEY_VALUE_HEADS), sem(2, KEY_VALUE_HEADS), sem(3, KEY_VALUE_HEADS), sem(2), sem(2), sem(2), sem(2), sem(2),
            sem(3, 2), sem(5, 2), sem(2), sem(2), sem(2), sem(2),
            sem(2, 2), sem(2, 4), sem(2, 2), sem(2, 4), sem(2, 3), sem(2, 5),
            sem(4), sem(4), sem(4), sem(4), sem(3), sem(5),
            sem(5, 8), sem(5, 4), sem(5, 4), sem(40),
        ],
        compiler_params=pltpu.CompilerParams(
            collective_id=2, has_side_effects=True, vmem_limit_bytes=61 * 2**20
        ),
        name="sums",
    )(gain_sums, gain_attn, *operands, *kept, *weights)


def finish_kernel(
    acts_h, first_h, second_h, t_h, gate_h, up_h, down_h,
    acts_o, grads_o, q_o, out_o, key_o, value_o, gain_a, gain_f, gate_o, up_o, down_o,
    row_v, t_v, gate_v, down_v, q_f, kv_f, gate_f, down_f, load, store,
):
    width = q_f.shape[2]
    loads = [
        pltpu.make_async_copy(h, v, load.at[i])
        for i, (h, v) in enumerate(
            [(gate_h, gate_v.at[0]), (up_h, gate_v.at[1]), (down_h, down_v), (t_h, t_v), (acts_h, row_v.at[0])]
        )
    ]
    stores = [
        pltpu.make_async_copy(v, h, store.at[i])
        for i, (v, h) in enumerate(
            [(row_v.at[0], acts_o), (row_v.at[1], grads_o), (gate_f.at[0], gate_o), (gate_f.at[1], up_o),
             (down_f, down_o), (q_f.at[0], q_o), (q_f.at[1], out_o), (kv_f.at[0], key_o), (kv_f.at[1], value_o)]
        )
    ]
    section = lax.axis_index("section")
    for copy in loads:
        copy.start()
    start_if(
        section == 0,
        lambda: pltpu.make_async_copy(first_h, row_v.at[1], load.at[5]),
        lambda: pltpu.make_async_copy(second_h, row_v.at[1], load.at[5]),
    )
    for k in range(2):
        loads[k].wait()
        gate_f[k] = gate_v[k].astype(F32)
        stores[2 + k].start()
    loads[2].wait()
    for at, size in tiles(width, 128):
        down_f[at : at + size, :] = down_v[:, at : at + 128].astype(F32).T[:size]
    stores[4].start()
    loads[3].wait()
    for core in range(2):
        q_f[core] = t_v[core, :, :width].astype(F32)
        stores[5 + core].start()
    pairs_at = width // 128 * 128 + 128
    half = KEY_VALUE_HEADS // 2 + 1
    for g in range(KEY_VALUE_HEADS):
        core = 0 if g < half else 1
        at = pairs_at + (g - core * (KEY_VALUE_HEADS - half)) * 128
        block = t_v[core, :, at : at + 128].astype(F32).T
        kv_f[0, g * HEAD_SIZE : (g + 1) * HEAD_SIZE, :] = block[:HEAD_SIZE]
        kv_f[1, g * HEAD_SIZE : (g + 1) * HEAD_SIZE, :] = block[HEAD_SIZE:]
    for copy in stores[7:]:
        copy.start()
    tail = slice(pairs_at - 128, pairs_at)
    both = t_v[0, :, tail].astype(F32) + t_v[1, :, tail].astype(F32)
    row = width % 128
    gain_rows = both.T
    gain_a[...] = gain_rows[row]
    gain_f[...] = gain_rows[row + 1]
    loads[4].wait()
    stores[0].start()
    pltpu.make_async_copy(first_h, row_v.at[1], load.at[5]).wait()
    stores[1].start()
    for copy in stores:
        copy.wait()


def run_finish(acts, grads_first, grads_second, t_sum, gate, up, down, width):
    per, ff = gate.shape
    vmem, hbm = pl.BlockSpec(memory_space=pltpu.VMEM), pl.BlockSpec(memory_space=pl.ANY)
    out = lambda *shape: jax.ShapeDtypeStruct(shape, F32)
    kv_rows = KEY_VALUE_HEADS * HEAD_SIZE
    return pl.pallas_call(
        finish_kernel,
        out_shape=[
            jax.ShapeDtypeStruct(acts.shape, BF16), jax.ShapeDtypeStruct(acts.shape, BF16),
            out(per, width), out(per, width), out(kv_rows, per), out(kv_rows, per), out(per), out(per),
            out(per, ff), out(per, ff), out(width, down.shape[0]),
        ],
        in_specs=[hbm] * 7,
        out_specs=[hbm] * 6 + [vmem] * 2 + [hbm] * 3,
        scratch_shapes=[
            pltpu.VMEM((2, *acts.shape), BF16), pltpu.VMEM(t_sum.shape, BF16), pltpu.VMEM((2, per, ff), BF16), pltpu.VMEM(down.shape, BF16),
            pltpu.VMEM((2, per, width), F32), pltpu.VMEM((2, kv_rows, per), F32),
            pltpu.VMEM((2, per, ff), F32), pltpu.VMEM((width, down.shape[0]), F32),
            pltpu.SemaphoreType.DMA((6,)), pltpu.SemaphoreType.DMA((9,)),
        ],
        compiler_params=pltpu.CompilerParams(vmem_limit_bytes=61 * 2**20),
        name="finish",
    )(acts, grads_first, grads_second, t_sum, gate, up, down)


def sums_by_xla(gain_sums, operands):
    nf, inner, gg, gu, br, la, ra, nr, kvg = operands
    width = nf.shape[1]

    def reduced(left, right):
        total = dot_lt(left, right).astype(BF16)
        piece = lax.psum_scatter(total, "dp", scatter_dimension=0, tiled=True)
        return lax.psum(piece, "ctx")

    def both(piece, axis):
        return lax.all_gather(piece, "section", axis=axis, tiled=axis > 0).astype(F32)

    attn = both(reduced(la, ra), 0)
    gain_sum = lax.psum(gain_sums[:2], ("section", "ctx"))
    return (
        attn[0],
        attn[1],
        both(reduced(nr, kvg), 0),
        lax.psum_scatter(gain_sum, "dp", scatter_dimension=1, tiled=True),
        both(reduced(nf, gg), 1),
        both(reduced(nf, gu), 1),
        both(reduced(inner, br), 1)[:, :width],
    )


def shards(
    ends,
    doc_lengths,
    w_query,
    key_projection_weight,
    value_projection_weight,
    w_out,
    w_gate,
    w_up,
    w_down,
    gain_attn,
    gain_ffn,
):
    width = ends.shape[3]
    half = HEAD_SIZE // 2
    turns = np.float32(10000.0) ** (
        np.float32(-2.0) * (np.arange(128) % half).astype(np.float32) / np.float32(HEAD_SIZE)
    )
    weights = (
        w_query,
        key_projection_weight.T,
        value_projection_weight.T,
        w_out,
        w_gate,
        w_up,
        w_down.T,
    )
    ff = w_gate.shape[1]
    fits = lax.axis_size("dp") == RANKS and width % 64 == 0 and ff % 1280 == 0
    acts, grads_in, gain_sums, *kept = run_layers(
        doc_lengths,
        ends,
        jnp.asarray(turns.reshape(1, 128), F32),
        gain_attn,
        gain_ffn,
        weights,
        not fits,
    )
    operands = kept[:9]
    if fits:
        grads_first, *sums = run_sums(
            gain_sums, gain_attn, operands, kept[9:], weights[:3], ends.shape
        )
        acts, grads_in, grad_query, grad_out, grad_key, grad_value, *gain_piece, grad_gate, grad_up, grad_down = (
            run_finish(acts, grads_first, grads_in, *sums, width)
        )
        grad_key, grad_value, grad_down = grad_key.T, grad_value.T, grad_down.T
    else:
        grad_query, grad_out, kv_parts, gain_piece, grad_gate, grad_up, grad_down = sums_by_xla(
            gain_sums, operands
        )
        kv_grad = jnp.concatenate([kv_parts[0], kv_parts[1][:, 128:]], axis=1).reshape(
            -1, KEY_VALUE_HEADS, 2, HEAD_SIZE
        )
        grad_key = kv_grad[:, :, 0].reshape(kv_grad.shape[0], -1)
        grad_value = kv_grad[:, :, 1].reshape(kv_grad.shape[0], -1)
    return (
        acts,
        grads_in,
        grad_query,
        grad_key,
        grad_value,
        grad_out,
        grad_gate,
        grad_up,
        grad_down,
        gain_piece[0],
        gain_piece[1],
    )


def solution(mesh):
    return jax.shard_map(
        shards,
        mesh=mesh,
        in_specs=(P("section", None, ("dp", "ctx"), None), P(None, "dp", None)) + (P(),) * 9,
        out_specs=(P("section", None, ("dp", "ctx"), None),) * 2
        + (P("dp", None),) * 7
        + (P("dp"),) * 2,
        check_vma=False,
    )
```

```python
import jax
import jax.numpy as jnp
import numpy as np
from jax import lax
from jax.experimental import pallas as pl
from jax.experimental.pallas import tpu as pltpu
from jax.sharding import PartitionSpec as P

MESH = pl.DeviceIdType.MESH
QUERY_HEADS = 15
KEY_VALUE_HEADS = 5
HEAD_SIZE = 64
SHARE = QUERY_HEADS // KEY_VALUE_HEADS
RANKS = 4
epsilon = 1e-05
masked_fill = -1e30
F32 = jnp.float32
BF16 = jnp.bfloat16


def dot(left, right):
    return jnp.dot(left, right, preferred_element_type=F32)


def dot_rt(left, right):
    return lax.dot_general(left, right, (((1,), (1,)), ((), ())), preferred_element_type=F32)


def dot_lt(left, right):
    return lax.dot_general(left, right, (((0,), (0,)), ((), ())), preferred_element_type=F32)


def tiles(total, width):
    return [(at, min(width, total - at)) for at in range(0, total, width)]


def wide(block):
    missing = 128 - block.shape[1]
    if not missing:
        return block
    return jnp.concatenate([block, jnp.zeros((block.shape[0], missing), block.dtype)], axis=1)


def lanes(rows):
    return lax.broadcasted_iota(jnp.int32, (rows, 128), 1)


def half_turn(block):
    front = lanes(block.shape[0]) % HEAD_SIZE < HEAD_SIZE // 2
    return jnp.where(front, pltpu.roll(block, 96, 1), pltpu.roll(block, 32, 1))


def inverse_rms(hidden):
    return lax.rsqrt(jnp.mean(hidden * hidden, axis=-1, keepdims=True) + epsilon)


def half_turned(block, cosines, sines, direction):
    return block * cosines + direction * (half_turn(block) * sines)


def norm_back(hidden, gain, upstream):
    scale = inverse_rms(hidden)
    weighted = upstream * gain
    inside = jnp.mean(weighted * hidden, axis=-1, keepdims=True)
    gain_row = jnp.sum(upstream * hidden * scale, axis=0, keepdims=True)
    return scale * weighted - hidden * (scale * scale * scale * inside), gain_row


def start_if(condition, here, there):
    @pl.when(condition)
    def _():
        here().start()

    @pl.when(jnp.logical_not(condition))
    def _():
        there().start()


class AttentionBack:
    def __init__(
        self, rank, device_of, qd, kv, o_raw, allowed, cos_sin, ra, pds, dkv, dkv_in, gkv, send, recv
    ):
        self.rank, self.device_of = rank, device_of
        self.qd, self.kv, self.o_raw, self.allowed, self.cos_sin = qd, kv, o_raw, allowed, cos_sin
        self.ra, self.pds, self.dkv, self.dkv_in, self.gkv = ra, pds, dkv, dkv_in, gkv
        self.send_sem, self.recv_sem = send, recv
        self.rows, self.width = ra.shape[1:]

    def head(self, g):
        rows = self.rows
        kv_g = self.kv[g]
        mine = [slice(i * rows, (i + 1) * rows) for i in range(SHARE)]
        other = [slice((SHARE + i) * rows, (SHARE + i + 1) * rows) for i in range(SHARE)]
        all_scores = [dot_rt(self.qd[g, span, :], kv_g) + self.allowed[...] for span in mine]
        for i, scores in enumerate(all_scores):
            kept = self.o_raw[g * SHARE + i]
            probs = jnp.exp(scores - kept[:, 0:1])
            grad_out = self.qd[g, other[i], :]
            grad_probs = dot_rt(grad_out, kv_g)
            weight = jnp.sum(grad_out.astype(F32) * kept, axis=-1, keepdims=True)
            grad_scores = (probs * (grad_probs - weight)).astype(BF16)
            self.pds[mine[i], :] = grad_scores
            self.pds[other[i], :] = probs.astype(BF16)
            self.o_raw[g * SHARE + i] = dot(grad_scores, kv_g)
        grad_kv = dot_lt(self.qd[g], self.pds[...])
        self.dkv[g] = grad_kv.T.astype(BF16)
        self.send(g)

    def heads(self, first, last):
        def body(g, carry):
            self.head(g)

            @pl.when(g > 0)
            def _():
                self.relay(g - 1)

            return carry

        lax.fori_loop(first, last, body, 0)

    def copy(self, quarter, count, dst, slot_in, slot, g):
        rows = self.rows
        return pltpu.make_async_remote_copy(
            src_ref=self.dkv.at[g, pl.ds(quarter * rows, count * rows)],
            dst_ref=self.dkv_in.at[g, pl.ds(slot_in * rows, count * rows)],
            send_sem=self.send_sem.at[slot, g],
            recv_sem=self.recv_sem.at[slot_in, g],
            device_id=self.device_of(dst),
            device_id_type=MESH,
        )

    def add(self, quarter, slots, g):
        rows = self.rows
        span = slice(quarter * rows, (quarter + 1) * rows)
        total = self.dkv[g, span].astype(F32)
        for slot in slots:
            total = total + self.dkv_in[g, slot * rows : (slot + 1) * rows].astype(F32)
        self.dkv[g, span] = total.astype(BF16)

    def send(self, g):
        @pl.when(self.rank == 3)
        def _():
            self.copy(2, 1, 2, 0, 0, g).start()
            self.copy(0, 2, 1, 0, 1, g).start()

        @pl.when(self.rank == 2)
        def _():
            self.copy(1, 1, 1, 2, 0, g).start()
            self.copy(0, 1, 0, 1, 1, g).start()

    def relay(self, g):
        @pl.when(self.rank == 1)
        def _():
            self.copy(0, 2, 1, 0, 0, g).wait_recv()
            self.add(0, (0,), g)
            self.copy(0, 1, 0, 0, 0, g).start()

    def queries(self):
        for at, size in tiles(self.width, 128):
            head = at // HEAD_SIZE
            block = self.o_raw[head]
            if size == 128:
                low = lanes(self.rows) < HEAD_SIZE
                block = jnp.where(low, block, pltpu.roll(self.o_raw[head + 1], 64, 1))
            turned = half_turned(block, self.cos_sin[0], self.cos_sin[1], -1.0) * 0.125
            self.ra[0, :, at : at + size] = turned[:, :size].astype(BF16)

    def collect(self):
        low = lanes(self.rows) < HEAD_SIZE
        cosines = jnp.where(low, self.cos_sin[0], 1.0)
        sines = jnp.where(low, self.cos_sin[1], 0.0)
        mine = pl.ds(pl.multiple_of(self.rank * self.rows, 16), self.rows)
        for g in range(KEY_VALUE_HEADS):
            self.arrive(g)
            block = half_turned(self.dkv[g, mine, :].astype(F32), cosines, sines, -1.0)
            self.gkv[:, 128 * g : 128 * g + 128] = block.astype(BF16)

    def arrive(self, g):
        @pl.when(self.rank == 3)
        def _():
            self.copy(2, 1, 2, 0, 0, g).wait_send()
            self.copy(0, 2, 1, 0, 1, g).wait_send()

        @pl.when(self.rank == 2)
        def _():
            self.copy(0, 1, 2, 0, 0, g).wait_recv()
            self.copy(1, 1, 1, 2, 0, g).wait_send()
            self.copy(0, 1, 0, 1, 1, g).wait_send()
            self.add(2, (0,), g)

        @pl.when(self.rank == 1)
        def _():
            self.copy(0, 1, 2, 2, 0, g).wait_recv()
            self.copy(0, 1, 0, 0, 0, g).wait_send()
            self.add(1, (1, 2), g)

        @pl.when(self.rank == 0)
        def _():
            self.copy(0, 1, 2, 0, 0, g).wait_recv()
            self.copy(0, 1, 2, 1, 0, g).wait_recv()
            self.add(0, (0, 1), g)

    def project(self, total, wq, wkv):
        for at, size in tiles(self.width, 256):
            total[:, at : at + size] = dot_rt(self.ra[0], wq[at : at + size, :]) + dot(
                self.gkv[...], wkv[:, at : at + size]
            )


class OutCopy:
    def __init__(self, out, send, recv):
        self.section, self.dp, ctx = (lax.axis_index(a) for a in ("section", "dp", "ctx"))
        self.home = 2 * self.section + ctx % 2
        self.ctx, self.micro = ctx, ctx // 2
        self.out, self.send, self.recv = out, send, recv

    def here(self, l):
        return (self.section == l) & (self.ctx == self.home)

    def remote(self, array, l):
        return pltpu.make_async_remote_copy(
            src_ref=array,
            dst_ref=self.out.at[0, self.micro],
            send_sem=self.send.at[l],
            recv_sem=self.recv.at[self.micro],
            device_id=(l, self.dp, self.home),
            device_id_type=MESH,
        )

    def local(self, array):
        return pltpu.make_async_copy(array, self.out.at[0, self.micro], self.recv.at[self.micro])

    def start(self, array, l):
        start_if(self.here(l), lambda: self.local(array), lambda: self.remote(array, l))

    def sent(self, array, l):
        @pl.when(jnp.logical_not(self.here(l)))
        def _():
            self.remote(array, l).wait_send()

    def arrived(self, array):
        for block in range(2):
            pltpu.make_async_copy(array, self.out.at[0, block], self.recv.at[block]).wait()


def greet(barrier, dp):
    section, ctx = lax.axis_index("section"), lax.axis_index("ctx")
    for step in range(1, 8):
        other = (4 * section + ctx + step) % 8
        pl.semaphore_signal(
            barrier, inc=1, device_id=(other // 4, dp, other % 4), device_id_type=MESH
        )


def layers_kernel(complete, *refs):
    refs = list(refs)

    def take(count):
        taken = refs[:count]
        del refs[:count]
        return taken

    lengths, ends, frequency, gain_a, gain_f, wq_h, wk_h, wv_h, wo_h, wg_h, wu_h, wd_h = take(12)
    acts_o, grads_o, gain_o, nf_o, in_o, gg_o, gu_o, br_o, la_o, ra_o, nr_o, kvg_o = take(12)
    kept_o = [] if complete else take(7)
    wq, wkv, wo, wg, wu, wd = take(6)
    act, go, middle, norm_ffn, fact_a, fact_b, inner, lm, qd, kv, o_raw = take(11)
    sum_acc, gm, gg, gu, br, ra, pds, dkv, dkv_in, gkv, cos_sin, allowed_add, gain_v = take(13)
    w_sem, kv_sem, in_send, in_recv, kv_send, kv_recv, dk_send, dk_recv = take(8)
    act_send, act_recv, grad_send, grad_recv, op_own, op_send, op_recv, kept_sem = take(8)

    section = lax.axis_index("section")
    dp = lax.axis_index("dp")
    ctx = lax.axis_index("ctx")
    micro = ctx // 2
    xbit = ctx % 2
    rank = 2 * section + xbit
    rows, width = act.shape[1], act.shape[2]
    ff = wg.shape[1]
    ff_half = ff // 2

    def device_of(r):
        return (r // 2, dp, 2 * micro + r % 2)

    partner = (1 - section, dp, ctx)

    loads = [
        pltpu.make_async_copy(h, v, w_sem.at[i])
        for i, (h, v) in enumerate([(wq_h, wq), (wo_h, wo), (wg_h, wg), (wu_h, wu), (wd_h, wd)])
    ]
    kv_loads = [
        pltpu.make_async_copy(
            h.at[pl.ds(g * HEAD_SIZE, HEAD_SIZE)],
            wkv.at[pl.ds((2 * g + i) * HEAD_SIZE, HEAD_SIZE)],
            kv_sem.at[i, g],
        )
        for g in range(KEY_VALUE_HEADS)
        for i, h in enumerate((wk_h, wv_h))
    ]
    for load in kv_loads + loads:
        load.start()
    kv[...] = jnp.zeros_like(kv)
    barrier = pltpu.get_barrier_semaphore()
    greet(barrier, dp)
    pl.semaphore_wait(barrier, 7)

    def in_local(block, into_x):
        dst, slot = (act.at[0], 0) if into_x else (go.at[2], 1)
        return pltpu.make_async_copy(ends.at[0, block], dst, in_recv.at[slot])

    def in_remote(block, into_x):
        dst, slot = (act.at[0], 0) if into_x else (go.at[2], 1)
        return pltpu.make_async_remote_copy(
            src_ref=ends.at[0, block],
            dst_ref=dst,
            send_sem=in_send.at[block],
            recv_sem=in_recv.at[slot],
            device_id=(ctx // 2, dp, 2 * block + xbit),
            device_id_type=MESH,
        )

    def in_mine(block):
        return (section == ctx // 2) & (ctx // 2 == block)

    def in_start(into_x):
        @pl.when(section == (0 if into_x else 1))
        def _():
            for block in range(2):
                start_if(
                    in_mine(block),
                    lambda block=block: in_local(block, into_x),
                    lambda block=block: in_remote(block, into_x),
                )

    in_start(True)
    lane = lanes(rows)
    low = lane < HEAD_SIZE
    gain_attn = gain_a[...].astype(F32).reshape(1, width)
    gain_ffn = gain_f[...].astype(F32).reshape(1, width)

    def place(token_index):
        segment = jnp.zeros_like(token_index)
        start = jnp.zeros_like(token_index)
        finish = jnp.int32(0)
        for slot in range(lengths.shape[2]):
            length = lengths[micro, 0, slot]
            finish = finish + length
            passed = (token_index >= finish).astype(jnp.int32)
            segment = segment + passed
            start = start + passed * length
        return segment, token_index - start

    seg_mine, position = place(rank * rows + lax.broadcasted_iota(jnp.int32, (rows, 128), 0))
    angles = position.astype(F32) * frequency[...]
    cos_sin[0] = jnp.cos(angles)
    cos_sin[1] = jnp.where(lane % HEAD_SIZE < HEAD_SIZE // 2, -1.0, 1.0) * jnp.sin(angles)
    key_index = lax.broadcasted_iota(jnp.int32, (1, RANKS * rows), 1)
    query_index = rank * rows + lax.broadcasted_iota(jnp.int32, (rows, 1), 0)
    allowed_add[...] = jnp.where(
        (seg_mine[:, 0:1] == place(key_index)[0]) & (query_index >= key_index), 0.0, masked_fill
    )

    def kv_rows(l, r, g):
        return kv.at[l, g, pl.ds(pl.multiple_of(r * rows, 16), rows)]

    def kv_copy(l, quarter, dst, slot, g):
        return pltpu.make_async_remote_copy(
            src_ref=kv_rows(l, quarter, g),
            dst_ref=kv_rows(l, quarter, g),
            send_sem=kv_send.at[l, slot, g],
            recv_sem=kv_recv.at[l, quarter, g],
            device_id=device_of(dst),
            device_id_type=MESH,
        )

    def kv_start(l, g):
        @pl.when(rank < 3)
        def _():
            kv_copy(l, rank, rank + 1, 0, g).start()

        @pl.when(rank < 2)
        def _():
            kv_copy(l, rank, rank + 2, 1, g).start()

    def kv_relayed(l, g):
        @pl.when(rank == 1)
        def _():
            kv_copy(l, 0, 3, 2, g).wait_recv()
            kv_copy(l, 0, 3, 2, g).start()

    def kv_finish(l, g):
        @pl.when(rank >= 2)
        def _():
            kv_copy(l, 0, 0, 0, g).wait_recv()
            kv_copy(l, 1, 0, 0, g).wait_recv()

        @pl.when(rank == 3)
        def _():
            kv_copy(l, 2, 0, 0, g).wait_recv()

    def kv_sent(l):
        for senders, slot in ((3, 0), (2, 1)):

            @pl.when(rank < senders)
            def _(slot=slot):
                for g in range(KEY_VALUE_HEADS):
                    kv_copy(l, rank, rank + 1 + slot, slot, g).wait_send()

        @pl.when(rank == 1)
        def _():
            for g in range(KEY_VALUE_HEADS):
                kv_copy(l, 0, 3, 2, g).wait_send()

    acts_out = OutCopy(acts_o, act_send, act_recv)
    grads_out = OutCopy(grads_o, grad_send, grad_recv)

    def op_copy(kind, l, own):
        role = section if own else 1 - section
        half = pl.ds(pl.multiple_of(role * ff_half, 128), ff_half)
        src = [
            lambda: norm_ffn.at[l],
            lambda: inner.at[l],
            lambda: gg.at[:, half],
            lambda: gu.at[:, half],
            lambda: br.at[:, pl.ds(pl.multiple_of(role * 512, 128), 512)],
            lambda: lm.at[l, role],
            lambda: ra.at[role],
            lambda: lm.at[l, 0],
            lambda: gkv.at[:, pl.ds(pl.multiple_of(role * 256, 128), 384)],
        ][kind]()
        block = section if kind in (6, 8) and not complete else 2 * section + l
        dst = [nf_o, in_o, gg_o, gu_o, br_o, la_o, ra_o, nr_o, kvg_o][kind].at[
            pl.ds(pl.multiple_of(block * rows, 16), rows)
        ]
        if own:
            return pltpu.make_async_copy(src, dst, op_own.at[kind, l])
        return pltpu.make_async_remote_copy(
            src_ref=src,
            dst_ref=dst,
            send_sem=op_send.at[kind, l],
            recv_sem=op_recv.at[kind, l],
            device_id=partner,
            device_id_type=MESH,
        )

    def op_start(kinds, l):
        for kind in kinds:
            op_copy(kind, l, True).start()
            op_copy(kind, l, False).start()

    def op_sent(kinds, l):
        for kind in kinds:
            op_copy(kind, l, True).wait()
            op_copy(kind, l, False).wait_send()

    def kept_copy(i):
        if i == 7:
            part = pl.ds(0, SHARE * rows)
            return pltpu.make_async_copy(qd.at[0, :, part], kept_o[5].at[:, part], kept_sem.at[8])
        if i == 5:
            part = pl.ds(SHARE * rows, SHARE * rows)
            return pltpu.make_async_copy(qd.at[0, :, part], kept_o[5].at[:, part], kept_sem.at[5])
        src = [act.at[0], kv.at[0], o_raw.at[0], cos_sin, allowed_add, None, gm][i]
        return pltpu.make_async_copy(src, kept_o[i], kept_sem.at[i])

    def kept_start(*which):
        if not complete:
            for i in which:
                kept_copy(i).start()

    in_remote(0, True).wait_recv()
    for load in kv_loads:
        load.wait()

    def forward(l, carry):
        hidden = act[l].astype(F32)
        cos_q, sin_q = cos_sin[0], cos_sin[1]
        lm[l, 0] = (hidden * inverse_rms(hidden) * gain_attn).astype(BF16)
        cos_kv = jnp.where(low, cos_q, 1.0)
        sin_kv = jnp.where(low, sin_q, 0.0)
        mine = pl.ds(pl.multiple_of(rank * rows, 16), rows)
        for g in range(KEY_VALUE_HEADS):
            block = dot_rt(lm[l, 0], wkv[128 * g : 128 * g + 128, :])
            turned = half_turned(block, cos_kv, sin_kv, 1.0)
            kv[l, g, mine, :] = turned.astype(BF16)
        for g in range(KEY_VALUE_HEADS):
            kv_start(l, g)

        @pl.when(l == 0)
        def _():
            loads[0].wait()
            in_start(False)
            kept_start(0, 3, 4)

        for at, size in tiles(width, 256):
            product = dot(lm[l, 0], wq[:, at : at + size])
            for inside, part in tiles(size, 128):
                block = wide(product[:, inside : inside + part])
                turned = half_turned(block, cos_q, sin_q, 1.0) * 0.125
                head = (at + inside) // HEAD_SIZE
                qd[l, head // SHARE, pl.ds(head % SHARE * rows, rows), :] = jnp.where(
                    low, turned, 0.0
                ).astype(BF16)
                head += 1
                if head < QUERY_HEADS:
                    qd[l, head // SHARE, pl.ds(head % SHARE * rows, rows), :] = jnp.where(
                        low, pltpu.roll(turned, 64, 1), 0.0
                    ).astype(BF16)
        kv_relayed(l, 0)
        kv_finish(l, 0)

        def heads(g, carry):
            @pl.when(g < KEY_VALUE_HEADS - 1)
            def _():
                kv_relayed(l, g + 1)

            @pl.when(g > 0)
            def _():
                kv_finish(l, g)

            kv_g = kv[l, g]
            all_scores = [
                dot_rt(qd[l, g, i * rows : (i + 1) * rows, :], kv_g) + allowed_add[...]
                for i in range(SHARE)
            ]
            for i, scores in enumerate(all_scores):
                peak = jnp.max(scores, axis=-1, keepdims=True)
                exponent = jnp.exp(scores - peak)
                total = jnp.sum(exponent, axis=-1, keepdims=True)
                out = dot(exponent.astype(BF16), kv_g) * (1.0 / total)
                o_raw[l, g * SHARE + i] = jnp.where(low, peak + jnp.log(total), out)
            return carry

        lax.fori_loop(0, KEY_VALUE_HEADS, heads, 0)

        @pl.when(l == 0)
        def _():
            kept_start(1, 2, 7)
            loads[1].wait()

        for at, size in tiles(width, 128):
            head = at // HEAD_SIZE
            block = pltpu.roll(o_raw[l, head], 64, 1)
            if size == 128:
                block = jnp.where(low, block, o_raw[l, head + 1])
            lm[l, 1, :, at : at + size] = block[:, :size].astype(BF16)
        for at, size in tiles(width, 256):
            middle[l, :, at : at + size] = act[l, :, at : at + size].astype(F32) + dot(
                lm[l, 1], wo[:, at : at + size]
            )
        mid = middle[l]
        norm_ffn[l] = (mid * inverse_rms(mid) * gain_ffn).astype(BF16)
        op_start((0, 5, 7), l)

        @pl.when(l == 0)
        def _():
            loads[2].wait()
            loads[3].wait()

        def gates(j, carry):
            part = pl.ds(pl.multiple_of(j * 1280, 128), 1280)
            gate = dot(norm_ffn[l], wg[:, part])
            upper = dot(norm_ffn[l], wu[:, part])
            s = 0.5 * jnp.tanh(0.5 * gate) + 0.5
            swish = gate * s
            inner[l, :, part] = (swish * upper).astype(BF16)
            fact_a[l, :, part] = (upper * s * (1.0 + gate * (1.0 - s))).astype(BF16)
            fact_b[l, :, part] = swish.astype(BF16)
            return carry

        lax.fori_loop(0, ff // 1280, gates, 0)

        @pl.when(l == 0)
        def _():
            loads[4].wait()

        op_start((1,), l)
        for at, size in tiles(width, 256):
            act[l + 1, :, at : at + size] = (
                middle[l, :, at : at + size] + dot_rt(inner[l], wd[at : at + size, :])
            ).astype(BF16)
        acts_out.start(act.at[l + 1], l)
        kv_sent(l)
        return carry

    lax.fori_loop(0, 2, forward, 0)

    in_remote(0, False).wait_recv()
    gain_v[...] = jnp.zeros_like(gain_v)
    br[...] = jnp.zeros_like(br)
    late = (6, 8)

    def backward(step, carry):
        l = 1 - step

        @pl.when(l == 0)
        def _():
            op_sent((2, 3, 4) + (late if complete else ()), 1)

        br[:, :width] = go[l + 1]
        op_start((4,), l)

        def gates(j, carry):
            part = pl.ds(pl.multiple_of(j * 1280, 128), 1280)
            grad_inner = dot(go[l + 1], wd[:, part])
            gg[:, part] = (grad_inner * fact_a[l, :, part].astype(F32)).astype(BF16)
            gu[:, part] = (grad_inner * fact_b[l, :, part].astype(F32)).astype(BF16)
            return carry

        lax.fori_loop(0, ff // 1280, gates, 0)
        op_start((2, 3), l)
        for at, size in tiles(width, 256):
            sum_acc[:, at : at + size] = dot_rt(gg[...], wg[at : at + size, :]) + dot_rt(
                gu[...], wu[at : at + size, :]
            )
        grad, gain_row = norm_back(middle[l], gain_ffn, sum_acc[...])
        gain_v[1:2, :] += gain_row
        gm[...] = go[l + 1].astype(F32) + grad
        ra[1] = gm[...].astype(BF16)

        @pl.when(l == 0)
        def _():
            kept_start(6)

        for at, size in tiles(width, 256):
            product = dot_rt(ra[1], wo[at : at + size, :])
            for inside, part in tiles(size, 128):
                block = wide(product[:, inside : inside + part])
                head = (at + inside) // HEAD_SIZE
                qd[l, head // SHARE, pl.ds((SHARE + head % SHARE) * rows, rows), :] = jnp.where(
                    low, 0.0, pltpu.roll(block, 64, 1)
                ).astype(BF16)
                head += 1
                if head < QUERY_HEADS:
                    qd[l, head // SHARE, pl.ds((SHARE + head % SHARE) * rows, rows), :] = (
                        jnp.where(low, 0.0, block).astype(BF16)
                    )

        def attention():
            back = AttentionBack(
                rank, device_of, qd.at[l], kv.at[l], o_raw.at[l], allowed_add, cos_sin, ra, pds,
                dkv, dkv_in.at[l] if complete else dkv_in, gkv,
                dk_send.at[l] if complete else dk_send, dk_recv.at[l] if complete else dk_recv,
            )
            back.heads(0, KEY_VALUE_HEADS)
            back.relay(KEY_VALUE_HEADS - 1)
            back.queries()
            op_start((6,), l)
            back.collect()
            op_start((8,), l)
            back.project(sum_acc, wq, wkv)
            grad, gain_row = norm_back(act[l].astype(F32), gain_attn, sum_acc[...])
            gain_v[0:1, :] += gain_row
            go[l] = (gm[...] + grad).astype(BF16)
            grads_out.start(go.at[l], l)

        if complete:
            attention()
        else:

            @pl.when(l == 1)
            def _():
                attention()

            @pl.when(l == 1)
            def _():
                op_sent(late, 1)

        return carry

    lax.fori_loop(0, 2, backward, 0)

    gain_copy = pltpu.make_async_copy(gain_v, gain_o, kept_sem.at[7])
    gain_copy.start()
    kept_start(5)
    for into_x in (True, False):

        @pl.when(section == (0 if into_x else 1))
        def _(into_x=into_x):
            for block in range(2):

                @pl.when(jnp.logical_not(in_mine(block)))
                def _(block=block):
                    in_remote(block, into_x).wait_send()

    op_sent((2, 3, 4) + (late if complete else ()), 0)
    for l in range(2):
        op_sent((0, 1, 5, 7), l)
        for kind in range(9):
            if l == 1 or complete or kind not in late:
                op_copy(kind, l, False).wait_recv()
        acts_out.sent(act.at[l + 1], l)
        if l == 1 or complete:
            grads_out.sent(go.at[l], l)
    gain_copy.wait()
    acts_out.arrived(act.at[0])
    if complete:
        grads_out.arrived(act.at[0])
    else:

        @pl.when(section == 1)
        def _():
            grads_out.arrived(act.at[0])

        for i in range(len(kept_o) + 1):
            kept_copy(i).wait()


def run_layers(lengths, ends, frequency, gain_attn, gain_ffn, weights, complete):
    micro_count, rows, width = ends.shape[1:]
    wq, wk, wv, wo, wg, wu, wd = weights
    ff = wg.shape[1]
    keys = RANKS * rows
    kv_width = 2 * wk.shape[0]
    vmem, hbm = pl.BlockSpec(memory_space=pltpu.VMEM), pl.BlockSpec(memory_space=pl.ANY)
    op_rows = 4 * rows
    late_rows = op_rows if complete else 2 * rows
    out = lambda *shape: jax.ShapeDtypeStruct(shape, BF16)
    out_f = lambda *shape: jax.ShapeDtypeStruct(shape, F32)
    dma = lambda *shape: pltpu.SemaphoreType.DMA(shape)
    kept = [
        out(rows, width),
        out(KEY_VALUE_HEADS, keys, 128),
        out_f(QUERY_HEADS, rows, 128),
        out_f(2, rows, 128),
        out_f(rows, keys),
        out(KEY_VALUE_HEADS, 2 * SHARE * rows, 128),
        out_f(rows, width),
    ]
    layers = (2,) if complete else ()
    return pl.pallas_call(
        lambda *refs: layers_kernel(complete, *refs),
        out_shape=[
            out(*ends.shape),
            out(*ends.shape),
            out_f(8, width),
            out(op_rows, width),
            out(op_rows, ff),
            out(op_rows, ff // 2),
            out(op_rows, ff // 2),
            out(op_rows, 512),
            out(op_rows, width),
            out(late_rows, width),
            out(op_rows, width),
            out(late_rows, 384),
        ]
        + ([] if complete else kept),
        in_specs=[pl.BlockSpec(memory_space=pltpu.SMEM), hbm] + [vmem] * 3 + [hbm] * 7,
        out_specs=[hbm] * (12 if complete else 19),
        scratch_shapes=[
            pltpu.VMEM(wq.shape, BF16),
            pltpu.VMEM((kv_width, width), BF16),
            pltpu.VMEM(wo.shape, BF16),
            pltpu.VMEM(wg.shape, BF16),
            pltpu.VMEM(wu.shape, BF16),
            pltpu.VMEM(wd.shape, BF16),
            pltpu.VMEM((3, rows, width), BF16),
            pltpu.VMEM((3, rows, width), BF16),
            pltpu.VMEM((2, rows, width), F32),
            pltpu.VMEM((2, rows, width), BF16),
            pltpu.VMEM((2, rows, ff), BF16),
            pltpu.VMEM((2, rows, ff), BF16),
            pltpu.VMEM((2, rows, ff), BF16),
            pltpu.VMEM((2, 2, rows, width), BF16),
            pltpu.VMEM((2, KEY_VALUE_HEADS, 2 * SHARE * rows, 128), BF16),
            pltpu.VMEM((2, KEY_VALUE_HEADS, keys, 128), BF16),
            pltpu.VMEM((2, QUERY_HEADS, rows, 128), F32),
            pltpu.VMEM((rows, width), F32),
            pltpu.VMEM((rows, width), F32),
            pltpu.VMEM((rows, ff), BF16),
            pltpu.VMEM((rows, ff), BF16),
            pltpu.VMEM((rows, 1024), BF16),
            pltpu.VMEM((2, rows, width), BF16),
            pltpu.VMEM((2 * SHARE * rows, keys), BF16),
            pltpu.VMEM((KEY_VALUE_HEADS, keys, 128), BF16),
            pltpu.VMEM(layers + (KEY_VALUE_HEADS, 3 * rows, 128), BF16),
            pltpu.VMEM((rows, kv_width), BF16),
            pltpu.VMEM((2, rows, 128), F32),
            pltpu.VMEM((rows, keys), F32),
            pltpu.VMEM((8, width), F32),
            dma(5),
            dma(2, KEY_VALUE_HEADS),
            dma(2),
            dma(2),
            dma(2, 3, KEY_VALUE_HEADS),
            dma(2, 3, KEY_VALUE_HEADS),
            dma(*layers, 2, KEY_VALUE_HEADS),
            dma(*layers, 3, KEY_VALUE_HEADS),
            dma(2),
            dma(2),
            dma(2),
            dma(2),
            dma(9, 2),
            dma(9, 2),
            dma(9, 2),
            dma(len(kept) + 2),
        ],
        compiler_params=pltpu.CompilerParams(
            collective_id=1, has_side_effects=True, vmem_limit_bytes=61 * 2**20
        ),
        name="layers",
    )(lengths, ends, frequency, gain_attn, gain_ffn, *weights)


MIDDLE_ORDER = (
    "near1", "head0", "head1", "head2", "head3", "near3", "down0", "head4",
    "down1", "far1", "query0", "near0", "far3", "near2", "aend0", "tready0",
    "far0", "fadd1", "down2", "fadd3", "tnear3", "tnear1", "down3", "down4",
    "far2", "fadd0", "down5", "fz0", "tnear0", "tnear2", "fadd2", "dfirst0",
    "tfar3", "fz1", "tfar0", "tfar2", "fz2", "tfar1", "tadd0", "dsecond0",
    "ftotal0", "tadd2", "tadd3", "dgather0", "tz0", "tz1", "tadd1", "tz2",
    "fmiddle0", "ttotal0", "dmiddle0",
)
END_ORDER = (
    "near0", "down0", "head0", "head1", "down1", "near1", "head2", "head3",
    "head4", "far0", "near3", "down2", "query0", "far1", "down3", "down4",
    "near2", "aend0", "fadd0", "tready0", "down5", "fadd1", "fz0", "tnear3",
    "far3", "far2", "tnear0", "fadd3", "fz2", "tnear2", "fadd2", "tnear1",
    "fz1", "tfar3", "tfar0", "dfirst0", "tadd0", "tfar2", "tfar1", "tadd3",
    "tz0", "dsecond0", "tadd1", "tz2", "ftotal0", "tadd2", "tz1", "dgather0",
    "fmiddle0", "ttotal0", "dmiddle0",
)


def sums_kernel(*refs):
    refs = list(refs)

    def take(count):
        taken = refs[:count]
        del refs[:count]
        return taken

    gain_h, gain_a, nf_h, in_h, gg_h, gu_h, br_h, la_h, ra_h, nr_h, kvg_h = take(11)
    act_h, kv_h, o_h, cs_h, allowed_h, qd_h, gm_h, wq_h, wk_h, wv_h = take(10)
    grads_o, t_o, gate_o, up_o, down_o = take(5)
    stage, in_v, br_v, gg_v, gu_v, ra_v, kvg_v, nf_t, ln_t, in_t, gain_t = take(11)
    act, kv, o_raw, cos_sin, allowed, qd, gm, wq, wkv = take(9)
    go, ra, dkv, dkv_in, gkv, sum_acc, gain_rows = take(7)
    d_out, d_in, d_keep, d1_out, d1_in, d2_out, d2_in = take(7)
    f1_out, f1_in, f2_out, f2_in, f_keep, fz_in = take(6)
    t1_out, t1_in, t2_out, t2_in, t_keep, tz_in = take(6)
    d_all, f_all, t_all = take(3)
    load, kept_sem, w_sem, dk_s, dk_r, grad_s, grad_r, op_own, op_s, op_r = take(10)
    dz_s, dz_r, d1_s, d1_r, d2_s, d2_r, f1_s, f1_r, f2_s, f2_r, fz_s, fz_r = take(12)
    t1_s, t1_r, t2_s, t2_r, tz_s, tz_r, all_s, all_r, pair_r, write = take(10)

    section = lax.axis_index("section")
    z = lax.axis_index("dp")
    ctx = lax.axis_index("ctx")
    x, y = ctx % 2, ctx // 2
    rank = 2 * section + x
    x_next = (section, z, 2 * y + 1 - x)
    y_next = (section, z, 2 * (1 - y) + x)
    partner = (1 - section, z, ctx)
    rows = act.shape[0]
    width = nf_h.shape[1]
    per = width // RANKS
    part = f_keep.shape[2]
    shift = per - part
    quarter = gg_v.shape[1] // 2
    deep = in_t.shape[0]
    fine = deep // 2
    last = RANKS - 1
    edge = ((z == 0) | (z == last)).astype(jnp.int32)

    def pick(index, values):
        if isinstance(index, int):
            return values[index]
        return sum((index == i).astype(jnp.int32) * v for i, v in enumerate(values) if not (type(v) is int and v == 0))

    def remote(src, dst, send, recv, device):
        return pltpu.make_async_remote_copy(
            src_ref=src, dst_ref=dst, send_sem=send, recv_sem=recv,
            device_id=device, device_id_type=MESH,
        )

    def some(start, size, unit=16):
        return pl.ds(pl.multiple_of(start, unit), size)

    gain_load = pltpu.make_async_copy(gain_h, gain_rows.at[pl.ds(0, gain_h.shape[0])], load.at[9])
    by_need = ((3, 2, 1, 0), (3, 0, 2, 1), (0, 3, 1, 2), (0, 1, 2, 3))
    by_turns = ((3, 2, 1, 0), (3, 0, 2, 1), (0, 3, 1, 2), (0, 2, 1, 3))

    def turn_of(k, order=by_need):
        return pick(k, [pick(z, [row[i] for row in order]) for i in range(RANKS)])

    def in_load(k):
        return pltpu.make_async_copy(
            in_h.at[:, some(turn_of(k) * deep, deep, 128)], in_v, load.at[0]
        )

    loads = [None] + [
        pltpu.make_async_copy(h, v, load.at[1 + i])
        for i, (h, v) in enumerate(
            [(br_h, br_v), (nf_h, stage), (la_h, stage), (nr_h, stage)]
        )
    ]
    halves = [
        [
            pltpu.make_async_copy(h.at[:, span], v.at[:, span], load.at[slot + 2 * own])
            for h, v, first, slot in ((gg_h, gg_v, x, 5), (gu_h, gu_v, y, 6))
            for span in (some((own * first + (1 - own) * (1 - first)) * quarter, quarter, 128),)
        ]
        for own in range(2)
    ]
    kept = [
        pltpu.make_async_copy(h, v, kept_sem.at[i])
        for i, (h, v) in enumerate(
            [(qd_h, qd), (kv_h, kv), (o_h, o_raw), (allowed_h, allowed), (cs_h, cos_sin),
             (gm_h, gm), (act_h, act)]
        )
    ]
    late = [
        pltpu.make_async_copy(h.at[pl.ds(c * rows, rows)], v.at[pl.ds((2 * c + 1) * rows, rows)], w_sem.at[i, c])
        for i, (h, v) in enumerate([(ra_h, ra_v), (kvg_h, kvg_v)])
        for c in range(2)
    ]
    weights = [pltpu.make_async_copy(wq_h, wq, w_sem.at[2, 0])] + [
        pltpu.make_async_copy(
            h.at[pl.ds(g * HEAD_SIZE, HEAD_SIZE)],
            wkv.at[pl.ds((2 * g + i) * HEAD_SIZE, HEAD_SIZE)],
            w_sem.at[3 + i, g],
        )
        for g in range(KEY_VALUE_HEADS)
        for i, h in enumerate((wk_h, wv_h))
    ]
    loads[2].start()
    for copy in halves[0]:
        copy.start()
    gain_rows[...] = jnp.zeros_like(gain_rows)

    barrier = pltpu.get_barrier_semaphore()
    greet(barrier, z)
    not_first = (z > 0).astype(jnp.int32)
    not_last = (z < last).astype(jnp.int32)

    @pl.when(z > 0)
    def _():
        pl.semaphore_signal(barrier, inc=1, device_id=(section, z - 1, ctx), device_id_type=MESH)

    @pl.when(z < last)
    def _():
        pl.semaphore_signal(barrier, inc=1, device_id=(section, z + 1, ctx), device_id_type=MESH)

    def turn(src, dst, base=0):
        for at, size in tiles(src.shape[1], 128):
            block = src[:, at : at + size]
            if size < 128:
                block = wide(block)
            dst[base + at : base + at + size, :] = block.T[:size]

    def z_way(t):
        up = (z < t).astype(jnp.int32)
        to = z + 2 * up - 1
        arrives = up * not_first + (1 - up) * not_last
        meets = (1 - up) * (t == z - 1).astype(jnp.int32)
        return (section, to, ctx), arrives, t * (1 - meets) + RANKS * meets

    def d_block(k):
        in_load(k).wait()
        for b in range(deep // 128):
            in_t[b * 128 : (b + 1) * 128, :] = in_v[:, b * 128 : (b + 1) * 128].T

        if not isinstance(k, int):

            @pl.when(k < last)
            def _():
                in_load(k + 1).start()

    def d_send(k, sub):
        device, _, slot = z_way(turn_of(k))
        span = some(sub * fine, fine)
        return remote(d_out.at[k, span], d_in.at[slot, span], dz_s.at[k, sub], dz_r.at[slot, sub], device)

    def d_step(n):
        k, sub = n // 2, n % 2

        @pl.when(n == 0)
        def _():
            loads[1].wait()

        @pl.when(sub == 0)
        def _():
            d_block(k)

        t = turn_of(k)
        _, arrives, _ = z_way(t)
        span = some(sub * fine, fine)
        mine = dot(in_t[span, :], br_v[...])

        @pl.when(arrives == 0)
        def _():
            d_out[k, span, :] = mine.astype(BF16)

        @pl.when(arrives == 1)
        def _():
            remote(d_out.at[k, span], d_in.at[t, span], dz_s.at[k, sub], dz_r.at[t, sub], partner).wait_recv()
            d_out[k, span, :] = (mine + d_in[t, span, :].astype(F32)).astype(BF16)

        d_send(k, sub).start()

    def f_links(k):
        return (x_next, y_next, x, y) if k == 0 else (y_next, x_next, y, x)

    def f_right(k, column_half):
        src = gg_v if k == 0 else gu_v
        return src[:, some(column_half * quarter, quarter, 128)]

    turns = (3, 0, 2, 1)

    def f1_copy(k, i):
        d = pick(i, turns)
        return remote(f1_out.at[k, i % 2], f1_in.at[k, d], f1_s.at[k, i % 2], f1_r.at[k, d], f_links(k)[0])

    def f2_copy(k, i):
        d = pick(i, turns)
        return remote(f2_out.at[k, i % 2], f2_in.at[k, d], f2_s.at[k, i % 2], f2_r.at[k, d], f_links(k)[1])

    def f1_step(i):
        left = nf_t[some(pick(i, turns) * per, per), :]
        for k in range(2):
            value = dot(left, f_right(k, 1 - f_links(k)[2])).astype(BF16)

            @pl.when(i >= 2)
            def _():
                f1_copy(k, i).wait_send()

            f1_out[k, i % 2] = value
            f1_copy(k, i).start()

    def f2_step(i):
        d = pick(i, turns)
        for k in range(2):
            first, second = f_links(k)[2:]
            f1_copy(k, i).wait_recv()

            def total(which):
                return (
                    dot(nf_t[some(d * per + which * shift, part), :], f_right(k, first))
                    + f1_in[k, d, some(which * shift, part), :].astype(F32)
                ).astype(BF16)

            value = total(1 - second)

            @pl.when(i >= 2)
            def _():
                f2_copy(k, i).wait_send()

            f2_out[k, i % 2] = value
            f2_copy(k, i).start()
            f_keep[k, d] = total(second)

    def t_links(d):
        x_first = (d < RANKS // 2) * 1
        choose = lambda a, b: x_first * a + (1 - x_first) * b
        ways = [tuple(choose(a, b) for a, b in zip(*pair)) for pair in ((x_next[1:], y_next[1:]), (y_next[1:], x_next[1:]))]
        return (section, *ways[0]), (section, *ways[1]), choose(x, y), choose(y, x)

    def t_product(row, count, add, dst):
        full = width // 128 * 128
        mine = dot(ln_t[some(row, count), :], ra_v[...])
        dst[:, :full] = add(mine[:, :full], 0).astype(BF16)
        tail = jnp.concatenate([mine[:, full:], gain_t[some(row, count), width - full :]], axis=1)
        dst[:, full : full + 128] = add(tail, full).astype(BF16)
        pairs = dot(ln_t[some(width + row, count), :], kvg_v[...])
        dst[:, full + 128 :] = add(pairs, full + 128).astype(BF16)

    def t1_copy(d):
        return remote(t1_out.at[d], t1_in.at[d], t1_s.at[d], t1_r.at[d], t_links(d)[0])

    def t2_copy(d):
        return remote(t2_out.at[d], t2_in.at[d], t2_s.at[d], t2_r.at[d], t_links(d)[1])

    def t1_step(d):
        first = t_links(d)[2]
        t_product(d * per + (1 - first) * shift, part, lambda v, at: v, t1_out.at[d])
        t1_copy(d).start()

    def t2_step(d):
        _, _, first, second = t_links(d)
        t1_copy(d).wait_recv()
        for which, dst in ((1 - second, t2_out), (second, t_keep)):
            row = which * (part // 2)
            add = lambda v, at: v + t1_in[d, some(row, part // 2), at : at + v.shape[1]].astype(F32)
            t_product(d * per + first * shift + row, part // 2, add, dst.at[d])
            if dst is t2_out:
                t2_copy(d).start()

    class Line:
        def __init__(self, keep, second_in, z_in, send, recv):
            self.keep, self.second_in, self.z_in, self.send, self.recv = keep, second_in, z_in, send, recv

        def add(self, copy, d):
            copy.wait_recv()
            self.keep[d] = (self.keep[d].astype(F32) + self.second_in[d].astype(F32)).astype(BF16)

        def copy(self, k):
            d = turn_of(k, by_turns)
            device, _, slot = z_way(d)
            return remote(self.keep.at[d], self.z_in.at[slot], self.send.at[k], self.recv.at[slot], device)

        def step(self, k):
            d = turn_of(k, by_turns)
            _, arrives, _ = z_way(d)

            @pl.when(arrives == 1)
            def _():
                remote(self.keep.at[d], self.z_in.at[d], self.send.at[k], self.recv.at[d], partner).wait_recv()
                self.keep[d] = (self.keep[d].astype(F32) + self.z_in[d].astype(F32)).astype(BF16)

            self.copy(k).start()

        def total(self):
            for condition, slot in ((z > 0, z), (z < last, RANKS)):

                @pl.when(condition)
                def _(slot=slot):
                    remote(self.keep.at[0], self.z_in.at[slot], self.send.at[0], self.recv.at[slot], partner).wait_recv()

            value = self.keep[z].astype(F32)
            return z_total(value, self.z_in[z], self.z_in[RANKS])

    def z_total(value, up, down):
        value = value + jnp.where(z > 0, up.astype(F32), 0.0)
        return value + jnp.where(z < last, down.astype(F32), 0.0)

    lines = [
        Line(f_keep.at[k], f2_in.at[k], fz_in.at[k], fz_s.at[k], fz_r.at[k]) for k in range(2)
    ] + [Line(t_keep, t2_in, tz_in, tz_s, tz_r)]

    def f_add(i):
        for k in range(2):
            lines[k].add(f2_copy(k, i), pick(i, turns))

    def t_add(d):
        lines[2].add(t2_copy(d), d)

    def f_line(k):
        lines[0].step(k)
        lines[1].step(k)

    def places(x_first):
        a, b = (1, 0) if x_first is True else (0, 1) if x_first is False else (x_first, 1 - x_first)
        spot = lambda i, j: a * (2 * i + j) + b * (2 * j + i)
        return spot(x, y), spot(1 - x, y), spot(x, 1 - y), spot(1 - x, 1 - y)

    class Gather:
        def __init__(self, number, buffer, x_first):
            self.n, self.buffer = number, buffer
            self.own, self.over_x, self.over_y, self.across = places(x_first)
            size = buffer.shape[2]
            cut = (size // 2 + 15) // 16 * 16
            self.halves = (pl.ds(0, cut), pl.ds(cut, size - cut))

        def whole(self, spot, slot, device):
            ref = self.buffer.at[section, spot]
            return remote(ref, ref, all_s.at[self.n, slot], all_r.at[self.n, slot], device)

        def relay(self, spot, half, device):
            ref = self.buffer.at[section, spot, self.halves[half]]
            return remote(ref, ref, all_s.at[self.n, 2 + half], all_r.at[self.n, 2 + half], device)

        def pair(self, core, spot, slot):
            ref = self.buffer.at[core, spot]
            return remote(ref, ref, all_s.at[self.n, 4 + slot], pair_r.at[self.n, spot], partner)

        def start(self, value):
            self.buffer[section, self.own] = value.astype(BF16)
            self.whole(self.own, 0, x_next).start()
            self.whole(self.own, 1, y_next).start()
            self.pair(section, self.own, 0).start()

        def middle(self):
            self.whole(self.over_x, 0, x_next).wait_recv()
            self.relay(self.over_x, 0, y_next).start()
            self.pair(section, self.over_x, 1).start()
            self.whole(self.over_y, 1, y_next).wait_recv()
            self.relay(self.over_y, 1, x_next).start()
            self.pair(section, self.over_y, 2).start()

        def finish(self):
            self.relay(self.across, 0, y_next).wait_recv()
            self.relay(self.across, 1, x_next).wait_recv()
            self.pair(section, self.across, 3).start()
            for spot in (self.own, self.over_x, self.over_y, self.across):
                self.pair(1 - section, spot, 0).wait_recv()

        def sent(self):
            self.whole(self.own, 0, x_next).wait_send()
            self.whole(self.own, 1, y_next).wait_send()
            self.relay(self.over_x, 0, y_next).wait_send()
            self.relay(self.over_y, 1, x_next).wait_send()
            for slot, spot in enumerate((self.own, self.over_x, self.over_y, self.across)):
                self.pair(section, spot, slot).wait_send()

    below = (z < RANKS // 2).astype(jnp.int32)
    gathers = [
        Gather(0, d_all.at[0], True),
        Gather(1, d_all.at[1], False),
        Gather(2, f_all.at[0], True),
        Gather(3, f_all.at[1], False),
        Gather(4, t_all, below),
    ]

    def d1_copy(h):
        return remote(d1_out.at[h], d1_in.at[h], d1_s.at[h], d1_r.at[h], f_links(h)[0])

    def d2_copy(h):
        return remote(d2_out.at[h], d2_in.at[h], d2_s.at[h], d2_r.at[h], f_links(h)[1])

    def d_first(h):
        span = pl.ds(h * fine, fine)
        for condition, slot in ((z > 0, z), (z < last, RANKS)):

            @pl.when(condition)
            def _(slot=slot):
                remote(d_out.at[0, span], d_in.at[slot, span], dz_s.at[0, h], dz_r.at[slot, h], partner).wait_recv()

        first = f_links(h)[2]
        for mine in (False, True):
            at = h * fine + (first if mine else 1 - first) * (fine // 2)
            piece = some(at, fine // 2)
            total = z_total(dot(in_t[piece, :], br_v[...]), d_in[z, piece, :], d_in[RANKS, piece, :])
            if mine:
                d_keep[h] = total
            else:
                d1_out[h] = total.astype(BF16)
                d1_copy(h).start()

    def d_second(h):
        second = f_links(h)[3]
        d1_copy(h).wait_recv()
        for mine in (False, True):
            piece = some((second if mine else 1 - second) * (fine // 4), fine // 4)
            total = d_keep[h, piece, :] + d1_in[h, piece, :].astype(F32)
            if mine:
                d_keep[h, : fine // 4, :] = total
            else:
                d2_out[h] = total.astype(BF16)
                d2_copy(h).start()

    def d_gather(h):
        d2_copy(h).wait_recv()
        gathers[h].start(d_keep[h, : fine // 4, :] + d2_in[h].astype(F32))

    back = AttentionBack(
        rank, lambda r: (r // 2, z, 2 * y + r % 2), qd, kv, o_raw, allowed, cos_sin, ra,
        ln_t.at[pl.ds(0, 2 * SHARE * rows)], dkv, dkv_in, gkv, dk_s, dk_r,
    )
    grads_out = OutCopy(grads_o, grad_s, grad_r)

    def op_copy(kind, own):
        role = section if own else 1 - section
        src = ra.at[role] if kind == 0 else gkv.at[:, some(role * 256, 384, 128)]
        dst = (ra_v, kvg_v)[kind].at[some(2 * section * rows, rows)]
        if own:
            return pltpu.make_async_copy(src, dst, op_own.at[kind])
        return remote(src, dst, op_s.at[kind], op_r.at[kind], partner)

    def op_start(kind):
        op_copy(kind, True).start()
        op_copy(kind, False).start()

    def attention_end():
        back.collect()
        op_start(1)
        for copy in weights:
            copy.wait()
        kept[6].wait()
        back.project(sum_acc, wq, wkv)
        grad, gain_row = norm_back(act[...].astype(F32), gain_a[...].astype(F32).reshape(1, width), sum_acc[...])
        gain_load.wait()
        gain_rows[0:1, :] += gain_row
        go[...] = (gm[...] + grad).astype(BF16)
        grads_out.start(go, 0)

    def t_ready():
        loads[3].wait()
        turn(stage, ln_t)
        loads[4].start()
        block_of = lambda at, size: wide(gain_rows[:, at : at + size]).T
        for at, size in tiles(width, 128):
            gain_t[at : at + size, :] = pltpu.roll(block_of(at, size), 64, 1)[:size]
        loads[4].wait()
        turn(stage, ln_t, width)
        for copy in late:
            copy.wait()
        for kind in range(2):
            op_copy(kind, True).wait()
            op_copy(kind, False).wait_recv()

    def both(step):
        step(0)
        step(1)

    def head_step(g):
        @pl.when(g == 0)
        def _():
            for copy in halves[1] + kept[:6]:
                copy.wait()
            ra[1] = gm[...].astype(BF16)

        back.head(g)

        @pl.when(g > 0)
        def _():
            back.relay(g - 1)

    def queries_step():
        back.relay(KEY_VALUE_HEADS - 1)
        back.queries()
        op_start(0)

    def d_first_step():
        d_block(last)
        both(d_first)

    def f_total():
        both(lambda k: gathers[2 + k].start(lines[k].total()))

    actions = {
        "near": f1_step,
        "far": f2_step,
        "tnear": t1_step,
        "tfar": t2_step,
        "down": d_step,
        "head": head_step,
        "fadd": f_add,
        "fz": f_line,
        "tadd": t_add,
        "tz": lines[2].step,
        "query": lambda p: queries_step(),
        "aend": lambda p: attention_end(),
        "tready": lambda p: t_ready(),
        "dfirst": lambda p: d_first_step(),
        "dsecond": lambda p: both(d_second),
        "dgather": lambda p: both(d_gather),
        "ftotal": lambda p: f_total(),
        "ttotal": lambda p: gathers[4].start(lines[2].total()),
        "fmiddle": lambda p: both(lambda k: gathers[2 + k].middle()),
        "dmiddle": lambda p: both(lambda h: gathers[h].middle()),
    }
    names = list(actions)

    def codes(table):
        return [8 * names.index(step.rstrip("0123456789")) + int(step[-1]) for step in table]

    tables = [codes(MIDDLE_ORDER), codes(END_ORDER)]
    steps = max(len(t) for t in tables)

    loads[2].wait()
    turn(stage, nf_t)
    for copy in halves[0]:
        copy.wait()
    in_load(0).start()
    loads[1].start()
    for copy in halves[1] + kept + weights + late + [gain_load]:
        copy.start()
    pl.semaphore_wait(barrier, 7 + not_first + not_last)
    loads[3].start()

    def one(n, carry):
        code = (1 - edge) * pick(n, tables[0]) + edge * pick(n, tables[1])
        lax.switch(code // 8, list(actions.values()), code % 8)
        return carry

    lax.fori_loop(0, steps, one, 0)

    writes = []

    def leave(src, dst):
        writes.append(pltpu.make_async_copy(src, dst, write.at[len(writes)]))
        writes[-1].start()

    for k in range(2):
        gathers[2 + k].finish()
        for core in range(2):
            for f in range(2):
                columns = pl.ds((2 * core + f) * quarter, quarter)
                out = (gate_o, up_o)[k]
                leave(f_all.at[k, core, 2 * f], out.at[pl.ds(0, part), columns])
                rest = pl.ds(part - shift, per - part)
                leave(f_all.at[k, core, 2 * f + 1, rest], out.at[pl.ds(part, per - part), columns])
    gathers[4].middle()
    for h in range(2):
        gathers[h].finish()
        for core in range(2):
            for spot in range(4):
                span = pl.ds(h * fine + spot * (fine // 4), fine // 4)
                leave(d_all.at[h, core, spot], down_o.at[span, pl.ds(core * br_v.shape[1], br_v.shape[1])])
    gathers[4].finish()
    t_rows = part // 2
    for core in range(2):
        for spot in range(4):
            row = spot % 2 * t_rows + spot // 2 * shift
            skip = part - shift if spot == 2 else 0
            rest = pl.ds(skip, t_rows - skip)
            leave(t_all.at[core, spot, rest], t_o.at[core, pl.ds(row + skip, t_rows - skip)])

    for k in range(last):
        for sub in range(2):
            d_send(k, sub).wait_send()
        for line in lines:
            line.copy(k).wait_send()
    for h in range(2):
        d1_copy(h).wait_send()
        d2_copy(h).wait_send()
    for k in range(2):
        for i in (2, 3):
            f1_copy(k, i).wait_send()
            f2_copy(k, i).wait_send()
    for d in range(RANKS):
        t1_copy(d).wait_send()
        t2_copy(d).wait_send()
    for kind in range(2):
        op_copy(kind, False).wait_send()
    grads_out.sent(go, 0)

    @pl.when(section == 0)
    def _():
        grads_out.arrived(go)

    for gather in gathers:
        gather.sent()
    for copy in writes:
        copy.wait()


def run_sums(gain_sums, gain_attn, operands, kept, weights, ends_shape):
    nf, inner, gg, gu, br, la, ra, nr, kvg = operands
    act, kv, o_raw, cos_sin, allowed, qd, gm = kept
    depth, width = nf.shape
    rows = act.shape[0]
    ff, half = inner.shape[1], gg.shape[1]
    per, deep = width // RANKS, ff // RANKS
    part = (per // 2 + 15) // 16 * 16
    quarter, fine = half // 2, deep // 2
    columns = br.shape[1]
    wide_t = width // 128 * 128 + 128 + kvg.shape[1]
    vmem, hbm = pl.BlockSpec(memory_space=pltpu.VMEM), pl.BlockSpec(memory_space=pl.ANY)
    out = lambda *shape: jax.ShapeDtypeStruct(shape, BF16)
    b = lambda *shape: pltpu.VMEM(shape, BF16)
    f = lambda *shape: pltpu.VMEM(shape, F32)
    like = lambda a: pltpu.VMEM(a.shape, a.dtype)
    sem = lambda *shape: pltpu.SemaphoreType.DMA(shape)
    return pl.pallas_call(
        sums_kernel,
        out_shape=[
            out(*ends_shape), out(2, per, wide_t), out(per, ff), out(per, ff), out(deep, 2 * columns),
        ],
        in_specs=[hbm, vmem] + [hbm] * 19,
        out_specs=[hbm] * 5,
        scratch_shapes=[
            b(depth, width), b(depth, deep), b(depth, columns), b(depth, half), b(depth, half),
            b(depth, width), b(depth, kvg.shape[1]),
            b(width, depth), b(2 * width, depth), b(deep, depth), f(width, 128),
            like(act), like(kv), like(o_raw), like(cos_sin), like(allowed), like(qd), like(gm),
            like(weights[0]), b(2 * weights[1].shape[0], width),
            b(rows, width), b(2, rows, width), like(kv), b(KEY_VALUE_HEADS, 3 * rows, 128), b(rows, KEY_VALUE_HEADS * 128),
            f(rows, width), f(128, width),
            b(RANKS - 1, deep, columns), b(5, deep, columns), f(2, fine // 2, columns),
            b(2, fine // 2, columns), b(2, fine // 2, columns), b(2, fine // 4, columns), b(2, fine // 4, columns),
            b(2, 2, per, quarter), b(2, RANKS, per, quarter),
            b(2, 2, part, quarter), b(2, RANKS, part, quarter), b(2, RANKS, part, quarter), b(2, 5, part, quarter),
            b(RANKS, part, wide_t), b(RANKS, part, wide_t),
            b(RANKS, part // 2, wide_t), b(RANKS, part // 2, wide_t), b(RANKS, part // 2, wide_t), b(5, part // 2, wide_t),
            b(2, 2, 4, fine // 4, columns), b(2, 2, 4, part, quarter), b(2, 4, part // 2, wide_t),
            sem(10), sem(7), sem(5, KEY_VALUE_HEADS), sem(2, KEY_VALUE_HEADS), sem(3, KEY_VALUE_HEADS), sem(2), sem(2), sem(2), sem(2), sem(2),
            sem(3, 2), sem(5, 2), sem(2), sem(2), sem(2), sem(2),
            sem(2, 2), sem(2, 4), sem(2, 2), sem(2, 4), sem(2, 3), sem(2, 5),
            sem(4), sem(4), sem(4), sem(4), sem(3), sem(5),
            sem(5, 8), sem(5, 4), sem(5, 4), sem(40),
        ],
        compiler_params=pltpu.CompilerParams(
            collective_id=2, has_side_effects=True, vmem_limit_bytes=61 * 2**20
        ),
        name="sums",
    )(gain_sums, gain_attn, *operands, *kept, *weights)


def finish_kernel(
    acts_h, first_h, second_h, t_h, gate_h, up_h, down_h,
    acts_o, grads_o, q_o, out_o, key_o, value_o, gain_a, gain_f, gate_o, up_o, down_o,
    row_v, t_v, gate_v, down_v, q_f, kv_f, gate_f, down_f, load, store,
):
    width = q_f.shape[2]
    loads = [
        pltpu.make_async_copy(h, v, load.at[i])
        for i, (h, v) in enumerate(
            [(gate_h, gate_v.at[0]), (up_h, gate_v.at[1]), (down_h, down_v), (t_h, t_v), (acts_h, row_v.at[0])]
        )
    ]
    stores = [
        pltpu.make_async_copy(v, h, store.at[i])
        for i, (v, h) in enumerate(
            [(row_v.at[0], acts_o), (row_v.at[1], grads_o), (gate_f.at[0], gate_o), (gate_f.at[1], up_o),
             (down_f, down_o), (q_f.at[0], q_o), (q_f.at[1], out_o), (kv_f.at[0], key_o), (kv_f.at[1], value_o)]
        )
    ]
    section = lax.axis_index("section")
    for copy in loads[:4]:
        copy.start()
    for k in range(2):
        loads[k].wait()
        gate_f[k] = gate_v[k].astype(F32)
        stores[2 + k].start()
    loads[4].start()
    start_if(
        section == 0,
        lambda: pltpu.make_async_copy(first_h, row_v.at[1], load.at[5]),
        lambda: pltpu.make_async_copy(second_h, row_v.at[1], load.at[5]),
    )
    loads[2].wait()
    for at, size in tiles(width, 128):
        down_f[at : at + size, :] = down_v[:, at : at + 128].astype(F32).T[:size]
    stores[4].start()
    loads[3].wait()
    for core in range(2):
        q_f[core] = t_v[core, :, :width].astype(F32)
        stores[5 + core].start()
    pairs_at = width // 128 * 128 + 128
    half = KEY_VALUE_HEADS // 2 + 1
    for g in range(KEY_VALUE_HEADS):
        core = 0 if g < half else 1
        at = pairs_at + (g - core * (KEY_VALUE_HEADS - half)) * 128
        block = t_v[core, :, at : at + 128].astype(F32).T
        kv_f[0, g * HEAD_SIZE : (g + 1) * HEAD_SIZE, :] = block[:HEAD_SIZE]
        kv_f[1, g * HEAD_SIZE : (g + 1) * HEAD_SIZE, :] = block[HEAD_SIZE:]
    for copy in stores[7:]:
        copy.start()
    tail = slice(pairs_at - 128, pairs_at)
    both = t_v[0, :, tail].astype(F32) + t_v[1, :, tail].astype(F32)
    row = width % 128
    gain_rows = both.T
    gain_a[...] = gain_rows[row]
    gain_f[...] = gain_rows[row + 1]
    loads[4].wait()
    stores[0].start()
    pltpu.make_async_copy(first_h, row_v.at[1], load.at[5]).wait()
    stores[1].start()
    for copy in stores:
        copy.wait()


def run_finish(acts, grads_first, grads_second, t_sum, gate, up, down, width):
    per, ff = gate.shape
    vmem, hbm = pl.BlockSpec(memory_space=pltpu.VMEM), pl.BlockSpec(memory_space=pl.ANY)
    out = lambda *shape: jax.ShapeDtypeStruct(shape, F32)
    kv_rows = KEY_VALUE_HEADS * HEAD_SIZE
    return pl.pallas_call(
        finish_kernel,
        out_shape=[
            jax.ShapeDtypeStruct(acts.shape, BF16), jax.ShapeDtypeStruct(acts.shape, BF16),
            out(per, width), out(per, width), out(kv_rows, per), out(kv_rows, per), out(per), out(per),
            out(per, ff), out(per, ff), out(width, down.shape[0]),
        ],
        in_specs=[hbm] * 7,
        out_specs=[hbm] * 6 + [vmem] * 2 + [hbm] * 3,
        scratch_shapes=[
            pltpu.VMEM((2, *acts.shape), BF16), pltpu.VMEM(t_sum.shape, BF16), pltpu.VMEM((2, per, ff), BF16), pltpu.VMEM(down.shape, BF16),
            pltpu.VMEM((2, per, width), F32), pltpu.VMEM((2, kv_rows, per), F32),
            pltpu.VMEM((2, per, ff), F32), pltpu.VMEM((width, down.shape[0]), F32),
            pltpu.SemaphoreType.DMA((6,)), pltpu.SemaphoreType.DMA((9,)),
        ],
        compiler_params=pltpu.CompilerParams(vmem_limit_bytes=61 * 2**20),
        name="finish",
    )(acts, grads_first, grads_second, t_sum, gate, up, down)


def sums_by_xla(gain_sums, operands):
    nf, inner, gg, gu, br, la, ra, nr, kvg = operands
    width = nf.shape[1]

    def reduced(left, right):
        total = dot_lt(left, right).astype(BF16)
        piece = lax.psum_scatter(total, "dp", scatter_dimension=0, tiled=True)
        return lax.psum(piece, "ctx")

    def both(piece, axis):
        return lax.all_gather(piece, "section", axis=axis, tiled=axis > 0).astype(F32)

    attn = both(reduced(la, ra), 0)
    gain_sum = lax.psum(gain_sums[:2], ("section", "ctx"))
    return (
        attn[0],
        attn[1],
        both(reduced(nr, kvg), 0),
        lax.psum_scatter(gain_sum, "dp", scatter_dimension=1, tiled=True),
        both(reduced(nf, gg), 1),
        both(reduced(nf, gu), 1),
        both(reduced(inner, br), 1)[:, :width],
    )


def shards(
    ends,
    doc_lengths,
    w_query,
    key_projection_weight,
    value_projection_weight,
    w_out,
    w_gate,
    w_up,
    w_down,
    gain_attn,
    gain_ffn,
):
    width = ends.shape[3]
    half = HEAD_SIZE // 2
    turns = np.float32(10000.0) ** (
        np.float32(-2.0) * (np.arange(128) % half).astype(np.float32) / np.float32(HEAD_SIZE)
    )
    weights = (
        w_query,
        key_projection_weight.T,
        value_projection_weight.T,
        w_out,
        w_gate,
        w_up,
        w_down.T,
    )
    ff = w_gate.shape[1]
    fits = lax.axis_size("dp") == RANKS and width % 64 == 0 and ff % 1280 == 0
    acts, grads_in, gain_sums, *kept = run_layers(
        doc_lengths,
        ends,
        jnp.asarray(turns.reshape(1, 128), F32),
        gain_attn,
        gain_ffn,
        weights,
        not fits,
    )
    operands = kept[:9]
    if fits:
        grads_first, *sums = run_sums(
            gain_sums, gain_attn, operands, kept[9:], weights[:3], ends.shape
        )
        acts, grads_in, grad_query, grad_out, grad_key, grad_value, *gain_piece, grad_gate, grad_up, grad_down = (
            run_finish(acts, grads_first, grads_in, *sums, width)
        )
        grad_key, grad_value, grad_down = grad_key.T, grad_value.T, grad_down.T
    else:
        grad_query, grad_out, kv_parts, gain_piece, grad_gate, grad_up, grad_down = sums_by_xla(
            gain_sums, operands
        )
        kv_grad = jnp.concatenate([kv_parts[0], kv_parts[1][:, 128:]], axis=1).reshape(
            -1, KEY_VALUE_HEADS, 2, HEAD_SIZE
        )
        grad_key = kv_grad[:, :, 0].reshape(kv_grad.shape[0], -1)
        grad_value = kv_grad[:, :, 1].reshape(kv_grad.shape[0], -1)
    return (
        acts,
        grads_in,
        grad_query,
        grad_key,
        grad_value,
        grad_out,
        grad_gate,
        grad_up,
        grad_down,
        gain_piece[0],
        gain_piece[1],
    )


def solution(mesh):
    return jax.shard_map(
        shards,
        mesh=mesh,
        in_specs=(P("section", None, ("dp", "ctx"), None), P(None, "dp", None)) + (P(),) * 9,
        out_specs=(P("section", None, ("dp", "ctx"), None),) * 2
        + (P("dp", None),) * 7
        + (P("dp"),) * 2,
        check_vma=False,
    )
```
